32 devices in a mesh: section: 4 (over y, x), batch: 8 (over z, core).
Axes of the slice: x: 2, y: 2, z: 4, core: 2. Of those that a mesh axis runs over, the one named last changes fastest.
Arguments:
- tokens: bfloat16 [4096, 1024], P('batch'), may hold values from -6 to 6
- cotangent: bfloat16 [4096, 1024], P('batch'), may hold values from -6 to 6
- params: bfloat16 [4, 8455168], P('section'), may hold values from -4 to 4
- lengths: int32 [8, 2, 4], P('batch'), may hold values from 1 to 160, 256 in all within a row
Outputs:
- activations: bfloat16 [4, 4096, 1024], P('section', 'batch')
- input_grads: float32 [4, 4096, 1024], P('section', 'batch')
- weight_grads: float32 [4, 8455168], P('section', 'batch')
The draws below stay inside these ranges and needn't reach their ends.
Inputs may be any that keep to these rules, and one draw needn't show every extreme that they name: Each row of lengths sums to 256, and its largest entry is exactly 160.
All inputs are finite; a program needn't handle non-finite values.
Results may differ from the reference program's by a relative error of at most 0.02.
Values may be sent and summed in bfloat16 or wider, within the bound.
A program may use at most 448 MiB of HBM per device.

```python
import math
import jax
import jax.numpy as jnp
import numpy as np
from jax import lax

D = 1024
FF = 2752
HEADS = 16
FEAT = 16
WIN = 64
MICRO = 2
DOCS = 4
MB_TOK = 256
GROUPS = 8
TOKENS = 4096
PARAMS = 8455168
N_SECTION = 4
N_BATCH = 8


def steps_of(stream_key, extent, split, low, largest):
    def one(dim, blocks):
        steps = jax.random.uniform(jax.random.fold_in(jax.random.fold_in(stream_key, 6), dim), (blocks,), jnp.float32, low / len(split), largest / len(split))
        return jnp.repeat(jnp.exp(steps), extent[dim] // blocks).reshape((-1,) + (1,) * (len(extent) - dim - 1))

    level = one(*split[0])
    for cut in split[1:]:
        level = level * one(*cut)
    return level


def profile(count, total, limit, lean):
    portions = [(1 << 20) // math.isqrt(grade ** lean) + 1 for grade in range(2, count + 1)]
    spare, holding = total - limit - (count - 1), [1] * (count - 1)
    while spare > 0:
        movable = [i for i in range(count - 1) if holding[i] < limit]
        whole, budget = sum([portions[i] for i in movable]), spare
        for i in movable:
            more = min(limit - holding[i], max(1, budget * portions[i] // whole), spare)
            holding[i] = holding[i] + more
            spare = spare - more
    return np.array([limit] + holding)


def uneven(own_key, amount, total, reach, lean):
    if amount == 2:
        one = jax.random.randint(own_key, (), max(1, total - reach), min(reach, total - 1) + 1)
        return jnp.stack([one, total - one])
    sizes = jnp.asarray(profile(amount, total, reach, lean), jnp.int32)
    twos = (amount - 1) // 2
    giver, sink = sizes[1:1 + 2 * twos:2], sizes[2:2 + 2 * twos:2]
    room = jnp.minimum(giver - 1, reach - sink)
    moved = jax.random.randint(jax.random.fold_in(own_key, 1), (twos,), 0, 1 << 20) % (room + 1)
    sizes = sizes.at[1:1 + 2 * twos:2].set(giver - moved).at[2:2 + 2 * twos:2].set(sink + moved)
    return sizes[jax.random.permutation(jax.random.fold_in(own_key, 2), amount)]


def normal_values(key, dims, width, limit, split=(), held_as=jnp.bfloat16):
    factor_of = steps_of(key, dims, split, -0.22, 0.18) if split else 1.0
    result = jax.random.normal(key, dims, jnp.float32) * width * factor_of
    return jnp.minimum(jnp.maximum(result, -limit), limit).astype(held_as)


def setup_inputs(seed: int = 0) -> dict:
    splits = jax.random.split(jax.random.key(seed), 5)
    return {
        "tokens": normal_values(splits[0], (TOKENS, D), 1.0, 6.0, ((0, 8),)),
        "cotangent": normal_values(splits[1], (TOKENS, D), 1.0, 6.0, ((0, 8),)),
        "params": normal_values(splits[2], (N_SECTION, PARAMS), 1.0, 4.0, ((0, 4),)),
        "lengths": jax.vmap(lambda own: uneven(own, DOCS, MB_TOK, MB_TOK * 5 // 8, 2))(jax.random.split(splits[3], GROUPS * MICRO)).reshape((GROUPS, MICRO, DOCS)).astype(jnp.int32),
    }


@jax.custom_vjp
def low(v):
    return lax.optimization_barrier(v.astype(jnp.bfloat16)).astype(jnp.float32)

@jax.custom_vjp
def low_back(v):
    return v

def low_keep(v):
    return (low(v), None)

def low_pass(kept, grad):
    return (grad,)

def back_keep(v):
    return (v, None)

def back_low(kept, grad):
    return (low(grad),)
low.defvjp(low_keep, low_pass)
low_back.defvjp(back_keep, back_low)
EPSILON = 1e-06
HIGHEST = lax.Precision.HIGHEST

def matmul(left, right):
    return jnp.dot(left, right, precision=HIGHEST)

def unpack(flat, shapes):
    pieces = []
    offset = 0
    for row_count, col_count in shapes:
        pieces.append(flat[offset:offset + row_count * col_count].reshape(row_count, col_count))
        offset += row_count * col_count
    return pieces

def linear_shapes():
    return [(1, D), (D, HEADS * FEAT), (D, HEADS * FEAT), (D, D), (D, D)]

def window_shapes():
    return [(1, D), (D, D), (D, D), (D, D), (D, D)]

def feed_shapes():
    return [(1, D), (D, FF), (D, FF), (FF, D)]

def doc_masks(doc_lengths, length, window):
    positions = jnp.arange(length, dtype=jnp.int32)
    doc_ends = jnp.cumsum(doc_lengths).astype(jnp.int32)
    doc_ids = lax.optimization_barrier(jnp.sum((positions[:, None] >= doc_ends[None, :]).astype(jnp.int32), axis=1))
    causal = positions[None, :] <= positions[:, None]
    same_doc = (doc_ids[:, None] == doc_ids[None, :]) & causal
    nearby = same_doc & (positions[:, None] - positions[None, :] < window)
    return (same_doc, nearby)

def rms_norm(values, gain_raw):
    scaled = lax.rsqrt(lax.optimization_barrier(jnp.mean(values * values, axis=1, keepdims=True)) + EPSILON)
    return values * scaled * (1.0 + gain_raw / 8.0)

def attention_section(inputs, flat, shapes, mask, taylor, out_scale):
    gain_raw, w_query, w_key, w_value, w_out = unpack(flat, shapes)
    scale = 1.0 / math.sqrt(D)
    length = inputs.shape[0]
    key_width = w_query.shape[1] // HEADS
    normed = low(rms_norm(inputs, gain_raw))
    queries = low_back(low(matmul(normed, w_query) * scale)).reshape(length, HEADS, key_width)
    key_rows = low_back(low(matmul(normed, w_key) * scale)).reshape(length, HEADS, key_width)
    value_rows = low_back(low(matmul(normed, w_value) * scale)).reshape(length, HEADS, D // HEADS)
    scores = low_back(jnp.einsum('ihe,jhe->hij', queries, key_rows, precision=HIGHEST) / math.sqrt(key_width))
    if taylor:
        weighted = jnp.where(mask[None], 1.0 + scores + 0.5 * scores * scores, 0.0)
        weights = low(weighted / lax.optimization_barrier(jnp.sum(weighted, axis=2, keepdims=True)))
    else:
        masked = jnp.where(mask[None], scores, -jnp.inf)
        top_score = lax.optimization_barrier(jnp.max(masked, axis=2, keepdims=True))
        expo = jnp.exp(masked - top_score)
        weights = low(expo / lax.optimization_barrier(jnp.sum(expo, axis=2, keepdims=True)))
    mixed = jnp.einsum('hij,jhe->ihe', weights, value_rows, precision=HIGHEST).reshape(length, D)
    mixed = low_back(low(mixed))
    branch = low_back(matmul(mixed, w_out) * (out_scale * scale))
    return inputs + branch

def feed_section(inputs, flat):
    gain_raw, w_gate, w_up, w_down = unpack(flat, feed_shapes())
    scale = 1.0 / math.sqrt(D)
    normed = low(rms_norm(inputs, gain_raw))
    gate_act = low_back(matmul(normed, w_gate) * scale)
    up_act = low_back(matmul(normed, w_up) * scale)
    hidden = low(jax.nn.silu(gate_act) * up_act)
    branch = low_back(matmul(hidden, w_down) * scale)
    return inputs + branch

def block(tokens_block, extras, params_f32, doc_lengths):
    same_doc, nearby = doc_masks(doc_lengths, tokens_block.shape[0], WIN)
    first = low_back(low(attention_section(tokens_block + extras[0], params_f32[0], linear_shapes(), same_doc, True, 8.0)))
    second = low_back(low(feed_section(first + extras[1], params_f32[1])))
    third = low_back(low(attention_section(second + extras[2], params_f32[2], window_shapes(), nearby, False, 4.0)))
    fourth = low_back(low(feed_section(third + extras[3], params_f32[3])))
    return (fourth, jnp.stack([first, second, third, fourth]))

def reference(tokens, cotangent, params, lengths):
    block_count = N_BATCH * MICRO
    token_blocks = tokens.astype(jnp.float32).reshape(block_count, MB_TOK, D)
    tangent_blocks = cotangent.astype(jnp.float32).reshape(block_count, MB_TOK, D)
    doc_blocks = lengths.reshape(block_count, DOCS)
    params_f32 = params.astype(jnp.float32)
    extras = jnp.zeros((block_count, 4, MB_TOK, D), jnp.float32)

    def forward(weights_all, extras_all):

        def one_block(block_items):
            return jax.checkpoint(block)(block_items[0], block_items[1], weights_all, block_items[2])
        return lax.map(one_block, (token_blocks, extras_all, doc_blocks))
    outputs, pullback, section_outs = jax.vjp(forward, params_f32, extras, has_aux=True)
    weight_grads, extra_grads = pullback(tangent_blocks)
    activations = section_outs.transpose(1, 0, 2, 3).reshape(4, block_count * MB_TOK, D).astype(jnp.bfloat16)
    input_grads = extra_grads.transpose(1, 0, 2, 3).reshape(4, block_count * MB_TOK, D)
    return (activations, input_grads, weight_grads)
```

```python
import functools
import math

import jax
import jax.numpy as jnp
from jax import lax
from jax.experimental import pallas as pl
from jax.experimental.pallas import tpu as pltpu
from jax.sharding import PartitionSpec as P

D = 1024
FF = 2752
FP = 2816
HEADS = 16
FEAT = 16
WIN = 64
MICRO = 2
LEN = 256
EPSILON = 1e-06
SCALE = 1.0 / math.sqrt(D)
LINEAR, FEED, WINDOW, FEED2 = 0, 1, 2, 3
MIB = 2**20
MESH = pl.DeviceIdType.MESH
BF = jnp.bfloat16
F32 = jnp.float32


def any_spec():
    return pl.BlockSpec(memory_space=pl.ANY)


def vmem_spec():
    return pl.BlockSpec(memory_space=pltpu.VMEM)


def dot(left, right):
    return jnp.dot(left, right, preferred_element_type=F32)


def dot_t(left, right):
    return lax.dot_general(left, right, (((1,), (1,)), ((), ())), preferred_element_type=F32)


def dot_0(left, right):
    return lax.dot_general(left, right, (((0,), (0,)), ((), ())), preferred_element_type=F32)


def at256(index):
    return pl.ds(pl.multiple_of(index * 256, 256), 256)


def is_feed(section):
    return (section == FEED) | (section == FEED2)


PAIR_STEP = 32 * FF
ROW_STEP = 64 * D


def prepare_kernel(flat, wide, tall, chunk, blocks, woven, stage_pair, stage_row, stage_low, load_sem, store_sem):
    section = lax.axis_index("section")

    def run(steps, count, source, target, stage, work):
        def load(i, slot):
            return pltpu.make_async_copy(
                flat.at[:, pl.ds(pl.multiple_of(source(i), 1024), count)],
                chunk.at[slot, :, pl.ds(0, count)],
                load_sem.at[slot],
            )

        def store(i, slot):
            return pltpu.make_async_copy(stage.at[slot], target(i), store_sem.at[slot])

        load(0, 0).start()

        def step(i, carry):
            slot = lax.rem(i, 2)

            @pl.when(i + 1 < steps)
            def _():
                load(i + 1, 1 - slot).start()

            load(i, slot).wait()

            @pl.when(i >= 2)
            def _():
                store(i - 2, slot).wait()

            rows = count // 128
            blocks[pl.ds(0, rows), :] = chunk[slot, :, pl.ds(0, count)].astype(F32).reshape(rows, 128)
            work(slot)
            store(i, slot).start()
            return carry

        lax.fori_loop(0, steps, step, 0)
        store(steps - 2, steps % 2).wait()
        store(steps - 1, (steps - 1) % 2).wait()

    def pair_work(slot):
        low_half = lax.broadcasted_iota(jnp.int32, (16, 128), 1) < 64
        rolled = None
        for c in range(22):
            even = blocks[pl.ds(c, 16, stride=43), :]
            if c == 21:
                even = jnp.where(low_half, even, 0.0)
            if rolled is None:
                rolled = pltpu.roll(blocks[pl.ds(21, 16, stride=43), :], 64, 1)
            if c < 21:
                after = pltpu.roll(blocks[pl.ds(22 + c, 16, stride=43), :], 64, 1)
                odd = jnp.where(low_half, rolled, after)
                rolled = after
            else:
                odd = jnp.where(low_half, rolled, 0.0)
            woven[c, pl.ds(0, 16, stride=2), :] = even
            woven[c, pl.ds(1, 16, stride=2), :] = odd
        for c in range(22):
            stage_pair[slot, :, pl.ds(128 * c, 128)] = woven[c].astype(BF)

    def row_work(slot):
        for c in range(8):
            stage_row[slot, :, pl.ds(128 * c, 128)] = blocks[pl.ds(c, 64, stride=8), :].astype(BF)

    def low_work(slot):
        for c in range(2):
            stage_low[slot, :, pl.ds(128 * c, 128)] = blocks[pl.ds(c, 256, stride=2), :].astype(BF)

    def rows_of(index, count):
        return pl.ds(pl.multiple_of(index * count, count), count)

    def square(first, target):
        run(16, ROW_STEP, lambda i: D + first + i * ROW_STEP, target, stage_row, row_work)

    @pl.when(is_feed(section))
    def _():
        run(
            64,
            PAIR_STEP,
            lambda i: D + i * PAIR_STEP,
            lambda i: wide.at[i // 32, rows_of(lax.rem(i, 32), 32), :],
            stage_pair,
            pair_work,
        )
        run(
            43,
            ROW_STEP,
            lambda i: D + 2 * D * FF + i * ROW_STEP,
            lambda i: tall.at[rows_of(i, 64), :],
            stage_row,
            row_work,
        )
        stage_row[0] = jnp.zeros((64, D), BF)
        last = pltpu.make_async_copy(stage_row.at[0], tall.at[pl.ds(FF, 64), :], store_sem.at[0])
        last.start()
        last.wait()

    @pl.when(section == WINDOW)
    def _():
        square(0, lambda i: wide.at[0, rows_of(i, 64), pl.ds(0, D)])
        square(D * D, lambda i: wide.at[0, rows_of(i, 64), pl.ds(D, D)])
        square(2 * D * D, lambda i: wide.at[1, rows_of(i, 64), pl.ds(0, D)])
        square(3 * D * D, lambda i: tall.at[rows_of(i, 64), :])

    @pl.when(section == LINEAR)
    def _():
        width = HEADS * FEAT
        for part in range(2):
            run(
                4,
                ROW_STEP,
                lambda i, part=part: D + part * D * width + i * ROW_STEP,
                lambda i, part=part: wide.at[0, rows_of(i, 256), pl.ds(part * width, width)],
                stage_low,
                low_work,
            )
        square(2 * D * width, lambda i: wide.at[1, rows_of(i, 64), pl.ds(0, D)])
        square(2 * D * width + D * D, lambda i: tall.at[rows_of(i, 64), :])


def prepare(flat):
    return pl.pallas_call(
        prepare_kernel,
        out_shape=(jax.ShapeDtypeStruct((2, D, FP), BF), jax.ShapeDtypeStruct((FP, D), BF)),
        in_specs=[any_spec()],
        out_specs=(any_spec(), any_spec()),
        scratch_shapes=[
            pltpu.VMEM((2, 1, PAIR_STEP), BF),
            pltpu.VMEM((PAIR_STEP // 128, 128), F32),
            pltpu.VMEM((22, 32, 128), F32),
            pltpu.VMEM((2, 32, FP), BF),
            pltpu.VMEM((2, 64, D), BF),
            pltpu.VMEM((2, 256, 256), BF),
            pltpu.SemaphoreType.DMA((2,)),
            pltpu.SemaphoreType.DMA((2,)),
        ],
        compiler_params=pltpu.CompilerParams(vmem_limit_bytes=32 * MIB),
        name="prepare",
    )(flat)


def lane_of_head(section_kind, block, half):
    lanes = lax.broadcasted_iota(jnp.int32, (1, 128), 1)
    if section_kind == WINDOW:
        return lanes // 64 == half
    return lanes // FEAT == lax.rem(2 * block + half, 8)


def lane_of_value(half):
    return lax.broadcasted_iota(jnp.int32, (1, 128), 1) // 64 == half


def only(mask, values):
    return jnp.where(mask, values, jnp.zeros_like(values))


def query_block(section_kind, block):
    index = block if section_kind == WINDOW else block // 4
    return pl.ds(pl.multiple_of(index * 128, 128), 128)


def key_block(section_kind, block):
    first = D if section_kind == WINDOW else HEADS * FEAT
    index = block if section_kind == WINDOW else block // 4
    return pl.ds(pl.multiple_of(first + index * 128, 128), 128)


def value_block(block, first=0):
    return pl.ds(pl.multiple_of(first + block * 128, 128), 128)


def mask_of(section_kind, doc_col, doc_row):
    rows = lax.broadcasted_iota(jnp.int32, (LEN, LEN), 0)
    cols = lax.broadcasted_iota(jnp.int32, (LEN, LEN), 1)
    mask = (doc_col == doc_row) & (cols <= rows)
    if section_kind == WINDOW:
        mask = mask & (rows - cols < WIN)
    return mask.astype(F32)


def root_of(section_kind):
    return 1.0 / math.sqrt(D // HEADS if section_kind == WINDOW else FEAT)


def weigh(section_kind, scores, mask):
    if section_kind == WINDOW:
        kept = jnp.where(mask > 0.0, scores, -1e30)
        raised = jnp.exp(kept - jnp.max(kept, axis=1, keepdims=True))
        raised = raised * mask
        inverse = 1.0 / jnp.sum(raised, axis=1, keepdims=True)
        return raised * inverse, inverse
    raised = mask * (1.0 + scores + 0.5 * scores * scores)
    inverse = 1.0 / jnp.sum(raised, axis=1, keepdims=True)
    return raised * inverse, inverse


def unweigh(section_kind, scores, mask, weights, inverse, d_weights):
    centred = d_weights - jnp.sum(d_weights * weights, axis=1, keepdims=True)
    if section_kind == WINDOW:
        return weights * centred
    return centred * inverse * (mask * (1.0 + scores))


def out_scale(section_kind):
    return {LINEAR: 8.0, WINDOW: 4.0, FEED: 1.0}[section_kind] * SCALE


def load_weights(section, wide, tall, wide_v, tall_v, sems):
    def copies(kind):
        if kind == FEED:
            return [
                pltpu.make_async_copy(wide, wide_v, sems.at[0]),
                pltpu.make_async_copy(tall, tall_v, sems.at[1]),
            ]
        first = 2 * D if kind == WINDOW else 2 * HEADS * FEAT
        return [
            pltpu.make_async_copy(wide.at[0, :, pl.ds(0, first)], wide_v.at[0, :, pl.ds(0, first)], sems.at[0]),
            pltpu.make_async_copy(wide.at[1, :, pl.ds(0, D)], wide_v.at[1, :, pl.ds(0, D)], sems.at[1]),
            pltpu.make_async_copy(tall.at[pl.ds(0, D), :], tall_v.at[pl.ds(0, D), :], sems.at[2]),
        ]

    def each(act):
        for kind, here in ((FEED, is_feed(section)), (WINDOW, section == WINDOW), (LINEAR, section == LINEAR)):

            @pl.when(here)
            def _(kind=kind):
                for copy in copies(kind):
                    act(copy)

    each(lambda copy: copy.start())
    return lambda: each(lambda copy: copy.wait())


def forward_kernel(
    tokens, flat, wide, tall, doc_col, doc_row,
    acts, inputs, normed, first, second,
    wide_v, tall_v, gain_v, z_v, h_v, x_v, first_v, second_v, mid_v, mask_v,
    weight_sem, gain_sem, in_sem, out_sem, send_sem, recv_sem,
):
    section = lax.axis_index("section")
    batch = lax.axis_index("batch")
    last = lax.axis_size("section") - 1
    barrier = pltpu.get_barrier_semaphore()

    @pl.when(section > 0)
    def _():
        pl.semaphore_signal(barrier, inc=1, device_id=(section - 1, batch), device_id_type=MESH)

    @pl.when(section < last)
    def _():
        pl.semaphore_signal(barrier, inc=1, device_id=(section + 1, batch), device_id_type=MESH)

    gain_copy = pltpu.make_async_copy(flat.at[:, pl.ds(0, D)], gain_v, gain_sem)
    gain_copy.start()
    wait_weights = load_weights(section, wide, tall, wide_v, tall_v, weight_sem)

    def rows_at(micro):
        return pl.ds(micro * LEN, LEN)

    def token_copy(micro):
        return pltpu.make_async_copy(tokens.at[rows_at(micro), :], z_v.at[micro], in_sem.at[micro])

    @pl.when(section == 0)
    def _():
        for micro in range(MICRO):
            token_copy(micro).start()

    pl.semaphore_wait(barrier, jnp.where((section > 0) & (section < last), 2, 1))
    gain_copy.wait()
    wait_weights()
    gain = 1.0 + gain_v[...].astype(F32) / 8.0

    def hand_on(micro):
        return pltpu.make_async_remote_copy(
            src_ref=x_v.at[micro],
            dst_ref=z_v.at[micro],
            send_sem=send_sem.at[micro],
            recv_sem=recv_sem.at[micro],
            device_id=(section + 1, batch),
            device_id_type=MESH,
        )

    def norm(micro):
        z = z_v[micro].astype(F32)
        scaled = lax.rsqrt(jnp.mean(z * z, axis=1, keepdims=True) + EPSILON)
        h_v[micro] = (z * scaled * gain).astype(BF)

    def finish(micro, source, depth, scale):
        def tile(n, carry):
            cols = at256(n)
            branch = dot(source[:, pl.ds(0, depth)], tall_v[pl.ds(0, depth), cols]) * scale
            x_v[micro, :, cols] = (z_v[micro, :, cols].astype(F32) + branch).astype(BF)
            return carry

        lax.fori_loop(0, D // 256, tile, 0)

    def feed(micro):
        def tile(t, carry):
            cols = at256(t)
            gate = dot(h_v[micro], wide_v[0, :, cols]) * SCALE
            up = dot(h_v[micro], wide_v[1, :, cols]) * SCALE
            first_v[micro, :, cols] = gate.astype(BF)
            second_v[micro, :, cols] = up.astype(BF)
            mid_v[:, cols] = (gate / (1.0 + jnp.exp(-gate)) * up).astype(BF)
            return carry

        lax.fori_loop(0, FP // 256, tile, 0)
        finish(micro, mid_v, FP, SCALE)

    def attend(micro, kind):
        def project(which, count, target):
            def tile(t, carry):
                cols = at256(t)
                target[micro, :, cols] = (dot(h_v[micro], wide_v[which, :, cols]) * SCALE).astype(BF)
                return carry

            lax.fori_loop(0, count, tile, 0)

        project(0, 8 if kind == WINDOW else 2, first_v)
        project(1, 4, second_v)
        mask_v[...] = mask_of(kind, doc_col[micro], doc_row[micro])

        def block(t, carry):
            queries = first_v[micro, :, query_block(kind, t)]
            keys = first_v[micro, :, key_block(kind, t)]
            values = second_v[micro, :, value_block(t)]
            mixed = jnp.zeros((LEN, 128), F32)
            for half in range(2):
                scores = dot_t(only(lane_of_head(kind, t, half), queries), keys) * root_of(kind)
                weights, _ = weigh(kind, scores, mask_v[...])
                mixed += dot(weights.astype(BF), only(lane_of_value(half), values))
            second_v[micro, :, value_block(t, D)] = mixed.astype(BF)
            mid_v[:, value_block(t)] = mixed.astype(BF)
            return carry

        lax.fori_loop(0, 8, block, 0)
        finish(micro, mid_v, D, out_scale(kind))

    def outs(micro):
        rows = rows_at(micro)
        return [
            pltpu.make_async_copy(x_v.at[micro], acts.at[rows, :], out_sem.at[micro, 0]),
            pltpu.make_async_copy(z_v.at[micro], inputs.at[rows, :], out_sem.at[micro, 1]),
            pltpu.make_async_copy(h_v.at[micro], normed.at[rows, :], out_sem.at[micro, 2]),
            pltpu.make_async_copy(first_v.at[micro], first.at[rows, :], out_sem.at[micro, 3]),
            pltpu.make_async_copy(second_v.at[micro], second.at[rows, :], out_sem.at[micro, 4]),
        ]

    for micro in range(MICRO):

        @pl.when(section == 0)
        def _(micro=micro):
            token_copy(micro).wait()

        @pl.when(section > 0)
        def _(micro=micro):
            hand_on(micro).wait_recv()

        norm(micro)

        @pl.when(is_feed(section))
        def _(micro=micro):
            feed(micro)

        @pl.when(section == WINDOW)
        def _(micro=micro):
            attend(micro, WINDOW)

        @pl.when(section == LINEAR)
        def _(micro=micro):
            attend(micro, LINEAR)

        @pl.when(section < last)
        def _(micro=micro):
            hand_on(micro).start()

        for copy in outs(micro):
            copy.start()

    for micro in range(MICRO):

        @pl.when(section < last)
        def _(micro=micro):
            hand_on(micro).wait_send()

        for copy in outs(micro):
            copy.wait()


def forward(tokens, flat, wide, tall, doc_col, doc_row):
    count = MICRO * LEN
    return pl.pallas_call(
        forward_kernel,
        out_shape=(
            jax.ShapeDtypeStruct((count, D), BF),
            jax.ShapeDtypeStruct((count, D), BF),
            jax.ShapeDtypeStruct((count, D), BF),
            jax.ShapeDtypeStruct((count, FP), BF),
            jax.ShapeDtypeStruct((count, FP), BF),
        ),
        in_specs=[any_spec()] * 4 + [vmem_spec()] * 2,
        out_specs=(any_spec(),) * 5,
        scratch_shapes=[
            pltpu.VMEM((2, D, FP), BF),
            pltpu.VMEM((FP, D), BF),
            pltpu.VMEM((1, D), BF),
            pltpu.VMEM((MICRO, LEN, D), BF),
            pltpu.VMEM((MICRO, LEN, D), BF),
            pltpu.VMEM((MICRO, LEN, D), BF),
            pltpu.VMEM((MICRO, LEN, FP), BF),
            pltpu.VMEM((MICRO, LEN, FP), BF),
            pltpu.VMEM((LEN, FP), BF),
            pltpu.VMEM((LEN, LEN), F32),
            pltpu.SemaphoreType.DMA((3,)),
            pltpu.SemaphoreType.DMA,
            pltpu.SemaphoreType.DMA((MICRO,)),
            pltpu.SemaphoreType.DMA((MICRO, 5)),
            pltpu.SemaphoreType.DMA((MICRO,)),
            pltpu.SemaphoreType.DMA((MICRO,)),
        ],
        compiler_params=pltpu.CompilerParams(
            collective_id=0, has_side_effects=True, vmem_limit_bytes=56 * MIB
        ),
        name="forward",
    )(tokens, flat, wide, tall, doc_col, doc_row)


def backward_kernel(
    cotangent, flat, wide, tall, doc_col, doc_row, inputs, first, second,
    d_inputs, grads, d_first, d_second, middle, d_gain,
    wide_v, tall_v, gain_v, g_v, z_v, dz_v, back_v, first_v, second_v, d_first_v, d_second_v, mid_v, dh_v, mask_v,
    weight_sem, gain_sem, in_sem, out_sem, send_sem, recv_sem,
):
    section = lax.axis_index("section")
    batch = lax.axis_index("batch")
    last = lax.axis_size("section") - 1
    barrier = pltpu.get_barrier_semaphore()

    @pl.when(section > 0)
    def _():
        pl.semaphore_signal(barrier, inc=1, device_id=(section - 1, batch), device_id_type=MESH)

    @pl.when(section < last)
    def _():
        pl.semaphore_signal(barrier, inc=1, device_id=(section + 1, batch), device_id_type=MESH)

    gain_copy = pltpu.make_async_copy(flat.at[:, pl.ds(0, D)], gain_v, gain_sem)
    gain_copy.start()
    wait_weights = load_weights(section, wide, tall, wide_v, tall_v, weight_sem)

    def rows_at(micro):
        return pl.ds(micro * LEN, LEN)

    def loads(micro):
        rows = rows_at(micro)
        return [
            pltpu.make_async_copy(inputs.at[rows, :], z_v.at[micro], in_sem.at[micro, 0]),
            pltpu.make_async_copy(first.at[rows, :], first_v.at[micro], in_sem.at[micro, 1]),
            pltpu.make_async_copy(second.at[rows, :], second_v.at[micro], in_sem.at[micro, 2]),
        ]

    def tangent_copy(micro):
        return pltpu.make_async_copy(cotangent.at[rows_at(micro), :], g_v.at[micro], in_sem.at[micro, 3])

    for micro in range(MICRO):
        for copy in loads(micro):
            copy.start()

        @pl.when(section == last)
        def _(micro=micro):
            tangent_copy(micro).start()

    pl.semaphore_wait(barrier, jnp.where((section > 0) & (section < last), 2, 1))
    gain_copy.wait()
    wait_weights()
    gain = 1.0 + gain_v[...].astype(F32) / 8.0
    d_gain[...] = jnp.zeros_like(d_gain)

    def hand_back(micro):
        return pltpu.make_async_remote_copy(
            src_ref=back_v.at[micro],
            dst_ref=g_v.at[micro],
            send_sem=send_sem.at[micro],
            recv_sem=recv_sem.at[micro],
            device_id=(section - 1, batch),
            device_id_type=MESH,
        )

    def feed(micro):
        def tile(t, carry):
            cols = at256(t)
            d_mid = dot_t(g_v[micro], tall_v[cols, :]) * SCALE
            gate = first_v[micro, :, cols].astype(F32)
            up = second_v[micro, :, cols].astype(F32)
            sig = 1.0 / (1.0 + jnp.exp(-gate))
            silu = gate * sig
            d_first_v[micro, :, cols] = (d_mid * up * (sig * (1.0 + gate * (1.0 - sig)))).astype(BF)
            d_second_v[micro, :, cols] = (d_mid * silu).astype(BF)
            mid_v[micro, :, cols] = (silu * up).astype(BF)
            return carry

        lax.fori_loop(0, FP // 256, tile, 0)

        def back(n, carry):
            rows = at256(n)
            total = dot_t(d_first_v[micro], wide_v[0, rows, :])
            total += dot_t(d_second_v[micro], wide_v[1, rows, :])
            dh_v[:, rows] = total * SCALE
            return carry

        lax.fori_loop(0, D // 256, back, 0)

    def attend(micro, kind):
        width = 2 * D if kind == WINDOW else 2 * HEADS * FEAT

        def mix(t, carry):
            rows = at256(t)
            mid_v[micro, :, rows] = (dot_t(g_v[micro], tall_v[rows, :]) * out_scale(kind)).astype(BF)
            return carry

        lax.fori_loop(0, D // 256, mix, 0)
        mask_v[...] = mask_of(kind, doc_col[micro], doc_row[micro])

        def block(t, d_low):
            queries = first_v[micro, :, query_block(kind, t)]
            keys = first_v[micro, :, key_block(kind, t)]
            values = second_v[micro, :, value_block(t)]
            d_mixed = mid_v[micro, :, value_block(t)]
            d_values = jnp.zeros((LEN, 128), F32)
            d_queries, d_keys = d_low
            for half in range(2):
                mask = mask_v[...]
                head = lane_of_head(kind, t, half)
                own_queries = only(head, queries)
                own_keys = only(head, keys)
                own_mixed = only(lane_of_value(half), d_mixed)
                scores = dot_t(own_queries, keys) * root_of(kind)
                weights, inverse = weigh(kind, scores, mask)
                d_weights = dot_t(own_mixed, values)
                d_values += dot_0(weights.astype(BF), own_mixed)
                d_scores = unweigh(kind, scores, mask, weights, inverse, d_weights).astype(BF)
                d_queries += dot(d_scores, own_keys)
                d_keys += dot_0(d_scores, own_queries)
            d_second_v[micro, :, value_block(t)] = d_values.astype(BF)
            return d_queries, d_keys

        zero = jnp.zeros((LEN, 128), F32)

        def store(t, d_low):
            d_queries, d_keys = d_low
            d_first_v[micro, :, query_block(kind, t)] = (d_queries * root_of(kind)).astype(BF)
            d_first_v[micro, :, key_block(kind, t)] = (d_keys * root_of(kind)).astype(BF)

        if kind == WINDOW:

            def whole(t, carry):
                store(t, block(t, (zero, zero)))
                return carry

            lax.fori_loop(0, 8, whole, 0)
        else:

            def group(q, carry):
                store(4 * q, lax.fori_loop(0, 4, lambda i, low: block(4 * q + i, low), (zero, zero)))
                return carry

            lax.fori_loop(0, 2, group, 0)

        def back(n, carry):
            rows = at256(n)
            total = dot_t(d_first_v[micro, :, pl.ds(0, width)], wide_v[0, rows, pl.ds(0, width)])
            total += dot_t(d_second_v[micro, :, pl.ds(0, D)], wide_v[1, rows, pl.ds(0, D)])
            dh_v[:, rows] = total * SCALE
            return carry

        lax.fori_loop(0, D // 256, back, 0)

    def unnorm(micro):
        z = z_v[micro].astype(F32)
        scaled = lax.rsqrt(jnp.mean(z * z, axis=1, keepdims=True) + EPSILON)
        unit = z * scaled
        d_normed = dh_v[...]
        d_gain[0:1, :] += jnp.sum(d_normed * unit, axis=0, keepdims=True) * 0.125
        d_unit = d_normed * gain
        d_z = scaled * (d_unit - unit * jnp.mean(d_unit * unit, axis=1, keepdims=True))
        d_z += g_v[micro].astype(F32)
        dz_v[micro] = d_z
        back_v[micro] = d_z.astype(BF)

    def outs(micro):
        rows = rows_at(micro)
        return [
            pltpu.make_async_copy(dz_v.at[micro], d_inputs.at[rows, :], out_sem.at[micro, 0]),
            pltpu.make_async_copy(g_v.at[micro], grads.at[rows, :], out_sem.at[micro, 1]),
            pltpu.make_async_copy(d_first_v.at[micro], d_first.at[rows, :], out_sem.at[micro, 2]),
            pltpu.make_async_copy(d_second_v.at[micro], d_second.at[rows, :], out_sem.at[micro, 3]),
            pltpu.make_async_copy(mid_v.at[micro], middle.at[rows, :], out_sem.at[micro, 4]),
        ]

    for micro in range(MICRO):
        for copy in loads(micro):
            copy.wait()

        @pl.when(section == last)
        def _(micro=micro):
            tangent_copy(micro).wait()

        @pl.when(section < last)
        def _(micro=micro):
            hand_back(micro).wait_recv()

        @pl.when(is_feed(section))
        def _(micro=micro):
            feed(micro)

        @pl.when(section == WINDOW)
        def _(micro=micro):
            attend(micro, WINDOW)

        @pl.when(section == LINEAR)
        def _(micro=micro):
            attend(micro, LINEAR)

        unnorm(micro)

        @pl.when(section > 0)
        def _(micro=micro):
            hand_back(micro).start()

        for copy in outs(micro):
            copy.start()

    for micro in range(MICRO):

        @pl.when(section > 0)
        def _(micro=micro):
            hand_back(micro).wait_send()

        for copy in outs(micro):
            copy.wait()


def backward(cotangent, flat, wide, tall, doc_col, doc_row, inputs, first, second):
    count = MICRO * LEN
    return pl.pallas_call(
        backward_kernel,
        out_shape=(
            jax.ShapeDtypeStruct((count, D), F32),
            jax.ShapeDtypeStruct((count, D), BF),
            jax.ShapeDtypeStruct((count, FP), BF),
            jax.ShapeDtypeStruct((count, FP), BF),
            jax.ShapeDtypeStruct((count, FP), BF),
            jax.ShapeDtypeStruct((8, D), F32),
        ),
        in_specs=[any_spec()] * 4 + [vmem_spec()] * 2 + [any_spec()] * 3,
        out_specs=(any_spec(),) * 5 + (vmem_spec(),),
        scratch_shapes=[
            pltpu.VMEM((2, D, FP), BF),
            pltpu.VMEM((FP, D), BF),
            pltpu.VMEM((1, D), BF),
            pltpu.VMEM((MICRO, LEN, D), BF),
            pltpu.VMEM((MICRO, LEN, D), BF),
            pltpu.VMEM((MICRO, LEN, D), F32),
            pltpu.VMEM((MICRO, LEN, D), BF),
            pltpu.VMEM((MICRO, LEN, FP), BF),
            pltpu.VMEM((MICRO, LEN, FP), BF),
            pltpu.VMEM((MICRO, LEN, FP), BF),
            pltpu.VMEM((MICRO, LEN, FP), BF),
            pltpu.VMEM((MICRO, LEN, FP), BF),
            pltpu.VMEM((LEN, D), F32),
            pltpu.VMEM((LEN, LEN), F32),
            pltpu.SemaphoreType.DMA((3,)),
            pltpu.SemaphoreType.DMA,
            pltpu.SemaphoreType.DMA((MICRO, 4)),
            pltpu.SemaphoreType.DMA((MICRO, 5)),
            pltpu.SemaphoreType.DMA((MICRO,)),
            pltpu.SemaphoreType.DMA((MICRO,)),
        ],
        compiler_params=pltpu.CompilerParams(
            collective_id=1, has_side_effects=True, vmem_limit_bytes=56 * MIB
        ),
        name="backward",
    )(cotangent, flat, wide, tall, doc_col, doc_row, inputs, first, second)


HEAD_ROWS = 16
PAIR_ROWS = 128 * 43


def flip(source, rows, width, target):
    def piece(t, carry):
        cols = pl.ds(pl.multiple_of(t * 128, 128), 128)
        target[cols, :] = source[:, cols].astype(F32).T.astype(target.dtype)
        return carry

    lax.fori_loop(0, width // 128, piece, 0)


def products_kernel(
    normed, d_first, d_second, middle, second, grads, d_gain, out,
    h_v, d_v, shift_v, m_v, g_v, turned, even, odd, m_turned, stage, packed, in_sem, out_sem,
):
    section = lax.axis_index("section")
    count = MICRO * LEN

    def fetch(source, target, index):
        return pltpu.make_async_copy(source, target, in_sem.at[index])

    shared = [fetch(normed, h_v, 0), fetch(grads, g_v, 1), fetch(d_first, d_v.at[0], 2), fetch(d_second, d_v.at[1], 3)]
    for copy in shared:
        copy.start()
    own_middle = fetch(middle, m_v, 4)
    own_mixed = fetch(second.at[:, pl.ds(D, D)], m_v.at[:, pl.ds(0, D)], 4)

    @pl.when(is_feed(section))
    def _():
        own_middle.start()

    @pl.when(jnp.logical_not(is_feed(section)))
    def _():
        own_mixed.start()

    def put(slot, first_row, rows):
        return pltpu.make_async_copy(
            packed.at[slot, pl.ds(0, rows), :], out.at[pl.ds(first_row, rows), :], out_sem.at[slot]
        )

    stage[pl.ds(0, 8), :] = jnp.zeros((8, 128), F32)
    stage[pl.ds(8, 8), :] = d_gain[0:1, :].reshape(8, 128)
    packed[0, pl.ds(0, 16), :] = stage[pl.ds(0, 16), :].astype(BF)
    head = put(0, 0, HEAD_ROWS)
    head.start()
    head.wait()

    def emit(steps, rows, first_row, work):
        def place(i):
            return pl.multiple_of(HEAD_ROWS + first_row + i * rows, 16)

        def step(i, carry):
            slot = lax.rem(i, 2)
            work(i)

            @pl.when(i >= 2)
            def _():
                put(slot, place(i - 2), rows).wait()

            def cut(j, inner):
                piece = pl.ds(pl.multiple_of(j * 32, 32), 32)
                packed[slot, piece, :] = stage[piece, :].astype(BF)
                return inner

            lax.fori_loop(0, rows // 32, cut, 0, unroll=4)
            put(slot, place(i), rows).start()
            return carry

        lax.fori_loop(0, steps, step, 0)
        for i in range(max(steps - 2, 0), steps):
            put(i % 2, place(i), rows).wait()

    def zeros(first_row, rows):
        packed[0, pl.ds(0, 512), :] = jnp.zeros((512, 128), BF)

        def place(i):
            return pl.multiple_of(HEAD_ROWS + first_row + i * 512, 16)

        def start(i, carry):
            put(0, place(i), 512).start()
            put(0, place(i), 512).wait()
            return carry

        lax.fori_loop(0, rows // 512, start, 0)

    for copy in shared:
        copy.wait()

    def tall_product(turned_ref, rows, step_rows, scale):
        def work(i):
            def tile(j, carry):
                left = turned_ref[pl.ds(pl.multiple_of(i * step_rows, 16), step_rows), :]
                piece = dot(left, g_v[:, at256(j)]) * scale
                stage[pl.ds(2 * j, step_rows, stride=8), :] = piece[:, :128]
                stage[pl.ds(2 * j + 1, step_rows, stride=8), :] = piece[:, 128:]
                return carry

            lax.fori_loop(0, 4, tile, 0)

        return work

    def wide_product(which, first_col, width, step_rows):
        stride = width // 128

        def work(i):
            def tile(j, carry):
                left = turned[pl.ds(pl.multiple_of(i * step_rows, 16), step_rows), :]
                cols = pl.ds(pl.multiple_of(first_col + j * 256, 256), 256)
                piece = dot(left, d_v[which, :, cols]) * SCALE
                stage[pl.ds(2 * j, step_rows, stride=stride), :] = piece[:, :128]
                stage[pl.ds(2 * j + 1, step_rows, stride=stride), :] = piece[:, 128:]
                return carry

            lax.fori_loop(0, width // 256, tile, 0)

        return work

    @pl.when(is_feed(section))
    def _():
        own_middle.wait()
        flip(m_v, count, FP, m_turned)

        def halves(t, carry):
            cols = pl.ds(pl.multiple_of(t * 128, 128), 128)
            stage[pl.ds(0, 512), :] = h_v[:, cols].astype(F32)
            for part in range(4):
                turned_piece = stage[pl.ds(128 * part, 128), :].T
                shift_v[0, pl.ds(0, 128), pl.ds(128 * part, 128)] = turned_piece.astype(BF)
                stage[pl.ds(512 + 128 * part, 128), :] = turned_piece
                rows = pl.ds(pl.multiple_of(t * 64, 64), 64)
                even[rows, pl.ds(128 * part, 128)] = stage[pl.ds(512 + 128 * part, 64, stride=2), :].astype(BF)
                odd[rows, pl.ds(128 * part, 128)] = stage[pl.ds(513 + 128 * part, 64, stride=2), :].astype(BF)
            return carry

        lax.fori_loop(0, 8, halves, 0)

        low_half = lax.broadcasted_iota(jnp.int32, (1, 128), 1) < 64

        for which in range(2):

            def shift(t, before, which=which):
                cols = pl.ds(pl.multiple_of(t * 128, 128), 128)
                here = pltpu.roll(d_v[which, :, cols].astype(F32), 64, 1)
                shift_v[which, :, cols] = jnp.where(low_half, before, here).astype(BF)
                return here

            lax.fori_loop(0, FP // 128, shift, jnp.zeros((count, 128), F32))

        def pairs(i):
            which = i // 4
            rows = pl.ds(pl.multiple_of(lax.rem(i, 4) * 128, 128), 128)

            def even_tile(j, carry):
                piece = dot(even[rows, :], d_v[which, :, at256(j)]) * SCALE
                stage[pl.ds(2 * j, 128, stride=43), :] = piece[:, :128]
                stage[pl.ds(2 * j + 1, 128, stride=43), :] = piece[:, 128:]
                return carry

            lax.fori_loop(0, FP // 256, even_tile, 0)
            piece = dot(odd[rows, :], shift_v[which, :, pl.ds(0, 256)]) * SCALE
            stage[pl.ds(21, 128, stride=43), :] += piece[:, :128]
            stage[pl.ds(22, 128, stride=43), :] = piece[:, 128:]

            def odd_tile(j, carry):
                piece = dot(odd[rows, :], shift_v[which, :, at256(j)]) * SCALE
                stage[pl.ds(21 + 2 * j, 128, stride=43), :] = piece[:, :128]
                stage[pl.ds(22 + 2 * j, 128, stride=43), :] = piece[:, 128:]
                return carry

            lax.fori_loop(1, FP // 256, odd_tile, 0)

        emit(8, PAIR_ROWS, 0, pairs)
        emit(4, PAIR_ROWS, 8 * PAIR_ROWS, tall_product(m_turned, FF, 688, SCALE))

    def attention(kind):
        own_mixed.wait()
        flip(h_v, count, D, turned)
        flip(m_v, count, D, m_turned)
        low = D if kind == WINDOW else HEADS * FEAT
        low_rows = 8 * low
        step_rows = 1024 * 128 // low
        for part in range(2):
            emit(low_rows // 1024, 1024, part * low_rows, wide_product(0, part * low, low, step_rows))
        emit(8, 1024, 2 * low_rows, wide_product(1, 0, D, 128))
        emit(8, 1024, 2 * low_rows + 8192, tall_product(m_turned, D, 128, out_scale(kind)))
        done = 2 * low_rows + 16384
        zeros(done, 66048 - done)

    @pl.when(section == WINDOW)
    def _():
        attention(WINDOW)

    @pl.when(section == LINEAR)
    def _():
        attention(LINEAR)


def products(normed, d_first, d_second, middle, second, grads, d_gain, total_rows):
    count = MICRO * LEN
    return pl.pallas_call(
        products_kernel,
        out_shape=jax.ShapeDtypeStruct((total_rows, 128), BF),
        in_specs=[any_spec()] * 6 + [vmem_spec()],
        out_specs=any_spec(),
        scratch_shapes=[
            pltpu.VMEM((count, D), BF),
            pltpu.VMEM((2, count, FP), BF),
            pltpu.VMEM((2, count, FP), BF),
            pltpu.VMEM((count, FP), BF),
            pltpu.VMEM((count, D), BF),
            pltpu.VMEM((D, count), BF),
            pltpu.VMEM((512, count), BF),
            pltpu.VMEM((512, count), BF),
            pltpu.VMEM((FP, count), BF),
            pltpu.VMEM((PAIR_ROWS, 128), F32),
            pltpu.VMEM((2, PAIR_ROWS, 128), BF),
            pltpu.SemaphoreType.DMA((5,)),
            pltpu.SemaphoreType.DMA((2,)),
        ],
        compiler_params=pltpu.CompilerParams(vmem_limit_bytes=56 * MIB),
        name="products",
    )(normed, d_first, d_second, middle, second, grads, d_gain)


def document_ids(lengths):
    ends = jnp.cumsum(lengths, axis=1)
    places = jnp.arange(LEN, dtype=jnp.int32)
    return jnp.sum((places[None, :, None] >= ends[:, None, :]).astype(jnp.int32), axis=2)


def shards(tokens, cotangent, params, lengths):
    docs = document_ids(lengths[0])
    doc_col, doc_row = docs[:, :, None], docs[:, None, :]
    wide, tall = prepare(params)
    acts, inputs, normed, first, second = forward(tokens, params, wide, tall, doc_col, doc_row)
    d_inputs, grads, d_first, d_second, middle, d_gain = backward(
        cotangent, params, wide, tall, doc_col, doc_row, inputs, first, second
    )
    total_rows = params.shape[1] // 128 + 8
    parts = products(normed, d_first, d_second, middle, second, grads, d_gain, total_rows)
    mine = lax.psum_scatter(parts[8:].reshape(-1), "batch", scatter_dimension=0, tiled=True)
    return acts[None], d_inputs[None], mine.astype(F32)[None]


def solution(mesh):
    return jax.shard_map(
        shards,
        mesh=mesh,
        in_specs=(P("batch", None), P("batch", None), P("section", None), P("batch", None, None)),
        out_specs=(P("section", "batch", None), P("section", "batch", None), P("section", "batch")),
        check_vma=False,
    )
```

```python
import functools
import math

import jax
import jax.numpy as jnp
from jax import lax
from jax.experimental import pallas as pl
from jax.experimental.pallas import tpu as pltpu
from jax.sharding import PartitionSpec as P

D = 1024
FF = 2752
FP = 2816
HEADS = 16
FEAT = 16
WIN = 64
MICRO = 2
LEN = 256
EPSILON = 1e-06
SCALE = 1.0 / math.sqrt(D)
LINEAR, FEED, WINDOW, FEED2 = 0, 1, 2, 3
MIB = 2**20
MESH = pl.DeviceIdType.MESH
BF = jnp.bfloat16
F32 = jnp.float32


def any_spec():
    return pl.BlockSpec(memory_space=pl.ANY)


def vmem_spec():
    return pl.BlockSpec(memory_space=pltpu.VMEM)


def dot(left, right):
    return jnp.dot(left, right, preferred_element_type=F32)


def dot_t(left, right):
    return lax.dot_general(left, right, (((1,), (1,)), ((), ())), preferred_element_type=F32)


def dot_0(left, right):
    return lax.dot_general(left, right, (((0,), (0,)), ((), ())), preferred_element_type=F32)


def at256(index):
    return pl.ds(pl.multiple_of(index * 256, 256), 256)


def is_feed(section):
    return (section == FEED) | (section == FEED2)


PAIR_STEP = 32 * FF
ROW_STEP = 64 * D


def prepare_kernel(flat, wide, tall, chunk, blocks, woven, stage_pair, stage_row, stage_low, load_sem, store_sem):
    section = lax.axis_index("section")

    def run(steps, count, source, target, stage, work):
        def load(i, slot):
            return pltpu.make_async_copy(
                flat.at[:, pl.ds(pl.multiple_of(source(i), 1024), count)],
                chunk.at[slot, :, pl.ds(0, count)],
                load_sem.at[slot],
            )

        def store(i, slot):
            return pltpu.make_async_copy(stage.at[slot], target(i), store_sem.at[slot])

        load(0, 0).start()

        def step(i, carry):
            slot = lax.rem(i, 2)

            @pl.when(i + 1 < steps)
            def _():
                load(i + 1, 1 - slot).start()

            load(i, slot).wait()

            @pl.when(i >= 2)
            def _():
                store(i - 2, slot).wait()

            rows = count // 128
            blocks[pl.ds(0, rows), :] = chunk[slot, :, pl.ds(0, count)].astype(F32).reshape(rows, 128)
            work(slot)
            store(i, slot).start()
            return carry

        lax.fori_loop(0, steps, step, 0)
        store(steps - 2, steps % 2).wait()
        store(steps - 1, (steps - 1) % 2).wait()

    def pair_work(slot):
        low_half = lax.broadcasted_iota(jnp.int32, (16, 128), 1) < 64
        rolled = None
        for c in range(22):
            even = blocks[pl.ds(c, 16, stride=43), :]
            if c == 21:
                even = jnp.where(low_half, even, 0.0)
            if rolled is None:
                rolled = pltpu.roll(blocks[pl.ds(21, 16, stride=43), :], 64, 1)
            if c < 21:
                after = pltpu.roll(blocks[pl.ds(22 + c, 16, stride=43), :], 64, 1)
                odd = jnp.where(low_half, rolled, after)
                rolled = after
            else:
                odd = jnp.where(low_half, rolled, 0.0)
            woven[c, pl.ds(0, 16, stride=2), :] = even
            woven[c, pl.ds(1, 16, stride=2), :] = odd
        for c in range(22):
            stage_pair[slot, :, pl.ds(128 * c, 128)] = woven[c].astype(BF)

    def row_work(slot):
        for c in range(8):
            stage_row[slot, :, pl.ds(128 * c, 128)] = blocks[pl.ds(c, 64, stride=8), :].astype(BF)

    def low_work(slot):
        for c in range(2):
            stage_low[slot, :, pl.ds(128 * c, 128)] = blocks[pl.ds(c, 256, stride=2), :].astype(BF)

    def rows_of(index, count):
        return pl.ds(pl.multiple_of(index * count, count), count)

    def square(first, target):
        run(16, ROW_STEP, lambda i: D + first + i * ROW_STEP, target, stage_row, row_work)

    @pl.when(is_feed(section))
    def _():
        run(
            64,
            PAIR_STEP,
            lambda i: D + i * PAIR_STEP,
            lambda i: wide.at[i // 32, rows_of(lax.rem(i, 32), 32), :],
            stage_pair,
            pair_work,
        )
        run(
            43,
            ROW_STEP,
            lambda i: D + 2 * D * FF + i * ROW_STEP,
            lambda i: tall.at[rows_of(i, 64), :],
            stage_row,
            row_work,
        )
        stage_row[0] = jnp.zeros((64, D), BF)
        last = pltpu.make_async_copy(stage_row.at[0], tall.at[pl.ds(FF, 64), :], store_sem.at[0])
        last.start()
        last.wait()

    @pl.when(section == WINDOW)
    def _():
        square(0, lambda i: wide.at[0, rows_of(i, 64), pl.ds(0, D)])
        square(D * D, lambda i: wide.at[0, rows_of(i, 64), pl.ds(D, D)])
        square(2 * D * D, lambda i: wide.at[1, rows_of(i, 64), pl.ds(0, D)])
        square(3 * D * D, lambda i: tall.at[rows_of(i, 64), :])

    @pl.when(section == LINEAR)
    def _():
        width = HEADS * FEAT
        for part in range(2):
            run(
                4,
                ROW_STEP,
                lambda i, part=part: D + part * D * width + i * ROW_STEP,
                lambda i, part=part: wide.at[0, rows_of(i, 256), pl.ds(part * width, width)],
                stage_low,
                low_work,
            )
        square(2 * D * width, lambda i: wide.at[1, rows_of(i, 64), pl.ds(0, D)])
        square(2 * D * width + D * D, lambda i: tall.at[rows_of(i, 64), :])


def prepare(flat):
    return pl.pallas_call(
        prepare_kernel,
        out_shape=(jax.ShapeDtypeStruct((2, D, FP), BF), jax.ShapeDtypeStruct((FP, D), BF)),
        in_specs=[any_spec()],
        out_specs=(any_spec(), any_spec()),
        scratch_shapes=[
            pltpu.VMEM((2, 1, PAIR_STEP), BF),
            pltpu.VMEM((PAIR_STEP // 128, 128), F32),
            pltpu.VMEM((22, 32, 128), F32),
            pltpu.VMEM((2, 32, FP), BF),
            pltpu.VMEM((2, 64, D), BF),
            pltpu.VMEM((2, 256, 256), BF),
            pltpu.SemaphoreType.DMA((2,)),
            pltpu.SemaphoreType.DMA((2,)),
        ],
        compiler_params=pltpu.CompilerParams(vmem_limit_bytes=32 * MIB),
        name="prepare",
    )(flat)


def lane_of_head(section_kind, block, half):
    lanes = lax.broadcasted_iota(jnp.int32, (1, 128), 1)
    if section_kind == WINDOW:
        return lanes // 64 == half
    return lanes // FEAT == lax.rem(2 * block + half, 8)


def lane_of_value(half):
    return lax.broadcasted_iota(jnp.int32, (1, 128), 1) // 64 == half


def only(mask, values):
    return jnp.where(mask, values, jnp.zeros_like(values))


def query_block(section_kind, block):
    index = block if section_kind == WINDOW else block // 4
    return pl.ds(pl.multiple_of(index * 128, 128), 128)


def key_block(section_kind, block):
    first = D if section_kind == WINDOW else HEADS * FEAT
    index = block if section_kind == WINDOW else block // 4
    return pl.ds(pl.multiple_of(first + index * 128, 128), 128)


def value_block(block, first=0):
    return pl.ds(pl.multiple_of(first + block * 128, 128), 128)


def mask_of(section_kind, doc_col, doc_row):
    rows = lax.broadcasted_iota(jnp.int32, (LEN, LEN), 0)
    cols = lax.broadcasted_iota(jnp.int32, (LEN, LEN), 1)
    mask = (doc_col == doc_row) & (cols <= rows)
    if section_kind == WINDOW:
        mask = mask & (rows - cols < WIN)
    return mask.astype(F32)


def root_of(section_kind):
    return 1.0 / math.sqrt(D // HEADS if section_kind == WINDOW else FEAT)


def weigh(section_kind, scores, mask):
    if section_kind == WINDOW:
        kept = jnp.where(mask > 0.0, scores, -1e30)
        raised = jnp.exp(kept - jnp.max(kept, axis=1, keepdims=True))
        raised = raised * mask
        inverse = 1.0 / jnp.sum(raised, axis=1, keepdims=True)
        return raised * inverse, inverse
    raised = mask * (1.0 + scores + 0.5 * scores * scores)
    inverse = 1.0 / jnp.sum(raised, axis=1, keepdims=True)
    return raised * inverse, inverse


def unweigh(section_kind, scores, mask, weights, inverse, d_weights):
    centred = d_weights - jnp.sum(d_weights * weights, axis=1, keepdims=True)
    if section_kind == WINDOW:
        return weights * centred
    return centred * inverse * (mask * (1.0 + scores))


def out_scale(section_kind):
    return {LINEAR: 8.0, WINDOW: 4.0, FEED: 1.0}[section_kind] * SCALE


def load_weights(section, wide, tall, wide_v, tall_v, sems):
    def copies(kind):
        if kind == FEED:
            return [
                pltpu.make_async_copy(wide, wide_v, sems.at[0]),
                pltpu.make_async_copy(tall, tall_v, sems.at[1]),
            ]
        first = 2 * D if kind == WINDOW else 2 * HEADS * FEAT
        return [
            pltpu.make_async_copy(wide.at[0, :, pl.ds(0, first)], wide_v.at[0, :, pl.ds(0, first)], sems.at[0]),
            pltpu.make_async_copy(wide.at[1, :, pl.ds(0, D)], wide_v.at[1, :, pl.ds(0, D)], sems.at[1]),
            pltpu.make_async_copy(tall.at[pl.ds(0, D), :], tall_v.at[pl.ds(0, D), :], sems.at[2]),
        ]

    def each(act):
        for kind, here in ((FEED, is_feed(section)), (WINDOW, section == WINDOW), (LINEAR, section == LINEAR)):

            @pl.when(here)
            def _(kind=kind):
                for copy in copies(kind):
                    act(copy)

    each(lambda copy: copy.start())
    return lambda: each(lambda copy: copy.wait())


def forward_kernel(
    tokens, flat, wide, tall, doc_col, doc_row,
    acts, inputs, normed, first, second,
    wide_v, tall_v, gain_v, z_v, h_v, x_v, first_v, second_v, mid_v, mask_v,
    weight_sem, gain_sem, in_sem, out_sem, send_sem, recv_sem,
):
    section = lax.axis_index("section")
    batch = lax.axis_index("batch")
    last = lax.axis_size("section") - 1
    barrier = pltpu.get_barrier_semaphore()

    @pl.when(section > 0)
    def _():
        pl.semaphore_signal(barrier, inc=1, device_id=(section - 1, batch), device_id_type=MESH)

    @pl.when(section < last)
    def _():
        pl.semaphore_signal(barrier, inc=1, device_id=(section + 1, batch), device_id_type=MESH)

    gain_copy = pltpu.make_async_copy(flat.at[:, pl.ds(0, D)], gain_v, gain_sem)
    gain_copy.start()
    wait_weights = load_weights(section, wide, tall, wide_v, tall_v, weight_sem)

    def rows_at(micro):
        return pl.ds(micro * LEN, LEN)

    def token_copy(micro):
        return pltpu.make_async_copy(tokens.at[rows_at(micro), :], z_v.at[micro], in_sem.at[micro])

    @pl.when(section == 0)
    def _():
        for micro in range(MICRO):
            token_copy(micro).start()

    pl.semaphore_wait(barrier, jnp.where((section > 0) & (section < last), 2, 1))
    gain_copy.wait()
    wait_weights()
    gain = 1.0 + gain_v[...].astype(F32) / 8.0

    def hand_on(micro):
        return pltpu.make_async_remote_copy(
            src_ref=x_v.at[micro],
            dst_ref=z_v.at[micro],
            send_sem=send_sem.at[micro],
            recv_sem=recv_sem.at[micro],
            device_id=(section + 1, batch),
            device_id_type=MESH,
        )

    def norm(micro):
        z = z_v[micro].astype(F32)
        scaled = lax.rsqrt(jnp.mean(z * z, axis=1, keepdims=True) + EPSILON)
        h_v[micro] = (z * scaled * gain).astype(BF)

    def finish(micro, source, depth, scale):
        def tile(n, carry):
            cols = at256(n)
            branch = dot(source[:, pl.ds(0, depth)], tall_v[pl.ds(0, depth), cols]) * scale
            x_v[micro, :, cols] = (z_v[micro, :, cols].astype(F32) + branch).astype(BF)
            return carry

        lax.fori_loop(0, D // 256, tile, 0)

    def feed(micro):
        def tile(t, carry):
            cols = at256(t)
            gate = dot(h_v[micro], wide_v[0, :, cols]) * SCALE
            up = dot(h_v[micro], wide_v[1, :, cols]) * SCALE
            first_v[micro, :, cols] = gate.astype(BF)
            second_v[micro, :, cols] = up.astype(BF)
            mid_v[:, cols] = (gate / (1.0 + jnp.exp(-gate)) * up).astype(BF)
            return carry

        lax.fori_loop(0, FP // 256, tile, 0)
        finish(micro, mid_v, FP, SCALE)

    def attend(micro, kind):
        def project(which, count, target):
            def tile(t, carry):
                cols = at256(t)
                target[micro, :, cols] = (dot(h_v[micro], wide_v[which, :, cols]) * SCALE).astype(BF)
                return carry

            lax.fori_loop(0, count, tile, 0)

        project(0, 8 if kind == WINDOW else 2, first_v)
        project(1, 4, second_v)
        mask_v[...] = mask_of(kind, doc_col[micro], doc_row[micro])

        def block(t, carry):
            queries = first_v[micro, :, query_block(kind, t)]
            keys = first_v[micro, :, key_block(kind, t)]
            values = second_v[micro, :, value_block(t)]
            mixed = jnp.zeros((LEN, 128), F32)
            for half in range(2):
                scores = dot_t(only(lane_of_head(kind, t, half), queries), keys) * root_of(kind)
                weights, _ = weigh(kind, scores, mask_v[...])
                mixed += dot(weights.astype(BF), only(lane_of_value(half), values))
            second_v[micro, :, value_block(t, D)] = mixed.astype(BF)
            mid_v[:, value_block(t)] = mixed.astype(BF)
            return carry

        lax.fori_loop(0, 8, block, 0)
        finish(micro, mid_v, D, out_scale(kind))

    def outs(micro):
        rows = rows_at(micro)
        return [
            pltpu.make_async_copy(x_v.at[micro], acts.at[rows, :], out_sem.at[micro, 0]),
            pltpu.make_async_copy(z_v.at[micro], inputs.at[rows, :], out_sem.at[micro, 1]),
            pltpu.make_async_copy(h_v.at[micro], normed.at[rows, :], out_sem.at[micro, 2]),
            pltpu.make_async_copy(first_v.at[micro], first.at[rows, :], out_sem.at[micro, 3]),
            pltpu.make_async_copy(second_v.at[micro], second.at[rows, :], out_sem.at[micro, 4]),
        ]

    for micro in range(MICRO):

        @pl.when(section == 0)
        def _(micro=micro):
            token_copy(micro).wait()

        @pl.when(section > 0)
        def _(micro=micro):
            hand_on(micro).wait_recv()

        norm(micro)

        @pl.when(is_feed(section))
        def _(micro=micro):
            feed(micro)

        @pl.when(section == WINDOW)
        def _(micro=micro):
            attend(micro, WINDOW)

        @pl.when(section == LINEAR)
        def _(micro=micro):
            attend(micro, LINEAR)

        @pl.when(section < last)
        def _(micro=micro):
            hand_on(micro).start()

        for copy in outs(micro):
            copy.start()

    for micro in range(MICRO):

        @pl.when(section < last)
        def _(micro=micro):
            hand_on(micro).wait_send()

        for copy in outs(micro):
            copy.wait()


def forward(tokens, flat, wide, tall, doc_col, doc_row):
    count = MICRO * LEN
    return pl.pallas_call(
        forward_kernel,
        out_shape=(
            jax.ShapeDtypeStruct((count, D), BF),
            jax.ShapeDtypeStruct((count, D), BF),
            jax.ShapeDtypeStruct((count, D), BF),
            jax.ShapeDtypeStruct((count, FP), BF),
            jax.ShapeDtypeStruct((count, FP), BF),
        ),
        in_specs=[any_spec()] * 4 + [vmem_spec()] * 2,
        out_specs=(any_spec(),) * 5,
        scratch_shapes=[
            pltpu.VMEM((2, D, FP), BF),
            pltpu.VMEM((FP, D), BF),
            pltpu.VMEM((1, D), BF),
            pltpu.VMEM((MICRO, LEN, D), BF),
            pltpu.VMEM((MICRO, LEN, D), BF),
            pltpu.VMEM((MICRO, LEN, D), BF),
            pltpu.VMEM((MICRO, LEN, FP), BF),
            pltpu.VMEM((MICRO, LEN, FP), BF),
            pltpu.VMEM((LEN, FP), BF),
            pltpu.VMEM((LEN, LEN), F32),
            pltpu.SemaphoreType.DMA((3,)),
            pltpu.SemaphoreType.DMA,
            pltpu.SemaphoreType.DMA((MICRO,)),
            pltpu.SemaphoreType.DMA((MICRO, 5)),
            pltpu.SemaphoreType.DMA((MICRO,)),
            pltpu.SemaphoreType.DMA((MICRO,)),
        ],
        compiler_params=pltpu.CompilerParams(
            collective_id=0, has_side_effects=True, vmem_limit_bytes=56 * MIB
        ),
        name="forward",
    )(tokens, flat, wide, tall, doc_col, doc_row)


def backward_kernel(
    cotangent, flat, wide, tall, doc_col, doc_row, inputs, first, second,
    d_inputs, grads, d_first, d_second, middle, d_gain,
    wide_v, tall_v, gain_v, g_v, z_v, dz_v, back_v, first_v, second_v, d_first_v, d_second_v, mid_v, dh_v, mask_v,
    weight_sem, gain_sem, in_sem, out_sem, send_sem, recv_sem,
):
    section = lax.axis_index("section")
    batch = lax.axis_index("batch")
    last = lax.axis_size("section") - 1
    barrier = pltpu.get_barrier_semaphore()

    @pl.when(section > 0)
    def _():
        pl.semaphore_signal(barrier, inc=1, device_id=(section - 1, batch), device_id_type=MESH)

    @pl.when(section < last)
    def _():
        pl.semaphore_signal(barrier, inc=1, device_id=(section + 1, batch), device_id_type=MESH)

    gain_copy = pltpu.make_async_copy(flat.at[:, pl.ds(0, D)], gain_v, gain_sem)
    gain_copy.start()
    wait_weights = load_weights(section, wide, tall, wide_v, tall_v, weight_sem)

    def rows_at(micro):
        return pl.ds(micro * LEN, LEN)

    def loads(micro):
        rows = rows_at(micro)
        return [
            pltpu.make_async_copy(inputs.at[rows, :], z_v.at[micro], in_sem.at[micro, 0]),
            pltpu.make_async_copy(first.at[rows, :], first_v.at[micro], in_sem.at[micro, 1]),
            pltpu.make_async_copy(second.at[rows, :], second_v.at[micro], in_sem.at[micro, 2]),
        ]

    def tangent_copy(micro):
        return pltpu.make_async_copy(cotangent.at[rows_at(micro), :], g_v.at[micro], in_sem.at[micro, 3])

    for micro in range(MICRO):
        for copy in loads(micro):
            copy.start()

        @pl.when(section == last)
        def _(micro=micro):
            tangent_copy(micro).start()

    pl.semaphore_wait(barrier, jnp.where((section > 0) & (section < last), 2, 1))
    gain_copy.wait()
    wait_weights()
    gain = 1.0 + gain_v[...].astype(F32) / 8.0
    d_gain[...] = jnp.zeros_like(d_gain)

    def hand_back(micro):
        return pltpu.make_async_remote_copy(
            src_ref=back_v.at[micro],
            dst_ref=g_v.at[micro],
            send_sem=send_sem.at[micro],
            recv_sem=recv_sem.at[micro],
            device_id=(section - 1, batch),
            device_id_type=MESH,
        )

    def feed(micro):
        def tile(t, carry):
            cols = at256(t)
            d_mid = dot_t(g_v[micro], tall_v[cols, :]) * SCALE
            gate = first_v[micro, :, cols].astype(F32)
            up = second_v[micro, :, cols].astype(F32)
            sig = 1.0 / (1.0 + jnp.exp(-gate))
            silu = gate * sig
            d_first_v[micro, :, cols] = (d_mid * up * (sig * (1.0 + gate * (1.0 - sig)))).astype(BF)
            d_second_v[micro, :, cols] = (d_mid * silu).astype(BF)
            mid_v[micro, :, cols] = (silu * up).astype(BF)
            return carry

        lax.fori_loop(0, FP // 256, tile, 0)

        def back(n, carry):
            rows = at256(n)
            total = dot_t(d_first_v[micro], wide_v[0, rows, :])
            total += dot_t(d_second_v[micro], wide_v[1, rows, :])
            dh_v[:, rows] = total * SCALE
            return carry

        lax.fori_loop(0, D // 256, back, 0)

    def attend(micro, kind):
        width = 2 * D if kind == WINDOW else 2 * HEADS * FEAT

        def mix(t, carry):
            rows = at256(t)
            mid_v[micro, :, rows] = (dot_t(g_v[micro], tall_v[rows, :]) * out_scale(kind)).astype(BF)
            return carry

        lax.fori_loop(0, D // 256, mix, 0)
        mask_v[...] = mask_of(kind, doc_col[micro], doc_row[micro])

        def block(t, d_low):
            queries = first_v[micro, :, query_block(kind, t)]
            keys = first_v[micro, :, key_block(kind, t)]
            values = second_v[micro, :, value_block(t)]
            d_mixed = mid_v[micro, :, value_block(t)]
            d_values = jnp.zeros((LEN, 128), F32)
            d_queries, d_keys = d_low
            for half in range(2):
                mask = mask_v[...]
                head = lane_of_head(kind, t, half)
                own_queries = only(head, queries)
                own_keys = only(head, keys)
                own_mixed = only(lane_of_value(half), d_mixed)
                scores = dot_t(own_queries, keys) * root_of(kind)
                weights, inverse = weigh(kind, scores, mask)
                d_weights = dot_t(own_mixed, values)
                d_values += dot_0(weights.astype(BF), own_mixed)
                d_scores = unweigh(kind, scores, mask, weights, inverse, d_weights).astype(BF)
                d_queries += dot(d_scores, own_keys)
                d_keys += dot_0(d_scores, own_queries)
            d_second_v[micro, :, value_block(t)] = d_values.astype(BF)
            return d_queries, d_keys

        zero = jnp.zeros((LEN, 128), F32)

        def store(t, d_low):
            d_queries, d_keys = d_low
            d_first_v[micro, :, query_block(kind, t)] = (d_queries * root_of(kind)).astype(BF)
            d_first_v[micro, :, key_block(kind, t)] = (d_keys * root_of(kind)).astype(BF)

        if kind == WINDOW:

            def whole(t, carry):
                store(t, block(t, (zero, zero)))
                return carry

            lax.fori_loop(0, 8, whole, 0)
        else:

            def group(q, carry):
                store(4 * q, lax.fori_loop(0, 4, lambda i, low: block(4 * q + i, low), (zero, zero)))
                return carry

            lax.fori_loop(0, 2, group, 0)

        def back(n, carry):
            rows = at256(n)
            total = dot_t(d_first_v[micro, :, pl.ds(0, width)], wide_v[0, rows, pl.ds(0, width)])
            total += dot_t(d_second_v[micro, :, pl.ds(0, D)], wide_v[1, rows, pl.ds(0, D)])
            dh_v[:, rows] = total * SCALE
            return carry

        lax.fori_loop(0, D // 256, back, 0)

    def unnorm(micro):
        z = z_v[micro].astype(F32)
        scaled = lax.rsqrt(jnp.mean(z * z, axis=1, keepdims=True) + EPSILON)
        unit = z * scaled
        d_normed = dh_v[...]
        d_gain[0:1, :] += jnp.sum(d_normed * unit, axis=0, keepdims=True) * 0.125
        d_unit = d_normed * gain
        d_z = scaled * (d_unit - unit * jnp.mean(d_unit * unit, axis=1, keepdims=True))
        d_z += g_v[micro].astype(F32)
        dz_v[micro] = d_z
        back_v[micro] = d_z.astype(BF)

    def outs(micro):
        rows = rows_at(micro)
        return [
            pltpu.make_async_copy(dz_v.at[micro], d_inputs.at[rows, :], out_sem.at[micro, 0]),
            pltpu.make_async_copy(g_v.at[micro], grads.at[rows, :], out_sem.at[micro, 1]),
            pltpu.make_async_copy(d_first_v.at[micro], d_first.at[rows, :], out_sem.at[micro, 2]),
            pltpu.make_async_copy(d_second_v.at[micro], d_second.at[rows, :], out_sem.at[micro, 3]),
            pltpu.make_async_copy(mid_v.at[micro], middle.at[rows, :], out_sem.at[micro, 4]),
        ]

    for micro in range(MICRO):
        for copy in loads(micro):
            copy.wait()

        @pl.when(section == last)
        def _(micro=micro):
            tangent_copy(micro).wait()

        @pl.when(section < last)
        def _(micro=micro):
            hand_back(micro).wait_recv()

        @pl.when(is_feed(section))
        def _(micro=micro):
            feed(micro)

        @pl.when(section == WINDOW)
        def _(micro=micro):
            attend(micro, WINDOW)

        @pl.when(section == LINEAR)
        def _(micro=micro):
            attend(micro, LINEAR)

        unnorm(micro)

        @pl.when(section > 0)
        def _(micro=micro):
            hand_back(micro).start()

        for copy in outs(micro):
            copy.start()

    for micro in range(MICRO):

        @pl.when(section > 0)
        def _(micro=micro):
            hand_back(micro).wait_send()

        for copy in outs(micro):
            copy.wait()


def backward(cotangent, flat, wide, tall, doc_col, doc_row, inputs, first, second):
    count = MICRO * LEN
    return pl.pallas_call(
        backward_kernel,
        out_shape=(
            jax.ShapeDtypeStruct((count, D), F32),
            jax.ShapeDtypeStruct((count, D), BF),
            jax.ShapeDtypeStruct((count, FP), BF),
            jax.ShapeDtypeStruct((count, FP), BF),
            jax.ShapeDtypeStruct((count, FP), BF),
            jax.ShapeDtypeStruct((8, D), F32),
        ),
        in_specs=[any_spec()] * 4 + [vmem_spec()] * 2 + [any_spec()] * 3,
        out_specs=(any_spec(),) * 5 + (vmem_spec(),),
        scratch_shapes=[
            pltpu.VMEM((2, D, FP), BF),
            pltpu.VMEM((FP, D), BF),
            pltpu.VMEM((1, D), BF),
            pltpu.VMEM((MICRO, LEN, D), BF),
            pltpu.VMEM((MICRO, LEN, D), BF),
            pltpu.VMEM((MICRO, LEN, D), F32),
            pltpu.VMEM((MICRO, LEN, D), BF),
            pltpu.VMEM((MICRO, LEN, FP), BF),
            pltpu.VMEM((MICRO, LEN, FP), BF),
            pltpu.VMEM((MICRO, LEN, FP), BF),
            pltpu.VMEM((MICRO, LEN, FP), BF),
            pltpu.VMEM((MICRO, LEN, FP), BF),
            pltpu.VMEM((LEN, D), F32),
            pltpu.VMEM((LEN, LEN), F32),
            pltpu.SemaphoreType.DMA((3,)),
            pltpu.SemaphoreType.DMA,
            pltpu.SemaphoreType.DMA((MICRO, 4)),
            pltpu.SemaphoreType.DMA((MICRO, 5)),
            pltpu.SemaphoreType.DMA((MICRO,)),
            pltpu.SemaphoreType.DMA((MICRO,)),
        ],
        compiler_params=pltpu.CompilerParams(
            collective_id=1, has_side_effects=True, vmem_limit_bytes=56 * MIB
        ),
        name="backward",
    )(cotangent, flat, wide, tall, doc_col, doc_row, inputs, first, second)


HEAD_ROWS = 16
PAIR_ROWS = 128 * 43
CHUNKS = 11


def flip(source, first, width, target):
    def piece(t, carry):
        cols = pl.ds(pl.multiple_of(t * 128, 128), 128)
        rows = pl.ds(pl.multiple_of(first + t * 128, 128), 128)
        target[rows, :] = source[:, cols].astype(F32).T.astype(target.dtype)
        return carry

    lax.fori_loop(0, width // 128, piece, 0)


class Products:
    def __init__(self, sources, scratch):
        self.normed, self.d_first, self.d_second, self.middle, self.second, self.grads, self.d_gain = sources
        self.h_v, self.d_v, self.m_v, self.g_v, self.turned, self.m_turned, self.stage, self.in_sem = scratch

    def fetch(self, source, target, index):
        return pltpu.make_async_copy(source, target, self.in_sem.at[index])

    def shared(self):
        return [
            self.fetch(self.normed, self.h_v, 0),
            self.fetch(self.grads, self.g_v, 1),
            self.fetch(self.d_first, self.d_v.at[0], 2),
            self.fetch(self.d_second, self.d_v.at[1], 3),
        ]

    def middle_half(self, part):
        half = FP // 2
        return self.fetch(self.middle.at[:, pl.ds(part * half, half)], self.m_v, 4)

    def mixed(self):
        return self.fetch(self.second.at[:, pl.ds(D, D)], self.m_v.at[:, pl.ds(0, D)], 4)

    def head(self, out):
        stage = self.stage
        stage[pl.ds(0, 8), :] = jnp.zeros((8, 128), F32)
        stage[pl.ds(8, 8), :] = self.d_gain[0:1, :].reshape(8, 128)
        out[pl.ds(0, 16), :] = stage[pl.ds(0, 16), :].astype(BF)

    def cut(self, out, first_row, rows, piece):
        def step(j, carry):
            source = pl.ds(pl.multiple_of(j * piece, 16), piece)
            target = pl.ds(pl.multiple_of(first_row + j * piece, 16), piece)
            out[target, :] = self.stage[source, :].astype(BF)
            return carry

        lax.fori_loop(0, rows // piece, step, 0)

    def start_feed(self):
        self.middle_half(0).start()
        for copy in self.shared():
            copy.wait()
        stage = self.stage

        def halves(t, carry):
            cols = pl.ds(pl.multiple_of(t * 128, 128), 128)
            stage[pl.ds(0, 512), :] = self.h_v[:, cols].astype(F32)
            for part in range(4):
                stage[pl.ds(512 + 128 * part, 128), :] = stage[pl.ds(128 * part, 128), :].T
            for part in range(4):
                for odd in range(2):
                    rows = pl.ds(pl.multiple_of(512 * odd + t * 64, 64), 64)
                    piece = stage[pl.ds(512 + 128 * part + odd, 64, stride=2), :]
                    self.turned[rows, pl.ds(128 * part, 128)] = piece.astype(BF)
            return carry

        lax.fori_loop(0, 8, halves, 0)
        half = FP // 2
        for part in range(2):
            self.middle_half(part).wait()
            flip(self.m_v, part * half, half, self.m_turned)
            if part == 0:
                self.middle_half(1).start()

    def pairs(self, out, which, first_pair, count, first_row):
        stage = self.stage
        half = FP // 2
        low_half = lax.broadcasted_iota(jnp.int32, (count, 128), 1) < 64
        even = self.turned[pl.ds(pl.multiple_of(first_pair, 16), count), :]
        odd = self.turned[pl.ds(pl.multiple_of(512 + first_pair, 16), count), :]
        for part in range(2):
            piece = dot(even, self.d_v[which, :, pl.ds(part * half, half)]) * SCALE
            for c in range(11):
                stage[pl.ds(11 * part + c, count, stride=43), :] = piece[:, 128 * c : 128 * c + 128]
        before = stage[pl.ds(21, count, stride=43), :]
        for part in range(2):
            piece = dot(odd, self.d_v[which, :, pl.ds(part * half, half)]) * SCALE
            for c in range(11):
                here = pltpu.roll(piece[:, 128 * c : 128 * c + 128], 64, 1)
                stage[pl.ds(21 + 11 * part + c, count, stride=43), :] = jnp.where(low_half, before, here)
                before = here
        self.cut(out, first_row, 43 * count, 688)

    def tall(self, out, left, right, stride, rows, first_row, scale, piece):
        product = dot(left, right) * scale
        for c in range(stride):
            self.stage[pl.ds(c, rows, stride=stride), :] = product[:, 128 * c : 128 * c + 128]
        self.cut(out, first_row, rows * stride, piece)

    def down(self, out, first_channel, rows, first_row, piece):
        left = self.m_turned[pl.ds(pl.multiple_of(first_channel, 16), rows), :]
        self.tall(out, left, self.g_v[...], 8, rows, first_row, SCALE, piece)

    def feed_tile(self, out, k):
        first_row = pl.multiple_of(HEAD_ROWS + k * PAIR_ROWS, 16)

        @pl.when(k < 8)
        def _():
            self.pairs(out, k // 4, lax.rem(k, 4) * 128, 128, first_row)

        @pl.when(k >= 8)
        def _():
            self.down(out, (k - 8) * 688, 688, first_row, 688)

    def start_attention(self):
        self.mixed().start()
        for copy in self.shared():
            copy.wait()
        flip(self.h_v, 0, D, self.turned)
        self.mixed().wait()
        flip(self.m_v, 0, D, self.m_turned)

    def square(self, out, left, right, first_row, scale):
        def step(i, carry):
            rows = pl.ds(pl.multiple_of(i * 512, 512), 512)
            self.tall(out, left[rows, :], right(), 8, 512, pl.multiple_of(first_row + i * 4096, 16), scale, 512)
            return carry

        lax.fori_loop(0, 2, step, 0)

    def window(self, out, part):
        first_row = HEAD_ROWS + part * 8192
        if part < 3:
            cols = pl.ds(D if part == 1 else 0, D)
            self.square(out, self.turned, lambda: self.d_v[part // 2, :, cols], first_row, SCALE)
        else:
            self.square(out, self.m_turned, lambda: self.g_v[...], first_row, out_scale(WINDOW))

    def linear(self, out):
        width = HEADS * FEAT
        for part in range(2):
            right = self.d_v[0, :, pl.ds(part * width, width)]
            self.tall(out, self.turned[...], right, 2, D, HEAD_ROWS + part * 2048, SCALE, 512)
        self.square(out, self.turned, lambda: self.d_v[1, :, pl.ds(0, D)], HEAD_ROWS + 4096, SCALE)
        self.square(out, self.m_turned, lambda: self.g_v[...], HEAD_ROWS + 12288, out_scale(LINEAR))


def product_scratch():
    count = MICRO * LEN
    return [
        pltpu.VMEM((count, D), BF),
        pltpu.VMEM((2, count, FP), BF),
        pltpu.VMEM((count, FP // 2), BF),
        pltpu.VMEM((count, D), BF),
        pltpu.VMEM((D, count), BF),
        pltpu.VMEM((FP, count), BF),
        pltpu.VMEM((PAIR_ROWS, 128), F32),
        pltpu.SemaphoreType.DMA((5,)),
    ]


def clear(out, first_row, rows):
    def step(i, carry):
        out[pl.ds(pl.multiple_of(first_row + i * 128, 16), 128), :] = jnp.zeros((128, 128), BF)
        return carry

    lax.fori_loop(0, rows // 128, step, 0)
    if rows % 128:
        out[pl.ds(first_row + rows // 128 * 128, rows % 128), :] = jnp.zeros((rows % 128, 128), BF)


def products_kernel(*refs):
    section = lax.axis_index("section")
    work = Products(refs[:7], refs[9:])
    out, out_v = refs[7:9]
    total = out_v.shape[0]
    for copy in work.shared():
        copy.start()
    work.head(out_v)

    @pl.when(is_feed(section))
    def _():
        work.start_feed()

        def tile(k, carry):
            work.feed_tile(out_v, k)
            return carry

        lax.fori_loop(0, 12, tile, 0)

    @pl.when(section == WINDOW)
    def _():
        work.start_attention()
        for part in range(4):
            work.window(out_v, part)
        done = HEAD_ROWS + 4 * 8192
        clear(out_v, done, total - done)

    @pl.when(section == LINEAR)
    def _():
        work.start_attention()
        work.linear(out_v)
        done = HEAD_ROWS + 20480
        clear(out_v, done, total - done)

    store = pltpu.make_async_copy(out_v, out, work.in_sem.at[0])
    store.start()
    store.wait()


def products(sources, total_rows):
    return pl.pallas_call(
        products_kernel,
        out_shape=jax.ShapeDtypeStruct((total_rows, 128), BF),
        in_specs=[any_spec()] * 6 + [vmem_spec()],
        out_specs=any_spec(),
        scratch_shapes=[pltpu.VMEM((total_rows, 128), BF)] + product_scratch(),
        compiler_params=pltpu.CompilerParams(vmem_limit_bytes=56 * MIB),
        name="products",
    )(*sources)


def reduce_kernel(chain, *refs):
    section = lax.axis_index("section")
    batch = lax.axis_index("batch")
    place, core = batch // 2, lax.rem(batch, 2)
    work = Products(refs[:7], refs[14:])
    out, part, own, passing, total, flat, sems = refs[7:14]
    ex_send, ex_recv, up_send, down_send, recv, out_sem = sems
    width = own.shape[1]
    step_rows = width - HEAD_ROWS
    piece = width // CHUNKS
    feed_here = is_feed(section)
    ends = jnp.where(feed_here, chain, 2)
    barrier = pltpu.get_barrier_semaphore()

    def greet(other):
        pl.semaphore_signal(barrier, inc=1, device_id=(section, other), device_id_type=MESH)

    for copy in work.shared():
        copy.start()
    greet(2 * place + 1 - core)

    @pl.when(place > 0)
    def _():
        greet(batch - 2)

    @pl.when(place < chain - 1)
    def _():
        greet(batch + 2)

    work.head(part)
    pl.semaphore_wait(barrier, jnp.where((place > 0) & (place < chain - 1), 3, 2))

    def rows_of(i):
        return pl.ds(pl.multiple_of(i * piece, 16), piece)

    def share(index, i):
        return pl.ds(pl.multiple_of(step_rows * index + i * piece, 16), piece)

    def swap(to):
        other = 2 * to + 1 - core
        return pltpu.make_async_remote_copy(
            src_ref=part.at[pl.ds(pl.multiple_of(step_rows * other, 16), width), :],
            dst_ref=own.at[to],
            send_sem=ex_send.at[to],
            recv_sem=ex_recv.at[to],
            device_id=(section, 2 * place + 1 - core),
            device_id_type=MESH,
        )

    def up_slot(at, to):
        return to - at

    def down_slot(at, to):
        return chain - at + to

    def go_up(source, to, i):
        slot = up_slot(place + 1, to)
        return pltpu.make_async_remote_copy(
            src_ref=source,
            dst_ref=passing.at[slot, rows_of(i), :],
            send_sem=up_send.at[to - 1, i],
            recv_sem=recv.at[slot, i],
            device_id=(section, batch + 2),
            device_id_type=MESH,
        )

    def go_down(source, to, i):
        slot = down_slot(place - 1, to)
        return pltpu.make_async_remote_copy(
            src_ref=source,
            dst_ref=passing.at[slot, rows_of(i), :],
            send_sem=down_send.at[to, i],
            recv_sem=recv.at[slot, i],
            device_id=(section, batch - 2),
            device_id_type=MESH,
        )

    def arrived(slot, i):
        here = passing.at[slot, rows_of(i), :]
        pltpu.make_async_copy(here, here, recv.at[slot, i]).wait()

    def each_chunk(act):
        def step(i, carry):
            act(i)
            return carry

        lax.fori_loop(0, CHUNKS, step, 0)

    def trade(to):
        swap(to).start()
        swap(to).wait()

        def add(i):
            rows = rows_of(i)
            mine = part[share(2 * to + core, i), :].astype(F32)
            own[to, rows, :] = (own[to, rows, :].astype(F32) + mine).astype(BF)

            @pl.when((place == 0) & (to > 0))
            def _():
                go_up(own.at[to, rows, :], to, i).start()

            @pl.when((place == chain - 1) & (to < chain - 1))
            def _():
                go_down(own.at[to, rows, :], to, i).start()

        each_chunk(add)

    @pl.when(feed_here)
    def _():
        work.start_feed()

        def group(t, carry):
            to = jnp.where(place < chain // 2, chain - 1 - t, t)

            def tile(k, inner):
                work.feed_tile(part, 3 * to + k)
                return inner

            lax.fori_loop(0, 3, tile, 0)

            before = HEAD_ROWS + 3 * PAIR_ROWS * to

            @pl.when((place < chain // 2) & ((to == 1) | (to == 2)))
            def _():
                first_pair = jnp.where(to == 1, 368, 240)
                work.pairs(part, to - 1, first_pair, 16, pl.multiple_of(before - 688, 16))

            @pl.when((place < chain // 2) & (to == 3))
            def _():
                work.down(part, 672, 16, pl.multiple_of(before - 128, 16), 128)

            trade(to)
            return carry

        lax.fori_loop(0, chain, group, 0)

    last_row = 4 * step_rows + HEAD_ROWS

    @pl.when(section == WINDOW)
    def _():
        work.start_attention()
        for index in range(3):
            work.window(part, index)
        trade(0)
        work.window(part, 3)
        done = HEAD_ROWS + 4 * 8192
        clear(part, done, last_row - done)
        trade(1)

    @pl.when(section == LINEAR)
    def _():
        work.start_attention()
        work.linear(part)
        done = HEAD_ROWS + 20480
        clear(part, done, last_row - done)
        trade(0)
        trade(1)

    def pass_on(t, carry):
        upward, downward = ends - 1 - t, t

        def step(i):
            @pl.when((place > 0) & (upward > place))
            def _():
                slot = up_slot(place, upward)
                rows = rows_of(i)
                arrived(slot, i)
                added = passing[slot, rows, :].astype(F32) + own[upward, rows, :].astype(F32)
                passing[slot, rows, :] = added.astype(BF)
                go_up(passing.at[slot, rows, :], upward, i).start()

            @pl.when((place < chain - 1) & (downward < place))
            def _():
                slot = down_slot(place, downward)
                rows = rows_of(i)
                arrived(slot, i)
                added = passing[slot, rows, :].astype(F32) + own[downward, rows, :].astype(F32)
                passing[slot, rows, :] = added.astype(BF)
                go_down(passing.at[slot, rows, :], downward, i).start()

        each_chunk(step)
        return carry

    lax.fori_loop(0, ends, pass_on, 0)

    def finish(i):
        rows = rows_of(i)

        @pl.when(place < ends)
        def _():
            total[...] = own[place, rows, :].astype(F32)

        @pl.when(place >= ends)
        def _():
            total[...] = jnp.zeros_like(total)

        @pl.when((place > 0) & (place < ends))
        def _():
            arrived(0, i)
            total[...] += passing[0, rows, :].astype(F32)

        @pl.when((place < chain - 1) & (place < ends))
        def _():
            arrived(chain, i)
            total[...] += passing[chain, rows, :].astype(F32)

        flat[0:1, pl.ds(pl.multiple_of(i * piece * 128, 1024), piece * 128)] = total[...].reshape(1, piece * 128)

    each_chunk(finish)
    count = out.shape[1]
    first = pl.multiple_of((8 + batch) * 128, 128)
    store = pltpu.make_async_copy(flat.at[:, pl.ds(first, count)], out, out_sem)
    store.start()

    def drain(t, carry):
        upward, downward = ends - 1 - t, t

        def step(i):
            @pl.when((place < chain - 1) & (upward > place))
            def _():
                go_up(passing.at[0, rows_of(i), :], upward, i).wait_send()

            @pl.when((place > 0) & (downward < place))
            def _():
                go_down(passing.at[0, rows_of(i), :], downward, i).wait_send()

        each_chunk(step)
        return carry

    lax.fori_loop(0, ends, drain, 0)
    store.wait()


def reduce_products(sources, total_rows, batches):
    chain = batches // 2
    step_rows = (total_rows - 8) // batches - 1
    width = step_rows + HEAD_ROWS
    return pl.pallas_call(
        functools.partial(reduce_kernel, chain),
        out_shape=jax.ShapeDtypeStruct((1, (step_rows + 1) * 128), F32),
        in_specs=[any_spec()] * 6 + [vmem_spec()],
        out_specs=any_spec(),
        scratch_shapes=[
            pltpu.VMEM((total_rows, 128), BF),
            pltpu.VMEM((chain, width, 128), BF),
            pltpu.VMEM((chain + 1, width, 128), BF),
            pltpu.VMEM((width // CHUNKS, 128), F32),
            pltpu.VMEM((1, width * 128), F32),
            (
                pltpu.SemaphoreType.DMA((chain,)),
                pltpu.SemaphoreType.DMA((chain,)),
                pltpu.SemaphoreType.DMA((chain - 1, CHUNKS)),
                pltpu.SemaphoreType.DMA((chain - 1, CHUNKS)),
                pltpu.SemaphoreType.DMA((chain + 1, CHUNKS)),
                pltpu.SemaphoreType.DMA,
            ),
        ]
        + product_scratch(),
        compiler_params=pltpu.CompilerParams(
            collective_id=2, has_side_effects=True, vmem_limit_bytes=62 * MIB
        ),
        name="reduce_products",
    )(*sources)


def document_ids(lengths):
    ends = jnp.cumsum(lengths, axis=1)
    places = jnp.arange(LEN, dtype=jnp.int32)
    return jnp.sum((places[None, :, None] >= ends[:, None, :]).astype(jnp.int32), axis=2)


def shards(tokens, cotangent, params, lengths):
    docs = document_ids(lengths[0])
    doc_col, doc_row = docs[:, :, None], docs[:, None, :]
    wide, tall = prepare(params)
    acts, inputs, normed, first, second = forward(tokens, params, wide, tall, doc_col, doc_row)
    d_inputs, grads, d_first, d_second, middle, d_gain = backward(
        cotangent, params, wide, tall, doc_col, doc_row, inputs, first, second
    )
    total_rows = params.shape[1] // 128 + 8
    sources = (normed, d_first, d_second, middle, second, grads, d_gain)
    batches = lax.axis_size("batch")
    if batches == 8:
        mine = reduce_products(sources, total_rows, batches)
    else:
        parts = products(sources, total_rows)
        mine = lax.psum_scatter(parts[8:].reshape(-1), "batch", scatter_dimension=0, tiled=True)
        mine = mine.astype(F32)[None]
    return acts[None], d_inputs[None], mine


def solution(mesh):
    return jax.shard_map(
        shards,
        mesh=mesh,
        in_specs=(P("batch", None), P("batch", None), P("section", None), P("batch", None, None)),
        out_specs=(P("section", "batch", None), P("section", "batch", None), P("section", "batch")),
        check_vma=False,
    )
```

```python
import functools
import math

import jax
import jax.numpy as jnp
from jax import lax
from jax.experimental import pallas as pl
from jax.experimental.pallas import tpu as pltpu
from jax.sharding import PartitionSpec as P

D = 1024
FF = 2752
FP = 2816
HEADS = 16
FEAT = 16
WIN = 64
MICRO = 2
LEN = 256
EPSILON = 1e-06
SCALE = 1.0 / math.sqrt(D)
LINEAR, FEED, WINDOW, FEED2 = 0, 1, 2, 3
MIB = 2**20
MESH = pl.DeviceIdType.MESH
BF = jnp.bfloat16
F32 = jnp.float32


def any_spec():
    return pl.BlockSpec(memory_space=pl.ANY)


def vmem_spec():
    return pl.BlockSpec(memory_space=pltpu.VMEM)


def dot(left, right):
    return jnp.dot(left, right, preferred_element_type=F32)


def dot_t(left, right):
    return lax.dot_general(left, right, (((1,), (1,)), ((), ())), preferred_element_type=F32)


def dot_0(left, right):
    return lax.dot_general(left, right, (((0,), (0,)), ((), ())), preferred_element_type=F32)


def is_feed(section):
    return (section == FEED) | (section == FEED2)


PAIR_STEP = 32 * FF
ROW_STEP = 64 * D
AHEAD = 8


def prepare(section, flat, wide_v, tall_v, chunk, blocks, woven, load_sem):
    def run(steps, count, first, work):
        def load(i):
            slot = lax.rem(i, AHEAD)
            return pltpu.make_async_copy(
                flat.at[:, pl.ds(pl.multiple_of(first + i * count, 1024), count)],
                chunk.at[slot, :, pl.ds(0, count)],
                load_sem.at[slot],
            )

        def start(i, carry):
            load(i).start()
            return carry

        lax.fori_loop(0, AHEAD, start, 0)

        def step(i, carry):
            load(i).wait()
            rows = count // 128
            blocks[pl.ds(0, rows), :] = chunk[lax.rem(i, AHEAD), :, pl.ds(0, count)].astype(F32).reshape(rows, 128)
            work(i)

            @pl.when(i + AHEAD < steps)
            def _():
                load(i + AHEAD).start()

            return carry

        lax.fori_loop(0, steps, step, 0)

    def rows_of(index, count):
        return pl.ds(pl.multiple_of(index * count, count), count)

    def pair_work(i):
        low_half = lax.broadcasted_iota(jnp.int32, (16, 128), 1) < 64
        rolled = pltpu.roll(blocks[pl.ds(21, 16, stride=43), :], 64, 1)
        for c in range(22):
            even = blocks[pl.ds(c, 16, stride=43), :]
            if c == 21:
                even = jnp.where(low_half, even, 0.0)
                odd = jnp.where(low_half, rolled, 0.0)
            else:
                after = pltpu.roll(blocks[pl.ds(22 + c, 16, stride=43), :], 64, 1)
                odd = jnp.where(low_half, rolled, after)
                rolled = after
            woven[c, pl.ds(0, 16, stride=2), :] = even
            woven[c, pl.ds(1, 16, stride=2), :] = odd
        rows = rows_of(lax.rem(i, 32), 32)
        for c in range(22):
            wide_v[i // 32, rows, pl.ds(128 * c, 128)] = woven[c].astype(BF)

    def row_work(target, rows, first_col):
        for c in range(8):
            target[rows, pl.ds(first_col + 128 * c, 128)] = blocks[pl.ds(c, 64, stride=8), :].astype(BF)

    def square(i, first, target, first_col):
        @pl.when((i >= first) & (i < first + 16))
        def _():
            row_work(target, rows_of(i - first, 64), first_col)

    @pl.when(is_feed(section))
    def _():
        run(64, PAIR_STEP, D, pair_work)
        run(43, ROW_STEP, D + 2 * D * FF, lambda i: row_work(tall_v, rows_of(i, 64), 0))
        tall_v[pl.ds(FF, FP - FF), :] = jnp.zeros((FP - FF, D), BF)

    @pl.when(section == WINDOW)
    def _():
        def work(i):
            square(i, 0, wide_v.at[0], 0)
            square(i, 16, wide_v.at[0], D)
            square(i, 32, wide_v.at[1], 0)
            square(i, 48, tall_v, 0)

        run(64, ROW_STEP, D, work)

    @pl.when(section == LINEAR)
    def _():
        def work(i):
            for part in range(2):

                @pl.when(i // 4 == part)
                def _(part=part):
                    rows = rows_of(i - 4 * part, 256)
                    for c in range(2):
                        cols = pl.ds(part * HEADS * FEAT + 128 * c, 128)
                        wide_v[0, rows, cols] = blocks[pl.ds(c, 256, stride=2), :].astype(BF)

            square(i, 8, wide_v.at[1], 0)
            square(i, 24, tall_v, 0)

        run(40, ROW_STEP, D, work)


ROWS = 128
CHUNKS_OF = LEN // ROWS


def lanes_of_head(kind, block, half):
    lanes = lax.broadcasted_iota(jnp.int32, (1, 128), 1)
    if kind == WINDOW:
        return lanes // 64 == half
    return lanes // FEAT == lax.rem(2 * block + half, 8)


def lanes_of_value(half):
    return lax.broadcasted_iota(jnp.int32, (1, 128), 1) // 64 == half


def only(mask, values):
    return jnp.where(mask, values, jnp.zeros_like(values))


def both(masks, values):
    return jnp.concatenate([only(masks[0], values), only(masks[1], values)], axis=0)


def merge(masks, stacked):
    return only(masks[0], stacked[:ROWS]) + only(masks[1], stacked[ROWS:])


def block_of(index, first=0):
    return pl.ds(pl.multiple_of(first + index * 128, 128), 128)


def query_index(kind, block):
    return block if kind == WINDOW else block // 4


def low_width(kind):
    return D if kind == WINDOW else HEADS * FEAT


def mask_of(kind, doc_col, doc_row, first_row):
    shape = (doc_col.shape[0], doc_row.shape[1])
    rows = lax.broadcasted_iota(jnp.int32, shape, 0) + first_row
    cols = lax.broadcasted_iota(jnp.int32, shape, 1)
    mask = (doc_col == doc_row) & (cols <= rows)
    if kind == WINDOW:
        mask = mask & (rows - cols < WIN)
    return mask.astype(F32)


def root_of(kind):
    return 1.0 / math.sqrt(D // HEADS if kind == WINDOW else FEAT)


def out_scale(kind):
    return {LINEAR: 8.0, WINDOW: 4.0, FEED: 1.0}[kind] * SCALE


def train_kernel(
    tokens, cotangent, flat, doc_col, doc_row,
    acts, d_inputs, normed, middle, d_first, d_second, grads, d_gain,
    wide_v, tall_v, gain_v, z_v, h_v, x_v, g_v, dz_v, first_v, second_v, mid_v, dh_v,
    raised_v, slope_v, inverse_v, mask_v, dy_v, dq_v, dk_v, dv_v, chunk, blocks, woven,
    load_sem, gain_sem, in_sem, act_sem, out_sem, on_send, on_recv, back_send, back_recv,
):
    section = lax.axis_index("section")
    batch = lax.axis_index("batch")
    last = lax.axis_size("section") - 1
    barrier = pltpu.get_barrier_semaphore()

    @pl.when(section > 0)
    def _():
        pl.semaphore_signal(barrier, inc=1, device_id=(section - 1, batch), device_id_type=MESH)

    @pl.when(section < last)
    def _():
        pl.semaphore_signal(barrier, inc=1, device_id=(section + 1, batch), device_id_type=MESH)

    gain_copy = pltpu.make_async_copy(flat.at[:, pl.ds(0, D)], gain_v, gain_sem)
    gain_copy.start()
    token_copy = pltpu.make_async_copy(tokens, z_v, in_sem.at[0])
    tangent_copy = pltpu.make_async_copy(cotangent, g_v, in_sem.at[1])

    @pl.when(section == 0)
    def _():
        token_copy.start()

    @pl.when(section == last)
    def _():
        tangent_copy.start()

    prepare(section, flat, wide_v, tall_v, chunk, blocks, woven, load_sem)
    gain_copy.wait()
    gain = 1.0 + gain_v[...].astype(F32) / 8.0
    d_gain[...] = jnp.zeros_like(d_gain)

    @pl.when(section == 0)
    def _():
        token_copy.wait()

    pl.semaphore_wait(barrier, jnp.where((section > 0) & (section < last), 2, 1))

    def rows_at(step):
        return pl.ds(pl.multiple_of(step * ROWS, ROWS), ROWS)

    def hand_on(step):
        rows = rows_at(step)
        return pltpu.make_async_remote_copy(
            src_ref=x_v.at[rows, :],
            dst_ref=z_v.at[rows, :],
            send_sem=on_send.at[step],
            recv_sem=on_recv.at[step],
            device_id=(section + 1, batch),
            device_id_type=MESH,
        )

    def hand_back(step):
        rows = rows_at(step)
        return pltpu.make_async_remote_copy(
            src_ref=x_v.at[rows, :],
            dst_ref=g_v.at[rows, :],
            send_sem=back_send.at[step],
            recv_sem=back_recv.at[step],
            device_id=(section - 1, batch),
            device_id_type=MESH,
        )

    def forward_outs(step):
        rows = rows_at(step)
        return [
            pltpu.make_async_copy(x_v.at[rows, :], acts.at[rows, :], act_sem.at[0, step]),
            pltpu.make_async_copy(h_v.at[rows, :], normed.at[rows, :], act_sem.at[1, step]),
            pltpu.make_async_copy(mid_v.at[rows, :], middle.at[rows, :], act_sem.at[2, step]),
        ]

    def backward_outs(step):
        rows = rows_at(step)
        return [
            pltpu.make_async_copy(dz_v.at[rows, :], d_inputs.at[rows, :], out_sem.at[0, step]),
            pltpu.make_async_copy(g_v.at[rows, :], grads.at[rows, :], out_sem.at[1, step]),
            pltpu.make_async_copy(first_v.at[rows, :], d_first.at[rows, :], out_sem.at[2, step]),
            pltpu.make_async_copy(second_v.at[rows, :], d_second.at[rows, :], out_sem.at[3, step]),
        ]


    def forward_step(step, branch):
        rows = rows_at(step)

        @pl.when(section > 0)
        def _():
            hand_on(step).wait_recv()

        z = z_v[rows, :].astype(F32)
        scaled = lax.rsqrt(jnp.mean(z * z, axis=1, keepdims=True) + EPSILON)
        h_v[rows, :] = (z * scaled * gain).astype(BF)
        x_v[rows, :] = (z_v[rows, :].astype(F32) + branch(rows)).astype(BF)

        @pl.when(section < last)
        def _():
            hand_on(step).start()

        for copy in forward_outs(step):
            copy.start()

    def backward_step(step, branch):
        rows = rows_at(step)

        @pl.when(section < last)
        def _():
            hand_back(step).wait_recv()

        branch(rows)
        z = z_v[rows, :].astype(F32)
        scaled = lax.rsqrt(jnp.mean(z * z, axis=1, keepdims=True) + EPSILON)
        unit = z * scaled
        d_normed = dh_v[...]
        d_gain[0:1, :] += jnp.sum(d_normed * unit, axis=0, keepdims=True) * 0.125
        d_unit = d_normed * gain
        d_z = scaled * (d_unit - unit * jnp.mean(d_unit * unit, axis=1, keepdims=True))
        d_z += g_v[rows, :].astype(F32)
        dz_v[rows, :] = d_z
        x_v[rows, :] = d_z.astype(BF)

        @pl.when(section > 0)
        def _():
            hand_back(step).start()

        for copy in backward_outs(step):
            copy.start()

    def feed_forward(rows):
        half = FP // 2
        for part in range(2):
            cols = pl.ds(part * half, half)
            gate = dot(h_v[rows, :], wide_v[0, :, cols]) * SCALE
            up = dot(h_v[rows, :], wide_v[1, :, cols]) * SCALE
            sig = 1.0 / (1.0 + jnp.exp(-gate))
            silu = gate * sig
            first_v[rows, cols] = (up * (sig + silu * (1.0 - sig))).astype(BF)
            second_v[rows, cols] = silu.astype(BF)
            mid_v[rows, cols] = (silu * up).astype(BF)
        return dot(mid_v[rows, :], tall_v[...]) * SCALE

    def feed_backward(rows):
        half = FP // 2
        for part in range(2):
            cols = pl.ds(part * half, half)
            d_mid = dot_t(g_v[rows, :], tall_v[cols, :]) * SCALE
            first_v[rows, cols] = (d_mid * first_v[rows, cols].astype(F32)).astype(BF)
            second_v[rows, cols] = (d_mid * second_v[rows, cols].astype(F32)).astype(BF)
        total = dot_t(first_v[rows, :], wide_v[0]) + dot_t(second_v[rows, :], wide_v[1])
        dh_v[...] = total * SCALE

    def attend_forward(kind, micro, part, rows):
        width = low_width(kind)
        span = ROWS * (part + 1)
        keys_at = pl.ds(pl.multiple_of(micro * LEN, LEN), span)
        step = micro * CHUNKS_OF + part
        first_v[rows, pl.ds(0, 2 * width)] = (dot(h_v[rows, :], wide_v[0, :, pl.ds(0, 2 * width)]) * SCALE).astype(BF)
        second_v[rows, pl.ds(0, D)] = (dot(h_v[rows, :], wide_v[1, :, pl.ds(0, D)]) * SCALE).astype(BF)
        cols = pl.ds(0, span)
        mask_v[:, cols] = mask_of(
            kind, doc_col[micro, pl.ds(part * ROWS, ROWS), :], doc_row[micro, :, pl.ds(0, span)], part * ROWS
        )

        def block(t, carry):
            index = query_index(kind, t)
            queries = first_v[rows, block_of(index)]
            keys = first_v[keys_at, block_of(index, width)]
            values = second_v[keys_at, block_of(t)]
            heads = [lanes_of_head(kind, t, half) for half in range(2)]
            scores = (dot_t(both(heads, queries), keys) * root_of(kind)).reshape(2, ROWS, span)
            mask = mask_v[:, cols]
            if kind == WINDOW:
                kept = jnp.where((mask > 0.0)[None], scores, -1e30)
                raised = jnp.exp(kept - jnp.max(kept, axis=2, keepdims=True))
            else:
                slope = mask[None] * (1.0 + scores)
                slope_v[step, t, :, cols] = slope.astype(BF).reshape(2 * ROWS, span)
                raised = 0.5 * (mask[None] + slope * slope)
            raised = raised.astype(BF).reshape(2 * ROWS, span)
            raised_v[step, t, :, cols] = raised
            summed = dot(raised, jnp.concatenate([values, jnp.ones((span, 128), BF)], axis=1))
            inverse = 1.0 / summed[:, 128:]
            sides = [lanes_of_value(half) for half in range(2)]
            mid_v[rows, block_of(t)] = merge(sides, summed[:, :128] * inverse).astype(BF)
            inverse_v[rows, block_of(t)] = merge(sides, inverse)
            return carry

        lax.fori_loop(0, 8, block, 0, unroll=UNROLL)
        return dot(mid_v[rows, pl.ds(0, D)], tall_v[pl.ds(0, D), :]) * out_scale(kind)

    def attend_backward(kind, micro, part, rows):
        width = low_width(kind)
        span = ROWS * (part + 1)
        keys_at = pl.ds(pl.multiple_of(micro * LEN, LEN), span)
        own = pl.ds(0, span)
        step = micro * CHUNKS_OF + part
        d_mixed = dot_t(g_v[rows, :], tall_v[pl.ds(0, D), :]) * out_scale(kind)
        dy_v[...] = (d_mixed * inverse_v[rows, :]).astype(BF)
        if part == CHUNKS_OF - 1:
            dk_v[...] = jnp.zeros_like(dk_v)
            dv_v[...] = jnp.zeros_like(dv_v)
        if kind == LINEAR:
            dq_v[...] = jnp.zeros_like(dq_v)

        def block(t, carry):
            index = query_index(kind, t)
            queries = first_v[rows, block_of(index)]
            keys = first_v[keys_at, block_of(index, width)]
            values = second_v[keys_at, block_of(t)]
            heads = [lanes_of_head(kind, t, half) for half in range(2)]
            sides = [lanes_of_value(half) for half in range(2)]
            d_mixed = both(sides, dy_v[:, block_of(t)])
            mixed = mid_v[rows, block_of(t)].astype(F32)
            shift = jnp.sum(d_mixed.astype(F32) * jnp.concatenate([mixed, mixed], axis=0), axis=1, keepdims=True)
            d_weights = dot_t(d_mixed, values) - shift
            raised = raised_v[step, t, :, own]
            slope = raised if kind == WINDOW else slope_v[step, t, :, own]
            d_scores = (slope.astype(F32) * d_weights).astype(BF)
            dv_v[own, block_of(t)] += dot_0(raised, d_mixed)
            d_queries = merge(heads, dot(d_scores, keys)) * root_of(kind)
            dk_v[own, block_of(index)] += dot_0(d_scores, both(heads, queries)) * root_of(kind)
            if kind == WINDOW:
                dq_v[:, block_of(t)] = d_queries
            else:
                dq_v[:, block_of(index)] += d_queries
            return carry

        lax.fori_loop(0, 8, block, 0, unroll=UNROLL)
        done = pl.ds(part * ROWS, ROWS)
        first_v[rows, pl.ds(0, width)] = dq_v[:, pl.ds(0, width)].astype(BF)
        first_v[rows, pl.ds(width, width)] = dk_v[done, pl.ds(0, width)].astype(BF)
        second_v[rows, pl.ds(0, D)] = dv_v[done, :].astype(BF)
        total = dot_t(first_v[rows, pl.ds(0, 2 * width)], wide_v[0, :, pl.ds(0, 2 * width)])
        total += dot_t(second_v[rows, pl.ds(0, D)], wide_v[1, :, pl.ds(0, D)])
        dh_v[...] = total * SCALE

    steps = MICRO * CHUNKS_OF

    @pl.when(is_feed(section))
    def _():
        def forward(step, carry):
            forward_step(step, feed_forward)
            return carry

        lax.fori_loop(0, steps, forward, 0)

    for kind in (WINDOW, LINEAR):

        @pl.when(section == kind)
        def _(kind=kind):
            def forward(micro, carry):
                for part in range(CHUNKS_OF):
                    forward_step(
                        micro * CHUNKS_OF + part, functools.partial(attend_forward, kind, micro, part)
                    )
                return carry

            lax.fori_loop(0, MICRO, forward, 0)

    def settle(step, carry):
        @pl.when(section < last)
        def _():
            hand_on(step).wait_send()

        for copy in forward_outs(step):
            copy.wait()
        return carry

    lax.fori_loop(0, steps, settle, 0)

    @pl.when(section == last)
    def _():
        tangent_copy.wait()

    @pl.when(is_feed(section))
    def _():
        def backward(step, carry):
            micro, part = step // CHUNKS_OF, CHUNKS_OF - 1 - lax.rem(step, CHUNKS_OF)
            backward_step(micro * CHUNKS_OF + part, feed_backward)
            return carry

        lax.fori_loop(0, steps, backward, 0)

    for kind in (WINDOW, LINEAR):

        @pl.when(section == kind)
        def _(kind=kind):
            def backward(micro, carry):
                for part in reversed(range(CHUNKS_OF)):
                    backward_step(
                        micro * CHUNKS_OF + part, functools.partial(attend_backward, kind, micro, part)
                    )
                return carry

            lax.fori_loop(0, MICRO, backward, 0)

    def finish(step, carry):
        @pl.when(section > 0)
        def _():
            hand_back(step).wait_send()

        for copy in backward_outs(step):
            copy.wait()
        return carry

    lax.fori_loop(0, steps, finish, 0)


UNROLL = 2


def train(tokens, cotangent, flat, doc_col, doc_row):
    count = MICRO * LEN
    steps = MICRO * CHUNKS_OF
    return pl.pallas_call(
        train_kernel,
        out_shape=(
            jax.ShapeDtypeStruct((count, D), BF),
            jax.ShapeDtypeStruct((count, D), F32),
            jax.ShapeDtypeStruct((count, D), BF),
            jax.ShapeDtypeStruct((count, FP), BF),
            jax.ShapeDtypeStruct((count, FP), BF),
            jax.ShapeDtypeStruct((count, FP), BF),
            jax.ShapeDtypeStruct((count, D), BF),
            jax.ShapeDtypeStruct((8, D), F32),
        ),
        in_specs=[any_spec()] * 3 + [vmem_spec()] * 2,
        out_specs=(any_spec(),) * 7 + (vmem_spec(),),
        scratch_shapes=[
            pltpu.VMEM((2, D, FP), BF),
            pltpu.VMEM((FP, D), BF),
            pltpu.VMEM((1, D), BF),
            pltpu.VMEM((count, D), BF),
            pltpu.VMEM((count, D), BF),
            pltpu.VMEM((count, D), BF),
            pltpu.VMEM((count, D), BF),
            pltpu.VMEM((count, D), F32),
            pltpu.VMEM((count, FP), BF),
            pltpu.VMEM((count, FP), BF),
            pltpu.VMEM((count, FP), BF),
            pltpu.VMEM((ROWS, D), F32),
            pltpu.VMEM((steps, 8, 2 * ROWS, LEN), BF),
            pltpu.VMEM((steps, 8, 2 * ROWS, LEN), BF),
            pltpu.VMEM((count, D), F32),
            pltpu.VMEM((ROWS, LEN), F32),
            pltpu.VMEM((ROWS, D), BF),
            pltpu.VMEM((ROWS, D), F32),
            pltpu.VMEM((LEN, D), F32),
            pltpu.VMEM((LEN, D), F32),
            pltpu.VMEM((AHEAD, 1, PAIR_STEP), BF),
            pltpu.VMEM((PAIR_STEP // 128, 128), F32),
            pltpu.VMEM((22, 32, 128), F32),
            pltpu.SemaphoreType.DMA((AHEAD,)),
            pltpu.SemaphoreType.DMA,
            pltpu.SemaphoreType.DMA((2,)),
            pltpu.SemaphoreType.DMA((3, steps)),
            pltpu.SemaphoreType.DMA((4, steps)),
            pltpu.SemaphoreType.DMA((steps,)),
            pltpu.SemaphoreType.DMA((steps,)),
            pltpu.SemaphoreType.DMA((steps,)),
            pltpu.SemaphoreType.DMA((steps,)),
        ],
        compiler_params=pltpu.CompilerParams(
            collective_id=0, has_side_effects=True, vmem_limit_bytes=62 * MIB
        ),
        name="train",
    )(tokens, cotangent, flat, doc_col, doc_row)


HEAD_ROWS = 16
PAIR_ROWS = 128 * 43
CHUNKS = 11


def flip(source, first, width, target):
    def piece(t, carry):
        cols = pl.ds(pl.multiple_of(t * 128, 128), 128)
        rows = pl.ds(pl.multiple_of(first + t * 128, 128), 128)
        target[rows, :] = source[:, cols].astype(F32).T.astype(target.dtype)
        return carry

    lax.fori_loop(0, width // 128, piece, 0)


class Products:
    def __init__(self, sources, scratch):
        self.normed, self.d_first, self.d_second, self.middle, self.grads, self.d_gain = sources
        self.h_v, self.d_v, self.m_v, self.g_v, self.turned, self.m_turned, self.stage, self.in_sem = scratch

    def fetch(self, source, target, index):
        return pltpu.make_async_copy(source, target, self.in_sem.at[index])

    def shared(self):
        return [
            self.fetch(self.normed, self.h_v, 0),
            self.fetch(self.grads, self.g_v, 1),
            self.fetch(self.d_first, self.d_v.at[0], 2),
            self.fetch(self.d_second, self.d_v.at[1], 3),
        ]

    def middle_half(self, part):
        half = FP // 2
        return self.fetch(self.middle.at[:, pl.ds(part * half, half)], self.m_v, 4)

    def mixed(self):
        return self.fetch(self.middle.at[:, pl.ds(0, D)], self.m_v.at[:, pl.ds(0, D)], 4)

    def head(self, out):
        stage = self.stage
        stage[pl.ds(0, 8), :] = jnp.zeros((8, 128), F32)
        stage[pl.ds(8, 8), :] = self.d_gain[0:1, :].reshape(8, 128)
        out[pl.ds(0, 16), :] = stage[pl.ds(0, 16), :].astype(BF)

    def cut(self, out, first_row, rows, piece):
        def step(j, carry):
            source = pl.ds(pl.multiple_of(j * piece, 16), piece)
            target = pl.ds(pl.multiple_of(first_row + j * piece, 16), piece)
            out[target, :] = self.stage[source, :].astype(BF)
            return carry

        lax.fori_loop(0, rows // piece, step, 0)

    def start_feed(self):
        self.middle_half(0).start()
        for copy in self.shared():
            copy.wait()
        stage = self.stage

        def halves(t, carry):
            cols = pl.ds(pl.multiple_of(t * 128, 128), 128)
            stage[pl.ds(0, 512), :] = self.h_v[:, cols].astype(F32)
            for part in range(4):
                stage[pl.ds(512 + 128 * part, 128), :] = stage[pl.ds(128 * part, 128), :].T
            for part in range(4):
                for odd in range(2):
                    rows = pl.ds(pl.multiple_of(512 * odd + t * 64, 64), 64)
                    piece = stage[pl.ds(512 + 128 * part + odd, 64, stride=2), :]
                    self.turned[rows, pl.ds(128 * part, 128)] = piece.astype(BF)
            return carry

        lax.fori_loop(0, 8, halves, 0)
        half = FP // 2
        for part in range(2):
            self.middle_half(part).wait()
            flip(self.m_v, part * half, half, self.m_turned)
            if part == 0:
                self.middle_half(1).start()

    def pairs(self, out, which, first_pair, count, first_row):
        stage = self.stage
        half = FP // 2
        low_half = lax.broadcasted_iota(jnp.int32, (count, 128), 1) < 64
        even = self.turned[pl.ds(pl.multiple_of(first_pair, 16), count), :]
        odd = self.turned[pl.ds(pl.multiple_of(512 + first_pair, 16), count), :]
        for part in range(2):
            piece = dot(even, self.d_v[which, :, pl.ds(part * half, half)]) * SCALE
            for c in range(11):
                stage[pl.ds(11 * part + c, count, stride=43), :] = piece[:, 128 * c : 128 * c + 128]
        before = stage[pl.ds(21, count, stride=43), :]
        for part in range(2):
            piece = dot(odd, self.d_v[which, :, pl.ds(part * half, half)]) * SCALE
            for c in range(11):
                here = pltpu.roll(piece[:, 128 * c : 128 * c + 128], 64, 1)
                stage[pl.ds(21 + 11 * part + c, count, stride=43), :] = jnp.where(low_half, before, here)
                before = here
        self.cut(out, first_row, 43 * count, 688)

    def tall(self, out, left, right, stride, rows, first_row, scale, piece):
        product = dot(left, right) * scale
        for c in range(stride):
            self.stage[pl.ds(c, rows, stride=stride), :] = product[:, 128 * c : 128 * c + 128]
        self.cut(out, first_row, rows * stride, piece)

    def down(self, out, first_channel, rows, first_row, piece):
        left = self.m_turned[pl.ds(pl.multiple_of(first_channel, 16), rows), :]
        self.tall(out, left, self.g_v[...], 8, rows, first_row, SCALE, piece)

    def feed_tile(self, out, k):
        first_row = pl.multiple_of(HEAD_ROWS + k * PAIR_ROWS, 16)

        @pl.when(k < 8)
        def _():
            self.pairs(out, k // 4, lax.rem(k, 4) * 128, 128, first_row)

        @pl.when(k >= 8)
        def _():
            self.down(out, (k - 8) * 688, 688, first_row, 688)

    def start_attention(self):
        self.mixed().start()
        for copy in self.shared():
            copy.wait()
        flip(self.h_v, 0, D, self.turned)
        self.mixed().wait()
        flip(self.m_v, 0, D, self.m_turned)

    def square(self, out, left, right, first_row, scale):
        def step(i, carry):
            rows = pl.ds(pl.multiple_of(i * 512, 512), 512)
            self.tall(out, left[rows, :], right(), 8, 512, pl.multiple_of(first_row + i * 4096, 16), scale, 512)
            return carry

        lax.fori_loop(0, 2, step, 0)

    def window(self, out, part):
        first_row = HEAD_ROWS + part * 8192
        if part < 3:
            cols = pl.ds(D if part == 1 else 0, D)
            self.square(out, self.turned, lambda: self.d_v[part // 2, :, cols], first_row, SCALE)
        else:
            self.square(out, self.m_turned, lambda: self.g_v[...], first_row, out_scale(WINDOW))

    def linear(self, out):
        width = HEADS * FEAT
        for part in range(2):
            right = self.d_v[0, :, pl.ds(part * width, width)]
            self.tall(out, self.turned[...], right, 2, D, HEAD_ROWS + part * 2048, SCALE, 512)
        self.square(out, self.turned, lambda: self.d_v[1, :, pl.ds(0, D)], HEAD_ROWS + 4096, SCALE)
        self.square(out, self.m_turned, lambda: self.g_v[...], HEAD_ROWS + 12288, out_scale(LINEAR))


def product_scratch():
    count = MICRO * LEN
    return [
        pltpu.VMEM((count, D), BF),
        pltpu.VMEM((2, count, FP), BF),
        pltpu.VMEM((count, FP // 2), BF),
        pltpu.VMEM((count, D), BF),
        pltpu.VMEM((D, count), BF),
        pltpu.VMEM((FP, count), BF),
        pltpu.VMEM((PAIR_ROWS, 128), F32),
        pltpu.SemaphoreType.DMA((5,)),
    ]


def clear(out, first_row, rows):
    def step(i, carry):
        out[pl.ds(pl.multiple_of(first_row + i * 128, 16), 128), :] = jnp.zeros((128, 128), BF)
        return carry

    lax.fori_loop(0, rows // 128, step, 0)
    if rows % 128:
        out[pl.ds(first_row + rows // 128 * 128, rows % 128), :] = jnp.zeros((rows % 128, 128), BF)


def products_kernel(*refs):
    section = lax.axis_index("section")
    work = Products(refs[:6], refs[8:])
    out, out_v = refs[6:8]
    total = out_v.shape[0]
    for copy in work.shared():
        copy.start()
    work.head(out_v)

    @pl.when(is_feed(section))
    def _():
        work.start_feed()

        def tile(k, carry):
            work.feed_tile(out_v, k)
            return carry

        lax.fori_loop(0, 12, tile, 0)

    @pl.when(section == WINDOW)
    def _():
        work.start_attention()
        for part in range(4):
            work.window(out_v, part)
        done = HEAD_ROWS + 4 * 8192
        clear(out_v, done, total - done)

    @pl.when(section == LINEAR)
    def _():
        work.start_attention()
        work.linear(out_v)
        done = HEAD_ROWS + 20480
        clear(out_v, done, total - done)

    store = pltpu.make_async_copy(out_v, out, work.in_sem.at[0])
    store.start()
    store.wait()


def products(sources, total_rows):
    return pl.pallas_call(
        products_kernel,
        out_shape=jax.ShapeDtypeStruct((total_rows, 128), BF),
        in_specs=[any_spec()] * 5 + [vmem_spec()],
        out_specs=any_spec(),
        scratch_shapes=[pltpu.VMEM((total_rows, 128), BF)] + product_scratch(),
        compiler_params=pltpu.CompilerParams(vmem_limit_bytes=56 * MIB),
        name="products",
    )(*sources)


def reduce_kernel(chain, *refs):
    section = lax.axis_index("section")
    batch = lax.axis_index("batch")
    place, core = batch // 2, lax.rem(batch, 2)
    work = Products(refs[:6], refs[13:])
    out, part, own, passing, total, flat, sems = refs[6:13]
    ex_send, ex_recv, up_send, down_send, recv, out_sem = sems
    width = own.shape[1]
    step_rows = width - HEAD_ROWS
    piece = width // CHUNKS
    feed_here = is_feed(section)
    ends = jnp.where(feed_here, chain, 2)
    barrier = pltpu.get_barrier_semaphore()

    def greet(other):
        pl.semaphore_signal(barrier, inc=1, device_id=(section, other), device_id_type=MESH)

    for copy in work.shared():
        copy.start()
    greet(2 * place + 1 - core)

    @pl.when(place > 0)
    def _():
        greet(batch - 2)

    @pl.when(place < chain - 1)
    def _():
        greet(batch + 2)

    work.head(part)
    pl.semaphore_wait(barrier, jnp.where((place > 0) & (place < chain - 1), 3, 2))

    def rows_of(i):
        return pl.ds(pl.multiple_of(i * piece, 16), piece)

    def share(index, i):
        return pl.ds(pl.multiple_of(step_rows * index + i * piece, 16), piece)

    def swap(to):
        other = 2 * to + 1 - core
        return pltpu.make_async_remote_copy(
            src_ref=part.at[pl.ds(pl.multiple_of(step_rows * other, 16), width), :],
            dst_ref=own.at[to],
            send_sem=ex_send.at[to],
            recv_sem=ex_recv.at[to],
            device_id=(section, 2 * place + 1 - core),
            device_id_type=MESH,
        )

    def up_slot(at, to):
        return to - at

    def down_slot(at, to):
        return chain - at + to

    def go_up(source, to, i):
        slot = up_slot(place + 1, to)
        return pltpu.make_async_remote_copy(
            src_ref=source,
            dst_ref=passing.at[slot, rows_of(i), :],
            send_sem=up_send.at[to - 1, i],
            recv_sem=recv.at[slot, i],
            device_id=(section, batch + 2),
            device_id_type=MESH,
        )

    def go_down(source, to, i):
        slot = down_slot(place - 1, to)
        return pltpu.make_async_remote_copy(
            src_ref=source,
            dst_ref=passing.at[slot, rows_of(i), :],
            send_sem=down_send.at[to, i],
            recv_sem=recv.at[slot, i],
            device_id=(section, batch - 2),
            device_id_type=MESH,
        )

    def arrived(slot, i):
        here = passing.at[slot, rows_of(i), :]
        pltpu.make_async_copy(here, here, recv.at[slot, i]).wait()

    def each_chunk(act):
        def step(i, carry):
            act(i)
            return carry

        lax.fori_loop(0, CHUNKS, step, 0)

    def trade(to):
        swap(to).start()
        swap(to).wait()

        def add(i):
            rows = rows_of(i)
            mine = part[share(2 * to + core, i), :].astype(F32)
            own[to, rows, :] = (own[to, rows, :].astype(F32) + mine).astype(BF)

            @pl.when((place == 0) & (to > 0))
            def _():
                go_up(own.at[to, rows, :], to, i).start()

            @pl.when((place == chain - 1) & (to < chain - 1))
            def _():
                go_down(own.at[to, rows, :], to, i).start()

        each_chunk(add)

    @pl.when(feed_here)
    def _():
        work.start_feed()

        def group(t, carry):
            to = jnp.where(place < chain // 2, chain - 1 - t, t)

            def tile(k, inner):
                work.feed_tile(part, 3 * to + k)
                return inner

            lax.fori_loop(0, 3, tile, 0)

            before = HEAD_ROWS + 3 * PAIR_ROWS * to

            @pl.when((place < chain // 2) & ((to == 1) | (to == 2)))
            def _():
                first_pair = jnp.where(to == 1, 368, 240)
                work.pairs(part, to - 1, first_pair, 16, pl.multiple_of(before - 688, 16))

            @pl.when((place < chain // 2) & (to == 3))
            def _():
                work.down(part, 672, 16, pl.multiple_of(before - 128, 16), 128)

            trade(to)
            return carry

        lax.fori_loop(0, chain, group, 0)

    last_row = 4 * step_rows + HEAD_ROWS

    @pl.when(section == WINDOW)
    def _():
        work.start_attention()
        for index in range(3):
            work.window(part, index)
        trade(0)
        work.window(part, 3)
        done = HEAD_ROWS + 4 * 8192
        clear(part, done, last_row - done)
        trade(1)

    @pl.when(section == LINEAR)
    def _():
        work.start_attention()
        work.linear(part)
        done = HEAD_ROWS + 20480
        clear(part, done, last_row - done)
        trade(0)
        trade(1)

    def pass_on(t, carry):
        upward, downward = ends - 1 - t, t

        def step(i):
            @pl.when((place > 0) & (upward > place))
            def _():
                slot = up_slot(place, upward)
                rows = rows_of(i)
                arrived(slot, i)
                added = passing[slot, rows, :].astype(F32) + own[upward, rows, :].astype(F32)
                passing[slot, rows, :] = added.astype(BF)
                go_up(passing.at[slot, rows, :], upward, i).start()

            @pl.when((place < chain - 1) & (downward < place))
            def _():
                slot = down_slot(place, downward)
                rows = rows_of(i)
                arrived(slot, i)
                added = passing[slot, rows, :].astype(F32) + own[downward, rows, :].astype(F32)
                passing[slot, rows, :] = added.astype(BF)
                go_down(passing.at[slot, rows, :], downward, i).start()

        each_chunk(step)
        return carry

    lax.fori_loop(0, ends, pass_on, 0)

    def finish(i):
        rows = rows_of(i)

        @pl.when(place < ends)
        def _():
            total[...] = own[place, rows, :].astype(F32)

        @pl.when(place >= ends)
        def _():
            total[...] = jnp.zeros_like(total)

        @pl.when((place > 0) & (place < ends))
        def _():
            arrived(0, i)
            total[...] += passing[0, rows, :].astype(F32)

        @pl.when((place < chain - 1) & (place < ends))
        def _():
            arrived(chain, i)
            total[...] += passing[chain, rows, :].astype(F32)

        flat[0:1, pl.ds(pl.multiple_of(i * piece * 128, 1024), piece * 128)] = total[...].reshape(1, piece * 128)

    each_chunk(finish)
    count = out.shape[1]
    first = pl.multiple_of((8 + batch) * 128, 128)
    store = pltpu.make_async_copy(flat.at[:, pl.ds(first, count)], out, out_sem)
    store.start()

    def drain(t, carry):
        upward, downward = ends - 1 - t, t

        def step(i):
            @pl.when((place < chain - 1) & (upward > place))
            def _():
                go_up(passing.at[0, rows_of(i), :], upward, i).wait_send()

            @pl.when((place > 0) & (downward < place))
            def _():
                go_down(passing.at[0, rows_of(i), :], downward, i).wait_send()

        each_chunk(step)
        return carry

    lax.fori_loop(0, ends, drain, 0)
    store.wait()


def reduce_products(sources, total_rows, batches):
    chain = batches // 2
    step_rows = (total_rows - 8) // batches - 1
    width = step_rows + HEAD_ROWS
    return pl.pallas_call(
        functools.partial(reduce_kernel, chain),
        out_shape=jax.ShapeDtypeStruct((1, (step_rows + 1) * 128), F32),
        in_specs=[any_spec()] * 5 + [vmem_spec()],
        out_specs=any_spec(),
        scratch_shapes=[
            pltpu.VMEM((total_rows, 128), BF),
            pltpu.VMEM((chain, width, 128), BF),
            pltpu.VMEM((chain + 1, width, 128), BF),
            pltpu.VMEM((width // CHUNKS, 128), F32),
            pltpu.VMEM((1, width * 128), F32),
            (
                pltpu.SemaphoreType.DMA((chain,)),
                pltpu.SemaphoreType.DMA((chain,)),
                pltpu.SemaphoreType.DMA((chain - 1, CHUNKS)),
                pltpu.SemaphoreType.DMA((chain - 1, CHUNKS)),
                pltpu.SemaphoreType.DMA((chain + 1, CHUNKS)),
                pltpu.SemaphoreType.DMA,
            ),
        ]
        + product_scratch(),
        compiler_params=pltpu.CompilerParams(
            collective_id=1, has_side_effects=True, vmem_limit_bytes=62 * MIB
        ),
        name="reduce_products",
    )(*sources)


def document_ids(lengths):
    ends = jnp.cumsum(lengths, axis=1)
    places = jnp.arange(LEN, dtype=jnp.int32)
    return jnp.sum((places[None, :, None] >= ends[:, None, :]).astype(jnp.int32), axis=2)


def shards(tokens, cotangent, params, lengths):
    docs = document_ids(lengths[0])
    doc_col, doc_row = docs[:, :, None], docs[:, None, :]
    acts, d_inputs, normed, middle, d_first, d_second, grads, d_gain = train(
        tokens, cotangent, params, doc_col, doc_row
    )
    total_rows = params.shape[1] // 128 + 8
    sources = (normed, d_first, d_second, middle, grads, d_gain)
    batches = lax.axis_size("batch")
    if batches == 8:
        mine = reduce_products(sources, total_rows, batches)
    else:
        parts = products(sources, total_rows)
        mine = lax.psum_scatter(parts[8:].reshape(-1), "batch", scatter_dimension=0, tiled=True)
        mine = mine.astype(F32)[None]
    return acts[None], d_inputs[None], mine


def solution(mesh):
    return jax.shard_map(
        shards,
        mesh=mesh,
        in_specs=(P("batch", None), P("batch", None), P("section", None), P("batch", None, None)),
        out_specs=(P("section", "batch", None), P("section", "batch", None), P("section", "batch")),
        check_vma=False,
    )
```

```python
import functools
import math

import jax
import jax.numpy as jnp
from jax import lax
from jax.experimental import pallas as pl
from jax.experimental.pallas import tpu as pltpu
from jax.sharding import PartitionSpec as P

D = 1024
FF = 2752
FP = 2816
HEADS = 16
FEAT = 16
WIN = 64
MICRO = 2
LEN = 256
EPSILON = 1e-06
SCALE = 1.0 / math.sqrt(D)
LINEAR, FEED, WINDOW, FEED2 = 0, 1, 2, 3
MIB = 2**20
MESH = pl.DeviceIdType.MESH
BF = jnp.bfloat16
F32 = jnp.float32


def any_spec():
    return pl.BlockSpec(memory_space=pl.ANY)


def vmem_spec():
    return pl.BlockSpec(memory_space=pltpu.VMEM)


def dot(left, right):
    return jnp.dot(left, right, preferred_element_type=F32)


def dot_t(left, right):
    return lax.dot_general(left, right, (((1,), (1,)), ((), ())), preferred_element_type=F32)


def dot_0(left, right):
    return lax.dot_general(left, right, (((0,), (0,)), ((), ())), preferred_element_type=F32)


def is_feed(section):
    return (section == FEED) | (section == FEED2)


PAIR_STEP = 32 * FF
ROW_STEP = 64 * D
AHEAD = 8


def prepare(section, flat, wide_v, tall_v, chunk, blocks, woven, load_sem):
    def run(steps, count, first, work):
        def load(i):
            slot = lax.rem(i, AHEAD)
            return pltpu.make_async_copy(
                flat.at[:, pl.ds(pl.multiple_of(first + i * count, 1024), count)],
                chunk.at[slot, :, pl.ds(0, count)],
                load_sem.at[slot],
            )

        def start(i, carry):
            load(i).start()
            return carry

        lax.fori_loop(0, AHEAD, start, 0)

        def step(i, carry):
            load(i).wait()
            rows = count // 128
            blocks[pl.ds(0, rows), :] = chunk[lax.rem(i, AHEAD), :, pl.ds(0, count)].astype(F32).reshape(rows, 128)
            work(i)

            @pl.when(i + AHEAD < steps)
            def _():
                load(i + AHEAD).start()

            return carry

        lax.fori_loop(0, steps, step, 0)

    def rows_of(index, count):
        return pl.ds(pl.multiple_of(index * count, count), count)

    def pair_work(i):
        low_half = lax.broadcasted_iota(jnp.int32, (16, 128), 1) < 64
        rolled = pltpu.roll(blocks[pl.ds(21, 16, stride=43), :], 64, 1)
        for c in range(22):
            even = blocks[pl.ds(c, 16, stride=43), :]
            if c == 21:
                even = jnp.where(low_half, even, 0.0)
                odd = jnp.where(low_half, rolled, 0.0)
            else:
                after = pltpu.roll(blocks[pl.ds(22 + c, 16, stride=43), :], 64, 1)
                odd = jnp.where(low_half, rolled, after)
                rolled = after
            woven[c, pl.ds(0, 16, stride=2), :] = even
            woven[c, pl.ds(1, 16, stride=2), :] = odd
        rows = rows_of(lax.rem(i, 32), 32)
        for c in range(22):
            wide_v[i // 32, rows, pl.ds(128 * c, 128)] = woven[c].astype(BF)

    def row_work(target, rows, first_col):
        for c in range(8):
            target[rows, pl.ds(first_col + 128 * c, 128)] = blocks[pl.ds(c, 64, stride=8), :].astype(BF)

    def square(i, first, target, first_col):
        @pl.when((i >= first) & (i < first + 16))
        def _():
            row_work(target, rows_of(i - first, 64), first_col)

    @pl.when(is_feed(section))
    def _():
        run(64, PAIR_STEP, D, pair_work)
        run(43, ROW_STEP, D + 2 * D * FF, lambda i: row_work(tall_v, rows_of(i, 64), 0))
        tall_v[pl.ds(FF, FP - FF), :] = jnp.zeros((FP - FF, D), BF)

    @pl.when(section == WINDOW)
    def _():
        def work(i):
            square(i, 0, wide_v.at[0], 0)
            square(i, 16, wide_v.at[0], D)
            square(i, 32, wide_v.at[1], 0)
            square(i, 48, tall_v, 0)

        run(64, ROW_STEP, D, work)

    @pl.when(section == LINEAR)
    def _():
        def work(i):
            for part in range(2):

                @pl.when(i // 4 == part)
                def _(part=part):
                    rows = rows_of(i - 4 * part, 256)
                    for c in range(2):
                        cols = pl.ds(part * HEADS * FEAT + 128 * c, 128)
                        wide_v[0, rows, cols] = blocks[pl.ds(c, 256, stride=2), :].astype(BF)

            square(i, 8, wide_v.at[1], 0)
            square(i, 24, tall_v, 0)

        run(40, ROW_STEP, D, work)


ROWS = 128
CHUNKS_OF = LEN // ROWS


def lanes_of_head(kind, block, half):
    lanes = lax.broadcasted_iota(jnp.int32, (1, 128), 1)
    if kind == WINDOW:
        return lanes // 64 == half
    return lanes // FEAT == lax.rem(2 * block + half, 8)


def lanes_of_value(half):
    return lax.broadcasted_iota(jnp.int32, (1, 128), 1) // 64 == half


def only(mask, values):
    return jnp.where(mask, values, jnp.zeros_like(values))


def both(masks, values):
    return jnp.concatenate([only(masks[0], values), only(masks[1], values)], axis=0)


def merge(masks, stacked):
    return only(masks[0], stacked[:ROWS]) + only(masks[1], stacked[ROWS:])


def block_of(index, first=0):
    return pl.ds(pl.multiple_of(first + index * 128, 128), 128)


def query_index(kind, block):
    return block if kind == WINDOW else block // 4


def low_width(kind):
    return D if kind == WINDOW else HEADS * FEAT


def mask_of(kind, doc_col, doc_row, first_row):
    shape = (doc_col.shape[0], doc_row.shape[1])
    rows = lax.broadcasted_iota(jnp.int32, shape, 0) + first_row
    cols = lax.broadcasted_iota(jnp.int32, shape, 1)
    mask = (doc_col == doc_row) & (cols <= rows)
    if kind == WINDOW:
        mask = mask & (rows - cols < WIN)
    return mask.astype(F32)


def root_of(kind):
    return 1.0 / math.sqrt(D // HEADS if kind == WINDOW else FEAT)


def out_scale(kind):
    return {LINEAR: 8.0, WINDOW: 4.0, FEED: 1.0}[kind] * SCALE


def train_kernel(
    swapping,
    tokens, cotangent, flat, doc_col, doc_row,
    acts, d_inputs, normed, middle, d_first, d_second, grads, d_gain,
    wide_v, tall_v, gain_v, z_v, h_v, x_v, g_v, dz_v, first_v, second_v, mid_v, dh_v, far_z_v, far_g_v, gain_sum, far_gain,
    raised_v, slope_v, inverse_v, mask_v, dy_v, dq_v, dk_v, dv_v, chunk, blocks, woven,
    load_sem, gain_sem, in_sem, act_sem, out_sem, on_send, on_recv, back_send, back_recv, far_send, far_recv,
):
    section = lax.axis_index("section")
    batch = lax.axis_index("batch")
    last = lax.axis_size("section") - 1
    batches = lax.axis_size("batch")
    far = lax.rem(batch + batches // 2, batches)
    barrier = pltpu.get_barrier_semaphore()
    swaps_here = is_feed(section) if swapping else section < 0

    @pl.when(swaps_here)
    def _():
        pl.semaphore_signal(barrier, inc=1, device_id=(section, far), device_id_type=MESH)

    @pl.when(section > 0)
    def _():
        pl.semaphore_signal(barrier, inc=1, device_id=(section - 1, batch), device_id_type=MESH)

    @pl.when(section < last)
    def _():
        pl.semaphore_signal(barrier, inc=1, device_id=(section + 1, batch), device_id_type=MESH)

    gain_copy = pltpu.make_async_copy(flat.at[:, pl.ds(0, D)], gain_v, gain_sem)
    gain_copy.start()
    token_copy = pltpu.make_async_copy(tokens, z_v, in_sem.at[0])
    tangent_copy = pltpu.make_async_copy(cotangent, g_v, in_sem.at[1])

    @pl.when(section == 0)
    def _():
        token_copy.start()

    @pl.when(section == last)
    def _():
        tangent_copy.start()

    prepare(section, flat, wide_v, tall_v, chunk, blocks, woven, load_sem)
    gain_copy.wait()
    gain = 1.0 + gain_v[...].astype(F32) / 8.0
    gain_sum[...] = jnp.zeros_like(gain_sum)

    @pl.when(section == 0)
    def _():
        token_copy.wait()

    greeted = jnp.where((section > 0) & (section < last), 2, 1)
    pl.semaphore_wait(barrier, greeted + jnp.where(swaps_here, 1, 0))

    def rows_at(step):
        return pl.ds(pl.multiple_of(step * ROWS, ROWS), ROWS)

    def hand_on(step):
        rows = rows_at(step)
        return pltpu.make_async_remote_copy(
            src_ref=x_v.at[rows, :],
            dst_ref=z_v.at[rows, :],
            send_sem=on_send.at[step],
            recv_sem=on_recv.at[step],
            device_id=(section + 1, batch),
            device_id_type=MESH,
        )

    def hand_back(step):
        rows = rows_at(step)
        return pltpu.make_async_remote_copy(
            src_ref=x_v.at[rows, :],
            dst_ref=g_v.at[rows, :],
            send_sem=back_send.at[step],
            recv_sem=back_recv.at[step],
            device_id=(section - 1, batch),
            device_id_type=MESH,
        )

    def far_copy(kind, step):
        rows = rows_at(step)
        source, target = ((z_v, far_z_v), (g_v, far_g_v), (gain_sum, far_gain))[kind]
        return pltpu.make_async_remote_copy(
            src_ref=source if kind == 2 else source.at[rows, :],
            dst_ref=target if kind == 2 else target.at[rows, :],
            send_sem=far_send.at[kind, step],
            recv_sem=far_recv.at[kind, step],
            device_id=(section, far),
            device_id_type=MESH,
        )

    def forward_outs(step):
        rows = rows_at(step)
        return [
            pltpu.make_async_copy(x_v.at[rows, :], acts.at[rows, :], act_sem.at[0, step]),
            pltpu.make_async_copy(h_v.at[rows, :], normed.at[rows, :], act_sem.at[1, step]),
            pltpu.make_async_copy(mid_v.at[rows, :], middle.at[rows, :], act_sem.at[2, step]),
        ]

    def backward_outs(step):
        rows = rows_at(step)
        return [
            pltpu.make_async_copy(dz_v.at[rows, :], d_inputs.at[rows, :], out_sem.at[0, step]),
            pltpu.make_async_copy(g_v.at[rows, :], grads.at[rows, :], out_sem.at[1, step]),
            pltpu.make_async_copy(first_v.at[rows, :], d_first.at[rows, :], out_sem.at[2, step]),
            pltpu.make_async_copy(second_v.at[rows, :], d_second.at[rows, :], out_sem.at[3, step]),
        ]


    def forward_step(step, branch):
        rows = rows_at(step)

        @pl.when(section > 0)
        def _():
            hand_on(step).wait_recv()

        @pl.when(swaps_here)
        def _():
            far_copy(0, step).start()

        z = z_v[rows, :].astype(F32)
        scaled = lax.rsqrt(jnp.mean(z * z, axis=1, keepdims=True) + EPSILON)
        h_v[rows, :] = (z * scaled * gain).astype(BF)
        x_v[rows, :] = (z_v[rows, :].astype(F32) + branch(rows)).astype(BF)

        @pl.when(section < last)
        def _():
            hand_on(step).start()

        for copy in forward_outs(step):
            copy.start()

    def backward_step(step, branch):
        rows = rows_at(step)

        @pl.when(section < last)
        def _():
            hand_back(step).wait_recv()

        @pl.when(swaps_here & (section < last))
        def _():
            far_copy(1, step).start()

        branch(rows)
        z = z_v[rows, :].astype(F32)
        scaled = lax.rsqrt(jnp.mean(z * z, axis=1, keepdims=True) + EPSILON)
        unit = z * scaled
        d_normed = dh_v[...]
        gain_sum[0:1, :] += jnp.sum(d_normed * unit, axis=0, keepdims=True) * 0.125
        d_unit = d_normed * gain
        d_z = scaled * (d_unit - unit * jnp.mean(d_unit * unit, axis=1, keepdims=True))
        d_z += g_v[rows, :].astype(F32)
        dz_v[rows, :] = d_z
        x_v[rows, :] = d_z.astype(BF)

        @pl.when(section > 0)
        def _():
            hand_back(step).start()

        for copy in backward_outs(step):
            copy.start()

    def feed_hidden(rows):
        half = FP // 2
        for part in range(2):
            cols = pl.ds(part * half, half)
            gate = dot(h_v[rows, :], wide_v[0, :, cols]) * SCALE
            up = dot(h_v[rows, :], wide_v[1, :, cols]) * SCALE
            sig = 1.0 / (1.0 + jnp.exp(-gate))
            silu = gate * sig
            first_v[rows, cols] = (up * (sig + silu * (1.0 - sig))).astype(BF)
            second_v[rows, cols] = silu.astype(BF)
            mid_v[rows, cols] = (silu * up).astype(BF)

    def feed_forward(rows):
        feed_hidden(rows)
        return dot(mid_v[rows, :], tall_v[...]) * SCALE

    def feed_unhidden(source, rows):
        half = FP // 2
        for part in range(2):
            cols = pl.ds(part * half, half)
            d_mid = dot_t(source[rows, :], tall_v[cols, :]) * SCALE
            first_v[rows, cols] = (d_mid * first_v[rows, cols].astype(F32)).astype(BF)
            second_v[rows, cols] = (d_mid * second_v[rows, cols].astype(F32)).astype(BF)

    def feed_backward(rows):
        feed_unhidden(g_v, rows)
        total = dot_t(first_v[rows, :], wide_v[0]) + dot_t(second_v[rows, :], wide_v[1])
        dh_v[...] = total * SCALE

    def attend_forward(kind, micro, part, rows):
        width = low_width(kind)
        span = ROWS * (part + 1)
        keys_at = pl.ds(pl.multiple_of(micro * LEN, LEN), span)
        step = micro * CHUNKS_OF + part
        first_v[rows, pl.ds(0, 2 * width)] = (dot(h_v[rows, :], wide_v[0, :, pl.ds(0, 2 * width)]) * SCALE).astype(BF)
        second_v[rows, pl.ds(0, D)] = (dot(h_v[rows, :], wide_v[1, :, pl.ds(0, D)]) * SCALE).astype(BF)
        cols = pl.ds(0, span)
        mask_v[:, cols] = mask_of(
            kind, doc_col[micro, pl.ds(part * ROWS, ROWS), :], doc_row[micro, :, pl.ds(0, span)], part * ROWS
        )

        def block(t, carry):
            index = query_index(kind, t)
            queries = first_v[rows, block_of(index)]
            keys = first_v[keys_at, block_of(index, width)]
            values = second_v[keys_at, block_of(t)]
            heads = [lanes_of_head(kind, t, half) for half in range(2)]
            scores = (dot_t(both(heads, queries), keys) * root_of(kind)).reshape(2, ROWS, span)
            mask = mask_v[:, cols]
            if kind == WINDOW:
                kept = jnp.where((mask > 0.0)[None], scores, -1e30)
                raised = jnp.exp(kept - jnp.max(kept, axis=2, keepdims=True))
            else:
                slope = mask[None] * (1.0 + scores)
                slope_v[step, t, :, cols] = slope.astype(BF).reshape(2 * ROWS, span)
                raised = 0.5 * (mask[None] + slope * slope)
            raised = raised.astype(BF).reshape(2 * ROWS, span)
            raised_v[step, t, :, cols] = raised
            summed = dot(raised, jnp.concatenate([values, jnp.ones((span, 128), BF)], axis=1))
            inverse = 1.0 / summed[:, 128:]
            sides = [lanes_of_value(half) for half in range(2)]
            mid_v[rows, block_of(t)] = merge(sides, summed[:, :128] * inverse).astype(BF)
            inverse_v[rows, block_of(t)] = merge(sides, inverse)
            return carry

        lax.fori_loop(0, 8, block, 0, unroll=UNROLL)
        return dot(mid_v[rows, pl.ds(0, D)], tall_v[pl.ds(0, D), :]) * out_scale(kind)

    def attend_backward(kind, micro, part, rows):
        width = low_width(kind)
        span = ROWS * (part + 1)
        keys_at = pl.ds(pl.multiple_of(micro * LEN, LEN), span)
        own = pl.ds(0, span)
        step = micro * CHUNKS_OF + part
        d_mixed = dot_t(g_v[rows, :], tall_v[pl.ds(0, D), :]) * out_scale(kind)
        dy_v[...] = (d_mixed * inverse_v[rows, :]).astype(BF)
        if part == CHUNKS_OF - 1:
            dk_v[...] = jnp.zeros_like(dk_v)
            dv_v[...] = jnp.zeros_like(dv_v)
        if kind == LINEAR:
            dq_v[...] = jnp.zeros_like(dq_v)

        def block(t, carry):
            index = query_index(kind, t)
            queries = first_v[rows, block_of(index)]
            keys = first_v[keys_at, block_of(index, width)]
            values = second_v[keys_at, block_of(t)]
            heads = [lanes_of_head(kind, t, half) for half in range(2)]
            sides = [lanes_of_value(half) for half in range(2)]
            d_mixed = both(sides, dy_v[:, block_of(t)])
            mixed = mid_v[rows, block_of(t)].astype(F32)
            shift = jnp.sum(d_mixed.astype(F32) * jnp.concatenate([mixed, mixed], axis=0), axis=1, keepdims=True)
            d_weights = dot_t(d_mixed, values) - shift
            raised = raised_v[step, t, :, own]
            slope = raised if kind == WINDOW else slope_v[step, t, :, own]
            d_scores = (slope.astype(F32) * d_weights).astype(BF)
            dv_v[own, block_of(t)] += dot_0(raised, d_mixed)
            d_queries = merge(heads, dot(d_scores, keys)) * root_of(kind)
            dk_v[own, block_of(index)] += dot_0(d_scores, both(heads, queries)) * root_of(kind)
            if kind == WINDOW:
                dq_v[:, block_of(t)] = d_queries
            else:
                dq_v[:, block_of(index)] += d_queries
            return carry

        lax.fori_loop(0, 8, block, 0, unroll=UNROLL)
        done = pl.ds(part * ROWS, ROWS)
        first_v[rows, pl.ds(0, width)] = dq_v[:, pl.ds(0, width)].astype(BF)
        first_v[rows, pl.ds(width, width)] = dk_v[done, pl.ds(0, width)].astype(BF)
        second_v[rows, pl.ds(0, D)] = dv_v[done, :].astype(BF)
        total = dot_t(first_v[rows, pl.ds(0, 2 * width)], wide_v[0, :, pl.ds(0, 2 * width)])
        total += dot_t(second_v[rows, pl.ds(0, D)], wide_v[1, :, pl.ds(0, D)])
        dh_v[...] = total * SCALE

    steps = MICRO * CHUNKS_OF

    @pl.when(section == last)
    def _():
        tangent_copy.wait()

    @pl.when(swaps_here & (section == last))
    def _():
        for step in range(steps):
            far_copy(1, step).start()

    @pl.when(is_feed(section))
    def _():
        def forward(step, carry):
            forward_step(step, feed_forward)
            return carry

        lax.fori_loop(0, steps, forward, 0)

    for kind in (WINDOW, LINEAR):

        @pl.when(section == kind)
        def _(kind=kind):
            def forward(micro, carry):
                for part in range(CHUNKS_OF):
                    forward_step(
                        micro * CHUNKS_OF + part, functools.partial(attend_forward, kind, micro, part)
                    )
                return carry

            lax.fori_loop(0, MICRO, forward, 0)

    def settle(step, carry):
        @pl.when(section < last)
        def _():
            hand_on(step).wait_send()

        for copy in forward_outs(step):
            copy.wait()
        return carry

    lax.fori_loop(0, steps, settle, 0)

    @pl.when(is_feed(section))
    def _():
        def backward(step, carry):
            micro, part = step // CHUNKS_OF, CHUNKS_OF - 1 - lax.rem(step, CHUNKS_OF)
            backward_step(micro * CHUNKS_OF + part, feed_backward)
            return carry

        lax.fori_loop(0, steps, backward, 0)

    for kind in (WINDOW, LINEAR):

        @pl.when(section == kind)
        def _(kind=kind):
            def backward(micro, carry):
                for part in reversed(range(CHUNKS_OF)):
                    backward_step(
                        micro * CHUNKS_OF + part, functools.partial(attend_backward, kind, micro, part)
                    )
                return carry

            lax.fori_loop(0, MICRO, backward, 0)

    def finish(step, carry):
        @pl.when(section > 0)
        def _():
            hand_back(step).wait_send()

        for copy in backward_outs(step):
            copy.wait()
        return carry

    @pl.when(swaps_here)
    def _():
        far_copy(2, 0).start()

    lax.fori_loop(0, steps, finish, 0)

    @pl.when(jnp.logical_not(swaps_here))
    def _():
        d_gain[...] = gain_sum[...]

    if not swapping:
        return

    count = steps * ROWS
    wide_rows = 2 * ROWS

    def far_rows(t):
        return pl.ds(pl.multiple_of(t * wide_rows, wide_rows), wide_rows)

    def far_target(t):
        return pl.ds(pl.multiple_of(count + t * wide_rows, wide_rows), wide_rows)

    def far_acts(t):
        rows, target = far_rows(t), far_target(t)
        return [
            pltpu.make_async_copy(h_v.at[rows, :], normed.at[target, :], act_sem.at[1, t]),
            pltpu.make_async_copy(mid_v.at[rows, :], middle.at[target, :], act_sem.at[2, t]),
        ]

    def far_outs(t):
        rows, target = far_rows(t), far_target(t)
        return [
            pltpu.make_async_copy(far_g_v.at[rows, :], grads.at[target, :], out_sem.at[1, t]),
            pltpu.make_async_copy(first_v.at[rows, :], d_first.at[target, :], out_sem.at[2, t]),
            pltpu.make_async_copy(second_v.at[rows, :], d_second.at[target, :], out_sem.at[3, t]),
        ]

    @pl.when(swaps_here)
    def _():
        def far_forward(t, carry):
            rows = far_rows(t)
            for step in range(2):
                far_copy(0, 2 * t + step).wait_recv()
            z = far_z_v[rows, :].astype(F32)
            scaled = lax.rsqrt(jnp.mean(z * z, axis=1, keepdims=True) + EPSILON)
            h_v[rows, :] = (z * scaled * gain).astype(BF)
            feed_hidden(rows)
            for copy in far_acts(t):
                copy.start()
            return carry

        lax.fori_loop(0, steps // 2, far_forward, 0)

        def far_backward(t, carry):
            for step in range(2):
                far_copy(1, 2 * t + step).wait_recv()
            feed_unhidden(far_g_v, far_rows(t))
            for copy in far_outs(t):
                copy.start()
            return carry

        lax.fori_loop(0, steps // 2, far_backward, 0)
        far_copy(2, 0).wait()
        d_gain[...] = gain_sum[...] + far_gain[...]
        for kind in range(2):
            for step in range(steps):
                far_copy(kind, step).wait_send()

        def far_finish(t, carry):
            for copy in far_acts(t) + far_outs(t):
                copy.wait()
            return carry

        lax.fori_loop(0, steps // 2, far_finish, 0)


UNROLL = 2


def train(tokens, cotangent, flat, doc_col, doc_row, swapping):
    count = MICRO * LEN
    steps = MICRO * CHUNKS_OF
    kept = 2 * count if swapping else count
    return pl.pallas_call(
        functools.partial(train_kernel, swapping),
        out_shape=(
            jax.ShapeDtypeStruct((count, D), BF),
            jax.ShapeDtypeStruct((count, D), F32),
            jax.ShapeDtypeStruct((kept, D), BF),
            jax.ShapeDtypeStruct((kept, FP), BF),
            jax.ShapeDtypeStruct((kept, FP), BF),
            jax.ShapeDtypeStruct((kept, FP), BF),
            jax.ShapeDtypeStruct((kept, D), BF),
            jax.ShapeDtypeStruct((8, D), F32),
        ),
        in_specs=[any_spec()] * 3 + [vmem_spec()] * 2,
        out_specs=(any_spec(),) * 7 + (vmem_spec(),),
        scratch_shapes=[
            pltpu.VMEM((2, D, FP), BF),
            pltpu.VMEM((FP, D), BF),
            pltpu.VMEM((1, D), BF),
            pltpu.VMEM((count, D), BF),
            pltpu.VMEM((count, D), BF),
            pltpu.VMEM((count, D), BF),
            pltpu.VMEM((count, D), BF),
            pltpu.VMEM((count, D), F32),
            pltpu.VMEM((count, FP), BF),
            pltpu.VMEM((count, FP), BF),
            pltpu.VMEM((count, FP), BF),
            pltpu.VMEM((ROWS, D), F32),
            pltpu.VMEM((count, D), BF),
            pltpu.VMEM((count, D), BF),
            pltpu.VMEM((8, D), F32),
            pltpu.VMEM((8, D), F32),
            pltpu.VMEM((steps, 8, 2 * ROWS, LEN), BF),
            pltpu.VMEM((steps, 8, 2 * ROWS, LEN), BF),
            pltpu.VMEM((count, D), F32),
            pltpu.VMEM((ROWS, LEN), F32),
            pltpu.VMEM((ROWS, D), BF),
            pltpu.VMEM((ROWS, D), F32),
            pltpu.VMEM((LEN, D), F32),
            pltpu.VMEM((LEN, D), F32),
            pltpu.VMEM((AHEAD, 1, PAIR_STEP), BF),
            pltpu.VMEM((PAIR_STEP // 128, 128), F32),
            pltpu.VMEM((22, 32, 128), F32),
            pltpu.SemaphoreType.DMA((AHEAD,)),
            pltpu.SemaphoreType.DMA,
            pltpu.SemaphoreType.DMA((2,)),
            pltpu.SemaphoreType.DMA((3, steps)),
            pltpu.SemaphoreType.DMA((4, steps)),
            pltpu.SemaphoreType.DMA((steps,)),
            pltpu.SemaphoreType.DMA((steps,)),
            pltpu.SemaphoreType.DMA((steps,)),
            pltpu.SemaphoreType.DMA((steps,)),
            pltpu.SemaphoreType.DMA((3, steps)),
            pltpu.SemaphoreType.DMA((3, steps)),
        ],
        compiler_params=pltpu.CompilerParams(
            collective_id=0, has_side_effects=True, vmem_limit_bytes=62 * MIB
        ),
        name="train",
    )(tokens, cotangent, flat, doc_col, doc_row)


HEAD_ROWS = 16
PAIR_ROWS = 128 * 43
CHUNKS = 11


class Products:
    def __init__(self, sources, scratch, base):
        self.normed, self.d_first, self.d_second, self.middle, self.grads, self.d_gain = sources
        self.h_v, self.d_v, self.g_v, self.woven, self.stage, self.in_sem = scratch
        self.base = base

    def fetch(self, source, target, index):
        return pltpu.make_async_copy(source, target, self.in_sem.at[index])

    def loads(self, names):
        count = self.h_v.shape[0]
        mixed = MICRO * LEN
        some, low, high = pl.ds(0, mixed), pl.ds(0, D), pl.ds(D, D)
        table = {
            "h": (self.normed, self.h_v, 0),
            "g": (self.grads, self.g_v, 1),
            "first": (self.d_first, self.d_v.at[0], 2),
            "second": (self.d_second, self.d_v.at[1], 3),
            "middle": (self.middle, self.d_v.at[self.d_v.shape[0] - 1 if count == mixed else 0], 4),
            "some_h": (self.normed.at[some, :], self.h_v.at[some, :], 0),
            "some_g": (self.grads.at[some, :], self.g_v.at[some, :], 1),
            "some_first": (self.d_first.at[some, pl.ds(0, 2 * D)], self.d_v.at[0, some, pl.ds(0, 2 * D)], 2),
            "some_second": (self.d_second.at[some, low], self.d_v.at[1, some, low], 3),
            "mixed": (self.middle.at[some, low], self.d_v.at[1, some, high], 4),
        }
        return [self.fetch(*table[name]) for name in names]

    def head(self, out):
        stage = self.stage
        stage[pl.ds(0, 8), :] = jnp.zeros((8, 128), F32)
        stage[pl.ds(8, 8), :] = self.d_gain[0:1, :].reshape(8, 128)
        out[pl.ds(0, 16), :] = stage[pl.ds(0, 16), :].astype(BF)

    def cut(self, out, first_row, rows, piece, scale):
        target_row = first_row - self.base

        def step(j, carry):
            source = pl.ds(pl.multiple_of(j * piece, 16), piece)
            target = pl.ds(pl.multiple_of(target_row + j * piece, 16), piece)
            out[target, :] = (self.stage[source, :] * scale).astype(BF)
            return carry

        lax.fori_loop(0, rows // piece, step, 0)

    def pairs(self, which, first_pair, count):
        stage, woven = self.stage, self.woven
        half = FP // 2
        low_half = lax.broadcasted_iota(jnp.int32, (count, 128), 1) < 64
        left = self.h_v[:, pl.ds(pl.multiple_of(2 * first_pair, 128), 2 * count)]
        for part in range(2):
            piece = dot_0(left, self.d_v[which, :, pl.ds(part * half, half)])
            for c in range(11):
                woven[11 * part + c, pl.ds(0, 2 * count), :] = piece[:, 128 * c : 128 * c + 128]
        for c in range(22):
            stage[pl.ds(c, count, stride=43), :] = woven[c, pl.ds(0, count, stride=2), :]
        before = woven[21, pl.ds(0, count, stride=2), :]
        for c in range(22):
            here = pltpu.roll(woven[c, pl.ds(1, count, stride=2), :], 64, 1)
            stage[pl.ds(21 + c, count, stride=43), :] = jnp.where(low_half, before, here)
            before = here

    def pair_tile(self, out, k):
        self.pairs(k // 4, lax.rem(k, 4) * 128, 128)
        self.cut(out, HEAD_ROWS + k * PAIR_ROWS, PAIR_ROWS, 688, SCALE)

    def pair_strip(self, out, k):
        self.pairs(k // 4, lax.rem(k, 4) * 128 + 64, 64)
        target = pl.ds(pl.multiple_of((k + 1) * PAIR_ROWS - self.base, 16), 16)
        out[target, :] = (self.stage[pl.ds(64 * 43 - 16, 16), :] * SCALE).astype(BF)

    def tall(self, out, left, right, stride, rows, first_row, scale, piece):
        product = dot_0(left, right)
        for c in range(stride):
            self.stage[pl.ds(c, rows, stride=stride), :] = product[:, 128 * c : 128 * c + 128]
        self.cut(out, first_row, rows * stride, piece, scale)

    def down(self, out, first_channel, rows):
        slot = self.d_v.shape[0] - 1 if self.h_v.shape[0] == MICRO * LEN else 0
        left = self.d_v[slot, :, pl.ds(first_channel, rows)]
        first_row = HEAD_ROWS + 8 * PAIR_ROWS + 8 * first_channel
        self.tall(out, left, self.g_v[...], 8, rows, first_row, SCALE, 512)

    def square(self, out, left, right, first_row, part, scale):
        rows = left[:, pl.ds(part * 512, 512)]
        self.tall(out, rows, right[...], 8, 512, first_row + part * 4096, scale, 512)

    def window_tile(self, out, k):
        some = pl.ds(0, MICRO * LEN)
        index = k // 2
        left = self.h_v.at[some, :] if index < 3 else self.d_v.at[1, some, pl.ds(D, D)]
        right = (
            self.d_v.at[0, some, pl.ds(0, D)],
            self.d_v.at[0, some, pl.ds(D, D)],
            self.d_v.at[1, some, pl.ds(0, D)],
            self.g_v.at[some, :],
        )[index]
        scale = SCALE if index < 3 else out_scale(WINDOW)
        self.square(out, left, right, HEAD_ROWS + 8192 * index, k % 2, scale)

    def linear_tile(self, out, k):
        some = pl.ds(0, MICRO * LEN)
        width = HEADS * FEAT
        if k < 2:
            right = self.d_v[0, some, pl.ds(k * width, width)]
            self.tall(out, self.h_v[some, :], right, 2, D, HEAD_ROWS + k * 2048, SCALE, 512)
        elif k < 4:
            right = self.d_v.at[1, some, pl.ds(0, D)]
            self.square(out, self.h_v.at[some, :], right, HEAD_ROWS + 4096, k - 2, SCALE)
        else:
            left = self.d_v.at[1, some, pl.ds(D, D)]
            self.square(out, left, self.g_v.at[some, :], HEAD_ROWS + 12288, k - 4, out_scale(LINEAR))


WINDOW_ENDS = [HEAD_ROWS + 4096 * (k + 1) for k in range(8)]
LINEAR_ENDS = [HEAD_ROWS + rows for rows in (2048, 4096, 8192, 12288, 16384, 20480)]


def product_scratch(count, slots):
    return [
        pltpu.VMEM((count, D), BF),
        pltpu.VMEM((slots, count, FP), BF),
        pltpu.VMEM((count, D), BF),
        pltpu.VMEM((22, 256, 128), F32),
        pltpu.VMEM((6144, 128), F32),
        pltpu.SemaphoreType.DMA((5,)),
    ]


def clear(out, first_row, rows):
    def step(i, carry):
        out[pl.ds(pl.multiple_of(first_row + i * 128, 16), 128), :] = jnp.zeros((128, 128), BF)
        return carry

    lax.fori_loop(0, rows // 128, step, 0)
    if rows % 128:
        out[pl.ds(first_row + rows // 128 * 128, rows % 128), :] = jnp.zeros((rows % 128, 128), BF)


def products_kernel(*refs):
    section = lax.axis_index("section")
    work = Products(refs[:6], refs[8:], 0)
    out, out_v = refs[6:8]
    total = out_v.shape[0] - 512
    work.head(out_v)

    def load(*names):
        for copy in work.loads(names):
            copy.start()
        for copy in work.loads(names):
            copy.wait()

    @pl.when(is_feed(section))
    def _():
        load("h", "g", "first", "second", "middle")

        def tile(k, carry):
            work.pair_tile(out_v, k)
            return carry

        lax.fori_loop(0, 8, tile, 0)
        for first, rows in ((0, 640), (640, 640), (1280, 640), (1920, 640), (2560, 256)):
            work.down(out_v, first, rows)

    for kind in (WINDOW, LINEAR):

        @pl.when(section == kind)
        def _(kind=kind):
            load("some_h", "some_g", "some_first", "some_second", "mixed")
            ends = WINDOW_ENDS if kind == WINDOW else LINEAR_ENDS
            for k in range(len(ends)):
                (work.window_tile if kind == WINDOW else work.linear_tile)(out_v, k)
            clear(out_v, ends[-1], total - ends[-1])

    store = pltpu.make_async_copy(out_v.at[pl.ds(0, total), :], out, work.in_sem.at[0])
    store.start()
    store.wait()


def products(sources, total_rows):
    return pl.pallas_call(
        products_kernel,
        out_shape=jax.ShapeDtypeStruct((total_rows, 128), BF),
        in_specs=[any_spec()] * 5 + [vmem_spec()],
        out_specs=any_spec(),
        scratch_shapes=[pltpu.VMEM((total_rows + 512, 128), BF)] + product_scratch(MICRO * LEN, 3),
        compiler_params=pltpu.CompilerParams(vmem_limit_bytes=60 * MIB),
        name="products",
    )(*sources)


PLACES = 4


def reduce_kernel(*refs):
    section = lax.axis_index("section")
    batch = lax.axis_index("batch")
    place, core = batch // 2, lax.rem(batch, 2)
    mate = place + 1 - 2 * lax.rem(place, 2)
    out, part, own, passing, total, flat, sems = refs[6:13]
    ex_send, ex_recv, send, recv, out_sem = sems
    width = own.shape[1]
    step_rows = width - HEAD_ROWS
    piece = width // CHUNKS
    feed_here = is_feed(section)
    base = jnp.where(feed_here, place // 2, 0) * (4 * step_rows)
    work = Products(refs[:6], refs[13:], base)
    barrier = pltpu.get_barrier_semaphore()

    def greet(other):
        pl.semaphore_signal(barrier, inc=1, device_id=(section, other), device_id_type=MESH)

    sets = (
        (feed_here & (place < 2), ("h", "first", "second")),
        (feed_here & (place >= 2), ("h", "second", "middle", "g")),
        (jnp.logical_not(feed_here), ("some_h", "some_first", "some_second", "mixed", "some_g")),
    )
    for here, names in sets:

        @pl.when(here)
        def _(names=names):
            for copy in work.loads(names):
                copy.start()

    greet(2 * place + 1 - core)

    @pl.when(place > 0)
    def _():
        greet(batch - 2)

    @pl.when(place < PLACES - 1)
    def _():
        greet(batch + 2)

    @pl.when(base == 0)
    def _():
        work.head(part)

    pl.semaphore_wait(barrier, jnp.where((place > 0) & (place < PLACES - 1), 3, 2))
    for here, names in sets:

        @pl.when(here)
        def _(names=names):
            for copy in work.loads(names):
                copy.wait()

    def rows_of(i):
        return pl.ds(pl.multiple_of(i * piece, 16), piece)

    def share(index, i):
        return pl.ds(pl.multiple_of(step_rows * index - base + i * piece, 16), piece)

    def swap(to, i):
        slot = lax.rem(to, 2)
        return pltpu.make_async_remote_copy(
            src_ref=part.at[share(2 * to + 1 - core, i), :],
            dst_ref=own.at[slot, rows_of(i), :],
            send_sem=ex_send.at[slot, i],
            recv_sem=ex_recv.at[slot, i],
            device_id=(section, 2 * place + 1 - core),
            device_id_type=MESH,
        )

    def go(source, slot, to, i, other):
        return pltpu.make_async_remote_copy(
            src_ref=source,
            dst_ref=passing.at[slot, rows_of(i), :],
            send_sem=send.at[lax.rem(to, 2), i],
            recv_sem=recv.at[slot, i],
            device_id=(section, other),
            device_id_type=MESH,
        )

    def arrived(slot, i):
        here = passing.at[slot, rows_of(i), :]
        pltpu.make_async_copy(here, here, recv.at[slot, i]).wait()

    def chunks(first, last, act):
        def step(i, carry):
            act(i)
            return carry

        lax.fori_loop(first, last, step, 0)

    def release(to, before, after, limits=(CHUNKS, CHUNKS)):
        for parity in range(2):

            def bound(row, parity=parity):
                return max(0, min(limits[parity], (row - parity * step_rows) // piece))

            first, last = bound(before), bound(after)
            if first == last:
                continue

            @pl.when(core != parity)
            def _(first=first, last=last):
                chunks(first, last, lambda i: swap(to, i).start())

            def add(i):
                slot = lax.rem(to, 2)
                rows = rows_of(i)
                swap(to, i).wait_recv()
                mine = part[share(2 * to + core, i), :].astype(F32)
                own[slot, rows, :] = (own[slot, rows, :].astype(F32) + mine).astype(BF)
                source = own.at[slot, rows, :]

                @pl.when(feed_here & (to == mate))
                def _():
                    go(source, 0, to, i, 2 * mate + core).start()

                @pl.when(jnp.logical_not(feed_here) & (place == PLACES - 1))
                def _():
                    go(source, slot, to, i, batch - 2).start()

                @pl.when(jnp.logical_not(feed_here) & (place == 0) & (to == 1))
                def _():
                    go(source, 2, to, i, batch + 2).start()

            @pl.when(core == parity)
            def _(first=first, last=last):
                chunks(first, last, add)

    def swapped(to, limits=(CHUNKS, CHUNKS)):
        chunks(0, jnp.where(core == 0, limits[1], limits[0]), lambda i: swap(to, i).wait_send())

    @pl.when(feed_here)
    def _():
        @pl.when(place != 1)
        def _():
            work.pair_strip(part, jnp.where(place == 0, 2, 5))

        def group(t, carry):
            to = jnp.where(t == 0, mate, place)

            @pl.when(to < 3)
            def _():
                work.pair_tile(part, 3 * to)
                release(to, 0, 5520)
                work.pair_tile(part, 3 * to + 1)
                release(to, 5520, 11024)

                @pl.when(to < 2)
                def _():
                    work.pair_tile(part, 3 * to + 2)

                @pl.when(to == 2)
                def _():
                    work.down(part, 0, 768)

                release(to, 11024, 16528)

            @pl.when(to == 3)
            def _():
                row = 0
                for first, rows in ((640, 640), (1280, 640), (1920, 640), (2560, 256)):
                    work.down(part, first, rows)
                    after = HEAD_ROWS + 8 * PAIR_ROWS + 8 * (first + rows) - 6 * step_rows
                    release(to, row, after)
                    row = after

            swapped(to)
            return carry

        lax.fori_loop(0, 2, group, 0)

    def attention(kind):
        tile, ends = (work.window_tile, WINDOW_ENDS) if kind == WINDOW else (work.linear_tile, LINEAR_ENDS)
        filled = [max(0, min(CHUNKS, -(-(ends[-1] - step_rows * index) // piece))) for index in range(4)]
        limits = (tuple(filled[:2]), tuple(filled[2:]))
        cover = max(step_rows * index + piece * filled[index] for index in range(4) if filled[index])
        row = 0
        for k in range(len(ends)):
            tile(part, k)
            after = ends[k]
            if k == len(ends) - 1:
                clear(part, after, cover - after)
                after = cover
            for to in range(2):
                release(to, row - 2 * to * step_rows, after - 2 * to * step_rows, limits[to])
            row = after

        def own_count(to):
            return jnp.where(core == 0, limits[to][0], limits[to][1])

        def pass_down(to):
            def act(i):
                rows = rows_of(i)
                arrived(to, i)
                added = passing[to, rows, :].astype(F32) + own[to, rows, :].astype(F32)
                passing[to, rows, :] = added.astype(BF)
                go(passing.at[to, rows, :], to, to, i, batch - 2).start()

            chunks(0, own_count(to), act)

        @pl.when((place == 1) | (place == 2))
        def _():
            pass_down(0)

        @pl.when(place == 2)
        def _():
            pass_down(1)

        for to in range(2):
            swapped(to, limits[to])

        def sum_up(i):
            rows = rows_of(i)

            @pl.when((place == 0) & (i < own_count(0)))
            def _():
                arrived(0, i)
                total[...] = own[0, rows, :].astype(F32) + passing[0, rows, :].astype(F32)

            @pl.when((place == 1) & (i < own_count(1)))
            def _():
                arrived(1, i)
                arrived(2, i)
                both_ways = passing[1, rows, :].astype(F32) + passing[2, rows, :].astype(F32)
                total[...] = own[1, rows, :].astype(F32) + both_ways

            here = jnp.where(place == 0, own_count(0), jnp.where(place == 1, own_count(1), 0))

            @pl.when(i >= here)
            def _():
                total[...] = jnp.zeros_like(total)

            emit(i)

        chunks(0, CHUNKS, sum_up)

        @pl.when((place == 1) | (place >= 2))
        def _():
            chunks(0, own_count(0), lambda i: go(passing.at[0, rows_of(i), :], 0, 0, i, batch - 2).wait_send())

        @pl.when((place == 0) | (place >= 2))
        def _():
            chunks(0, own_count(1), lambda i: go(passing.at[0, rows_of(i), :], 0, 1, i, batch - 2).wait_send())

    def emit(i):
        cols = pl.ds(pl.multiple_of(i * piece * 128, 1024), piece * 128)
        flat[0:1, cols] = total[...].reshape(1, piece * 128)

    for kind in (WINDOW, LINEAR):

        @pl.when(section == kind)
        def _(kind=kind):
            attention(kind)

    @pl.when(feed_here)
    def _():
        slot = lax.rem(place, 2)

        def sum_up(i):
            rows = rows_of(i)
            arrived(0, i)
            total[...] = own[slot, rows, :].astype(F32) + passing[0, rows, :].astype(F32)
            emit(i)

        chunks(0, CHUNKS, sum_up)
        other = 2 * mate + core
        chunks(0, CHUNKS, lambda i: go(passing.at[0, rows_of(i), :], 0, mate, i, other).wait_send())

    count = out.shape[1]
    first = pl.multiple_of((8 + batch) * 128, 128)
    store = pltpu.make_async_copy(flat.at[:, pl.ds(first, count)], out, out_sem)
    store.start()
    store.wait()


def reduce_products(sources, total_rows, batches):
    step_rows = (total_rows - 8) // batches - 1
    width = step_rows + HEAD_ROWS
    return pl.pallas_call(
        reduce_kernel,
        out_shape=jax.ShapeDtypeStruct((1, (step_rows + 1) * 128), F32),
        in_specs=[any_spec()] * 5 + [vmem_spec()],
        out_specs=any_spec(),
        scratch_shapes=[
            pltpu.VMEM((4 * step_rows + HEAD_ROWS + 512, 128), BF),
            pltpu.VMEM((2, width, 128), BF),
            pltpu.VMEM((3, width, 128), BF),
            pltpu.VMEM((width // CHUNKS, 128), F32),
            pltpu.VMEM((1, width * 128), F32),
            (
                pltpu.SemaphoreType.DMA((2, CHUNKS)),
                pltpu.SemaphoreType.DMA((2, CHUNKS)),
                pltpu.SemaphoreType.DMA((2, CHUNKS)),
                pltpu.SemaphoreType.DMA((3, CHUNKS)),
                pltpu.SemaphoreType.DMA,
            ),
        ]
        + product_scratch(2 * MICRO * LEN, 2),
        compiler_params=pltpu.CompilerParams(
            collective_id=1, has_side_effects=True, vmem_limit_bytes=62 * MIB
        ),
        name="reduce_products",
    )(*sources)


def document_ids(lengths):
    ends = jnp.cumsum(lengths, axis=1)
    places = jnp.arange(LEN, dtype=jnp.int32)
    return jnp.sum((places[None, :, None] >= ends[:, None, :]).astype(jnp.int32), axis=2)


def shards(tokens, cotangent, params, lengths):
    docs = document_ids(lengths[0])
    doc_col, doc_row = docs[:, :, None], docs[:, None, :]
    batches = lax.axis_size("batch")
    paired = batches == 2 * PLACES
    acts, d_inputs, normed, middle, d_first, d_second, grads, d_gain = train(
        tokens, cotangent, params, doc_col, doc_row, paired
    )
    total_rows = params.shape[1] // 128 + 8
    sources = (normed, d_first, d_second, middle, grads, d_gain)
    if paired:
        mine = reduce_products(sources, total_rows, batches)
    else:
        parts = products(sources, total_rows)
        mine = lax.psum_scatter(parts[8:].reshape(-1), "batch", scatter_dimension=0, tiled=True)
        mine = mine.astype(F32)[None]
    return acts[None], d_inputs[None], mine


def solution(mesh):
    return jax.shard_map(
        shards,
        mesh=mesh,
        in_specs=(P("batch", None), P("batch", None), P("section", None), P("batch", None, None)),
        out_specs=(P("section", "batch", None), P("section", "batch", None), P("section", "batch")),
        check_vma=False,
    )
```

```python
import functools
import math

import jax
import jax.numpy as jnp
from jax import lax
from jax.experimental import pallas as pl
from jax.experimental.pallas import tpu as pltpu
from jax.sharding import PartitionSpec as P

D = 1024
FF = 2752
FP = 2816
HEADS = 16
FEAT = 16
WIN = 64
MICRO = 2
LEN = 256
EPSILON = 1e-06
SCALE = 1.0 / math.sqrt(D)
LINEAR, FEED, WINDOW, FEED2 = 0, 1, 2, 3
MIB = 2**20
MESH = pl.DeviceIdType.MESH
BF = jnp.bfloat16
F32 = jnp.float32


def any_spec():
    return pl.BlockSpec(memory_space=pl.ANY)


def vmem_spec():
    return pl.BlockSpec(memory_space=pltpu.VMEM)


def dot(left, right):
    return jnp.dot(left, right, preferred_element_type=F32)


def dot_t(left, right):
    return lax.dot_general(left, right, (((1,), (1,)), ((), ())), preferred_element_type=F32)


def dot_0(left, right):
    return lax.dot_general(left, right, (((0,), (0,)), ((), ())), preferred_element_type=F32)


def is_feed(section):
    return (section == FEED) | (section == FEED2)


PAIR_STEP = 32 * FF
ROW_STEP = 64 * D
AHEAD = 8


def prepare(section, flat, wide_v, tall_v, chunk, blocks, woven, load_sem):
    def run(steps, count, first, work):
        def load(i):
            slot = lax.rem(i, AHEAD)
            return pltpu.make_async_copy(
                flat.at[:, pl.ds(pl.multiple_of(first + i * count, 1024), count)],
                chunk.at[slot, :, pl.ds(0, count)],
                load_sem.at[slot],
            )

        def start(i, carry):
            load(i).start()
            return carry

        lax.fori_loop(0, AHEAD, start, 0)

        def step(i, carry):
            load(i).wait()
            rows = count // 128
            blocks[pl.ds(0, rows), :] = chunk[lax.rem(i, AHEAD), :, pl.ds(0, count)].astype(F32).reshape(rows, 128)
            work(i)

            @pl.when(i + AHEAD < steps)
            def _():
                load(i + AHEAD).start()

            return carry

        lax.fori_loop(0, steps, step, 0)

    def rows_of(index, count):
        return pl.ds(pl.multiple_of(index * count, count), count)

    def pair_work(i):
        low_half = lax.broadcasted_iota(jnp.int32, (16, 128), 1) < 64
        rolled = pltpu.roll(blocks[pl.ds(21, 16, stride=43), :], 64, 1)
        for c in range(22):
            even = blocks[pl.ds(c, 16, stride=43), :]
            if c == 21:
                even = jnp.where(low_half, even, 0.0)
                odd = jnp.where(low_half, rolled, 0.0)
            else:
                after = pltpu.roll(blocks[pl.ds(22 + c, 16, stride=43), :], 64, 1)
                odd = jnp.where(low_half, rolled, after)
                rolled = after
            woven[c, pl.ds(0, 16, stride=2), :] = even
            woven[c, pl.ds(1, 16, stride=2), :] = odd
        rows = rows_of(lax.rem(i, 32), 32)
        for c in range(22):
            wide_v[i // 32, rows, pl.ds(128 * c, 128)] = woven[c].astype(BF)

    def row_work(target, rows, first_col):
        for c in range(8):
            target[rows, pl.ds(first_col + 128 * c, 128)] = blocks[pl.ds(c, 64, stride=8), :].astype(BF)

    def square(i, first, target, first_col):
        @pl.when((i >= first) & (i < first + 16))
        def _():
            row_work(target, rows_of(i - first, 64), first_col)

    @pl.when(is_feed(section))
    def _():
        run(64, PAIR_STEP, D, pair_work)
        run(43, ROW_STEP, D + 2 * D * FF, lambda i: row_work(tall_v, rows_of(i, 64), 0))
        tall_v[pl.ds(FF, FP - FF), :] = jnp.zeros((FP - FF, D), BF)

    @pl.when(section == WINDOW)
    def _():
        def work(i):
            square(i, 0, wide_v.at[0], 0)
            square(i, 16, wide_v.at[0], D)
            square(i, 32, wide_v.at[1], 0)
            square(i, 48, tall_v, 0)

        run(64, ROW_STEP, D, work)

    @pl.when(section == LINEAR)
    def _():
        def work(i):
            for part in range(2):

                @pl.when(i // 4 == part)
                def _(part=part):
                    rows = rows_of(i - 4 * part, 256)
                    for c in range(2):
                        cols = pl.ds(part * HEADS * FEAT + 128 * c, 128)
                        wide_v[0, rows, cols] = blocks[pl.ds(c, 256, stride=2), :].astype(BF)

            square(i, 8, wide_v.at[1], 0)
            square(i, 24, tall_v, 0)

        run(40, ROW_STEP, D, work)


ROWS = 128
CHUNKS_OF = LEN // ROWS


def lanes_of_head(kind, block, half):
    lanes = lax.broadcasted_iota(jnp.int32, (1, 128), 1)
    if kind == WINDOW:
        return lanes // 64 == half
    return lanes // FEAT == lax.rem(2 * block + half, 8)


def lanes_of_value(half):
    return lax.broadcasted_iota(jnp.int32, (1, 128), 1) // 64 == half


def only(mask, values):
    return jnp.where(mask, values, jnp.zeros_like(values))


def both(masks, values):
    return jnp.concatenate([only(masks[0], values), only(masks[1], values)], axis=0)


def merge(masks, stacked):
    return only(masks[0], stacked[:ROWS]) + only(masks[1], stacked[ROWS:])


def block_of(index, first=0):
    return pl.ds(pl.multiple_of(first + index * 128, 128), 128)


def query_index(kind, block):
    return block if kind == WINDOW else block // 4


def low_width(kind):
    return D if kind == WINDOW else HEADS * FEAT


def mask_of(kind, doc_col, doc_row, first_row):
    shape = (doc_col.shape[0], doc_row.shape[1])
    rows = lax.broadcasted_iota(jnp.int32, shape, 0) + first_row
    cols = lax.broadcasted_iota(jnp.int32, shape, 1)
    mask = (doc_col == doc_row) & (cols <= rows)
    if kind == WINDOW:
        mask = mask & (rows - cols < WIN)
    return mask.astype(F32)


def root_of(kind):
    return 1.0 / math.sqrt(D // HEADS if kind == WINDOW else FEAT)


def out_scale(kind):
    return {LINEAR: 8.0, WINDOW: 4.0, FEED: 1.0}[kind] * SCALE


def train_kernel(
    swapping,
    tokens, cotangent, flat, docs,
    acts, d_inputs, normed, middle, d_first, d_second, grads, d_gain,
    wide_v, tall_v, gain_v, docs_v, z_v, h_v, x_v, g_v, dz_v, first_v, second_v, mid_v, dh_v, gain_sum, far_gain,
    raised_v, slope_v, inverse_v, mask_v, dy_v, dq_v, dk_v, dv_v, chunk, blocks, woven,
    load_sem, gain_sem, in_sem, act_sem, out_sem, on_send, on_recv, back_send, back_recv, far_send, far_recv,
):
    section = lax.axis_index("section")
    batch = lax.axis_index("batch")
    last = lax.axis_size("section") - 1
    batches = lax.axis_size("batch")
    steps = MICRO * CHUNKS_OF
    count = steps * ROWS
    barrier = pltpu.get_barrier_semaphore()

    far = lax.rem(batch + batches // 2, batches)
    nobody = section < 0
    lower = batch < batches // 2
    gives = is_feed(section) | ((section == WINDOW) & jnp.logical_not(lower)) if swapping else nobody
    takes = is_feed(section) | ((section == WINDOW) & lower) if swapping else nobody

    @pl.when(gives | takes)
    def _():
        pl.semaphore_signal(barrier, inc=1, device_id=(section, far), device_id_type=MESH)

    @pl.when(section > 0)
    def _():
        pl.semaphore_signal(barrier, inc=1, device_id=(section - 1, batch), device_id_type=MESH)

    @pl.when(section < last)
    def _():
        pl.semaphore_signal(barrier, inc=1, device_id=(section + 1, batch), device_id_type=MESH)

    gain_copy = pltpu.make_async_copy(flat.at[:, pl.ds(0, D)], gain_v, gain_sem)
    gain_copy.start()
    token_copy = pltpu.make_async_copy(tokens, z_v.at[pl.ds(0, count), :], in_sem.at[0])
    tangent_copy = pltpu.make_async_copy(cotangent, g_v.at[pl.ds(0, count), :], in_sem.at[1])

    @pl.when(section == 0)
    def _():
        token_copy.start()

    @pl.when(section == last)
    def _():
        tangent_copy.start()

    docs_v[pl.ds(0, MICRO)] = docs[...]
    prepare(section, flat, wide_v, tall_v, chunk, blocks, woven, load_sem)
    gain_copy.wait()
    gain = 1.0 + gain_v[...].astype(F32) / 8.0
    gain_sum[...] = jnp.zeros_like(gain_sum)

    @pl.when(section == 0)
    def _():
        token_copy.wait()

    @pl.when(section == last)
    def _():
        tangent_copy.wait()

    greeted = jnp.where((section > 0) & (section < last), 2, 1)
    pl.semaphore_wait(barrier, greeted + jnp.where(gives | takes, 1, 0))

    def rows_at(step, phase=0):
        return pl.ds(pl.multiple_of(phase * count + step * ROWS, ROWS), ROWS)

    def hand_on(step):
        rows = rows_at(step)
        return pltpu.make_async_remote_copy(
            src_ref=x_v.at[rows, :],
            dst_ref=z_v.at[rows, :],
            send_sem=on_send.at[step],
            recv_sem=on_recv.at[step],
            device_id=(section + 1, batch),
            device_id_type=MESH,
        )

    def hand_back(step):
        rows = rows_at(step)
        return pltpu.make_async_remote_copy(
            src_ref=x_v.at[rows, :],
            dst_ref=g_v.at[rows, :],
            send_sem=back_send.at[step],
            recv_sem=back_recv.at[step],
            device_id=(section - 1, batch),
            device_id_type=MESH,
        )

    def far_copy(kind, step=0):
        rows, target = rows_at(step), rows_at(step, 1)
        source, target = (
            (z_v.at[rows, :], z_v.at[target, :]),
            (g_v.at[rows, :], g_v.at[target, :]),
            (gain_sum, far_gain),
            (docs_v.at[pl.ds(0, MICRO)], docs_v.at[pl.ds(MICRO, MICRO)]),
        )[kind]
        return pltpu.make_async_remote_copy(
            src_ref=source,
            dst_ref=target,
            send_sem=far_send.at[kind, step],
            recv_sem=far_recv.at[kind, step],
            device_id=(section, far),
            device_id_type=MESH,
        )

    @pl.when(gives)
    def _():
        far_copy(3).start()

    @pl.when(gives & (section == last))
    def _():
        for step in range(steps):
            far_copy(1, step).start()

    def act_out(step):
        rows = rows_at(step)
        return pltpu.make_async_copy(x_v.at[rows, :], acts.at[rows, :], act_sem.at[0, step])

    def forward_outs(phase, step):
        rows, target = rows_at(step), rows_at(step, phase)
        return [
            pltpu.make_async_copy(h_v.at[rows, :], normed.at[target, :], act_sem.at[1, step]),
            pltpu.make_async_copy(mid_v.at[rows, :], middle.at[target, :], act_sem.at[2, step]),
        ]

    def gradient_out(step):
        rows = rows_at(step)
        return pltpu.make_async_copy(dz_v.at[rows, :], d_inputs.at[rows, :], out_sem.at[0, step])

    def backward_outs(phase, step):
        rows, target = rows_at(step), rows_at(step, phase)
        return [
            pltpu.make_async_copy(g_v.at[target, :], grads.at[target, :], out_sem.at[1, step]),
            pltpu.make_async_copy(first_v.at[rows, :], d_first.at[target, :], out_sem.at[2, step]),
            pltpu.make_async_copy(second_v.at[rows, :], d_second.at[target, :], out_sem.at[3, step]),
        ]


    def forward_step(phase, step, hidden, project):
        rows, here = rows_at(step), rows_at(step, phase)
        own = phase == 0

        @pl.when(own & (section > 0))
        def _():
            hand_on(step).wait_recv()

        @pl.when(own & gives)
        def _():
            far_copy(0, step).start()

        @pl.when(jnp.logical_not(own))
        def _():
            far_copy(0, step).wait_recv()

        z = z_v[here, :].astype(F32)
        scaled = lax.rsqrt(jnp.mean(z * z, axis=1, keepdims=True) + EPSILON)
        h_v[rows, :] = (z * scaled * gain).astype(BF)
        hidden(rows)

        @pl.when(own)
        def _():
            x_v[rows, :] = (z_v[here, :].astype(F32) + project(rows)).astype(BF)

            @pl.when(section < last)
            def _():
                hand_on(step).start()

            act_out(step).start()

        for copy in forward_outs(phase, step):
            copy.start()

    def backward_step(phase, step, unhidden, back):
        rows, here = rows_at(step), rows_at(step, phase)
        own = phase == 0

        @pl.when(own & (section < last))
        def _():
            hand_back(step).wait_recv()

            @pl.when(gives)
            def _():
                far_copy(1, step).start()

        @pl.when(jnp.logical_not(own))
        def _():
            far_copy(1, step).wait_recv()

        unhidden(here, rows)

        @pl.when(own)
        def _():
            dh_v[...] = back(rows) * SCALE
            z = z_v[rows, :].astype(F32)
            scaled = lax.rsqrt(jnp.mean(z * z, axis=1, keepdims=True) + EPSILON)
            unit = z * scaled
            d_normed = dh_v[...]
            gain_sum[0:1, :] += jnp.sum(d_normed * unit, axis=0, keepdims=True) * 0.125
            d_unit = d_normed * gain
            d_z = scaled * (d_unit - unit * jnp.mean(d_unit * unit, axis=1, keepdims=True))
            d_z += g_v[rows, :].astype(F32)
            dz_v[rows, :] = d_z
            x_v[rows, :] = d_z.astype(BF)

            @pl.when(section > 0)
            def _():
                hand_back(step).start()

            gradient_out(step).start()

        for copy in backward_outs(phase, step):
            copy.start()

    def feed_hidden(rows):
        half = FP // 2

        def piece(part, carry):
            cols = pl.ds(pl.multiple_of(part * half, half), half)
            gate = dot(h_v[rows, :], wide_v[0, :, cols]) * SCALE
            up = dot(h_v[rows, :], wide_v[1, :, cols]) * SCALE
            sig = 1.0 / (1.0 + jnp.exp(-gate))
            silu = gate * sig
            first_v[rows, cols] = (up * (sig + silu * (1.0 - sig))).astype(BF)
            second_v[rows, cols] = silu.astype(BF)
            mid_v[rows, cols] = (silu * up).astype(BF)
            return carry

        lax.fori_loop(0, 2, piece, 0)

    def feed_project(rows):
        return dot(mid_v[rows, :], tall_v[...]) * SCALE

    def feed_unhidden(here, rows):
        half = FP // 2

        def piece(part, carry):
            cols = pl.ds(pl.multiple_of(part * half, half), half)
            d_mid = dot_t(g_v[here, :], tall_v[cols, :]) * SCALE
            first_v[rows, cols] = (d_mid * first_v[rows, cols].astype(F32)).astype(BF)
            second_v[rows, cols] = (d_mid * second_v[rows, cols].astype(F32)).astype(BF)
            return carry

        lax.fori_loop(0, 2, piece, 0)

    def feed_back(rows):
        return dot_t(first_v[rows, :], wide_v[0]) + dot_t(second_v[rows, :], wide_v[1])

    def attend_hidden(kind, phase, micro, part, rows):
        width = low_width(kind)
        span = ROWS * (part + 1)
        keys_at = pl.ds(pl.multiple_of(micro * LEN, LEN), span)
        step = micro * CHUNKS_OF + part
        first_v[rows, pl.ds(0, 2 * width)] = (dot(h_v[rows, :], wide_v[0, :, pl.ds(0, 2 * width)]) * SCALE).astype(BF)
        second_v[rows, pl.ds(0, D)] = (dot(h_v[rows, :], wide_v[1, :, pl.ds(0, D)]) * SCALE).astype(BF)
        cols = pl.ds(0, span)
        index = phase * MICRO + micro
        own_docs = jnp.broadcast_to(docs_v[index, :, pl.ds(part * ROWS, ROWS)], (8, ROWS))
        mask_v[:, cols] = mask_of(kind, own_docs.T[:, 0:1], docs_v[index, :, cols], part * ROWS)

        def block(t, carry):
            index = query_index(kind, t)
            queries = first_v[rows, block_of(index)]
            keys = first_v[keys_at, block_of(index, width)]
            values = second_v[keys_at, block_of(t)]
            heads = [lanes_of_head(kind, t, half) for half in range(2)]
            scores = (dot_t(both(heads, queries), keys) * root_of(kind)).reshape(2, ROWS, span)
            mask = mask_v[:, cols]
            if kind == WINDOW:
                kept = jnp.where((mask > 0.0)[None], scores, -1e30)
                raised = jnp.exp(kept - jnp.max(kept, axis=2, keepdims=True))
            else:
                slope = mask[None] * (1.0 + scores)
                slope_v[step, t, :, cols] = slope.astype(BF).reshape(2 * ROWS, span)
                raised = 0.5 * (mask[None] + slope * slope)
            raised = raised.astype(BF).reshape(2 * ROWS, span)
            raised_v[step, t, :, cols] = raised
            summed = dot(raised, jnp.concatenate([values, jnp.ones((span, 128), BF)], axis=1))
            inverse = 1.0 / summed[:, 128:]
            sides = [lanes_of_value(half) for half in range(2)]
            mid_v[rows, block_of(t)] = merge(sides, summed[:, :128] * inverse).astype(BF)
            inverse_v[rows, block_of(t)] = merge(sides, inverse)
            return carry

        lax.fori_loop(0, 8, block, 0, unroll=UNROLL)

    def attend_project(kind, rows):
        return dot(mid_v[rows, pl.ds(0, D)], tall_v[pl.ds(0, D), :]) * out_scale(kind)

    def attend_unhidden(kind, micro, part, here, rows):
        width = low_width(kind)
        span = ROWS * (part + 1)
        keys_at = pl.ds(pl.multiple_of(micro * LEN, LEN), span)
        own = pl.ds(0, span)
        step = micro * CHUNKS_OF + part
        d_mixed = dot_t(g_v[here, :], tall_v[pl.ds(0, D), :]) * out_scale(kind)
        dy_v[...] = (d_mixed * inverse_v[rows, :]).astype(BF)
        if part == CHUNKS_OF - 1:
            dk_v[...] = jnp.zeros_like(dk_v)
            dv_v[...] = jnp.zeros_like(dv_v)
        if kind == LINEAR:
            dq_v[...] = jnp.zeros_like(dq_v)

        def block(t, carry):
            index = query_index(kind, t)
            queries = first_v[rows, block_of(index)]
            keys = first_v[keys_at, block_of(index, width)]
            values = second_v[keys_at, block_of(t)]
            heads = [lanes_of_head(kind, t, half) for half in range(2)]
            sides = [lanes_of_value(half) for half in range(2)]
            d_mixed = both(sides, dy_v[:, block_of(t)])
            mixed = mid_v[rows, block_of(t)].astype(F32)
            shift = jnp.sum(d_mixed.astype(F32) * jnp.concatenate([mixed, mixed], axis=0), axis=1, keepdims=True)
            d_weights = dot_t(d_mixed, values) - shift
            raised = raised_v[step, t, :, own]
            slope = raised if kind == WINDOW else slope_v[step, t, :, own]
            d_scores = (slope.astype(F32) * d_weights).astype(BF)
            dv_v[own, block_of(t)] += dot_0(raised, d_mixed)
            d_queries = merge(heads, dot(d_scores, keys)) * root_of(kind)
            dk_v[own, block_of(index)] += dot_0(d_scores, both(heads, queries)) * root_of(kind)
            if kind == WINDOW:
                dq_v[:, block_of(t)] = d_queries
            else:
                dq_v[:, block_of(index)] += d_queries
            return carry

        lax.fori_loop(0, 8, block, 0, unroll=UNROLL)
        done = pl.ds(part * ROWS, ROWS)
        first_v[rows, pl.ds(0, width)] = dq_v[:, pl.ds(0, width)].astype(BF)
        first_v[rows, pl.ds(width, width)] = dk_v[done, pl.ds(0, width)].astype(BF)
        second_v[rows, pl.ds(0, D)] = dv_v[done, :].astype(BF)

    def attend_back(kind, rows):
        width = low_width(kind)
        total = dot_t(first_v[rows, pl.ds(0, 2 * width)], wide_v[0, :, pl.ds(0, 2 * width)])
        total += dot_t(second_v[rows, pl.ds(0, D)], wide_v[1, :, pl.ds(0, D)])
        return total

    def one_phase(phase, carry):
        own = phase == 0

        @pl.when(is_feed(section))
        def _():
            def forward(step, inner):
                forward_step(phase, step, feed_hidden, feed_project)
                return inner

            lax.fori_loop(0, steps, forward, 0)

        for kind in (WINDOW, LINEAR):

            @pl.when(section == kind)
            def _(kind=kind):
                def forward(micro, inner):
                    for part in range(CHUNKS_OF):
                        forward_step(
                            phase,
                            micro * CHUNKS_OF + part,
                            functools.partial(attend_hidden, kind, phase, micro, part),
                            functools.partial(attend_project, kind),
                        )
                    return inner

                lax.fori_loop(0, MICRO, forward, 0)

        def settle(step, inner):
            @pl.when(own)
            def _():
                @pl.when(section < last)
                def _():
                    hand_on(step).wait_send()

                act_out(step).wait()

            for copy in forward_outs(phase, step):
                copy.wait()
            return inner

        lax.fori_loop(0, steps, settle, 0)

        @pl.when(is_feed(section))
        def _():
            def backward(step, inner):
                micro, part = step // CHUNKS_OF, CHUNKS_OF - 1 - lax.rem(step, CHUNKS_OF)
                backward_step(phase, micro * CHUNKS_OF + part, feed_unhidden, feed_back)
                return inner

            lax.fori_loop(0, steps, backward, 0)

        for kind in (WINDOW, LINEAR):

            @pl.when(section == kind)
            def _(kind=kind):
                def backward(micro, inner):
                    for part in reversed(range(CHUNKS_OF)):
                        backward_step(
                            phase,
                            micro * CHUNKS_OF + part,
                            functools.partial(attend_unhidden, kind, micro, part),
                            functools.partial(attend_back, kind),
                        )
                    return inner

                lax.fori_loop(0, MICRO, backward, 0)

        @pl.when(own & gives)
        def _():
            far_copy(2).start()

        def finish(step, inner):
            @pl.when(own)
            def _():
                @pl.when(section > 0)
                def _():
                    hand_back(step).wait_send()

                gradient_out(step).wait()

            for copy in backward_outs(phase, step):
                copy.wait()
            return inner

        lax.fori_loop(0, steps, finish, 0)

        @pl.when(own & takes)
        def _():
            far_copy(3).wait_recv()

        return carry

    lax.fori_loop(0, jnp.where(takes, 2, 1), one_phase, 0)
    d_gain[...] = gain_sum[...]

    @pl.when(takes)
    def _():
        far_copy(2).wait_recv()
        d_gain[...] += far_gain[...]

    @pl.when(gives)
    def _():
        for kind in range(2):
            for step in range(steps):
                far_copy(kind, step).wait_send()
        far_copy(2).wait_send()
        far_copy(3).wait_send()


UNROLL = 2


def train(tokens, cotangent, flat, docs, swapping):
    count = MICRO * LEN
    steps = MICRO * CHUNKS_OF
    kept = 2 * count if swapping else count
    return pl.pallas_call(
        functools.partial(train_kernel, swapping),
        out_shape=(
            jax.ShapeDtypeStruct((count, D), BF),
            jax.ShapeDtypeStruct((count, D), F32),
            jax.ShapeDtypeStruct((kept, D), BF),
            jax.ShapeDtypeStruct((kept, FP), BF),
            jax.ShapeDtypeStruct((kept, FP), BF),
            jax.ShapeDtypeStruct((kept, FP), BF),
            jax.ShapeDtypeStruct((kept, D), BF),
            jax.ShapeDtypeStruct((8, D), F32),
        ),
        in_specs=[any_spec()] * 3 + [vmem_spec()],
        out_specs=(any_spec(),) * 7 + (vmem_spec(),),
        scratch_shapes=[
            pltpu.VMEM((2, D, FP), BF),
            pltpu.VMEM((FP, D), BF),
            pltpu.VMEM((1, D), BF),
            pltpu.VMEM((2 * MICRO, 1, LEN), F32),
            pltpu.VMEM((2 * count, D), BF),
            pltpu.VMEM((count, D), BF),
            pltpu.VMEM((count, D), BF),
            pltpu.VMEM((2 * count, D), BF),
            pltpu.VMEM((count, D), F32),
            pltpu.VMEM((count, FP), BF),
            pltpu.VMEM((count, FP), BF),
            pltpu.VMEM((count, FP), BF),
            pltpu.VMEM((ROWS, D), F32),
            pltpu.VMEM((8, D), F32),
            pltpu.VMEM((8, D), F32),
            pltpu.VMEM((steps, 8, 2 * ROWS, LEN), BF),
            pltpu.VMEM((steps, 8, 2 * ROWS, LEN), BF),
            pltpu.VMEM((count, D), F32),
            pltpu.VMEM((ROWS, LEN), F32),
            pltpu.VMEM((ROWS, D), BF),
            pltpu.VMEM((ROWS, D), F32),
            pltpu.VMEM((LEN, D), F32),
            pltpu.VMEM((LEN, D), F32),
            pltpu.VMEM((AHEAD, 1, PAIR_STEP), BF),
            pltpu.VMEM((PAIR_STEP // 128, 128), F32),
            pltpu.VMEM((22, 32, 128), F32),
            pltpu.SemaphoreType.DMA((AHEAD,)),
            pltpu.SemaphoreType.DMA,
            pltpu.SemaphoreType.DMA((2,)),
            pltpu.SemaphoreType.DMA((3, steps)),
            pltpu.SemaphoreType.DMA((4, steps)),
            pltpu.SemaphoreType.DMA((steps,)),
            pltpu.SemaphoreType.DMA((steps,)),
            pltpu.SemaphoreType.DMA((steps,)),
            pltpu.SemaphoreType.DMA((steps,)),
            pltpu.SemaphoreType.DMA((4, steps)),
            pltpu.SemaphoreType.DMA((4, steps)),
        ],
        compiler_params=pltpu.CompilerParams(
            collective_id=0, has_side_effects=True, vmem_limit_bytes=62 * MIB
        ),
        name="train",
    )(tokens, cotangent, flat, docs)


HEAD_ROWS = 16
PAIR_ROWS = 128 * 43
CHUNKS = 11


class Products:
    def __init__(self, sources, scratch, base):
        self.normed, self.d_first, self.d_second, self.middle, self.grads, self.d_gain = sources
        self.left_v, self.d_v, self.woven, self.stage, self.in_sem = scratch
        self.base = base

    def fetch(self, source, target, index):
        return pltpu.make_async_copy(source, target, self.in_sem.at[index])

    def loads(self, names):
        count = self.left_v.shape[1]
        some = pl.ds(0, MICRO * LEN)
        every = pl.ds(0, count)
        low, both, high = pl.ds(0, D), pl.ds(0, 2 * D), pl.ds(D, D)
        table = {
            "h": (self.normed, self.left_v.at[0], 0),
            "g": (self.grads, self.left_v.at[1], 1),
            "first": (self.d_first, self.d_v.at[0], 2),
            "second": (self.d_second, self.d_v.at[1], 3),
            "middle": (self.middle, self.d_v.at[self.middle_slot()], 4),
        }
        for prefix, rows in (("all_", every), ("some_", some)):
            table[prefix + "h"] = (self.normed.at[rows, :], self.left_v.at[0, rows, :], 0)
            table[prefix + "mixed"] = (self.middle.at[rows, low], self.left_v.at[1, rows, :], 1)
            table[prefix + "low"] = (self.d_first.at[rows, both], self.d_v.at[0, rows, both], 2)
            table[prefix + "value"] = (self.d_second.at[rows, low], self.d_v.at[1, rows, low], 3)
            table[prefix + "g"] = (self.grads.at[rows, :], self.d_v.at[1, rows, high], 4)
        return [self.fetch(*table[name]) for name in names]

    def middle_slot(self):
        return 2 if self.d_v.shape[0] == 3 else 0

    def head(self, out):
        stage = self.stage
        stage[pl.ds(0, 8), :] = jnp.zeros((8, 128), F32)
        stage[pl.ds(8, 8), :] = self.d_gain[0:1, :].reshape(8, 128)
        out[pl.ds(0, 16), :] = stage[pl.ds(0, 16), :].astype(BF)

    def cut(self, out, first_row, rows, piece, scale):
        target_row = first_row - self.base

        def step(j, carry):
            source = pl.ds(pl.multiple_of(j * piece, 16), piece)
            target = pl.ds(pl.multiple_of(target_row + j * piece, 16), piece)
            out[target, :] = (self.stage[source, :] * scale).astype(BF)
            return carry

        lax.fori_loop(0, rows // piece, step, 0)

    def pairs(self, which, first_pair, count):
        stage, woven = self.stage, self.woven
        half = FP // 2
        low_half = lax.broadcasted_iota(jnp.int32, (count, 128), 1) < 64
        left = self.left_v[0, :, pl.ds(pl.multiple_of(2 * first_pair, 128), 2 * count)]
        for part in range(2):
            piece = dot_0(left, self.d_v[which, :, pl.ds(part * half, half)])
            for c in range(11):
                woven[11 * part + c, pl.ds(0, 2 * count), :] = piece[:, 128 * c : 128 * c + 128]
        for c in range(22):
            stage[pl.ds(c, count, stride=43), :] = woven[c, pl.ds(0, count, stride=2), :]
        before = woven[21, pl.ds(0, count, stride=2), :]
        for c in range(22):
            here = pltpu.roll(woven[c, pl.ds(1, count, stride=2), :], 64, 1)
            stage[pl.ds(21 + c, count, stride=43), :] = jnp.where(low_half, before, here)
            before = here

    def pair_tile(self, out, k):
        self.pairs(k // 4, lax.rem(k, 4) * 128, 128)
        self.cut(out, HEAD_ROWS + k * PAIR_ROWS, PAIR_ROWS, 688, SCALE)

    def pair_strip(self, out, k):
        self.pairs(k // 4, lax.rem(k, 4) * 128 + 64, 64)
        target = pl.ds(pl.multiple_of((k + 1) * PAIR_ROWS - self.base, 16), 16)
        out[target, :] = (self.stage[pl.ds(64 * 43 - 16, 16), :] * SCALE).astype(BF)

    def tall(self, out, left, right, stride, rows, first_row, scale, piece):
        product = dot_0(left, right)
        for c in range(stride):
            self.stage[pl.ds(c, rows, stride=stride), :] = product[:, 128 * c : 128 * c + 128]
        self.cut(out, first_row, rows * stride, piece, scale)

    def down(self, out, first_channel, rows):
        left = self.d_v[self.middle_slot(), :, pl.ds(first_channel, rows)]
        first_row = HEAD_ROWS + 8 * PAIR_ROWS + 8 * first_channel
        self.tall(out, left, self.left_v[1], 8, rows, first_row, SCALE, 512)

    def window_tile(self, out, k):
        left = self.left_v[k // 6, :, pl.ds(pl.multiple_of(lax.rem(k, 2) * 512, 512), 512)]
        right = self.d_v[k // 4, :, pl.ds(pl.multiple_of(lax.rem(k // 2, 2) * D, D), D)]
        scale = jnp.where(k < 6, SCALE, out_scale(WINDOW))
        self.tall(out, left, right, 8, 512, HEAD_ROWS + 4096 * k, scale, 512)

    def linear_tile(self, out, k):
        some = pl.ds(0, MICRO * LEN)
        width = HEADS * FEAT
        if k < 2:
            right = self.d_v[0, some, pl.ds(k * width, width)]
            self.tall(out, self.left_v[0, some, :], right, 2, D, HEAD_ROWS + k * 2048, SCALE, 512)
        else:
            which, part = (k - 2) // 2, k % 2
            left = self.left_v[which, some, pl.ds(part * 512, 512)]
            right = self.d_v[1, some, pl.ds(which * D, D)]
            scale = (SCALE, out_scale(LINEAR))[which]
            self.tall(out, left, right, 8, 512, HEAD_ROWS + 4096 * (k - 1), scale, 512)


WINDOW_END = HEAD_ROWS + 4 * 8192
LINEAR_ENDS = [HEAD_ROWS + rows for rows in (2048, 4096, 8192, 12288, 16384, 20480)]


def product_scratch(count, slots):
    return [
        pltpu.VMEM((2, count, D), BF),
        pltpu.VMEM((slots, count, FP), BF),
        pltpu.VMEM((22, 256, 128), F32),
        pltpu.VMEM((6144, 128), F32),
        pltpu.SemaphoreType.DMA((5,)),
    ]


def clear(out, first_row, rows):
    def step(i, carry):
        out[pl.ds(pl.multiple_of(first_row + i * 128, 16), 128), :] = jnp.zeros((128, 128), BF)
        return carry

    lax.fori_loop(0, rows // 128, step, 0)
    if rows % 128:
        out[pl.ds(first_row + rows // 128 * 128, rows % 128), :] = jnp.zeros((rows % 128, 128), BF)


def products_kernel(*refs):
    section = lax.axis_index("section")
    work = Products(refs[:6], refs[8:], 0)
    out, out_v = refs[6:8]
    total = out_v.shape[0] - 512
    work.head(out_v)

    def load(*names):
        for copy in work.loads(names):
            copy.start()
        for copy in work.loads(names):
            copy.wait()

    @pl.when(is_feed(section))
    def _():
        load("h", "g", "first", "second", "middle")

        def tile(k, carry):
            work.pair_tile(out_v, k)
            return carry

        lax.fori_loop(0, 8, tile, 0)
        for first, rows in ((0, 640), (640, 640), (1280, 640), (1920, 640), (2560, 256)):
            work.down(out_v, first, rows)

    for kind in (WINDOW, LINEAR):

        @pl.when(section == kind)
        def _(kind=kind):
            load("some_h", "some_mixed", "some_low", "some_value", "some_g")
            if kind == WINDOW:

                def tile(k, carry):
                    work.window_tile(out_v, k)
                    return carry

                lax.fori_loop(0, 8, tile, 0)
            else:
                for k in range(len(LINEAR_ENDS)):
                    work.linear_tile(out_v, k)
            done = WINDOW_END if kind == WINDOW else LINEAR_ENDS[-1]
            clear(out_v, done, total - done)

    store = pltpu.make_async_copy(out_v.at[pl.ds(0, total), :], out, work.in_sem.at[0])
    store.start()
    store.wait()


def products(sources, total_rows):
    return pl.pallas_call(
        products_kernel,
        out_shape=jax.ShapeDtypeStruct((total_rows, 128), BF),
        in_specs=[any_spec()] * 5 + [vmem_spec()],
        out_specs=any_spec(),
        scratch_shapes=[pltpu.VMEM((total_rows + 512, 128), BF)] + product_scratch(MICRO * LEN, 3),
        compiler_params=pltpu.CompilerParams(vmem_limit_bytes=60 * MIB),
        name="products",
    )(*sources)


PLACES = 4


def reduce_kernel(*refs):
    section = lax.axis_index("section")
    batch = lax.axis_index("batch")
    place, core = batch // 2, lax.rem(batch, 2)
    mate = place + 1 - 2 * lax.rem(place, 2)
    out, part, own, passing, total, flat, sems = refs[6:13]
    ex_send, ex_recv, send, recv, out_sem = sems
    width = own.shape[1]
    step_rows = width - HEAD_ROWS
    piece = width // CHUNKS
    feed_here = is_feed(section)
    base = jnp.where(feed_here, place // 2, 0) * (4 * step_rows)
    work = Products(refs[:6], refs[13:], base)
    barrier = pltpu.get_barrier_semaphore()

    def greet(other):
        pl.semaphore_signal(barrier, inc=1, device_id=(section, other), device_id_type=MESH)

    window_here = (section == WINDOW) & (place < 2)
    pair_here = feed_here | window_here
    linear_here = section == LINEAR
    sets = (
        (feed_here & (place < 2), ("h", "first", "second")),
        (feed_here & (place >= 2), ("h", "second", "middle", "g")),
        (window_here, ("all_h", "all_mixed", "all_low", "all_value", "all_g")),
        (linear_here, ("some_h", "some_mixed", "some_low", "some_value", "some_g")),
    )
    for here, names in sets:

        @pl.when(here)
        def _(names=names):
            for copy in work.loads(names):
                copy.start()

    greet(2 * place + 1 - core)

    @pl.when(place > 0)
    def _():
        greet(batch - 2)

    @pl.when(place < PLACES - 1)
    def _():
        greet(batch + 2)

    @pl.when(base == 0)
    def _():
        work.head(part)

    pl.semaphore_wait(barrier, jnp.where((place > 0) & (place < PLACES - 1), 3, 2))
    for here, names in sets:

        @pl.when(here)
        def _(names=names):
            for copy in work.loads(names):
                copy.wait()

    def rows_of(i):
        return pl.ds(pl.multiple_of(i * piece, 16), piece)

    def share(index, i):
        return pl.ds(pl.multiple_of(step_rows * index - base + i * piece, 16), piece)

    def swap(to, i):
        slot = lax.rem(to, 2)
        return pltpu.make_async_remote_copy(
            src_ref=part.at[share(2 * to + 1 - core, i), :],
            dst_ref=own.at[slot, rows_of(i), :],
            send_sem=ex_send.at[slot, i],
            recv_sem=ex_recv.at[slot, i],
            device_id=(section, 2 * place + 1 - core),
            device_id_type=MESH,
        )

    def go(source, slot, to, i, other):
        return pltpu.make_async_remote_copy(
            src_ref=source,
            dst_ref=passing.at[slot, rows_of(i), :],
            send_sem=send.at[lax.rem(to, 2), i],
            recv_sem=recv.at[slot, i],
            device_id=(section, other),
            device_id_type=MESH,
        )

    def arrived(slot, i):
        here = passing.at[slot, rows_of(i), :]
        pltpu.make_async_copy(here, here, recv.at[slot, i]).wait()

    def chunks(first, last, act):
        def step(i, carry):
            act(i)
            return carry

        lax.fori_loop(first, last, step, 0)

    def release(to, before, after, limits=(CHUNKS, CHUNKS)):
        for parity in range(2):

            def bound(row, parity=parity):
                return jnp.minimum(jnp.maximum(row - parity * step_rows, 0) // piece, limits[parity])

            first, last = bound(before), bound(after)

            @pl.when(core != parity)
            def _(first=first, last=last):
                chunks(first, last, lambda i: swap(to, i).start())

            def add(i):
                slot = lax.rem(to, 2)
                rows = rows_of(i)
                swap(to, i).wait_recv()
                mine = part[share(2 * to + core, i), :].astype(F32)
                own[slot, rows, :] = (own[slot, rows, :].astype(F32) + mine).astype(BF)
                source = own.at[slot, rows, :]

                @pl.when(pair_here & (to == mate))
                def _():
                    go(source, 0, to, i, 2 * mate + core).start()

                @pl.when(linear_here & (place == PLACES - 1))
                def _():
                    go(source, slot, to, i, batch - 2).start()

                @pl.when(linear_here & (place == 0) & (to == 1))
                def _():
                    go(source, 2, to, i, batch + 2).start()

            @pl.when(core == parity)
            def _(first=first, last=last):
                chunks(first, last, add)

    def swapped(to, limits=(CHUNKS, CHUNKS)):
        chunks(0, jnp.where(core == 0, limits[1], limits[0]), lambda i: swap(to, i).wait_send())

    def emit(i):
        cols = pl.ds(pl.multiple_of(i * piece * 128, 1024), piece * 128)
        flat[0:1, cols] = total[...].reshape(1, piece * 128)

    @pl.when(feed_here)
    def _():
        @pl.when(place != 1)
        def _():
            work.pair_strip(part, jnp.where(place == 0, 2, 5))

        def group(t, carry):
            to = jnp.where(t == 0, mate, place)

            @pl.when(to < 3)
            def _():
                work.pair_tile(part, 3 * to)
                release(to, 0, 5520)
                work.pair_tile(part, 3 * to + 1)
                release(to, 5520, 11024)

                @pl.when(to < 2)
                def _():
                    work.pair_tile(part, 3 * to + 2)

                @pl.when(to == 2)
                def _():
                    work.down(part, 0, 768)

                release(to, 11024, 16528)

            @pl.when(to == 3)
            def _():
                row = 0
                for first, rows in ((640, 640), (1280, 640), (1920, 640), (2560, 256)):
                    work.down(part, first, rows)
                    after = HEAD_ROWS + 8 * PAIR_ROWS + 8 * (first + rows) - 6 * step_rows
                    release(to, row, after)
                    row = after

            swapped(to)
            return carry

        lax.fori_loop(0, 2, group, 0)

    @pl.when(window_here)
    def _():
        def tile(t, carry):
            k = lax.rem(t + jnp.where(place == 0, 4, 0), 8)
            work.window_tile(part, k)
            start = HEAD_ROWS + 4096 * k
            stop = start + 4096

            @pl.when(k == 7)
            def _():
                clear(part, WINDOW_END, 4 * step_rows + HEAD_ROWS - WINDOW_END)

            whole = 2 * step_rows + HEAD_ROWS
            stop_0 = jnp.where(place == 0, jnp.where(k < 3, stop, jnp.where(k == 3, whole, start)), stop)
            stop_1 = jnp.where(k == 7, whole, stop - 2 * step_rows)
            release(0, start, stop_0)
            release(1, start - 2 * step_rows, stop_1)
            return carry

        lax.fori_loop(0, 8, tile, 0)
        for to in range(2):
            swapped(to)

    @pl.when(linear_here)
    def _():
        ends = LINEAR_ENDS
        filled = [max(0, min(CHUNKS, -(-(ends[-1] - step_rows * index) // piece))) for index in range(4)]
        limits = (tuple(filled[:2]), tuple(filled[2:]))
        cover = max(step_rows * index + piece * filled[index] for index in range(4) if filled[index])
        row = 0
        for k in range(len(ends)):
            work.linear_tile(part, k)
            after = ends[k]
            if k == len(ends) - 1:
                clear(part, after, cover - after)
                after = cover
            for to in range(2):
                if after > 2 * to * step_rows:
                    release(to, row - 2 * to * step_rows, after - 2 * to * step_rows, limits[to])
            row = after

        def own_count(to):
            return jnp.where(core == 0, limits[to][0], limits[to][1])

        def pass_down(to):
            def act(i):
                rows = rows_of(i)
                arrived(to, i)
                added = passing[to, rows, :].astype(F32) + own[to, rows, :].astype(F32)
                passing[to, rows, :] = added.astype(BF)
                go(passing.at[to, rows, :], to, to, i, batch - 2).start()

            chunks(0, own_count(to), act)

        @pl.when((place == 1) | (place == 2))
        def _():
            pass_down(0)

        @pl.when(place == 2)
        def _():
            pass_down(1)

        for to in range(2):
            swapped(to, limits[to])

        def sum_up(i):
            rows = rows_of(i)

            @pl.when((place == 0) & (i < own_count(0)))
            def _():
                arrived(0, i)
                total[...] = own[0, rows, :].astype(F32) + passing[0, rows, :].astype(F32)

            @pl.when((place == 1) & (i < own_count(1)))
            def _():
                arrived(1, i)
                arrived(2, i)
                both_ways = passing[1, rows, :].astype(F32) + passing[2, rows, :].astype(F32)
                total[...] = own[1, rows, :].astype(F32) + both_ways

            here = jnp.where(place == 0, own_count(0), jnp.where(place == 1, own_count(1), 0))

            @pl.when(i >= here)
            def _():
                total[...] = jnp.zeros_like(total)

            emit(i)

        chunks(0, CHUNKS, sum_up)

        @pl.when((place == 1) | (place >= 2))
        def _():
            chunks(0, own_count(0), lambda i: go(passing.at[0, rows_of(i), :], 0, 0, i, batch - 2).wait_send())

        @pl.when((place == 0) | (place >= 2))
        def _():
            chunks(0, own_count(1), lambda i: go(passing.at[0, rows_of(i), :], 0, 1, i, batch - 2).wait_send())

    @pl.when((section == WINDOW) & (place >= 2))
    def _():
        total[...] = jnp.zeros_like(total)
        chunks(0, CHUNKS, emit)

    @pl.when(pair_here)
    def _():
        slot = lax.rem(place, 2)

        def sum_up(i):
            rows = rows_of(i)
            arrived(0, i)
            total[...] = own[slot, rows, :].astype(F32) + passing[0, rows, :].astype(F32)
            emit(i)

        chunks(0, CHUNKS, sum_up)
        other = 2 * mate + core
        chunks(0, CHUNKS, lambda i: go(passing.at[0, rows_of(i), :], 0, mate, i, other).wait_send())

    count = out.shape[1]
    first = pl.multiple_of((8 + batch) * 128, 128)
    store = pltpu.make_async_copy(flat.at[:, pl.ds(first, count)], out, out_sem)
    store.start()
    store.wait()


def reduce_products(sources, total_rows, batches):
    step_rows = (total_rows - 8) // batches - 1
    width = step_rows + HEAD_ROWS
    return pl.pallas_call(
        reduce_kernel,
        out_shape=jax.ShapeDtypeStruct((1, (step_rows + 1) * 128), F32),
        in_specs=[any_spec()] * 5 + [vmem_spec()],
        out_specs=any_spec(),
        scratch_shapes=[
            pltpu.VMEM((4 * step_rows + HEAD_ROWS + 512, 128), BF),
            pltpu.VMEM((2, width, 128), BF),
            pltpu.VMEM((3, width, 128), BF),
            pltpu.VMEM((width // CHUNKS, 128), F32),
            pltpu.VMEM((1, width * 128), F32),
            (
                pltpu.SemaphoreType.DMA((2, CHUNKS)),
                pltpu.SemaphoreType.DMA((2, CHUNKS)),
                pltpu.SemaphoreType.DMA((2, CHUNKS)),
                pltpu.SemaphoreType.DMA((3, CHUNKS)),
                pltpu.SemaphoreType.DMA,
            ),
        ]
        + product_scratch(2 * MICRO * LEN, 2),
        compiler_params=pltpu.CompilerParams(
            collective_id=1, has_side_effects=True, vmem_limit_bytes=62 * MIB
        ),
        name="reduce_products",
    )(*sources)


def document_ids(lengths):
    ends = jnp.cumsum(lengths, axis=1)
    places = jnp.arange(LEN, dtype=jnp.int32)
    return jnp.sum((places[None, :, None] >= ends[:, None, :]).astype(jnp.int32), axis=2)


def shards(tokens, cotangent, params, lengths):
    docs = document_ids(lengths[0]).astype(F32)[:, None, :]
    batches = lax.axis_size("batch")
    paired = batches == 2 * PLACES
    acts, d_inputs, normed, middle, d_first, d_second, grads, d_gain = train(
        tokens, cotangent, params, docs, paired
    )
    total_rows = params.shape[1] // 128 + 8
    sources = (normed, d_first, d_second, middle, grads, d_gain)
    if paired:
        mine = reduce_products(sources, total_rows, batches)
    else:
        parts = products(sources, total_rows)
        mine = lax.psum_scatter(parts[8:].reshape(-1), "batch", scatter_dimension=0, tiled=True)
        mine = mine.astype(F32)[None]
    return acts[None], d_inputs[None], mine


def solution(mesh):
    return jax.shard_map(
        shards,
        mesh=mesh,
        in_specs=(P("batch", None), P("batch", None), P("section", None), P("batch", None, None)),
        out_specs=(P("section", "batch", None), P("section", "batch", None), P("section", "batch")),
        check_vma=False,
    )
```

```python
import functools
import math

import jax
import jax.numpy as jnp
from jax import lax
from jax.experimental import pallas as pl
from jax.experimental.pallas import tpu as pltpu
from jax.sharding import PartitionSpec as P

D = 1024
FF = 2752
FP = 2816
HEADS = 16
FEAT = 16
WIN = 64
MICRO = 2
LEN = 256
EPSILON = 1e-06
SCALE = 1.0 / math.sqrt(D)
LINEAR, FEED, WINDOW, FEED2 = 0, 1, 2, 3
MIB = 2**20
MESH = pl.DeviceIdType.MESH
BF = jnp.bfloat16
F32 = jnp.float32


def any_spec():
    return pl.BlockSpec(memory_space=pl.ANY)


def vmem_spec():
    return pl.BlockSpec(memory_space=pltpu.VMEM)


def dot(left, right):
    return jnp.dot(left, right, preferred_element_type=F32)


def dot_t(left, right):
    return lax.dot_general(left, right, (((1,), (1,)), ((), ())), preferred_element_type=F32)


def dot_0(left, right):
    return lax.dot_general(left, right, (((0,), (0,)), ((), ())), preferred_element_type=F32)


def is_feed(section):
    return (section == FEED) | (section == FEED2)


PAIR_STEP = 32 * FF
ROW_STEP = 64 * D
AHEAD = 8


def prepare(section, flat, wide_v, tall_v, chunk, blocks, woven, load_sem):
    def run(steps, count, first, work):
        def load(i):
            slot = lax.rem(i, AHEAD)
            return pltpu.make_async_copy(
                flat.at[:, pl.ds(pl.multiple_of(first + i * count, 1024), count)],
                chunk.at[slot, :, pl.ds(0, count)],
                load_sem.at[slot],
            )

        def start(i, carry):
            load(i).start()
            return carry

        lax.fori_loop(0, AHEAD, start, 0)

        def step(i, carry):
            load(i).wait()
            rows = count // 128
            blocks[pl.ds(0, rows), :] = chunk[lax.rem(i, AHEAD), :, pl.ds(0, count)].astype(F32).reshape(rows, 128)
            work(i)

            @pl.when(i + AHEAD < steps)
            def _():
                load(i + AHEAD).start()

            return carry

        lax.fori_loop(0, steps, step, 0)

    def rows_of(index, count):
        return pl.ds(pl.multiple_of(index * count, count), count)

    def pair_work(i):
        low_half = lax.broadcasted_iota(jnp.int32, (16, 128), 1) < 64
        rolled = pltpu.roll(blocks[pl.ds(21, 16, stride=43), :], 64, 1)
        for c in range(22):
            even = blocks[pl.ds(c, 16, stride=43), :]
            if c == 21:
                even = jnp.where(low_half, even, 0.0)
                odd = jnp.where(low_half, rolled, 0.0)
            else:
                after = pltpu.roll(blocks[pl.ds(22 + c, 16, stride=43), :], 64, 1)
                odd = jnp.where(low_half, rolled, after)
                rolled = after
            woven[c, pl.ds(0, 16, stride=2), :] = even
            woven[c, pl.ds(1, 16, stride=2), :] = odd
        rows = rows_of(lax.rem(i, 32), 32)
        for c in range(22):
            wide_v[i // 32, rows, pl.ds(128 * c, 128)] = woven[c].astype(BF)

    def row_work(target, rows, first_col):
        for c in range(8):
            target[rows, pl.ds(first_col + 128 * c, 128)] = blocks[pl.ds(c, 64, stride=8), :].astype(BF)

    def square(i, first, target, first_col):
        @pl.when((i >= first) & (i < first + 16))
        def _():
            row_work(target, rows_of(i - first, 64), first_col)

    @pl.when(is_feed(section))
    def _():
        run(64, PAIR_STEP, D, pair_work)
        run(43, ROW_STEP, D + 2 * D * FF, lambda i: row_work(tall_v, rows_of(i, 64), 0))
        tall_v[pl.ds(FF, FP - FF), :] = jnp.zeros((FP - FF, D), BF)

    @pl.when(section == WINDOW)
    def _():
        def work(i):
            square(i, 0, wide_v.at[0], 0)
            square(i, 16, wide_v.at[0], D)
            square(i, 32, wide_v.at[1], 0)
            square(i, 48, tall_v, 0)

        run(64, ROW_STEP, D, work)

    @pl.when(section == LINEAR)
    def _():
        def work(i):
            for part in range(2):

                @pl.when(i // 4 == part)
                def _(part=part):
                    rows = rows_of(i - 4 * part, 256)
                    for c in range(2):
                        cols = pl.ds(part * HEADS * FEAT + 128 * c, 128)
                        wide_v[0, rows, cols] = blocks[pl.ds(c, 256, stride=2), :].astype(BF)

            square(i, 8, wide_v.at[1], 0)
            square(i, 24, tall_v, 0)

        run(40, ROW_STEP, D, work)


ROWS = 128
CHUNKS_OF = LEN // ROWS


def lanes_of_head(kind, block, half):
    lanes = lax.broadcasted_iota(jnp.int32, (1, 128), 1)
    if kind == WINDOW:
        return lanes // 64 == half
    return lanes // FEAT == lax.rem(2 * block + half, 8)


def lanes_of_value(half):
    return lax.broadcasted_iota(jnp.int32, (1, 128), 1) // 64 == half


def only(mask, values):
    return jnp.where(mask, values, jnp.zeros_like(values))


def both(masks, values):
    return jnp.concatenate([only(masks[0], values), only(masks[1], values)], axis=0)


def merge(masks, stacked):
    return only(masks[0], stacked[:ROWS]) + only(masks[1], stacked[ROWS:])


def block_of(index, first=0):
    return pl.ds(pl.multiple_of(first + index * 128, 128), 128)


def query_index(kind, block):
    return block if kind == WINDOW else block // 4


def low_width(kind):
    return D if kind == WINDOW else HEADS * FEAT


def mask_of(kind, doc_col, doc_row, first_row):
    shape = (doc_col.shape[0], doc_row.shape[1])
    rows = lax.broadcasted_iota(jnp.int32, shape, 0) + first_row
    cols = lax.broadcasted_iota(jnp.int32, shape, 1)
    mask = (doc_col == doc_row) & (cols <= rows)
    if kind == WINDOW:
        mask = mask & (rows - cols < WIN)
    return mask.astype(F32)


def root_of(kind):
    return 1.0 / math.sqrt(D // HEADS if kind == WINDOW else FEAT)


def out_scale(kind):
    return {LINEAR: 8.0, WINDOW: 4.0, FEED: 1.0}[kind] * SCALE


def train_kernel(
    swapping,
    tokens, cotangent, flat, docs,
    acts, d_inputs, normed, middle, d_first, d_second, grads, d_gain,
    wide_v, tall_v, gain_v, docs_v, z_v, h_v, x_v, g_v, dz_v, first_v, second_v, mid_v, dh_v, gain_sum, far_gain,
    raised_v, slope_v, inverse_v, mask_v, dy_v, dq_v, dk_v, dv_v, chunk, blocks, woven,
    load_sem, gain_sem, in_sem, act_sem, out_sem, on_send, on_recv, back_send, back_recv, far_send, far_recv,
):
    section = lax.axis_index("section")
    batch = lax.axis_index("batch")
    last = lax.axis_size("section") - 1
    batches = lax.axis_size("batch")
    steps = MICRO * CHUNKS_OF
    count = steps * ROWS
    barrier = pltpu.get_barrier_semaphore()

    far = lax.rem(batch + batches // 2, batches)
    nobody = section < 0
    lower = batch < batches // 2
    gives = is_feed(section) | ((section == WINDOW) & jnp.logical_not(lower)) if swapping else nobody
    takes = is_feed(section) | ((section == WINDOW) & lower) if swapping else nobody

    @pl.when(gives | takes)
    def _():
        pl.semaphore_signal(barrier, inc=1, device_id=(section, far), device_id_type=MESH)

    @pl.when(section > 0)
    def _():
        pl.semaphore_signal(barrier, inc=1, device_id=(section - 1, batch), device_id_type=MESH)

    @pl.when(section < last)
    def _():
        pl.semaphore_signal(barrier, inc=1, device_id=(section + 1, batch), device_id_type=MESH)

    gain_copy = pltpu.make_async_copy(flat.at[:, pl.ds(0, D)], gain_v, gain_sem)
    gain_copy.start()
    token_copy = pltpu.make_async_copy(tokens, z_v.at[pl.ds(0, count), :], in_sem.at[0])
    tangent_copy = pltpu.make_async_copy(cotangent, g_v.at[pl.ds(0, count), :], in_sem.at[1])

    @pl.when(section == 0)
    def _():
        token_copy.start()

    @pl.when(section == last)
    def _():
        tangent_copy.start()

    docs_v[pl.ds(0, MICRO)] = docs[...]
    prepare(section, flat, wide_v, tall_v, chunk, blocks, woven, load_sem)
    gain_copy.wait()
    gain = 1.0 + gain_v[...].astype(F32) / 8.0
    gain_sum[...] = jnp.zeros_like(gain_sum)

    @pl.when(section == 0)
    def _():
        token_copy.wait()

    @pl.when(section == last)
    def _():
        tangent_copy.wait()

    greeted = jnp.where((section > 0) & (section < last), 2, 1)
    pl.semaphore_wait(barrier, greeted + jnp.where(gives | takes, 1, 0))

    def rows_at(step, phase=0):
        return pl.ds(pl.multiple_of(phase * count + step * ROWS, ROWS), ROWS)

    def hand_on(step):
        rows = rows_at(step)
        return pltpu.make_async_remote_copy(
            src_ref=x_v.at[rows, :],
            dst_ref=z_v.at[rows, :],
            send_sem=on_send.at[step],
            recv_sem=on_recv.at[step],
            device_id=(section + 1, batch),
            device_id_type=MESH,
        )

    def hand_back(step):
        rows = rows_at(step)
        return pltpu.make_async_remote_copy(
            src_ref=x_v.at[rows, :],
            dst_ref=g_v.at[rows, :],
            send_sem=back_send.at[step],
            recv_sem=back_recv.at[step],
            device_id=(section - 1, batch),
            device_id_type=MESH,
        )

    def far_copy(kind, step=0):
        rows, target = rows_at(step), rows_at(step, 1)
        source, target = (
            (z_v.at[rows, :], z_v.at[target, :]),
            (g_v.at[rows, :], g_v.at[target, :]),
            (gain_sum, far_gain),
            (docs_v.at[pl.ds(0, MICRO)], docs_v.at[pl.ds(MICRO, MICRO)]),
        )[kind]
        return pltpu.make_async_remote_copy(
            src_ref=source,
            dst_ref=target,
            send_sem=far_send.at[kind, step],
            recv_sem=far_recv.at[kind, step],
            device_id=(section, far),
            device_id_type=MESH,
        )

    @pl.when(gives)
    def _():
        far_copy(3).start()

    @pl.when(gives & (section == last))
    def _():
        for step in range(steps):
            far_copy(1, step).start()

    def act_out(step):
        rows = rows_at(step)
        return pltpu.make_async_copy(x_v.at[rows, :], acts.at[rows, :], act_sem.at[0, step])

    def forward_outs(phase, step):
        rows, target = rows_at(step), rows_at(step, phase)
        return [
            pltpu.make_async_copy(h_v.at[rows, :], normed.at[target, :], act_sem.at[1, step]),
            pltpu.make_async_copy(mid_v.at[rows, :], middle.at[target, :], act_sem.at[2, step]),
        ]

    def gradient_out(step):
        rows = rows_at(step)
        return pltpu.make_async_copy(dz_v.at[rows, :], d_inputs.at[rows, :], out_sem.at[0, step])

    def backward_outs(phase, step):
        rows, target = rows_at(step), rows_at(step, phase)
        return [
            pltpu.make_async_copy(g_v.at[target, :], grads.at[target, :], out_sem.at[1, step]),
            pltpu.make_async_copy(first_v.at[rows, :], d_first.at[target, :], out_sem.at[2, step]),
            pltpu.make_async_copy(second_v.at[rows, :], d_second.at[target, :], out_sem.at[3, step]),
        ]


    def forward_step(phase, step, hidden, project):
        rows, here = rows_at(step), rows_at(step, phase)
        own = phase == 0

        @pl.when(own & (section > 0))
        def _():
            hand_on(step).wait_recv()

        @pl.when(own & gives)
        def _():
            far_copy(0, step).start()

        @pl.when(jnp.logical_not(own))
        def _():
            far_copy(0, step).wait_recv()

        z = z_v[here, :].astype(F32)
        scaled = lax.rsqrt(jnp.mean(z * z, axis=1, keepdims=True) + EPSILON)
        h_v[rows, :] = (z * scaled * gain).astype(BF)
        hidden(rows)

        @pl.when(own)
        def _():
            x_v[rows, :] = (z_v[here, :].astype(F32) + project(rows)).astype(BF)

            @pl.when(section < last)
            def _():
                hand_on(step).start()

            act_out(step).start()

        for copy in forward_outs(phase, step):
            copy.start()

    def backward_step(phase, step, unhidden, back):
        rows, here = rows_at(step), rows_at(step, phase)
        own = phase == 0

        @pl.when(own & (section < last))
        def _():
            hand_back(step).wait_recv()

            @pl.when(gives)
            def _():
                far_copy(1, step).start()

        @pl.when(jnp.logical_not(own))
        def _():
            far_copy(1, step).wait_recv()

        unhidden(here, rows)

        @pl.when(own)
        def _():
            dh_v[...] = back(rows) * SCALE
            z = z_v[rows, :].astype(F32)
            scaled = lax.rsqrt(jnp.mean(z * z, axis=1, keepdims=True) + EPSILON)
            unit = z * scaled
            d_normed = dh_v[...]
            gain_sum[0:1, :] += jnp.sum(d_normed * unit, axis=0, keepdims=True) * 0.125
            d_unit = d_normed * gain
            d_z = scaled * (d_unit - unit * jnp.mean(d_unit * unit, axis=1, keepdims=True))
            d_z += g_v[rows, :].astype(F32)
            dz_v[rows, :] = d_z
            x_v[rows, :] = d_z.astype(BF)

            @pl.when(section > 0)
            def _():
                hand_back(step).start()

            gradient_out(step).start()

        for copy in backward_outs(phase, step):
            copy.start()

    def feed_hidden(rows):
        half = FP // 2

        def piece(part, carry):
            cols = pl.ds(pl.multiple_of(part * half, half), half)
            gate = dot(h_v[rows, :], wide_v[0, :, cols]) * SCALE
            up = dot(h_v[rows, :], wide_v[1, :, cols]) * SCALE
            sig = 1.0 / (1.0 + jnp.exp(-gate))
            silu = gate * sig
            first_v[rows, cols] = (up * (sig + silu * (1.0 - sig))).astype(BF)
            second_v[rows, cols] = silu.astype(BF)
            mid_v[rows, cols] = (silu * up).astype(BF)
            return carry

        lax.fori_loop(0, 2, piece, 0)

    def feed_project(rows):
        return dot(mid_v[rows, :], tall_v[...]) * SCALE

    def feed_unhidden(here, rows):
        half = FP // 2

        def piece(part, carry):
            cols = pl.ds(pl.multiple_of(part * half, half), half)
            d_mid = dot_t(g_v[here, :], tall_v[cols, :]) * SCALE
            first_v[rows, cols] = (d_mid * first_v[rows, cols].astype(F32)).astype(BF)
            second_v[rows, cols] = (d_mid * second_v[rows, cols].astype(F32)).astype(BF)
            return carry

        lax.fori_loop(0, 2, piece, 0)

    def feed_back(rows):
        return dot_t(first_v[rows, :], wide_v[0]) + dot_t(second_v[rows, :], wide_v[1])

    def attend_hidden(kind, phase, micro, part, rows):
        width = low_width(kind)
        span = ROWS * (part + 1)
        keys_at = pl.ds(pl.multiple_of(micro * LEN, LEN), span)
        step = micro * CHUNKS_OF + part
        first_v[rows, pl.ds(0, 2 * width)] = (dot(h_v[rows, :], wide_v[0, :, pl.ds(0, 2 * width)]) * SCALE).astype(BF)
        second_v[rows, pl.ds(0, D)] = (dot(h_v[rows, :], wide_v[1, :, pl.ds(0, D)]) * SCALE).astype(BF)
        cols = pl.ds(0, span)
        index = phase * MICRO + micro
        own_docs = jnp.broadcast_to(docs_v[index, :, pl.ds(part * ROWS, ROWS)], (8, ROWS))
        mask_v[:, cols] = mask_of(kind, own_docs.T[:, 0:1], docs_v[index, :, cols], part * ROWS)

        def block(t, carry):
            index = query_index(kind, t)
            queries = first_v[rows, block_of(index)]
            keys = first_v[keys_at, block_of(index, width)]
            values = second_v[keys_at, block_of(t)]
            heads = [lanes_of_head(kind, t, half) for half in range(2)]
            scores = (dot_t(both(heads, queries), keys) * root_of(kind)).reshape(2, ROWS, span)
            mask = mask_v[:, cols]
            if kind == WINDOW:
                kept = jnp.where((mask > 0.0)[None], scores, -1e30)
                raised = jnp.exp(kept - jnp.max(kept, axis=2, keepdims=True))
            else:
                slope = mask[None] * (1.0 + scores)
                slope_v[step, t, :, cols] = slope.astype(BF).reshape(2 * ROWS, span)
                raised = 0.5 * (mask[None] + slope * slope)
            raised = raised.astype(BF).reshape(2 * ROWS, span)
            raised_v[step, t, :, cols] = raised
            summed = dot(raised, jnp.concatenate([values, jnp.ones((span, 128), BF)], axis=1))
            inverse = 1.0 / summed[:, 128:]
            sides = [lanes_of_value(half) for half in range(2)]
            mid_v[rows, block_of(t)] = merge(sides, summed[:, :128] * inverse).astype(BF)
            inverse_v[rows, block_of(t)] = merge(sides, inverse)
            return carry

        lax.fori_loop(0, 8, block, 0, unroll=UNROLL)

    def attend_project(kind, rows):
        return dot(mid_v[rows, pl.ds(0, D)], tall_v[pl.ds(0, D), :]) * out_scale(kind)

    def attend_unhidden(kind, micro, part, here, rows):
        width = low_width(kind)
        span = ROWS * (part + 1)
        keys_at = pl.ds(pl.multiple_of(micro * LEN, LEN), span)
        own = pl.ds(0, span)
        step = micro * CHUNKS_OF + part
        d_mixed = dot_t(g_v[here, :], tall_v[pl.ds(0, D), :]) * out_scale(kind)
        dy_v[...] = (d_mixed * inverse_v[rows, :]).astype(BF)
        if part == CHUNKS_OF - 1:
            dk_v[...] = jnp.zeros_like(dk_v)
            dv_v[...] = jnp.zeros_like(dv_v)
        if kind == LINEAR:
            dq_v[...] = jnp.zeros_like(dq_v)

        def block(t, carry):
            index = query_index(kind, t)
            queries = first_v[rows, block_of(index)]
            keys = first_v[keys_at, block_of(index, width)]
            values = second_v[keys_at, block_of(t)]
            heads = [lanes_of_head(kind, t, half) for half in range(2)]
            sides = [lanes_of_value(half) for half in range(2)]
            d_mixed = both(sides, dy_v[:, block_of(t)])
            mixed = mid_v[rows, block_of(t)].astype(F32)
            shift = jnp.sum(d_mixed.astype(F32) * jnp.concatenate([mixed, mixed], axis=0), axis=1, keepdims=True)
            d_weights = dot_t(d_mixed, values) - shift
            raised = raised_v[step, t, :, own]
            slope = raised if kind == WINDOW else slope_v[step, t, :, own]
            d_scores = (slope.astype(F32) * d_weights).astype(BF)
            dv_v[own, block_of(t)] += dot_0(raised, d_mixed)
            d_queries = merge(heads, dot(d_scores, keys)) * root_of(kind)
            dk_v[own, block_of(index)] += dot_0(d_scores, both(heads, queries)) * root_of(kind)
            if kind == WINDOW:
                dq_v[:, block_of(t)] = d_queries
            else:
                dq_v[:, block_of(index)] += d_queries
            return carry

        lax.fori_loop(0, 8, block, 0, unroll=UNROLL)
        done = pl.ds(part * ROWS, ROWS)
        first_v[rows, pl.ds(0, width)] = dq_v[:, pl.ds(0, width)].astype(BF)
        first_v[rows, pl.ds(width, width)] = dk_v[done, pl.ds(0, width)].astype(BF)
        second_v[rows, pl.ds(0, D)] = dv_v[done, :].astype(BF)

    def attend_back(kind, rows):
        width = low_width(kind)
        total = dot_t(first_v[rows, pl.ds(0, 2 * width)], wide_v[0, :, pl.ds(0, 2 * width)])
        total += dot_t(second_v[rows, pl.ds(0, D)], wide_v[1, :, pl.ds(0, D)])
        return total

    def one_phase(phase, carry):
        own = phase == 0

        @pl.when(is_feed(section))
        def _():
            def forward(step, inner):
                forward_step(phase, step, feed_hidden, feed_project)
                return inner

            lax.fori_loop(0, steps, forward, 0)

        for kind in (WINDOW, LINEAR):

            @pl.when(section == kind)
            def _(kind=kind):
                def forward(micro, inner):
                    for part in range(CHUNKS_OF):
                        forward_step(
                            phase,
                            micro * CHUNKS_OF + part,
                            functools.partial(attend_hidden, kind, phase, micro, part),
                            functools.partial(attend_project, kind),
                        )
                    return inner

                lax.fori_loop(0, MICRO, forward, 0)

        def settle(step, inner):
            @pl.when(own)
            def _():
                @pl.when(section < last)
                def _():
                    hand_on(step).wait_send()

                act_out(step).wait()

            for copy in forward_outs(phase, step):
                copy.wait()
            return inner

        lax.fori_loop(0, steps, settle, 0)

        @pl.when(is_feed(section))
        def _():
            def backward(step, inner):
                micro, part = step // CHUNKS_OF, CHUNKS_OF - 1 - lax.rem(step, CHUNKS_OF)
                backward_step(phase, micro * CHUNKS_OF + part, feed_unhidden, feed_back)
                return inner

            lax.fori_loop(0, steps, backward, 0)

        for kind in (WINDOW, LINEAR):

            @pl.when(section == kind)
            def _(kind=kind):
                def backward(micro, inner):
                    for part in reversed(range(CHUNKS_OF)):
                        backward_step(
                            phase,
                            micro * CHUNKS_OF + part,
                            functools.partial(attend_unhidden, kind, micro, part),
                            functools.partial(attend_back, kind),
                        )
                    return inner

                lax.fori_loop(0, MICRO, backward, 0)

        @pl.when(own & gives)
        def _():
            far_copy(2).start()

        def finish(step, inner):
            @pl.when(own)
            def _():
                @pl.when(section > 0)
                def _():
                    hand_back(step).wait_send()

                gradient_out(step).wait()

            for copy in backward_outs(phase, step):
                copy.wait()
            return inner

        lax.fori_loop(0, steps, finish, 0)

        @pl.when(own & takes)
        def _():
            far_copy(3).wait_recv()

        return carry

    lax.fori_loop(0, jnp.where(takes, 2, 1), one_phase, 0)
    d_gain[...] = gain_sum[...]

    @pl.when(takes)
    def _():
        far_copy(2).wait_recv()
        d_gain[...] += far_gain[...]

    @pl.when(gives)
    def _():
        for kind in range(2):
            for step in range(steps):
                far_copy(kind, step).wait_send()
        far_copy(2).wait_send()
        far_copy(3).wait_send()


UNROLL = 2


def train(tokens, cotangent, flat, docs, swapping):
    count = MICRO * LEN
    steps = MICRO * CHUNKS_OF
    kept = 2 * count if swapping else count
    return pl.pallas_call(
        functools.partial(train_kernel, swapping),
        out_shape=(
            jax.ShapeDtypeStruct((count, D), BF),
            jax.ShapeDtypeStruct((count, D), F32),
            jax.ShapeDtypeStruct((kept, D), BF),
            jax.ShapeDtypeStruct((kept, FP), BF),
            jax.ShapeDtypeStruct((kept, FP), BF),
            jax.ShapeDtypeStruct((kept, FP), BF),
            jax.ShapeDtypeStruct((kept, D), BF),
            jax.ShapeDtypeStruct((8, D), F32),
        ),
        in_specs=[any_spec()] * 3 + [vmem_spec()],
        out_specs=(any_spec(),) * 7 + (vmem_spec(),),
        scratch_shapes=[
            pltpu.VMEM((2, D, FP), BF),
            pltpu.VMEM((FP, D), BF),
            pltpu.VMEM((1, D), BF),
            pltpu.VMEM((2 * MICRO, 1, LEN), F32),
            pltpu.VMEM((2 * count, D), BF),
            pltpu.VMEM((count, D), BF),
            pltpu.VMEM((count, D), BF),
            pltpu.VMEM((2 * count, D), BF),
            pltpu.VMEM((count, D), F32),
            pltpu.VMEM((count, FP), BF),
            pltpu.VMEM((count, FP), BF),
            pltpu.VMEM((count, FP), BF),
            pltpu.VMEM((ROWS, D), F32),
            pltpu.VMEM((8, D), F32),
            pltpu.VMEM((8, D), F32),
            pltpu.VMEM((steps, 8, 2 * ROWS, LEN), BF),
            pltpu.VMEM((steps, 8, 2 * ROWS, LEN), BF),
            pltpu.VMEM((count, D), F32),
            pltpu.VMEM((ROWS, LEN), F32),
            pltpu.VMEM((ROWS, D), BF),
            pltpu.VMEM((ROWS, D), F32),
            pltpu.VMEM((LEN, D), F32),
            pltpu.VMEM((LEN, D), F32),
            pltpu.VMEM((AHEAD, 1, PAIR_STEP), BF),
            pltpu.VMEM((PAIR_STEP // 128, 128), F32),
            pltpu.VMEM((22, 32, 128), F32),
            pltpu.SemaphoreType.DMA((AHEAD,)),
            pltpu.SemaphoreType.DMA,
            pltpu.SemaphoreType.DMA((2,)),
            pltpu.SemaphoreType.DMA((3, steps)),
            pltpu.SemaphoreType.DMA((4, steps)),
            pltpu.SemaphoreType.DMA((steps,)),
            pltpu.SemaphoreType.DMA((steps,)),
            pltpu.SemaphoreType.DMA((steps,)),
            pltpu.SemaphoreType.DMA((steps,)),
            pltpu.SemaphoreType.DMA((4, steps)),
            pltpu.SemaphoreType.DMA((4, steps)),
        ],
        compiler_params=pltpu.CompilerParams(
            collective_id=0, has_side_effects=True, vmem_limit_bytes=62 * MIB
        ),
        name="train",
    )(tokens, cotangent, flat, docs)


HEAD_ROWS = 16
PAIR_ROWS = 128 * 43
CHUNKS = 11


class Products:
    def __init__(self, sources, scratch, base):
        self.normed, self.d_first, self.d_second, self.middle, self.grads, self.d_gain = sources
        self.left_v, self.d_v, self.woven, self.stage, self.in_sem = scratch
        self.base = base

    def fetch(self, source, target, index):
        return pltpu.make_async_copy(source, target, self.in_sem.at[index])

    def loads(self, names):
        count = self.left_v.shape[1]
        some = pl.ds(0, MICRO * LEN)
        every = pl.ds(0, count)
        low, both, high = pl.ds(0, D), pl.ds(0, 2 * D), pl.ds(D, D)
        table = {
            "h": (self.normed, self.left_v.at[0], 0),
            "g": (self.grads, self.left_v.at[1], 1),
            "first": (self.d_first, self.d_v.at[0], 2),
            "second": (self.d_second, self.d_v.at[1], 3),
            "middle": (self.middle, self.d_v.at[self.middle_slot()], 4),
        }
        for prefix, rows in (("all_", every), ("some_", some)):
            table[prefix + "h"] = (self.normed.at[rows, :], self.left_v.at[0, rows, :], 0)
            table[prefix + "mixed"] = (self.middle.at[rows, low], self.left_v.at[1, rows, :], 1)
            table[prefix + "low"] = (self.d_first.at[rows, both], self.d_v.at[0, rows, both], 2)
            table[prefix + "value"] = (self.d_second.at[rows, low], self.d_v.at[1, rows, low], 3)
            table[prefix + "g"] = (self.grads.at[rows, :], self.d_v.at[1, rows, high], 4)
        return [self.fetch(*table[name]) for name in names]

    def middle_slot(self):
        return 2 if self.d_v.shape[0] == 3 else 0

    def head(self, out):
        stage = self.stage
        stage[pl.ds(0, 8), :] = jnp.zeros((8, 128), F32)
        stage[pl.ds(8, 8), :] = self.d_gain[0:1, :].reshape(8, 128)
        out[pl.ds(0, 16), :] = stage[pl.ds(0, 16), :].astype(BF)

    def cut(self, out, first_row, rows, piece, scale):
        target_row = first_row - self.base

        def step(j, carry):
            source = pl.ds(pl.multiple_of(j * piece, 16), piece)
            target = pl.ds(pl.multiple_of(target_row + j * piece, 16), piece)
            out[target, :] = (self.stage[source, :] * scale).astype(BF)
            return carry

        lax.fori_loop(0, rows // piece, step, 0)

    def pairs(self, which, first_pair):
        count = 128
        stage, woven = self.stage, self.woven
        half = FP // 2
        low_half = lax.broadcasted_iota(jnp.int32, (count, 128), 1) < 64
        left = self.left_v[0, :, pl.ds(pl.multiple_of(2 * first_pair, 128), 2 * count)]
        for part in range(2):
            piece = dot_0(left, self.d_v[which, :, pl.ds(part * half, half)])
            for c in range(11):
                woven[11 * part + c, pl.ds(0, 2 * count), :] = piece[:, 128 * c : 128 * c + 128]
        for c in range(22):
            stage[pl.ds(c, count, stride=43), :] = woven[c, pl.ds(0, count, stride=2), :]
        before = woven[21, pl.ds(0, count, stride=2), :]
        for c in range(22):
            here = pltpu.roll(woven[c, pl.ds(1, count, stride=2), :], 64, 1)
            stage[pl.ds(21 + c, count, stride=43), :] = jnp.where(low_half, before, here)
            before = here

    def pair_tile(self, out, k, tail_only):
        self.pairs(k // 4, lax.rem(k, 4) * 128)

        @pl.when(jnp.logical_not(tail_only))
        def _():
            self.cut(out, HEAD_ROWS + k * PAIR_ROWS, PAIR_ROWS, 688, SCALE)

        @pl.when(tail_only)
        def _():
            target = pl.ds(pl.multiple_of((k + 1) * PAIR_ROWS - self.base, 16), 16)
            out[target, :] = (self.stage[pl.ds(PAIR_ROWS - 16, 16), :] * SCALE).astype(BF)

    def tall(self, out, left, right, stride, rows, first_row, scale, piece):
        product = dot_0(left, right)
        for c in range(stride):
            self.stage[pl.ds(c, rows, stride=stride), :] = product[:, 128 * c : 128 * c + 128]
        self.cut(out, first_row, rows * stride, piece, scale)

    def down_tile(self, out, j):
        left = self.d_v[self.middle_slot(), :, pl.ds(pl.multiple_of(256 * j, 256), 256)]
        self.tall(out, left, self.left_v[1], 8, 256, DOWN_ROW + 2048 * j, SCALE, 512)

    def window_tile(self, out, k):
        left = self.left_v[k // 6, :, pl.ds(pl.multiple_of(lax.rem(k, 2) * 512, 512), 512)]
        right = self.d_v[k // 4, :, pl.ds(pl.multiple_of(lax.rem(k // 2, 2) * D, D), D)]
        scale = jnp.where(k < 6, SCALE, out_scale(WINDOW))
        self.tall(out, left, right, 8, 512, HEAD_ROWS + 4096 * k, scale, 512)

    def low_tile(self, out, k):
        some = pl.ds(0, MICRO * LEN)
        width = HEADS * FEAT
        right = self.d_v[0, some, pl.ds(pl.multiple_of(k * width, width), width)]
        self.tall(out, self.left_v[0, some, :], right, 2, D, HEAD_ROWS + k * 2048, SCALE, 512)

    def value_tile(self, out, k):
        some = pl.ds(0, MICRO * LEN)
        left = self.left_v[k // 2, some, pl.ds(pl.multiple_of(lax.rem(k, 2) * 512, 512), 512)]
        right = self.d_v[1, some, pl.ds(pl.multiple_of(k // 2 * D, D), D)]
        scale = jnp.where(k < 2, SCALE, out_scale(LINEAR))
        self.tall(out, left, right, 8, 512, HEAD_ROWS + 4096 * (k + 1), scale, 512)


DOWN_ROW = HEAD_ROWS + 8 * PAIR_ROWS
DOWN_TILES = FP // 256
WINDOW_END = HEAD_ROWS + 4 * 8192
LINEAR_END = HEAD_ROWS + 20480


def each(first, last, act):
    def step(i, carry):
        act(i)
        return carry

    lax.fori_loop(first, last, step, 0)


def product_scratch(count, slots):
    return [
        pltpu.VMEM((2, count, D), BF),
        pltpu.VMEM((slots, count, FP), BF),
        pltpu.VMEM((22, 256, 128), F32),
        pltpu.VMEM((6144, 128), F32),
        pltpu.SemaphoreType.DMA((5,)),
    ]


def clear(out, first_row, rows):
    def step(i, carry):
        out[pl.ds(pl.multiple_of(first_row + i * 128, 16), 128), :] = jnp.zeros((128, 128), BF)
        return carry

    lax.fori_loop(0, rows // 128, step, 0)
    if rows % 128:
        out[pl.ds(first_row + rows // 128 * 128, rows % 128), :] = jnp.zeros((rows % 128, 128), BF)


def products_kernel(*refs):
    section = lax.axis_index("section")
    work = Products(refs[:6], refs[8:], 0)
    out, out_v = refs[6:8]
    total = out_v.shape[0] - 512
    work.head(out_v)

    def load(*names):
        for copy in work.loads(names):
            copy.start()
        for copy in work.loads(names):
            copy.wait()

    @pl.when(is_feed(section))
    def _():
        load("h", "g", "first", "second", "middle")
        each(0, 8, lambda k: work.pair_tile(out_v, k, section < 0))
        each(0, DOWN_TILES, lambda j: work.down_tile(out_v, j))

    for kind in (WINDOW, LINEAR):

        @pl.when(section == kind)
        def _(kind=kind):
            load("some_h", "some_mixed", "some_low", "some_value", "some_g")
            if kind == WINDOW:
                each(0, 8, lambda k: work.window_tile(out_v, k))
            else:
                each(0, 2, lambda k: work.low_tile(out_v, k))
                each(0, 4, lambda k: work.value_tile(out_v, k))
            done = WINDOW_END if kind == WINDOW else LINEAR_END
            clear(out_v, done, total - done)

    store = pltpu.make_async_copy(out_v.at[pl.ds(0, total), :], out, work.in_sem.at[0])
    store.start()
    store.wait()


def products(sources, total_rows):
    return pl.pallas_call(
        products_kernel,
        out_shape=jax.ShapeDtypeStruct((total_rows, 128), BF),
        in_specs=[any_spec()] * 5 + [vmem_spec()],
        out_specs=any_spec(),
        scratch_shapes=[pltpu.VMEM((total_rows + 512, 128), BF)] + product_scratch(MICRO * LEN, 3),
        compiler_params=pltpu.CompilerParams(vmem_limit_bytes=60 * MIB),
        name="products",
    )(*sources)


PLACES = 4


def reduce_kernel(*refs):
    section = lax.axis_index("section")
    batch = lax.axis_index("batch")
    place, core = batch // 2, lax.rem(batch, 2)
    mate = place + 1 - 2 * lax.rem(place, 2)
    out, part, own, passing, total, flat, sems = refs[6:13]
    ex_send, ex_recv, send, recv, out_sem = sems
    width = own.shape[1]
    step_rows = width - HEAD_ROWS
    piece = width // CHUNKS
    feed_here = is_feed(section)
    base = jnp.where(feed_here, place // 2, 0) * (4 * step_rows)
    work = Products(refs[:6], refs[13:], base)
    barrier = pltpu.get_barrier_semaphore()

    def greet(other):
        pl.semaphore_signal(barrier, inc=1, device_id=(section, other), device_id_type=MESH)

    window_here = (section == WINDOW) & (place < 2)
    pair_here = feed_here | window_here
    linear_here = section == LINEAR
    sets = (
        (feed_here & (place < 2), ("h", "first", "second")),
        (feed_here & (place >= 2), ("h", "second", "middle", "g")),
        (window_here, ("all_h", "all_mixed", "all_low", "all_value", "all_g")),
        (linear_here, ("some_h", "some_mixed", "some_low", "some_value", "some_g")),
    )
    for here, names in sets:

        @pl.when(here)
        def _(names=names):
            for copy in work.loads(names):
                copy.start()

    greet(2 * place + 1 - core)

    @pl.when(place > 0)
    def _():
        greet(batch - 2)

    @pl.when(place < PLACES - 1)
    def _():
        greet(batch + 2)

    @pl.when(base == 0)
    def _():
        work.head(part)

    pl.semaphore_wait(barrier, jnp.where((place > 0) & (place < PLACES - 1), 3, 2))
    for here, names in sets:

        @pl.when(here)
        def _(names=names):
            for copy in work.loads(names):
                copy.wait()

    def rows_of(i):
        return pl.ds(pl.multiple_of(i * piece, 16), piece)

    def share(index, i):
        return pl.ds(pl.multiple_of(step_rows * index - base + i * piece, 16), piece)

    def swap(to, i):
        slot = lax.rem(to, 2)
        return pltpu.make_async_remote_copy(
            src_ref=part.at[share(2 * to + 1 - core, i), :],
            dst_ref=own.at[slot, rows_of(i), :],
            send_sem=ex_send.at[slot, i],
            recv_sem=ex_recv.at[slot, i],
            device_id=(section, 2 * place + 1 - core),
            device_id_type=MESH,
        )

    def go(source, slot, to, i, other):
        return pltpu.make_async_remote_copy(
            src_ref=source,
            dst_ref=passing.at[slot, rows_of(i), :],
            send_sem=send.at[lax.rem(to, 2), i],
            recv_sem=recv.at[slot, i],
            device_id=(section, other),
            device_id_type=MESH,
        )

    def arrived(slot, i):
        here = passing.at[slot, rows_of(i), :]
        pltpu.make_async_copy(here, here, recv.at[slot, i]).wait()

    def release(to, before, after, limits=(CHUNKS, CHUNKS)):
        for parity in range(2):

            def bound(row, parity=parity):
                return jnp.minimum(jnp.maximum(row - parity * step_rows, 0) // piece, limits[parity])

            first, last = bound(before), bound(after)

            @pl.when(core != parity)
            def _(first=first, last=last):
                each(first, last, lambda i: swap(to, i).start())

            def add(i):
                slot = lax.rem(to, 2)
                rows = rows_of(i)
                swap(to, i).wait_recv()
                mine = part[share(2 * to + core, i), :].astype(F32)
                own[slot, rows, :] = (own[slot, rows, :].astype(F32) + mine).astype(BF)
                source = own.at[slot, rows, :]

                @pl.when(pair_here & (to == mate))
                def _():
                    go(source, 0, to, i, 2 * mate + core).start()

                @pl.when(linear_here & (place == PLACES - 1))
                def _():
                    go(source, slot, to, i, batch - 2).start()

                @pl.when(linear_here & (place == 0) & (to == 1))
                def _():
                    go(source, 2, to, i, batch + 2).start()

            @pl.when(core == parity)
            def _(first=first, last=last):
                each(first, last, add)

    def swapped(to, limits=(CHUNKS, CHUNKS)):
        each(0, jnp.where(core == 0, limits[1], limits[0]), lambda i: swap(to, i).wait_send())

    def emit(i):
        cols = pl.ds(pl.multiple_of(i * piece * 128, 1024), piece * 128)
        flat[0:1, cols] = total[...].reshape(1, piece * 128)

    whole = 2 * step_rows + HEAD_ROWS

    @pl.when(feed_here)
    def _():
        upper = place >= 2

        def pair(t):
            k = jnp.where(upper, 5 + t, lax.rem(t + jnp.where(place == 0, 2, 0), 6))
            tail_only = upper & (t == 0)
            work.pair_tile(part, k, tail_only)
            start = HEAD_ROWS + PAIR_ROWS * k - base
            stop = start + PAIR_ROWS
            early = jnp.where(k == 1, whole, jnp.where(k < 1, stop, start))
            stop_0 = jnp.where(place == 0, early, stop)
            to = base // (2 * step_rows)
            release(to, jnp.where(tail_only, 0, start), jnp.where(tail_only, 0, stop_0))
            release(to + 1, start - 2 * step_rows, stop - 2 * step_rows)

        def down(j):
            work.down_tile(part, j)
            start = DOWN_ROW + 2048 * j - base
            stop = start + 2048
            early = jnp.where(j == 1, whole, jnp.where(j < 1, stop, start))
            release(2, start, jnp.where(place == 2, early, stop))
            release(3, start - 2 * step_rows, stop - 2 * step_rows)

        def turn(t):
            @pl.when(t == 1)
            def _():
                each(0, jnp.where(upper, 3, 6), pair)

            mate_first = place == 2
            first = jnp.where(mate_first & (t == 0), 2, 0)
            last = jnp.where(mate_first & (t == 1), 2, DOWN_TILES)
            here = upper & (mate_first | (t == 1))
            each(first, jnp.where(here, last, first), down)

        each(0, 2, turn)
        swapped(mate)
        swapped(place)

    @pl.when(window_here)
    def _():
        def tile(t, carry):
            k = lax.rem(t + jnp.where(place == 0, 4, 0), 8)
            work.window_tile(part, k)
            start = HEAD_ROWS + 4096 * k
            stop = start + 4096

            @pl.when(k == 7)
            def _():
                clear(part, WINDOW_END, 4 * step_rows + HEAD_ROWS - WINDOW_END)

            stop_0 = jnp.where(place == 0, jnp.where(k < 3, stop, jnp.where(k == 3, whole, start)), stop)
            stop_1 = jnp.where(k == 7, whole, stop - 2 * step_rows)
            release(0, start, stop_0)
            release(1, start - 2 * step_rows, stop_1)
            return carry

        lax.fori_loop(0, 8, tile, 0)
        for to in range(2):
            swapped(to)

    @pl.when(linear_here)
    def _():
        filled = [max(0, min(CHUNKS, -(-(LINEAR_END - step_rows * index) // piece))) for index in range(4)]
        limits = (tuple(filled[:2]), tuple(filled[2:]))
        cover = max(step_rows * index + piece * filled[index] for index in range(4) if filled[index])
        clear(part, LINEAR_END, cover - LINEAR_END)

        def low(k):
            work.low_tile(part, k)
            start = HEAD_ROWS + 2048 * k
            release(0, start, start + 2048, limits[0])

        def value(k):
            work.value_tile(part, k)
            start = HEAD_ROWS + 4096 * (k + 1)
            stop = jnp.where(k == 3, cover, start + 4096)
            release(0, start, stop, limits[0])
            release(1, start - 2 * step_rows, stop - 2 * step_rows, limits[1])

        each(0, 2, low)
        each(0, 4, value)

        def own_count(to):
            return jnp.where(core == 0, limits[to][0], limits[to][1])

        def pass_down(to):
            def act(i):
                rows = rows_of(i)
                arrived(to, i)
                added = passing[to, rows, :].astype(F32) + own[to, rows, :].astype(F32)
                passing[to, rows, :] = added.astype(BF)
                go(passing.at[to, rows, :], to, to, i, batch - 2).start()

            each(0, own_count(to), act)

        @pl.when((place == 1) | (place == 2))
        def _():
            pass_down(0)

        @pl.when(place == 2)
        def _():
            pass_down(1)

        for to in range(2):
            swapped(to, limits[to])

        def sum_up(i):
            rows = rows_of(i)

            @pl.when((place == 0) & (i < own_count(0)))
            def _():
                arrived(0, i)
                total[...] = own[0, rows, :].astype(F32) + passing[0, rows, :].astype(F32)

            @pl.when((place == 1) & (i < own_count(1)))
            def _():
                arrived(1, i)
                arrived(2, i)
                both_ways = passing[1, rows, :].astype(F32) + passing[2, rows, :].astype(F32)
                total[...] = own[1, rows, :].astype(F32) + both_ways

            here = jnp.where(place == 0, own_count(0), jnp.where(place == 1, own_count(1), 0))

            @pl.when(i >= here)
            def _():
                total[...] = jnp.zeros_like(total)

            emit(i)

        each(0, CHUNKS, sum_up)

        @pl.when((place == 1) | (place >= 2))
        def _():
            each(0, own_count(0), lambda i: go(passing.at[0, rows_of(i), :], 0, 0, i, batch - 2).wait_send())

        @pl.when((place == 0) | (place >= 2))
        def _():
            each(0, own_count(1), lambda i: go(passing.at[0, rows_of(i), :], 0, 1, i, batch - 2).wait_send())

    @pl.when((section == WINDOW) & (place >= 2))
    def _():
        total[...] = jnp.zeros_like(total)
        each(0, CHUNKS, emit)

    @pl.when(pair_here)
    def _():
        slot = lax.rem(place, 2)

        def sum_up(i):
            rows = rows_of(i)
            arrived(0, i)
            total[...] = own[slot, rows, :].astype(F32) + passing[0, rows, :].astype(F32)
            emit(i)

        each(0, CHUNKS, sum_up)
        other = 2 * mate + core
        each(0, CHUNKS, lambda i: go(passing.at[0, rows_of(i), :], 0, mate, i, other).wait_send())

    count = out.shape[1]
    first = pl.multiple_of((8 + batch) * 128, 128)
    store = pltpu.make_async_copy(flat.at[:, pl.ds(first, count)], out, out_sem)
    store.start()
    store.wait()


def reduce_products(sources, total_rows, batches):
    step_rows = (total_rows - 8) // batches - 1
    width = step_rows + HEAD_ROWS
    return pl.pallas_call(
        reduce_kernel,
        out_shape=jax.ShapeDtypeStruct((1, (step_rows + 1) * 128), F32),
        in_specs=[any_spec()] * 5 + [vmem_spec()],
        out_specs=any_spec(),
        scratch_shapes=[
            pltpu.VMEM((4 * step_rows + HEAD_ROWS + 512, 128), BF),
            pltpu.VMEM((2, width, 128), BF),
            pltpu.VMEM((3, width, 128), BF),
            pltpu.VMEM((width // CHUNKS, 128), F32),
            pltpu.VMEM((1, width * 128), F32),
            (
                pltpu.SemaphoreType.DMA((2, CHUNKS)),
                pltpu.SemaphoreType.DMA((2, CHUNKS)),
                pltpu.SemaphoreType.DMA((2, CHUNKS)),
                pltpu.SemaphoreType.DMA((3, CHUNKS)),
                pltpu.SemaphoreType.DMA,
            ),
        ]
        + product_scratch(2 * MICRO * LEN, 2),
        compiler_params=pltpu.CompilerParams(
            collective_id=1, has_side_effects=True, vmem_limit_bytes=62 * MIB
        ),
        name="reduce_products",
    )(*sources)


def document_ids(lengths):
    ends = jnp.cumsum(lengths, axis=1)
    places = jnp.arange(LEN, dtype=jnp.int32)
    return jnp.sum((places[None, :, None] >= ends[:, None, :]).astype(jnp.int32), axis=2)


def shards(tokens, cotangent, params, lengths):
    docs = document_ids(lengths[0]).astype(F32)[:, None, :]
    batches = lax.axis_size("batch")
    paired = batches == 2 * PLACES
    acts, d_inputs, normed, middle, d_first, d_second, grads, d_gain = train(
        tokens, cotangent, params, docs, paired
    )
    total_rows = params.shape[1] // 128 + 8
    sources = (normed, d_first, d_second, middle, grads, d_gain)
    if paired:
        mine = reduce_products(sources, total_rows, batches)
    else:
        parts = products(sources, total_rows)
        mine = lax.psum_scatter(parts[8:].reshape(-1), "batch", scatter_dimension=0, tiled=True)
        mine = mine.astype(F32)[None]
    return acts[None], d_inputs[None], mine


def solution(mesh):
    return jax.shard_map(
        shards,
        mesh=mesh,
        in_specs=(P("batch", None), P("batch", None), P("section", None), P("batch", None, None)),
        out_specs=(P("section", "batch", None), P("section", "batch", None), P("section", "batch")),
        check_vma=False,
    )
```

```python
import functools
import math

import jax
import jax.numpy as jnp
from jax import lax
from jax.experimental import pallas as pl
from jax.experimental.pallas import tpu as pltpu
from jax.sharding import PartitionSpec as P

D = 1024
FF = 2752
FP = 2816
HEADS = 16
FEAT = 16
WIN = 64
MICRO = 2
LEN = 256
EPSILON = 1e-06
SCALE = 1.0 / math.sqrt(D)
LINEAR, FEED, WINDOW, FEED2 = 0, 1, 2, 3
MIB = 2**20
MESH = pl.DeviceIdType.MESH
BF = jnp.bfloat16
F32 = jnp.float32


def any_spec():
    return pl.BlockSpec(memory_space=pl.ANY)


def vmem_spec():
    return pl.BlockSpec(memory_space=pltpu.VMEM)


def dot(left, right):
    return jnp.dot(left, right, preferred_element_type=F32)


def dot_t(left, right):
    return lax.dot_general(left, right, (((1,), (1,)), ((), ())), preferred_element_type=F32)


def dot_0(left, right):
    return lax.dot_general(left, right, (((0,), (0,)), ((), ())), preferred_element_type=F32)


def block256(index):
    return pl.ds(pl.multiple_of(index * 256, 256), 256)


def each(first, last, act):
    def step(i, carry):
        act(i)
        return carry

    lax.fori_loop(first, last, step, 0)


def is_feed(section):
    return (section == FEED) | (section == FEED2)


PAIR_STEP = 32 * FF
ROW_STEP = 64 * D
AHEAD = 8


def prepare(section, flat, wide_v, tall_v, chunk, blocks, woven, load_sem):
    def run(steps, count, first, work):
        def load(i):
            slot = lax.rem(i, AHEAD)
            return pltpu.make_async_copy(
                flat.at[:, pl.ds(pl.multiple_of(first + i * count, 1024), count)],
                chunk.at[slot, :, pl.ds(0, count)],
                load_sem.at[slot],
            )

        def start(i, carry):
            load(i).start()
            return carry

        lax.fori_loop(0, AHEAD, start, 0)

        def step(i, carry):
            load(i).wait()
            rows = count // 128
            blocks[pl.ds(0, rows), :] = chunk[lax.rem(i, AHEAD), :, pl.ds(0, count)].astype(F32).reshape(rows, 128)
            work(i)

            @pl.when(i + AHEAD < steps)
            def _():
                load(i + AHEAD).start()

            return carry

        lax.fori_loop(0, steps, step, 0)

    def rows_of(index, count):
        return pl.ds(pl.multiple_of(index * count, count), count)

    def pair_work(i):
        low_half = lax.broadcasted_iota(jnp.int32, (16, 128), 1) < 64
        rolled = pltpu.roll(blocks[pl.ds(21, 16, stride=43), :], 64, 1)
        for c in range(22):
            even = blocks[pl.ds(c, 16, stride=43), :]
            if c == 21:
                even = jnp.where(low_half, even, 0.0)
                odd = jnp.where(low_half, rolled, 0.0)
            else:
                after = pltpu.roll(blocks[pl.ds(22 + c, 16, stride=43), :], 64, 1)
                odd = jnp.where(low_half, rolled, after)
                rolled = after
            woven[c, pl.ds(0, 16, stride=2), :] = even
            woven[c, pl.ds(1, 16, stride=2), :] = odd
        rows = rows_of(lax.rem(i, 32), 32)
        for c in range(22):
            wide_v[i // 32, rows, pl.ds(128 * c, 128)] = woven[c].astype(BF)

    def row_work(target, rows, first_col):
        for c in range(8):
            target[rows, pl.ds(first_col + 128 * c, 128)] = blocks[pl.ds(c, 64, stride=8), :].astype(BF)

    def square(i, first, target, first_col):
        @pl.when((i >= first) & (i < first + 16))
        def _():
            row_work(target, rows_of(i - first, 64), first_col)

    @pl.when(is_feed(section))
    def _():
        run(64, PAIR_STEP, D, pair_work)
        run(43, ROW_STEP, D + 2 * D * FF, lambda i: row_work(tall_v, rows_of(i, 64), 0))
        tall_v[pl.ds(FF, FP - FF), :] = jnp.zeros((FP - FF, D), BF)

    @pl.when(section == WINDOW)
    def _():
        def work(i):
            square(i, 0, wide_v.at[0], 0)
            square(i, 16, wide_v.at[0], D)
            square(i, 32, wide_v.at[1], 0)
            square(i, 48, tall_v, 0)

        run(64, ROW_STEP, D, work)

    @pl.when(section == LINEAR)
    def _():
        def work(i):
            for part in range(2):

                @pl.when(i // 4 == part)
                def _(part=part):
                    rows = rows_of(i - 4 * part, 256)
                    for c in range(2):
                        cols = pl.ds(part * HEADS * FEAT + 128 * c, 128)
                        wide_v[0, rows, cols] = blocks[pl.ds(c, 256, stride=2), :].astype(BF)

            square(i, 8, wide_v.at[1], 0)
            square(i, 24, tall_v, 0)

        run(40, ROW_STEP, D, work)


ROWS = 128
CHUNKS_OF = LEN // ROWS


def lanes_of_head(kind, block, half):
    lanes = lax.broadcasted_iota(jnp.int32, (1, 128), 1)
    if kind == WINDOW:
        return lanes // 64 == half
    return lanes // FEAT == lax.rem(2 * block + half, 8)


def lanes_of_value(half):
    return lax.broadcasted_iota(jnp.int32, (1, 128), 1) // 64 == half


def only(mask, values):
    return jnp.where(mask, values, jnp.zeros_like(values))


def both(masks, values):
    return jnp.concatenate([only(masks[0], values), only(masks[1], values)], axis=0)


def merge(masks, stacked):
    return only(masks[0], stacked[:ROWS]) + only(masks[1], stacked[ROWS:])


def block_of(index, first=0):
    return pl.ds(pl.multiple_of(first + index * 128, 128), 128)


def query_index(kind, block):
    return block if kind == WINDOW else block // 4


def low_width(kind):
    return D if kind == WINDOW else HEADS * FEAT


def mask_of(kind, doc_col, doc_row, first_row):
    shape = (doc_col.shape[0], doc_row.shape[1])
    rows = lax.broadcasted_iota(jnp.int32, shape, 0) + first_row
    cols = lax.broadcasted_iota(jnp.int32, shape, 1)
    mask = (doc_col == doc_row) & (cols <= rows)
    if kind == WINDOW:
        mask = mask & (rows - cols < WIN)
    return mask.astype(F32)


def root_of(kind):
    return 1.0 / math.sqrt(D // HEADS if kind == WINDOW else FEAT)


def out_scale(kind):
    return {LINEAR: 8.0, WINDOW: 4.0, FEED: 1.0}[kind] * SCALE


def train_kernel(
    swapping,
    tokens, cotangent, flat, lengths,
    acts, d_inputs, normed, middle, d_first, d_second, grads, d_gain,
    wide_v, tall_v, gain_v, docs_v, z_v, h_v, x_v, g_v, dz_v, first_v, second_v, mid_v, dh_v, gain_sum, far_gain,
    wide_t, tall_t, inverse_v, mask_v, dy_v, dq_v, dk_v, dv_v, chunk, blocks, woven,
    load_sem, gain_sem, in_sem, act_sem, out_sem, on_send, on_recv, back_send, back_recv, far_send, far_recv,
):
    section = lax.axis_index("section")
    batch = lax.axis_index("batch")
    last = lax.axis_size("section") - 1
    batches = lax.axis_size("batch")
    steps = MICRO * CHUNKS_OF
    count = steps * ROWS
    barrier = pltpu.get_barrier_semaphore()

    far = lax.rem(batch + batches // 2, batches)
    nobody = section < 0
    lower = batch < batches // 2
    gives = is_feed(section) | ((section == WINDOW) & jnp.logical_not(lower)) if swapping else nobody
    takes = is_feed(section) | ((section == WINDOW) & lower) if swapping else nobody

    @pl.when(gives | takes)
    def _():
        pl.semaphore_signal(barrier, inc=1, device_id=(section, far), device_id_type=MESH)

    @pl.when(section > 0)
    def _():
        pl.semaphore_signal(barrier, inc=1, device_id=(section - 1, batch), device_id_type=MESH)

    @pl.when(section < last)
    def _():
        pl.semaphore_signal(barrier, inc=1, device_id=(section + 1, batch), device_id_type=MESH)

    gain_copy = pltpu.make_async_copy(flat.at[:, pl.ds(0, D)], gain_v, gain_sem)
    gain_copy.start()
    token_copy = pltpu.make_async_copy(tokens, z_v.at[pl.ds(0, count), :], in_sem.at[0])
    tangent_copy = pltpu.make_async_copy(cotangent, g_v.at[pl.ds(0, count), :], in_sem.at[1])

    @pl.when(section == 0)
    def _():
        token_copy.start()

    @pl.when(section == last)
    def _():
        tangent_copy.start()

    places = lax.broadcasted_iota(jnp.int32, (1, LEN), 1)
    for micro in range(MICRO):
        end = 0
        ids = jnp.zeros((1, LEN), F32)
        for document in range(lengths.shape[2]):
            end = end + lengths[0, micro, document]
            ids += (places >= end).astype(F32)
        docs_v[micro] = ids
    prepare(section, flat, wide_v, tall_v, chunk, blocks, woven, load_sem)
    gain_copy.wait()
    gain = 1.0 + gain_v[...].astype(F32) / 8.0
    gain_sum[...] = jnp.zeros_like(gain_sum)

    @pl.when(section == 0)
    def _():
        token_copy.wait()

    @pl.when(section == last)
    def _():
        tangent_copy.wait()

    greeted = jnp.where((section > 0) & (section < last), 2, 1)
    pl.semaphore_wait(barrier, greeted + jnp.where(gives | takes, 1, 0))

    def rows_at(step, phase=0):
        return pl.ds(pl.multiple_of(phase * count + step * ROWS, ROWS), ROWS)

    def hand_on(step):
        rows = rows_at(step)
        return pltpu.make_async_remote_copy(
            src_ref=x_v.at[rows, :],
            dst_ref=z_v.at[rows, :],
            send_sem=on_send.at[step],
            recv_sem=on_recv.at[step],
            device_id=(section + 1, batch),
            device_id_type=MESH,
        )

    def hand_back(step):
        rows = rows_at(step)
        return pltpu.make_async_remote_copy(
            src_ref=x_v.at[rows, :],
            dst_ref=g_v.at[rows, :],
            send_sem=back_send.at[step],
            recv_sem=back_recv.at[step],
            device_id=(section - 1, batch),
            device_id_type=MESH,
        )

    def far_copy(kind, step=0):
        rows, target = rows_at(step), rows_at(step, 1)
        source, target = (
            (z_v.at[rows, :], z_v.at[target, :]),
            (g_v.at[rows, :], g_v.at[target, :]),
            (gain_sum, far_gain),
            (docs_v.at[pl.ds(0, MICRO)], docs_v.at[pl.ds(MICRO, MICRO)]),
        )[kind]
        return pltpu.make_async_remote_copy(
            src_ref=source,
            dst_ref=target,
            send_sem=far_send.at[kind, step],
            recv_sem=far_recv.at[kind, step],
            device_id=(section, far),
            device_id_type=MESH,
        )

    @pl.when(gives)
    def _():
        far_copy(3).start()

    @pl.when(gives & (section == last))
    def _():
        for step in range(steps):
            far_copy(1, step).start()

    def act_out(step):
        rows = rows_at(step)
        return pltpu.make_async_copy(x_v.at[rows, :], acts.at[rows, :], act_sem.at[0, step])

    def forward_outs(phase, step):
        rows, target = rows_at(step), rows_at(step, phase)
        return [
            pltpu.make_async_copy(h_v.at[rows, :], normed.at[target, :], act_sem.at[1, step]),
            pltpu.make_async_copy(mid_v.at[rows, :], middle.at[target, :], act_sem.at[2, step]),
        ]

    def gradient_out(step):
        rows = rows_at(step)
        return pltpu.make_async_copy(dz_v.at[rows, :], d_inputs.at[rows, :], out_sem.at[0, step])

    def backward_outs(phase, step):
        rows, target = rows_at(step), rows_at(step, phase)
        return [
            pltpu.make_async_copy(g_v.at[target, :], grads.at[target, :], out_sem.at[1, step]),
            pltpu.make_async_copy(first_v.at[rows, :], d_first.at[target, :], out_sem.at[2, step]),
            pltpu.make_async_copy(second_v.at[rows, :], d_second.at[target, :], out_sem.at[3, step]),
        ]


    def forward_step(phase, step, hidden, project):
        rows, here = rows_at(step), rows_at(step, phase)
        own = phase == 0

        @pl.when(own & (section > 0))
        def _():
            hand_on(step).wait_recv()

        @pl.when(own & gives)
        def _():
            far_copy(0, step).start()

        @pl.when(jnp.logical_not(own))
        def _():
            far_copy(0, step).wait_recv()

        z = z_v[here, :].astype(F32)
        scaled = lax.rsqrt(jnp.mean(z * z, axis=1, keepdims=True) + EPSILON)
        h_v[rows, :] = (z * scaled * gain).astype(BF)
        hidden(rows)

        @pl.when(own)
        def _():
            x_v[rows, :] = (z_v[here, :].astype(F32) + project(rows)).astype(BF)

            @pl.when(section < last)
            def _():
                hand_on(step).start()

            act_out(step).start()

        for copy in forward_outs(phase, step):
            copy.start()

    def backward_step(phase, step, unhidden, back):
        rows, here = rows_at(step), rows_at(step, phase)
        own = phase == 0

        @pl.when(own & (section < last))
        def _():
            hand_back(step).wait_recv()

            @pl.when(gives)
            def _():
                far_copy(1, step).start()

        @pl.when(jnp.logical_not(own))
        def _():
            far_copy(1, step).wait_recv()

        unhidden(here, rows)

        @pl.when(own)
        def _():
            dh_v[...] = back(rows) * SCALE

            @pl.when(section < last)
            def _():
                hand_on(step).wait_send()

            act_out(step).wait()
            z = z_v[rows, :].astype(F32)
            scaled = lax.rsqrt(jnp.mean(z * z, axis=1, keepdims=True) + EPSILON)
            unit = z * scaled
            d_normed = dh_v[...]
            gain_sum[0:1, :] += jnp.sum(d_normed * unit, axis=0, keepdims=True) * 0.125
            d_unit = d_normed * gain
            d_z = scaled * (d_unit - unit * jnp.mean(d_unit * unit, axis=1, keepdims=True))
            d_z += g_v[rows, :].astype(F32)
            dz_v[rows, :] = d_z
            x_v[rows, :] = d_z.astype(BF)

            @pl.when(section > 0)
            def _():
                hand_back(step).start()

            gradient_out(step).start()

        for copy in backward_outs(phase, step):
            copy.start()

    def turn_weights(low, high):
        def wide_piece(which, t):
            wide_t[which, block256(t), :] = wide_v[which, :, block256(t)].T

        def tall_piece(t):
            tall_t[:, block256(t)] = tall_v[block256(t), :].T

        each(0, low // 256, functools.partial(wide_piece, 0))
        each(0, high // 256, functools.partial(wide_piece, 1))
        each(0, high // 256, tall_piece)

    def kept_at(kind, index):
        width = 2 * low_width(kind)
        room = (FP - width) // 256 * 4
        over = index >= room
        place = jnp.where(over, index - room, index)
        first = jnp.where(over, D, width) + place // 4 * 256
        rows = pl.ds(pl.multiple_of(first, 256), 256)
        return wide_t.at[jnp.where(over, 1, 0), rows, block256(lax.rem(place, 4))]

    def feed_hidden(rows):
        half = FP // 2

        def piece(part, carry):
            cols = pl.ds(pl.multiple_of(part * half, half), half)
            gate = dot(h_v[rows, :], wide_v[0, :, cols]) * SCALE
            up = dot(h_v[rows, :], wide_v[1, :, cols]) * SCALE
            sig = 1.0 / (1.0 + jnp.exp(-gate))
            silu = gate * sig
            first_v[rows, cols] = (up * (sig + silu * (1.0 - sig))).astype(BF)
            second_v[rows, cols] = silu.astype(BF)
            mid_v[rows, cols] = (silu * up).astype(BF)
            return carry

        lax.fori_loop(0, 2, piece, 0)

    def feed_project(rows):
        return dot(mid_v[rows, :], tall_v[...]) * SCALE

    def feed_unhidden(here, rows):
        half = FP // 2

        def piece(part, carry):
            cols = pl.ds(pl.multiple_of(part * half, half), half)
            d_mid = dot(g_v[here, :], tall_t[:, cols]) * SCALE
            first_v[rows, cols] = (d_mid * first_v[rows, cols].astype(F32)).astype(BF)
            second_v[rows, cols] = (d_mid * second_v[rows, cols].astype(F32)).astype(BF)
            return carry

        lax.fori_loop(0, 2, piece, 0)

    def feed_back(rows):
        return dot(first_v[rows, :], wide_t[0]) + dot(second_v[rows, :], wide_t[1])

    def attend_hidden(kind, phase, micro, part, rows):
        width = low_width(kind)
        span = ROWS * (part + 1)
        keys_at = pl.ds(pl.multiple_of(micro * LEN, LEN), span)
        step = micro * CHUNKS_OF + part
        first_v[rows, pl.ds(0, 2 * width)] = (dot(h_v[rows, :], wide_v[0, :, pl.ds(0, 2 * width)]) * SCALE).astype(BF)
        second_v[rows, pl.ds(0, D)] = (dot(h_v[rows, :], wide_v[1, :, pl.ds(0, D)]) * SCALE).astype(BF)
        cols = pl.ds(0, span)
        index = phase * MICRO + micro
        own_docs = jnp.broadcast_to(docs_v[index, :, pl.ds(part * ROWS, ROWS)], (8, ROWS))
        mask_v[:, cols] = mask_of(kind, own_docs.T[:, 0:1], docs_v[index, :, cols], part * ROWS)

        def block(t, carry):
            index = query_index(kind, t)
            queries = first_v[rows, block_of(index)]
            keys = first_v[keys_at, block_of(index, width)]
            values = second_v[keys_at, block_of(t)]
            heads = [lanes_of_head(kind, t, half) for half in range(2)]
            scores = (dot_t(both(heads, queries), keys) * root_of(kind)).reshape(2, ROWS, span)
            mask = mask_v[:, cols]
            if kind == WINDOW:
                kept = jnp.where((mask > 0.0)[None], scores, -1e30)
                raised = jnp.exp(kept - jnp.max(kept, axis=2, keepdims=True))
            else:
                slope = mask[None] * (1.0 + scores)
                kept_at(kind, (steps + step) * 8 + t)[:, cols] = slope.astype(BF).reshape(2 * ROWS, span)
                raised = 0.5 * (mask[None] + slope * slope)
            raised = raised.astype(BF).reshape(2 * ROWS, span)
            kept_at(kind, step * 8 + t)[:, cols] = raised
            summed = dot(raised, jnp.concatenate([values, jnp.ones((span, 128), BF)], axis=1))
            inverse = 1.0 / summed[:, 128:]
            sides = [lanes_of_value(half) for half in range(2)]
            mid_v[rows, block_of(t)] = merge(sides, summed[:, :128] * inverse).astype(BF)
            inverse_v[rows, block_of(t)] = merge(sides, inverse)
            return carry

        lax.fori_loop(0, 8, block, 0, unroll=UNROLL)

    def attend_project(kind, rows):
        return dot(mid_v[rows, pl.ds(0, D)], tall_v[pl.ds(0, D), :]) * out_scale(kind)

    def attend_unhidden(kind, micro, part, here, rows):
        width = low_width(kind)
        span = ROWS * (part + 1)
        keys_at = pl.ds(pl.multiple_of(micro * LEN, LEN), span)
        own = pl.ds(0, span)
        step = micro * CHUNKS_OF + part
        d_mixed = dot(g_v[here, :], tall_t[:, pl.ds(0, D)]) * out_scale(kind)
        dy_v[...] = (d_mixed * inverse_v[rows, :]).astype(BF)
        if part == CHUNKS_OF - 1:
            dk_v[...] = jnp.zeros_like(dk_v)
            dv_v[...] = jnp.zeros_like(dv_v)
        if kind == LINEAR:
            dq_v[...] = jnp.zeros_like(dq_v)

        def block(t, carry):
            index = query_index(kind, t)
            queries = first_v[rows, block_of(index)]
            keys = first_v[keys_at, block_of(index, width)]
            values = second_v[keys_at, block_of(t)]
            heads = [lanes_of_head(kind, t, half) for half in range(2)]
            sides = [lanes_of_value(half) for half in range(2)]
            d_mixed = both(sides, dy_v[:, block_of(t)])
            mixed = mid_v[rows, block_of(t)].astype(F32)
            shift = jnp.sum(d_mixed.astype(F32) * jnp.concatenate([mixed, mixed], axis=0), axis=1, keepdims=True)
            d_weights = dot_t(d_mixed, values) - shift
            raised = kept_at(kind, step * 8 + t)[:, own]
            slope = raised if kind == WINDOW else kept_at(kind, (steps + step) * 8 + t)[:, own]
            d_scores = (slope.astype(F32) * d_weights).astype(BF)
            dv_v[own, block_of(t)] += dot_0(raised, d_mixed)
            d_queries = merge(heads, dot(d_scores, keys)) * root_of(kind)
            dk_v[own, block_of(index)] += dot_0(d_scores, both(heads, queries)) * root_of(kind)
            if kind == WINDOW:
                dq_v[:, block_of(t)] = d_queries
            else:
                dq_v[:, block_of(index)] += d_queries
            return carry

        lax.fori_loop(0, 8, block, 0, unroll=UNROLL)
        done = pl.ds(part * ROWS, ROWS)
        first_v[rows, pl.ds(0, width)] = dq_v[:, pl.ds(0, width)].astype(BF)
        first_v[rows, pl.ds(width, width)] = dk_v[done, pl.ds(0, width)].astype(BF)
        second_v[rows, pl.ds(0, D)] = dv_v[done, :].astype(BF)

    def attend_back(kind, rows):
        width = low_width(kind)
        total = dot(first_v[rows, pl.ds(0, 2 * width)], wide_t[0, pl.ds(0, 2 * width), :])
        total += dot(second_v[rows, pl.ds(0, D)], wide_t[1, pl.ds(0, D), :])
        return total

    @pl.when(section == last)
    def _():
        turn_weights(FP, FP)

    @pl.when(section == WINDOW)
    def _():
        turn_weights(2 * D, D)

    def one_phase(phase, carry):
        own = phase == 0

        @pl.when(is_feed(section))
        def _():
            turns = jnp.where(own & (section == last), MICRO, 1)
            span = steps // turns

            def backward(step):
                micro, part = step // CHUNKS_OF, CHUNKS_OF - 1 - lax.rem(step, CHUNKS_OF)
                backward_step(phase, micro * CHUNKS_OF + part, feed_unhidden, feed_back)

            def turn(index):
                here = (index * span, index * span + span)
                each(*here, lambda step: forward_step(phase, step, feed_hidden, feed_project))

                @pl.when(own & (section < last))
                def _():
                    turn_weights(FP, FP)

                each(*here, backward)

            each(0, turns, turn)

        for kind in (WINDOW, LINEAR):

            @pl.when(section == kind)
            def _(kind=kind):
                def forward(micro, inner):
                    for part in range(CHUNKS_OF):
                        forward_step(
                            phase,
                            micro * CHUNKS_OF + part,
                            functools.partial(attend_hidden, kind, phase, micro, part),
                            functools.partial(attend_project, kind),
                        )
                    return inner

                lax.fori_loop(0, MICRO, forward, 0)

        for kind in (WINDOW, LINEAR):

            @pl.when(section == kind)
            def _(kind=kind):
                def backward(micro, inner):
                    for part in reversed(range(CHUNKS_OF)):
                        backward_step(
                            phase,
                            micro * CHUNKS_OF + part,
                            functools.partial(attend_unhidden, kind, micro, part),
                            functools.partial(attend_back, kind),
                        )
                    return inner

                if kind == LINEAR:
                    turn_weights(2 * low_width(kind), D)
                lax.fori_loop(0, MICRO, backward, 0)

        @pl.when(own & gives)
        def _():
            far_copy(2).start()

        def finish(step, inner):
            @pl.when(own)
            def _():
                @pl.when(section > 0)
                def _():
                    hand_back(step).wait_send()

                gradient_out(step).wait()

            for copy in forward_outs(phase, step) + backward_outs(phase, step):
                copy.wait()
            return inner

        lax.fori_loop(0, steps, finish, 0)

        @pl.when(own & takes)
        def _():
            far_copy(3).wait_recv()

        return carry

    lax.fori_loop(0, jnp.where(takes, 2, 1), one_phase, 0)
    d_gain[...] = gain_sum[...]

    @pl.when(takes)
    def _():
        far_copy(2).wait_recv()
        d_gain[...] += far_gain[...]

    @pl.when(gives)
    def _():
        for kind in range(2):
            for step in range(steps):
                far_copy(kind, step).wait_send()
        far_copy(2).wait_send()
        far_copy(3).wait_send()


UNROLL = 2


def train(tokens, cotangent, flat, lengths, swapping):
    count = MICRO * LEN
    steps = MICRO * CHUNKS_OF
    kept = 2 * count if swapping else count
    return pl.pallas_call(
        functools.partial(train_kernel, swapping),
        out_shape=(
            jax.ShapeDtypeStruct((count, D), BF),
            jax.ShapeDtypeStruct((count, D), F32),
            jax.ShapeDtypeStruct((kept, D), BF),
            jax.ShapeDtypeStruct((kept, FP), BF),
            jax.ShapeDtypeStruct((kept, FP), BF),
            jax.ShapeDtypeStruct((kept, FP), BF),
            jax.ShapeDtypeStruct((kept, D), BF),
            jax.ShapeDtypeStruct((8, D), F32),
        ),
        in_specs=[any_spec()] * 3 + [pl.BlockSpec(memory_space=pltpu.SMEM)],
        out_specs=(any_spec(),) * 7 + (vmem_spec(),),
        scratch_shapes=[
            pltpu.VMEM((2, D, FP), BF),
            pltpu.VMEM((FP, D), BF),
            pltpu.VMEM((1, D), BF),
            pltpu.VMEM((2 * MICRO, 1, LEN), F32),
            pltpu.VMEM((2 * count, D), BF),
            pltpu.VMEM((count, D), BF),
            pltpu.VMEM((count, D), BF),
            pltpu.VMEM((2 * count, D), BF),
            pltpu.VMEM((count, D), F32),
            pltpu.VMEM((count, FP), BF),
            pltpu.VMEM((count, FP), BF),
            pltpu.VMEM((count, FP), BF),
            pltpu.VMEM((ROWS, D), F32),
            pltpu.VMEM((8, D), F32),
            pltpu.VMEM((8, D), F32),
            pltpu.VMEM((2, FP, D), BF),
            pltpu.VMEM((D, FP), BF),
            pltpu.VMEM((count, D), F32),
            pltpu.VMEM((ROWS, LEN), F32),
            pltpu.VMEM((ROWS, D), BF),
            pltpu.VMEM((ROWS, D), F32),
            pltpu.VMEM((LEN, D), F32),
            pltpu.VMEM((LEN, D), F32),
            pltpu.VMEM((AHEAD, 1, PAIR_STEP), BF),
            pltpu.VMEM((PAIR_STEP // 128, 128), F32),
            pltpu.VMEM((22, 32, 128), F32),
            pltpu.SemaphoreType.DMA((AHEAD,)),
            pltpu.SemaphoreType.DMA,
            pltpu.SemaphoreType.DMA((2,)),
            pltpu.SemaphoreType.DMA((3, steps)),
            pltpu.SemaphoreType.DMA((4, steps)),
            pltpu.SemaphoreType.DMA((steps,)),
            pltpu.SemaphoreType.DMA((steps,)),
            pltpu.SemaphoreType.DMA((steps,)),
            pltpu.SemaphoreType.DMA((steps,)),
            pltpu.SemaphoreType.DMA((4, steps)),
            pltpu.SemaphoreType.DMA((4, steps)),
        ],
        compiler_params=pltpu.CompilerParams(
            collective_id=0, has_side_effects=True, vmem_limit_bytes=62 * MIB
        ),
        name="train",
    )(tokens, cotangent, flat, lengths)


HEAD_ROWS = 16
PAIRS = 64
PAIR_ROWS = PAIRS * 43
PAIR_TILES = D // 2 // PAIRS
CHUNKS = 11


class Products:
    def __init__(self, sources, scratch, base):
        self.normed, self.d_first, self.d_second, self.middle, self.grads, self.d_gain = sources
        self.left_v, self.d_v, self.woven, self.stage, self.in_sem = scratch
        self.base = base

    def fetch(self, source, target, index):
        return pltpu.make_async_copy(source, target, self.in_sem.at[index])

    def loads(self, names):
        count = self.left_v.shape[1]
        some = pl.ds(0, MICRO * LEN)
        every = pl.ds(0, count)
        low, both, high = pl.ds(0, D), pl.ds(0, 2 * D), pl.ds(D, D)
        table = {
            "h": (self.normed, self.left_v.at[0], 0),
            "g": (self.grads, self.left_v.at[1], 1),
            "first": (self.d_first, self.d_v.at[0], 2),
            "second": (self.d_second, self.d_v.at[1], 3),
            "middle": (self.middle, self.d_v.at[self.middle_slot()], 4),
        }
        for prefix, rows in (("all_", every), ("some_", some)):
            table[prefix + "h"] = (self.normed.at[rows, :], self.left_v.at[0, rows, :], 0)
            table[prefix + "mixed"] = (self.middle.at[rows, low], self.left_v.at[1, rows, :], 1)
            table[prefix + "low"] = (self.d_first.at[rows, both], self.d_v.at[0, rows, both], 2)
            table[prefix + "value"] = (self.d_second.at[rows, low], self.d_v.at[1, rows, low], 3)
            table[prefix + "g"] = (self.grads.at[rows, :], self.d_v.at[1, rows, high], 4)
        return [self.fetch(*table[name]) for name in names]

    def middle_slot(self):
        return 2 if self.d_v.shape[0] == 3 else 0

    def head(self, out):
        stage = self.stage
        stage[pl.ds(0, 8), :] = jnp.zeros((8, 128), F32)
        stage[pl.ds(8, 8), :] = self.d_gain[0:1, :].reshape(8, 128)
        out[pl.ds(0, 16), :] = stage[pl.ds(0, 16), :].astype(BF)

    def cut(self, out, first_row, rows, piece, scale):
        target_row = first_row - self.base

        def step(j, carry):
            source = pl.ds(pl.multiple_of(j * piece, 16), piece)
            target = pl.ds(pl.multiple_of(target_row + j * piece, 16), piece)
            out[target, :] = (self.stage[source, :] * scale).astype(BF)
            return carry

        lax.fori_loop(0, rows // piece, step, 0)

    def pairs(self, which, first_pair):
        count = PAIRS
        stage, woven = self.stage, self.woven
        half = FP // 2
        low_half = lax.broadcasted_iota(jnp.int32, (count, 128), 1) < 64
        left = self.left_v[0, :, pl.ds(pl.multiple_of(2 * first_pair, 128), 2 * count)]
        for part in range(2):
            piece = dot_0(left, self.d_v[which, :, pl.ds(part * half, half)])
            for c in range(11):
                woven[11 * part + c, pl.ds(0, 2 * count), :] = piece[:, 128 * c : 128 * c + 128]
        for c in range(22):
            stage[pl.ds(c, count, stride=43), :] = woven[c, pl.ds(0, count, stride=2), :]
        before = woven[21, pl.ds(0, count, stride=2), :]
        for c in range(22):
            here = pltpu.roll(woven[c, pl.ds(1, count, stride=2), :], 64, 1)
            stage[pl.ds(21 + c, count, stride=43), :] = jnp.where(low_half, before, here)
            before = here

    def pair_tile(self, out, k, tail_only):
        self.pairs(k // PAIR_TILES, lax.rem(k, PAIR_TILES) * PAIRS)

        @pl.when(jnp.logical_not(tail_only))
        def _():
            self.cut(out, HEAD_ROWS + k * PAIR_ROWS, PAIR_ROWS, 688, SCALE)

        @pl.when(tail_only)
        def _():
            target = pl.ds(pl.multiple_of((k + 1) * PAIR_ROWS - self.base, 16), 16)
            out[target, :] = (self.stage[pl.ds(PAIR_ROWS - 16, 16), :] * SCALE).astype(BF)

    def tall(self, out, left, right, stride, rows, first_row, scale, piece):
        product = dot_0(left, right)
        for c in range(stride):
            self.stage[pl.ds(c, rows, stride=stride), :] = product[:, 128 * c : 128 * c + 128]
        self.cut(out, first_row, rows * stride, piece, scale)

    def down_tile(self, out, j):
        left = self.d_v[self.middle_slot(), :, pl.ds(pl.multiple_of(256 * j, 256), 256)]
        self.tall(out, left, self.left_v[1], 8, 256, DOWN_ROW + 2048 * j, SCALE, 512)

    def window_tile(self, out, k):
        left = self.left_v[k // 6, :, pl.ds(pl.multiple_of(lax.rem(k, 2) * 512, 512), 512)]
        right = self.d_v[k // 4, :, pl.ds(pl.multiple_of(lax.rem(k // 2, 2) * D, D), D)]
        scale = jnp.where(k < 6, SCALE, out_scale(WINDOW))
        self.tall(out, left, right, 8, 512, HEAD_ROWS + 4096 * k, scale, 512)

    def low_tile(self, out, k):
        some = pl.ds(0, MICRO * LEN)
        width = HEADS * FEAT
        right = self.d_v[0, some, pl.ds(pl.multiple_of(k * width, width), width)]
        self.tall(out, self.left_v[0, some, :], right, 2, D, HEAD_ROWS + k * 2048, SCALE, 512)

    def value_tile(self, out, k):
        some = pl.ds(0, MICRO * LEN)
        left = self.left_v[k // 2, some, pl.ds(pl.multiple_of(lax.rem(k, 2) * 512, 512), 512)]
        right = self.d_v[1, some, pl.ds(pl.multiple_of(k // 2 * D, D), D)]
        scale = jnp.where(k < 2, SCALE, out_scale(LINEAR))
        self.tall(out, left, right, 8, 512, HEAD_ROWS + 4096 * (k + 1), scale, 512)


DOWN_ROW = HEAD_ROWS + 2 * PAIR_TILES * PAIR_ROWS
DOWN_TILES = FP // 256
WINDOW_END = HEAD_ROWS + 4 * 8192
LINEAR_END = HEAD_ROWS + 20480


def product_scratch(count, slots):
    return [
        pltpu.VMEM((2, count, D), BF),
        pltpu.VMEM((slots, count, FP), BF),
        pltpu.VMEM((22, 2 * PAIRS, 128), F32),
        pltpu.VMEM((4096, 128), F32),
        pltpu.SemaphoreType.DMA((5,)),
    ]


def clear(out, first_row, rows):
    def step(i, carry):
        out[pl.ds(pl.multiple_of(first_row + i * 128, 16), 128), :] = jnp.zeros((128, 128), BF)
        return carry

    lax.fori_loop(0, rows // 128, step, 0)
    if rows % 128:
        out[pl.ds(first_row + rows // 128 * 128, rows % 128), :] = jnp.zeros((rows % 128, 128), BF)


def products_kernel(*refs):
    section = lax.axis_index("section")
    work = Products(refs[:6], refs[8:], 0)
    out, out_v = refs[6:8]
    total = out_v.shape[0] - 512
    work.head(out_v)

    def load(*names):
        for copy in work.loads(names):
            copy.start()
        for copy in work.loads(names):
            copy.wait()

    @pl.when(is_feed(section))
    def _():
        load("h", "g", "first", "second", "middle")
        each(0, 2 * PAIR_TILES, lambda k: work.pair_tile(out_v, k, section < 0))
        each(0, DOWN_TILES, lambda j: work.down_tile(out_v, j))

    for kind in (WINDOW, LINEAR):

        @pl.when(section == kind)
        def _(kind=kind):
            load("some_h", "some_mixed", "some_low", "some_value", "some_g")
            if kind == WINDOW:
                each(0, 8, lambda k: work.window_tile(out_v, k))
            else:
                each(0, 2, lambda k: work.low_tile(out_v, k))
                each(0, 4, lambda k: work.value_tile(out_v, k))
            done = WINDOW_END if kind == WINDOW else LINEAR_END
            clear(out_v, done, total - done)

    store = pltpu.make_async_copy(out_v.at[pl.ds(0, total), :], out, work.in_sem.at[0])
    store.start()
    store.wait()


def products(sources, total_rows):
    return pl.pallas_call(
        products_kernel,
        out_shape=jax.ShapeDtypeStruct((total_rows, 128), BF),
        in_specs=[any_spec()] * 5 + [vmem_spec()],
        out_specs=any_spec(),
        scratch_shapes=[pltpu.VMEM((total_rows + 512, 128), BF)] + product_scratch(MICRO * LEN, 3),
        compiler_params=pltpu.CompilerParams(vmem_limit_bytes=60 * MIB),
        name="products",
    )(*sources)


PLACES = 4


def reduce_kernel(*refs):
    section = lax.axis_index("section")
    batch = lax.axis_index("batch")
    place, core = batch // 2, lax.rem(batch, 2)
    mate = place + 1 - 2 * lax.rem(place, 2)
    out, part, own, passing, total, flat, sems = refs[6:13]
    ex_send, ex_recv, send, recv, out_sem = sems
    width = own.shape[1]
    step_rows = width - HEAD_ROWS
    piece = width // CHUNKS
    feed_here = is_feed(section)
    base = jnp.where(feed_here, place // 2, 0) * (4 * step_rows)
    work = Products(refs[:6], refs[13:], base)
    barrier = pltpu.get_barrier_semaphore()

    def greet(other):
        pl.semaphore_signal(barrier, inc=1, device_id=(section, other), device_id_type=MESH)

    window_here = (section == WINDOW) & (place < 2)
    pair_here = feed_here | window_here
    linear_here = section == LINEAR
    sets = (
        (feed_here & (place < 2), ("h", "first")),
        (feed_here & (place == 2), ("middle", "g")),
        (feed_here & (place == 3), ("h", "second")),
        (window_here, ("all_h", "all_mixed", "all_low", "all_value", "all_g")),
        (linear_here, ("some_h", "some_mixed", "some_low", "some_value", "some_g")),
    )
    for here, names in sets:

        @pl.when(here)
        def _(names=names):
            for copy in work.loads(names):
                copy.start()

    greet(2 * place + 1 - core)

    @pl.when(place > 0)
    def _():
        greet(batch - 2)

    @pl.when(place < PLACES - 1)
    def _():
        greet(batch + 2)

    @pl.when(base == 0)
    def _():
        work.head(part)

    pl.semaphore_wait(barrier, jnp.where((place > 0) & (place < PLACES - 1), 3, 2))
    for here, names in sets:

        @pl.when(here)
        def _(names=names):
            for copy in work.loads(names):
                copy.wait()

    late_sets = (
        (feed_here & (place < 2), ("second",)),
        (feed_here & (place == 2), ("h", "second")),
        (feed_here & (place == 3), ("middle", "g")),
    )

    def late(act):
        for here, names in late_sets:

            @pl.when(here)
            def _(names=names):
                for copy in work.loads(names):
                    act(copy)

    late(lambda copy: copy.start())

    def rows_of(i):
        return pl.ds(pl.multiple_of(i * piece, 16), piece)

    def share(index, i):
        return pl.ds(pl.multiple_of(step_rows * index - base + i * piece, 16), piece)

    def swap(to, i):
        slot = lax.rem(to, 2)
        return pltpu.make_async_remote_copy(
            src_ref=part.at[share(2 * to + 1 - core, i), :],
            dst_ref=own.at[slot, rows_of(i), :],
            send_sem=ex_send.at[slot, i],
            recv_sem=ex_recv.at[slot, i],
            device_id=(section, 2 * place + 1 - core),
            device_id_type=MESH,
        )

    def go(source, slot, to, i, other):
        return pltpu.make_async_remote_copy(
            src_ref=source,
            dst_ref=passing.at[slot, rows_of(i), :],
            send_sem=send.at[lax.rem(to, 2), i],
            recv_sem=recv.at[slot, i],
            device_id=(section, other),
            device_id_type=MESH,
        )

    def arrived(slot, i):
        here = passing.at[slot, rows_of(i), :]
        pltpu.make_async_copy(here, here, recv.at[slot, i]).wait()

    def release(to, before, after, limits=(CHUNKS, CHUNKS)):
        for parity in range(2):

            def bound(row, parity=parity):
                return jnp.minimum(jnp.maximum(row - parity * step_rows, 0) // piece, limits[parity])

            first, last = bound(before), bound(after)

            @pl.when(core != parity)
            def _(first=first, last=last):
                each(first, last, lambda i: swap(to, i).start())

            def add(i):
                slot = lax.rem(to, 2)
                rows = rows_of(i)
                swap(to, i).wait_recv()
                mine = part[share(2 * to + core, i), :].astype(F32)
                own[slot, rows, :] = (own[slot, rows, :].astype(F32) + mine).astype(BF)
                source = own.at[slot, rows, :]

                @pl.when(pair_here & (to == mate))
                def _():
                    go(source, 0, to, i, 2 * mate + core).start()

                @pl.when(linear_here & (place == PLACES - 1))
                def _():
                    go(source, slot, to, i, batch - 2).start()

                @pl.when(linear_here & (place == 0) & (to == 1))
                def _():
                    go(source, 2, to, i, batch + 2).start()

            @pl.when(core == parity)
            def _(first=first, last=last):
                each(first, last, add)

    def swapped(to, limits=(CHUNKS, CHUNKS)):
        each(0, jnp.where(core == 0, limits[1], limits[0]), lambda i: swap(to, i).wait_send())

    def store(which):
        rows = out.shape[1] // 128
        early = (CHUNKS - 1) * piece - 32
        begin, size = ((0, early), (early, rows - early))[which]
        source = pl.ds(pl.multiple_of((8 + batch + begin) * 128, 128), size * 128)
        return pltpu.make_async_copy(
            flat.at[:, source], out.at[:, pl.ds(begin * 128, size * 128)], out_sem.at[which]
        )

    def emit(i):
        cols = pl.ds(pl.multiple_of(i * piece * 128, 1024), piece * 128)
        flat[0:1, cols] = total[...].reshape(1, piece * 128)

    whole = 2 * step_rows + HEAD_ROWS

    @pl.when(feed_here)
    def _():
        upper = place >= 2
        share_tiles = 2 * step_rows // PAIR_ROWS
        upper_tiles = 2 * PAIR_TILES - 2 * share_tiles

        def pair(t):
            turned = jnp.where(t < share_tiles, t + share_tiles, jnp.where(t == share_tiles, share_tiles - 1, t - share_tiles - 1))
            k = jnp.where(place == 0, turned, t)
            k = jnp.where(upper, jnp.where(t == upper_tiles, 2 * share_tiles - 1, 2 * share_tiles + t), k)
            tail_only = upper & (t == upper_tiles)

            @pl.when(jnp.logical_not(upper) & (k == PAIR_TILES))
            def _():
                late(lambda copy: copy.wait())

            work.pair_tile(part, k, tail_only)
            start = HEAD_ROWS + PAIR_ROWS * k - base
            stop = start + PAIR_ROWS
            ends_late = (place == 0) & (k == share_tiles - 1)
            to = base // (2 * step_rows)
            early = jnp.where(k == share_tiles - 2, whole, jnp.where(k < share_tiles - 2, stop, start))
            before_0 = jnp.where(tail_only, 0, jnp.where(upper & (k == 2 * share_tiles), piece, start))
            after_0 = jnp.where(tail_only, piece, jnp.where(place == 0, early, stop))
            release(to, before_0, after_0)
            before_1 = jnp.where(ends_late, 0, jnp.where((place == 0) & (k == share_tiles), piece, start - 2 * step_rows))
            after_1 = jnp.where(ends_late, piece, stop - 2 * step_rows)
            release(to + 1, before_1, after_1)

        def down(j):
            work.down_tile(part, j)
            start = DOWN_ROW + 2048 * j - base
            stop = start + 2048
            early = jnp.where(j == 1, whole, jnp.where(j < 1, stop, start))
            release(2, start, jnp.where(place == 2, early, stop))
            release(3, start - 2 * step_rows, stop - 2 * step_rows)

        def turn(t):
            @pl.when(t == 1)
            def _():
                @pl.when(place == 2)
                def _():
                    late(lambda copy: copy.wait())

                each(0, jnp.where(upper, upper_tiles + 1, 2 * share_tiles), pair)

                @pl.when(place == 3)
                def _():
                    late(lambda copy: copy.wait())

            mate_first = place == 2
            first = jnp.where(mate_first & (t == 0), 2, 0)
            last = jnp.where(mate_first & (t == 1), 2, DOWN_TILES)
            here = upper & (mate_first | (t == 1))
            each(first, jnp.where(here, last, first), down)

        each(0, 2, turn)
        swapped(mate)
        swapped(place)

    @pl.when(window_here)
    def _():
        def tile(t, carry):
            k = lax.rem(t + jnp.where(place == 0, 4, 0), 8)
            work.window_tile(part, k)
            start = HEAD_ROWS + 4096 * k
            stop = start + 4096

            @pl.when(k == 7)
            def _():
                clear(part, WINDOW_END, 4 * step_rows + HEAD_ROWS - WINDOW_END)

            stop_0 = jnp.where(place == 0, jnp.where(k < 3, stop, jnp.where(k == 3, whole, start)), stop)
            stop_1 = jnp.where(k == 7, whole, stop - 2 * step_rows)
            release(0, start, stop_0)
            release(1, start - 2 * step_rows, stop_1)
            return carry

        lax.fori_loop(0, 8, tile, 0)
        for to in range(2):
            swapped(to)

    @pl.when(linear_here)
    def _():
        filled = [max(0, min(CHUNKS, -(-(LINEAR_END - step_rows * index) // piece))) for index in range(4)]
        limits = (tuple(filled[:2]), tuple(filled[2:]))
        cover = max(step_rows * index + piece * filled[index] for index in range(4) if filled[index])
        clear(part, LINEAR_END, cover - LINEAR_END)

        def low(k):
            work.low_tile(part, k)
            start = HEAD_ROWS + 2048 * k
            release(0, start, start + 2048, limits[0])

        def value(k):
            work.value_tile(part, k)
            start = HEAD_ROWS + 4096 * (k + 1)
            stop = jnp.where(k == 3, cover, start + 4096)
            release(0, start, stop, limits[0])
            release(1, start - 2 * step_rows, stop - 2 * step_rows, limits[1])

        each(0, 2, low)
        each(0, 4, value)

        def own_count(to):
            return jnp.where(core == 0, limits[to][0], limits[to][1])

        def pass_down(to):
            def act(i):
                rows = rows_of(i)
                arrived(to, i)
                added = passing[to, rows, :].astype(F32) + own[to, rows, :].astype(F32)
                passing[to, rows, :] = added.astype(BF)
                go(passing.at[to, rows, :], to, to, i, batch - 2).start()

            each(0, own_count(to), act)

        @pl.when((place == 1) | (place == 2))
        def _():
            pass_down(0)

        @pl.when(place == 2)
        def _():
            pass_down(1)

        for to in range(2):
            swapped(to, limits[to])

        def sum_up(i):
            rows = rows_of(i)

            @pl.when((place == 0) & (i < own_count(0)))
            def _():
                arrived(0, i)
                total[...] = own[0, rows, :].astype(F32) + passing[0, rows, :].astype(F32)

            @pl.when((place == 1) & (i < own_count(1)))
            def _():
                arrived(1, i)
                arrived(2, i)
                both_ways = passing[1, rows, :].astype(F32) + passing[2, rows, :].astype(F32)
                total[...] = own[1, rows, :].astype(F32) + both_ways

            emit(i)

        here = jnp.where(place == 0, own_count(0), jnp.where(place == 1, own_count(1), 0))
        total[...] = jnp.zeros_like(total)
        each(here, CHUNKS, emit)
        each(0, here - 1, sum_up)

        @pl.when(here == CHUNKS)
        def _():
            store(0).start()

        each(jnp.maximum(here - 1, 0), here, sum_up)

        @pl.when(here < CHUNKS)
        def _():
            store(0).start()

        @pl.when((place == 1) | (place >= 2))
        def _():
            each(0, own_count(0), lambda i: go(passing.at[0, rows_of(i), :], 0, 0, i, batch - 2).wait_send())

        @pl.when((place == 0) | (place >= 2))
        def _():
            each(0, own_count(1), lambda i: go(passing.at[0, rows_of(i), :], 0, 1, i, batch - 2).wait_send())

    @pl.when((section == WINDOW) & (place >= 2))
    def _():
        total[...] = jnp.zeros_like(total)
        each(0, CHUNKS, emit)
        store(0).start()

    @pl.when(pair_here)
    def _():
        slot = lax.rem(place, 2)

        def sum_up(i):
            rows = rows_of(i)
            arrived(0, i)
            total[...] = own[slot, rows, :].astype(F32) + passing[0, rows, :].astype(F32)
            emit(i)

        each(0, CHUNKS - 1, sum_up)
        store(0).start()
        each(CHUNKS - 1, CHUNKS, sum_up)
        other = 2 * mate + core
        each(0, CHUNKS, lambda i: go(passing.at[0, rows_of(i), :], 0, mate, i, other).wait_send())

    store(1).start()
    store(0).wait()
    store(1).wait()


def reduce_products(sources, total_rows, batches):
    step_rows = (total_rows - 8) // batches - 1
    width = step_rows + HEAD_ROWS
    return pl.pallas_call(
        reduce_kernel,
        out_shape=jax.ShapeDtypeStruct((1, (step_rows + 1) * 128), F32),
        in_specs=[any_spec()] * 5 + [vmem_spec()],
        out_specs=any_spec(),
        scratch_shapes=[
            pltpu.VMEM((4 * step_rows + HEAD_ROWS + 512, 128), BF),
            pltpu.VMEM((2, width, 128), BF),
            pltpu.VMEM((3, width, 128), BF),
            pltpu.VMEM((width // CHUNKS, 128), F32),
            pltpu.VMEM((1, width * 128), F32),
            (
                pltpu.SemaphoreType.DMA((2, CHUNKS)),
                pltpu.SemaphoreType.DMA((2, CHUNKS)),
                pltpu.SemaphoreType.DMA((2, CHUNKS)),
                pltpu.SemaphoreType.DMA((3, CHUNKS)),
                pltpu.SemaphoreType.DMA((2,)),
            ),
        ]
        + product_scratch(2 * MICRO * LEN, 2),
        compiler_params=pltpu.CompilerParams(
            collective_id=1, has_side_effects=True, vmem_limit_bytes=60 * MIB
        ),
        name="reduce_products",
    )(*sources)


def shards(tokens, cotangent, params, lengths):
    batches = lax.axis_size("batch")
    paired = batches == 2 * PLACES
    acts, d_inputs, normed, middle, d_first, d_second, grads, d_gain = train(
        tokens, cotangent, params, lengths, paired
    )
    total_rows = params.shape[1] // 128 + 8
    sources = (normed, d_first, d_second, middle, grads, d_gain)
    if paired:
        mine = reduce_products(sources, total_rows, batches)
    else:
        parts = products(sources, total_rows)
        mine = lax.psum_scatter(parts[8:].reshape(-1), "batch", scatter_dimension=0, tiled=True)
        mine = mine.astype(F32)[None]
    return acts[None], d_inputs[None], mine


def solution(mesh):
    return jax.shard_map(
        shards,
        mesh=mesh,
        in_specs=(P("batch", None), P("batch", None), P("section", None), P("batch", None, None)),
        out_specs=(P("section", "batch", None), P("section", "batch", None), P("section", "batch")),
        check_vma=False,
    )
```

```python
import functools
import math

import jax
import jax.numpy as jnp
from jax import lax
from jax.experimental import pallas as pl
from jax.experimental.pallas import tpu as pltpu
from jax.sharding import PartitionSpec as P

D = 1024
FF = 2752
FP = 2816
HEADS = 16
FEAT = 16
WIN = 64
MICRO = 2
LEN = 256
EPSILON = 1e-06
SCALE = 1.0 / math.sqrt(D)
LINEAR, FEED, WINDOW, FEED2 = 0, 1, 2, 3
MIB = 2**20
MESH = pl.DeviceIdType.MESH
BF = jnp.bfloat16
F32 = jnp.float32


def any_spec():
    return pl.BlockSpec(memory_space=pl.ANY)


def vmem_spec():
    return pl.BlockSpec(memory_space=pltpu.VMEM)


def dot(left, right):
    return jnp.dot(left, right, preferred_element_type=F32)


def dot_t(left, right):
    return lax.dot_general(left, right, (((1,), (1,)), ((), ())), preferred_element_type=F32)


def dot_0(left, right):
    return lax.dot_general(left, right, (((0,), (0,)), ((), ())), preferred_element_type=F32)


def block256(index):
    return pl.ds(pl.multiple_of(index * 256, 256), 256)


def each(first, last, act):
    def step(i, carry):
        act(i)
        return carry

    lax.fori_loop(first, last, step, 0)


def is_feed(section):
    return (section == FEED) | (section == FEED2)


PAIR_STEP = 32 * FF
ROW_STEP = 64 * D
AHEAD = 12


def prepare(section, flat, wide_v, tall_v, chunk, blocks, woven, load_sem):
    def run(steps, count, first, work):
        def load(i):
            slot = lax.rem(i, AHEAD)
            return pltpu.make_async_copy(
                flat.at[:, pl.ds(pl.multiple_of(first + i * count, 1024), count)],
                chunk.at[slot, :, pl.ds(0, count)],
                load_sem.at[slot],
            )

        def start(i, carry):
            load(i).start()
            return carry

        lax.fori_loop(0, AHEAD, start, 0)

        def step(i, carry):
            load(i).wait()
            rows = count // 128
            blocks[pl.ds(0, rows), :] = chunk[lax.rem(i, AHEAD), :, pl.ds(0, count)].astype(F32).reshape(rows, 128)
            work(i)

            @pl.when(i + AHEAD < steps)
            def _():
                load(i + AHEAD).start()

            return carry

        lax.fori_loop(0, steps, step, 0)

    def rows_of(index, count):
        return pl.ds(pl.multiple_of(index * count, count), count)

    def pair_work(i):
        low_half = lax.broadcasted_iota(jnp.int32, (16, 128), 1) < 64
        rolled = pltpu.roll(blocks[pl.ds(21, 16, stride=43), :], 64, 1)
        for c in range(22):
            even = blocks[pl.ds(c, 16, stride=43), :]
            if c == 21:
                even = jnp.where(low_half, even, 0.0)
                odd = jnp.where(low_half, rolled, 0.0)
            else:
                after = pltpu.roll(blocks[pl.ds(22 + c, 16, stride=43), :], 64, 1)
                odd = jnp.where(low_half, rolled, after)
                rolled = after
            woven[c, pl.ds(0, 16, stride=2), :] = even
            woven[c, pl.ds(1, 16, stride=2), :] = odd
        rows = rows_of(lax.rem(i, 32), 32)
        for c in range(22):
            wide_v[i // 32, rows, pl.ds(128 * c, 128)] = woven[c].astype(BF)

    def row_work(target, rows, first_col):
        for c in range(8):
            target[rows, pl.ds(first_col + 128 * c, 128)] = blocks[pl.ds(c, 64, stride=8), :].astype(BF)

    def square(i, first, target, first_col):
        @pl.when((i >= first) & (i < first + 16))
        def _():
            row_work(target, rows_of(i - first, 64), first_col)

    @pl.when(is_feed(section))
    def _():
        run(64, PAIR_STEP, D, pair_work)
        run(43, ROW_STEP, D + 2 * D * FF, lambda i: row_work(tall_v, rows_of(i, 64), 0))
        tall_v[pl.ds(FF, FP - FF), :] = jnp.zeros((FP - FF, D), BF)

    @pl.when(section == WINDOW)
    def _():
        def work(i):
            square(i, 0, wide_v.at[0], 0)
            square(i, 16, wide_v.at[0], D)
            square(i, 32, wide_v.at[1], 0)
            square(i, 48, tall_v, 0)

        run(64, ROW_STEP, D, work)

    @pl.when(section == LINEAR)
    def _():
        def work(i):
            for part in range(2):

                @pl.when(i // 4 == part)
                def _(part=part):
                    rows = rows_of(i - 4 * part, 256)
                    for c in range(2):
                        cols = pl.ds(part * HEADS * FEAT + 128 * c, 128)
                        wide_v[0, rows, cols] = blocks[pl.ds(c, 256, stride=2), :].astype(BF)

            square(i, 8, wide_v.at[1], 0)
            square(i, 24, tall_v, 0)

        run(40, ROW_STEP, D, work)


ROWS = 128
CHUNKS_OF = LEN // ROWS


def lanes_of_head(kind, block, half):
    lanes = lax.broadcasted_iota(jnp.int32, (1, 128), 1)
    if kind == WINDOW:
        return lanes // 64 == half
    return lanes // FEAT == lax.rem(2 * block + half, 8)


def lanes_of_value(half):
    return lax.broadcasted_iota(jnp.int32, (1, 128), 1) // 64 == half


def only(mask, values):
    return jnp.where(mask, values, jnp.zeros_like(values))


def both(masks, values):
    return jnp.concatenate([only(masks[0], values), only(masks[1], values)], axis=0)


def merge(masks, stacked):
    return only(masks[0], stacked[:ROWS]) + only(masks[1], stacked[ROWS:])


def block_of(index, first=0):
    return pl.ds(pl.multiple_of(first + index * 128, 128), 128)


def query_index(kind, block):
    return block if kind == WINDOW else block // 4


def low_width(kind):
    return D if kind == WINDOW else HEADS * FEAT


def mask_of(kind, doc_col, doc_row, first_row):
    shape = (doc_col.shape[0], doc_row.shape[1])
    rows = lax.broadcasted_iota(jnp.int32, shape, 0) + first_row
    cols = lax.broadcasted_iota(jnp.int32, shape, 1)
    mask = (doc_col == doc_row) & (cols <= rows)
    if kind == WINDOW:
        mask = mask & (rows - cols < WIN)
    return mask.astype(F32)


def root_of(kind):
    return 1.0 / math.sqrt(D // HEADS if kind == WINDOW else FEAT)


def out_scale(kind):
    return {LINEAR: 8.0, WINDOW: 4.0, FEED: 1.0}[kind] * SCALE


def train_kernel(
    swapping,
    tokens, cotangent, flat, lengths,
    acts, d_inputs, normed, middle, d_first, d_second, grads, d_gain,
    wide_v, tall_v, gain_v, docs_v, z_v, h_v, x_v, g_v, dz_v, first_v, second_v, mid_v, dh_v, gain_sum, far_gain,
    wide_t, tall_t, inverse_v, mask_v, dy_v, dq_v, dk_v, dv_v, chunk, blocks, woven,
    load_sem, gain_sem, in_sem, act_sem, out_sem, on_send, on_recv, back_send, back_recv, far_send, far_recv,
):
    section = lax.axis_index("section")
    batch = lax.axis_index("batch")
    last = lax.axis_size("section") - 1
    batches = lax.axis_size("batch")
    steps = MICRO * CHUNKS_OF
    count = steps * ROWS
    barrier = pltpu.get_barrier_semaphore()

    far = lax.rem(batch + batches // 2, batches)
    nobody = section < 0
    lower = batch < batches // 2
    gives = is_feed(section) | ((section == WINDOW) & jnp.logical_not(lower)) if swapping else nobody
    takes = is_feed(section) | ((section == WINDOW) & lower) if swapping else nobody

    @pl.when(gives | takes)
    def _():
        pl.semaphore_signal(barrier, inc=1, device_id=(section, far), device_id_type=MESH)

    @pl.when(section > 0)
    def _():
        pl.semaphore_signal(barrier, inc=1, device_id=(section - 1, batch), device_id_type=MESH)

    @pl.when(section < last)
    def _():
        pl.semaphore_signal(barrier, inc=1, device_id=(section + 1, batch), device_id_type=MESH)

    gain_copy = pltpu.make_async_copy(flat.at[:, pl.ds(0, D)], gain_v, gain_sem)
    gain_copy.start()
    token_copy = pltpu.make_async_copy(tokens, z_v.at[pl.ds(0, count), :], in_sem.at[0])
    tangent_copy = pltpu.make_async_copy(cotangent, g_v.at[pl.ds(0, count), :], in_sem.at[1])

    @pl.when(section == 0)
    def _():
        token_copy.start()

    @pl.when(section == last)
    def _():
        tangent_copy.start()

    places = lax.broadcasted_iota(jnp.int32, (1, LEN), 1)
    for micro in range(MICRO):
        end = 0
        ids = jnp.zeros((1, LEN), F32)
        for document in range(lengths.shape[2]):
            end = end + lengths[0, micro, document]
            ids += (places >= end).astype(F32)
        docs_v[micro] = ids
    prepare(section, flat, wide_v, tall_v, chunk, blocks, woven, load_sem)
    gain_copy.wait()
    gain = 1.0 + gain_v[...].astype(F32) / 8.0
    gain_sum[...] = jnp.zeros_like(gain_sum)

    @pl.when(section == 0)
    def _():
        token_copy.wait()

    @pl.when(section == last)
    def _():
        tangent_copy.wait()

    greeted = jnp.where((section > 0) & (section < last), 2, 1)
    pl.semaphore_wait(barrier, greeted + jnp.where(gives | takes, 1, 0))

    def rows_at(step, phase=0):
        return pl.ds(pl.multiple_of(phase * count + step * ROWS, ROWS), ROWS)

    def hand_on(step):
        rows = rows_at(step)
        return pltpu.make_async_remote_copy(
            src_ref=x_v.at[rows, :],
            dst_ref=z_v.at[rows, :],
            send_sem=on_send.at[step],
            recv_sem=on_recv.at[step],
            device_id=(section + 1, batch),
            device_id_type=MESH,
        )

    def hand_back(step):
        rows = rows_at(step)
        return pltpu.make_async_remote_copy(
            src_ref=x_v.at[rows, :],
            dst_ref=g_v.at[rows, :],
            send_sem=back_send.at[step],
            recv_sem=back_recv.at[step],
            device_id=(section - 1, batch),
            device_id_type=MESH,
        )

    def far_copy(kind, step=0):
        rows, target = rows_at(step), rows_at(step, 1)
        source, target = (
            (z_v.at[rows, :], z_v.at[target, :]),
            (g_v.at[rows, :], g_v.at[target, :]),
            (gain_sum, far_gain),
            (docs_v.at[pl.ds(0, MICRO)], docs_v.at[pl.ds(MICRO, MICRO)]),
        )[kind]
        return pltpu.make_async_remote_copy(
            src_ref=source,
            dst_ref=target,
            send_sem=far_send.at[kind, step],
            recv_sem=far_recv.at[kind, step],
            device_id=(section, far),
            device_id_type=MESH,
        )

    @pl.when(gives)
    def _():
        far_copy(3).start()

    @pl.when(gives & (section == last))
    def _():
        for step in range(steps):
            far_copy(1, step).start()

    def act_out(step):
        rows = rows_at(step)
        return pltpu.make_async_copy(x_v.at[rows, :], acts.at[rows, :], act_sem.at[0, step])

    def forward_outs(phase, step):
        rows, target = rows_at(step), rows_at(step, phase)
        return [
            pltpu.make_async_copy(h_v.at[rows, :], normed.at[target, :], act_sem.at[1, step]),
            pltpu.make_async_copy(mid_v.at[rows, :], middle.at[target, :], act_sem.at[2, step]),
        ]

    def gradient_out(step):
        rows = rows_at(step)
        return pltpu.make_async_copy(dz_v.at[rows, :], d_inputs.at[rows, :], out_sem.at[0, step])

    def backward_outs(phase, step):
        rows, target = rows_at(step), rows_at(step, phase)
        return [
            pltpu.make_async_copy(g_v.at[target, :], grads.at[target, :], out_sem.at[1, step]),
            pltpu.make_async_copy(first_v.at[rows, :], d_first.at[target, :], out_sem.at[2, step]),
            pltpu.make_async_copy(second_v.at[rows, :], d_second.at[target, :], out_sem.at[3, step]),
        ]


    def forward_step(phase, step, hidden, project):
        rows, here = rows_at(step), rows_at(step, phase)
        own = phase == 0

        @pl.when(own & (section > 0))
        def _():
            hand_on(step).wait_recv()

        @pl.when(own & gives)
        def _():
            far_copy(0, step).start()

        @pl.when(jnp.logical_not(own))
        def _():
            far_copy(0, step).wait_recv()

        z = z_v[here, :].astype(F32)
        scaled = lax.rsqrt(jnp.mean(z * z, axis=1, keepdims=True) + EPSILON)
        h_v[rows, :] = (z * scaled * gain).astype(BF)
        hidden(rows)

        @pl.when(own)
        def _():
            x_v[rows, :] = (z_v[here, :].astype(F32) + project(rows)).astype(BF)

            @pl.when(section < last)
            def _():
                hand_on(step).start()

            act_out(step).start()

        for copy in forward_outs(phase, step):
            copy.start()

    def backward_step(phase, step, unhidden, back):
        rows, here = rows_at(step), rows_at(step, phase)
        own = phase == 0

        @pl.when(own & (section < last))
        def _():
            hand_back(step).wait_recv()

            @pl.when(gives)
            def _():
                far_copy(1, step).start()

        @pl.when(jnp.logical_not(own))
        def _():
            far_copy(1, step).wait_recv()

        unhidden(here, rows)

        @pl.when(own)
        def _():
            dh_v[...] = back(rows) * SCALE

            @pl.when(section < last)
            def _():
                hand_on(step).wait_send()

            act_out(step).wait()
            z = z_v[rows, :].astype(F32)
            scaled = lax.rsqrt(jnp.mean(z * z, axis=1, keepdims=True) + EPSILON)
            unit = z * scaled
            d_normed = dh_v[...]
            gain_sum[0:1, :] += jnp.sum(d_normed * unit, axis=0, keepdims=True) * 0.125
            d_unit = d_normed * gain
            d_z = scaled * (d_unit - unit * jnp.mean(d_unit * unit, axis=1, keepdims=True))
            d_z += g_v[rows, :].astype(F32)
            dz_v[rows, :] = d_z
            x_v[rows, :] = d_z.astype(BF)

            @pl.when(section > 0)
            def _():
                hand_back(step).start()

            gradient_out(step).start()

        for copy in backward_outs(phase, step):
            copy.start()

    def turn_weights(low, high):
        def wide_piece(which, t):
            wide_t[which, block256(t), :] = wide_v[which, :, block256(t)].T

        def tall_piece(t):
            tall_t[:, block256(t)] = tall_v[block256(t), :].T

        each(0, low // 256, functools.partial(wide_piece, 0))
        each(0, high // 256, functools.partial(wide_piece, 1))
        each(0, high // 256, tall_piece)

    def kept_at(kind, index):
        width = 2 * low_width(kind)
        room = (FP - width) // 256 * 4
        over = index >= room
        place = jnp.where(over, index - room, index)
        first = jnp.where(over, D, width) + place // 4 * 256
        rows = pl.ds(pl.multiple_of(first, 256), 256)
        return wide_t.at[jnp.where(over, 1, 0), rows, block256(lax.rem(place, 4))]

    def feed_hidden(rows):
        half = FP // 2

        def piece(part, carry):
            cols = pl.ds(pl.multiple_of(part * half, half), half)
            gate = dot(h_v[rows, :], wide_v[0, :, cols]) * SCALE
            up = dot(h_v[rows, :], wide_v[1, :, cols]) * SCALE
            sig = 1.0 / (1.0 + jnp.exp(-gate))
            silu = gate * sig
            first_v[rows, cols] = (up * (sig + silu * (1.0 - sig))).astype(BF)
            second_v[rows, cols] = silu.astype(BF)
            mid_v[rows, cols] = (silu * up).astype(BF)
            return carry

        lax.fori_loop(0, 2, piece, 0)

    def feed_project(rows):
        return dot(mid_v[rows, :], tall_v[...]) * SCALE

    def feed_unhidden(here, rows):
        half = FP // 2

        def piece(part, carry):
            cols = pl.ds(pl.multiple_of(part * half, half), half)
            d_mid = dot(g_v[here, :], tall_t[:, cols]) * SCALE
            first_v[rows, cols] = (d_mid * first_v[rows, cols].astype(F32)).astype(BF)
            second_v[rows, cols] = (d_mid * second_v[rows, cols].astype(F32)).astype(BF)
            return carry

        lax.fori_loop(0, 2, piece, 0)

    def feed_back(rows):
        return dot(first_v[rows, :], wide_t[0]) + dot(second_v[rows, :], wide_t[1])

    def attend_hidden(kind, phase, micro, part, rows):
        width = low_width(kind)
        span = ROWS * (part + 1)
        keys_at = pl.ds(pl.multiple_of(micro * LEN, LEN), span)
        step = micro * CHUNKS_OF + part
        first_v[rows, pl.ds(0, 2 * width)] = (dot(h_v[rows, :], wide_v[0, :, pl.ds(0, 2 * width)]) * SCALE).astype(BF)
        second_v[rows, pl.ds(0, D)] = (dot(h_v[rows, :], wide_v[1, :, pl.ds(0, D)]) * SCALE).astype(BF)
        cols = pl.ds(0, span)
        index = phase * MICRO + micro
        own_docs = jnp.broadcast_to(docs_v[index, :, pl.ds(part * ROWS, ROWS)], (8, ROWS))
        mask_v[:, cols] = mask_of(kind, own_docs.T[:, 0:1], docs_v[index, :, cols], part * ROWS)

        def block(t, carry):
            index = query_index(kind, t)
            queries = first_v[rows, block_of(index)]
            keys = first_v[keys_at, block_of(index, width)]
            values = second_v[keys_at, block_of(t)]
            heads = [lanes_of_head(kind, t, half) for half in range(2)]
            scores = (dot_t(both(heads, queries), keys) * root_of(kind)).reshape(2, ROWS, span)
            mask = mask_v[:, cols]
            if kind == WINDOW:
                kept = jnp.where((mask > 0.0)[None], scores, -1e30)
                raised = jnp.exp(kept - jnp.max(kept, axis=2, keepdims=True))
            else:
                slope = mask[None] * (1.0 + scores)
                kept_at(kind, (steps + step) * 8 + t)[:, cols] = slope.astype(BF).reshape(2 * ROWS, span)
                raised = 0.5 * (mask[None] + slope * slope)
            raised = raised.astype(BF).reshape(2 * ROWS, span)
            kept_at(kind, step * 8 + t)[:, cols] = raised
            summed = dot(raised, jnp.concatenate([values, jnp.ones((span, 128), BF)], axis=1))
            inverse = 1.0 / summed[:, 128:]
            sides = [lanes_of_value(half) for half in range(2)]
            mid_v[rows, block_of(t)] = merge(sides, summed[:, :128] * inverse).astype(BF)
            inverse_v[rows, block_of(t)] = merge(sides, inverse)
            return carry

        lax.fori_loop(0, 8, block, 0, unroll=UNROLL)

    def attend_project(kind, rows):
        return dot(mid_v[rows, pl.ds(0, D)], tall_v[pl.ds(0, D), :]) * out_scale(kind)

    def attend_unhidden(kind, micro, part, here, rows):
        width = low_width(kind)
        span = ROWS * (part + 1)
        keys_at = pl.ds(pl.multiple_of(micro * LEN, LEN), span)
        own = pl.ds(0, span)
        step = micro * CHUNKS_OF + part
        d_mixed = dot(g_v[here, :], tall_t[:, pl.ds(0, D)]) * out_scale(kind)
        dy_v[...] = (d_mixed * inverse_v[rows, :]).astype(BF)
        if part == CHUNKS_OF - 1:
            dk_v[...] = jnp.zeros_like(dk_v)
            dv_v[...] = jnp.zeros_like(dv_v)
        if kind == LINEAR:
            dq_v[...] = jnp.zeros_like(dq_v)

        def block(t, carry):
            index = query_index(kind, t)
            queries = first_v[rows, block_of(index)]
            keys = first_v[keys_at, block_of(index, width)]
            values = second_v[keys_at, block_of(t)]
            heads = [lanes_of_head(kind, t, half) for half in range(2)]
            sides = [lanes_of_value(half) for half in range(2)]
            d_mixed = both(sides, dy_v[:, block_of(t)])
            mixed = mid_v[rows, block_of(t)].astype(F32)
            shift = jnp.sum(d_mixed.astype(F32) * jnp.concatenate([mixed, mixed], axis=0), axis=1, keepdims=True)
            d_weights = dot_t(d_mixed, values) - shift
            raised = kept_at(kind, step * 8 + t)[:, own]
            slope = raised if kind == WINDOW else kept_at(kind, (steps + step) * 8 + t)[:, own]
            d_scores = (slope.astype(F32) * d_weights).astype(BF)
            dv_v[own, block_of(t)] += dot_0(raised, d_mixed)
            d_queries = merge(heads, dot(d_scores, keys)) * root_of(kind)
            dk_v[own, block_of(index)] += dot_0(d_scores, both(heads, queries)) * root_of(kind)
            if kind == WINDOW:
                dq_v[:, block_of(t)] = d_queries
            else:
                dq_v[:, block_of(index)] += d_queries
            return carry

        lax.fori_loop(0, 8, block, 0, unroll=UNROLL)
        done = pl.ds(part * ROWS, ROWS)
        first_v[rows, pl.ds(0, width)] = dq_v[:, pl.ds(0, width)].astype(BF)
        first_v[rows, pl.ds(width, width)] = dk_v[done, pl.ds(0, width)].astype(BF)
        second_v[rows, pl.ds(0, D)] = dv_v[done, :].astype(BF)

    def attend_back(kind, rows):
        width = low_width(kind)
        total = dot(first_v[rows, pl.ds(0, 2 * width)], wide_t[0, pl.ds(0, 2 * width), :])
        total += dot(second_v[rows, pl.ds(0, D)], wide_t[1, pl.ds(0, D), :])
        return total

    @pl.when(section == last)
    def _():
        turn_weights(FP, FP)

    @pl.when(section == WINDOW)
    def _():
        turn_weights(2 * D, D)

    def one_phase(phase, carry):
        own = phase == 0

        @pl.when(is_feed(section))
        def _():
            turns = jnp.where(own & (section == last), MICRO, 1)
            span = steps // turns

            def backward(step):
                micro, part = step // CHUNKS_OF, CHUNKS_OF - 1 - lax.rem(step, CHUNKS_OF)
                backward_step(phase, micro * CHUNKS_OF + part, feed_unhidden, feed_back)

            def turn(index):
                here = (index * span, index * span + span)
                each(*here, lambda step: forward_step(phase, step, feed_hidden, feed_project))

                @pl.when(own & (section < last))
                def _():
                    turn_weights(FP, FP)

                each(*here, backward)

            each(0, turns, turn)

        for kind in (WINDOW, LINEAR):

            @pl.when(section == kind)
            def _(kind=kind):
                def forward(micro, inner):
                    for part in range(CHUNKS_OF):
                        forward_step(
                            phase,
                            micro * CHUNKS_OF + part,
                            functools.partial(attend_hidden, kind, phase, micro, part),
                            functools.partial(attend_project, kind),
                        )
                    return inner

                lax.fori_loop(0, MICRO, forward, 0)

        for kind in (WINDOW, LINEAR):

            @pl.when(section == kind)
            def _(kind=kind):
                def backward(micro, inner):
                    for part in reversed(range(CHUNKS_OF)):
                        backward_step(
                            phase,
                            micro * CHUNKS_OF + part,
                            functools.partial(attend_unhidden, kind, micro, part),
                            functools.partial(attend_back, kind),
                        )
                    return inner

                if kind == LINEAR:
                    turn_weights(2 * low_width(kind), D)
                lax.fori_loop(0, MICRO, backward, 0)

        @pl.when(own & gives)
        def _():
            far_copy(2).start()

        def finish(step, inner):
            @pl.when(own)
            def _():
                @pl.when(section > 0)
                def _():
                    hand_back(step).wait_send()

                gradient_out(step).wait()

            for copy in forward_outs(phase, step) + backward_outs(phase, step):
                copy.wait()
            return inner

        lax.fori_loop(0, steps, finish, 0)

        @pl.when(own & takes)
        def _():
            far_copy(3).wait_recv()

        return carry

    lax.fori_loop(0, jnp.where(takes, 2, 1), one_phase, 0)
    d_gain[...] = gain_sum[...]

    @pl.when(takes)
    def _():
        far_copy(2).wait_recv()
        d_gain[...] += far_gain[...]

    @pl.when(gives)
    def _():
        for kind in range(2):
            for step in range(steps):
                far_copy(kind, step).wait_send()
        far_copy(2).wait_send()
        far_copy(3).wait_send()


UNROLL = 2


def train(tokens, cotangent, flat, lengths, swapping):
    count = MICRO * LEN
    steps = MICRO * CHUNKS_OF
    kept = 2 * count if swapping else count
    return pl.pallas_call(
        functools.partial(train_kernel, swapping),
        out_shape=(
            jax.ShapeDtypeStruct((count, D), BF),
            jax.ShapeDtypeStruct((count, D), F32),
            jax.ShapeDtypeStruct((kept, D), BF),
            jax.ShapeDtypeStruct((kept, FP), BF),
            jax.ShapeDtypeStruct((kept, FP), BF),
            jax.ShapeDtypeStruct((kept, FP), BF),
            jax.ShapeDtypeStruct((kept, D), BF),
            jax.ShapeDtypeStruct((8, D), F32),
        ),
        in_specs=[any_spec()] * 3 + [pl.BlockSpec(memory_space=pltpu.SMEM)],
        out_specs=(any_spec(),) * 7 + (vmem_spec(),),
        scratch_shapes=[
            pltpu.VMEM((2, D, FP), BF),
            pltpu.VMEM((FP, D), BF),
            pltpu.VMEM((1, D), BF),
            pltpu.VMEM((2 * MICRO, 1, LEN), F32),
            pltpu.VMEM((2 * count, D), BF),
            pltpu.VMEM((count, D), BF),
            pltpu.VMEM((count, D), BF),
            pltpu.VMEM((2 * count, D), BF),
            pltpu.VMEM((count, D), F32),
            pltpu.VMEM((count, FP), BF),
            pltpu.VMEM((count, FP), BF),
            pltpu.VMEM((count, FP), BF),
            pltpu.VMEM((ROWS, D), F32),
            pltpu.VMEM((8, D), F32),
            pltpu.VMEM((8, D), F32),
            pltpu.VMEM((2, FP, D), BF),
            pltpu.VMEM((D, FP), BF),
            pltpu.VMEM((count, D), F32),
            pltpu.VMEM((ROWS, LEN), F32),
            pltpu.VMEM((ROWS, D), BF),
            pltpu.VMEM((ROWS, D), F32),
            pltpu.VMEM((LEN, D), F32),
            pltpu.VMEM((LEN, D), F32),
            pltpu.VMEM((AHEAD, 1, PAIR_STEP), BF),
            pltpu.VMEM((PAIR_STEP // 128, 128), F32),
            pltpu.VMEM((22, 32, 128), F32),
            pltpu.SemaphoreType.DMA((AHEAD,)),
            pltpu.SemaphoreType.DMA,
            pltpu.SemaphoreType.DMA((2,)),
            pltpu.SemaphoreType.DMA((3, steps)),
            pltpu.SemaphoreType.DMA((4, steps)),
            pltpu.SemaphoreType.DMA((steps,)),
            pltpu.SemaphoreType.DMA((steps,)),
            pltpu.SemaphoreType.DMA((steps,)),
            pltpu.SemaphoreType.DMA((steps,)),
            pltpu.SemaphoreType.DMA((4, steps)),
            pltpu.SemaphoreType.DMA((4, steps)),
        ],
        compiler_params=pltpu.CompilerParams(
            collective_id=0, has_side_effects=True, vmem_limit_bytes=62 * MIB
        ),
        name="train",
    )(tokens, cotangent, flat, lengths)


HEAD_ROWS = 16
PAIRS = 64
PAIR_ROWS = PAIRS * 43
PAIR_TILES = D // 2 // PAIRS
CHUNKS = 11


class Products:
    def __init__(self, sources, scratch, base):
        self.normed, self.d_first, self.d_second, self.middle, self.grads, self.d_gain = sources
        self.left_v, self.d_v, self.woven, self.stage, self.in_sem = scratch
        self.base = base

    def fetch(self, source, target, index):
        return pltpu.make_async_copy(source, target, self.in_sem.at[index])

    def loads(self, names):
        count = self.left_v.shape[1]
        some = pl.ds(0, MICRO * LEN)
        every = pl.ds(0, count)
        low, both, high = pl.ds(0, D), pl.ds(0, 2 * D), pl.ds(D, D)
        table = {
            "h": (self.normed, self.left_v.at[0], 0),
            "g": (self.grads, self.left_v.at[1], 1),
            "first": (self.d_first, self.d_v.at[0], 2),
            "second": (self.d_second, self.d_v.at[1], 3),
            "middle": (self.middle, self.d_v.at[self.middle_slot()], 4),
        }
        for prefix, rows in (("all_", every), ("some_", some)):
            table[prefix + "h"] = (self.normed.at[rows, :], self.left_v.at[0, rows, :], 0)
            table[prefix + "mixed"] = (self.middle.at[rows, low], self.left_v.at[1, rows, :], 1)
            table[prefix + "low"] = (self.d_first.at[rows, both], self.d_v.at[0, rows, both], 2)
            table[prefix + "value"] = (self.d_second.at[rows, low], self.d_v.at[1, rows, low], 3)
            few = pl.ds(0, 2 * HEADS * FEAT)
            table["few_low"] = (self.d_first.at[some, few], self.d_v.at[0, some, few], 2)
            table[prefix + "g"] = (self.grads.at[rows, :], self.d_v.at[1, rows, high], 4)
        return [self.fetch(*table[name]) for name in names]

    def middle_slot(self):
        return 2 if self.d_v.shape[0] == 3 else 0

    def head(self, out):
        stage = self.stage
        stage[pl.ds(0, 8), :] = jnp.zeros((8, 128), F32)
        stage[pl.ds(8, 8), :] = self.d_gain[0:1, :].reshape(8, 128)
        out[pl.ds(0, 16), :] = stage[pl.ds(0, 16), :].astype(BF)

    def cut(self, out, first_row, rows, piece, scale):
        target_row = first_row - self.base

        def step(j, carry):
            source = pl.ds(pl.multiple_of(j * piece, 16), piece)
            target = pl.ds(pl.multiple_of(target_row + j * piece, 16), piece)
            out[target, :] = (self.stage[source, :] * scale).astype(BF)
            return carry

        lax.fori_loop(0, rows // piece, step, 0)

    def pairs(self, which, first_pair):
        count = PAIRS
        stage, woven = self.stage, self.woven
        half = FP // 2
        low_half = lax.broadcasted_iota(jnp.int32, (count, 128), 1) < 64
        left = self.left_v[0, :, pl.ds(pl.multiple_of(2 * first_pair, 128), 2 * count)]
        for part in range(2):
            piece = dot_0(left, self.d_v[which, :, pl.ds(part * half, half)])
            for c in range(11):
                woven[11 * part + c, pl.ds(0, 2 * count), :] = piece[:, 128 * c : 128 * c + 128]
        for c in range(22):
            stage[pl.ds(c, count, stride=43), :] = woven[c, pl.ds(0, count, stride=2), :]
        before = woven[21, pl.ds(0, count, stride=2), :]
        for c in range(22):
            here = pltpu.roll(woven[c, pl.ds(1, count, stride=2), :], 64, 1)
            stage[pl.ds(21 + c, count, stride=43), :] = jnp.where(low_half, before, here)
            before = here

    def pair_tile(self, out, k, tail_only):
        self.pairs(k // PAIR_TILES, lax.rem(k, PAIR_TILES) * PAIRS)

        @pl.when(jnp.logical_not(tail_only))
        def _():
            self.cut(out, HEAD_ROWS + k * PAIR_ROWS, PAIR_ROWS, 688, SCALE)

        @pl.when(tail_only)
        def _():
            target = pl.ds(pl.multiple_of((k + 1) * PAIR_ROWS - self.base, 16), 16)
            out[target, :] = (self.stage[pl.ds(PAIR_ROWS - 16, 16), :] * SCALE).astype(BF)

    def tall(self, out, left, right, stride, rows, first_row, scale, piece):
        product = dot_0(left, right)
        for c in range(stride):
            self.stage[pl.ds(c, rows, stride=stride), :] = product[:, 128 * c : 128 * c + 128]
        self.cut(out, first_row, rows * stride, piece, scale)

    def down_tile(self, out, j):
        left = self.d_v[self.middle_slot(), :, pl.ds(pl.multiple_of(256 * j, 256), 256)]
        self.tall(out, left, self.left_v[1], 8, 256, DOWN_ROW + 2048 * j, SCALE, 512)

    def window_tile(self, out, k):
        left = self.left_v[k // 6, :, pl.ds(pl.multiple_of(lax.rem(k, 2) * 512, 512), 512)]
        right = self.d_v[k // 4, :, pl.ds(pl.multiple_of(lax.rem(k // 2, 2) * D, D), D)]
        scale = jnp.where(k < 6, SCALE, out_scale(WINDOW))
        self.tall(out, left, right, 8, 512, HEAD_ROWS + 4096 * k, scale, 512)

    def low_tile(self, out, k):
        some = pl.ds(0, MICRO * LEN)
        width = HEADS * FEAT
        right = self.d_v[0, some, pl.ds(pl.multiple_of(k * width, width), width)]
        self.tall(out, self.left_v[0, some, :], right, 2, D, HEAD_ROWS + k * 2048, SCALE, 512)

    def value_tile(self, out, k):
        some = pl.ds(0, MICRO * LEN)
        left = self.left_v[k // 2, some, pl.ds(pl.multiple_of(lax.rem(k, 2) * 512, 512), 512)]
        right = self.d_v[1, some, pl.ds(pl.multiple_of(k // 2 * D, D), D)]
        scale = jnp.where(k < 2, SCALE, out_scale(LINEAR))
        self.tall(out, left, right, 8, 512, HEAD_ROWS + 4096 * (k + 1), scale, 512)


DOWN_ROW = HEAD_ROWS + 2 * PAIR_TILES * PAIR_ROWS
DOWN_TILES = FP // 256
WINDOW_END = HEAD_ROWS + 4 * 8192
LINEAR_END = HEAD_ROWS + 20480


def product_scratch(count, slots):
    return [
        pltpu.VMEM((2, count, D), BF),
        pltpu.VMEM((slots, count, FP), BF),
        pltpu.VMEM((22, 2 * PAIRS, 128), F32),
        pltpu.VMEM((4096, 128), F32),
        pltpu.SemaphoreType.DMA((5,)),
    ]


def clear(out, first_row, rows):
    def step(i, carry):
        out[pl.ds(pl.multiple_of(first_row + i * 128, 16), 128), :] = jnp.zeros((128, 128), BF)
        return carry

    lax.fori_loop(0, rows // 128, step, 0)
    if rows % 128:
        out[pl.ds(first_row + rows // 128 * 128, rows % 128), :] = jnp.zeros((rows % 128, 128), BF)


def products_kernel(*refs):
    section = lax.axis_index("section")
    work = Products(refs[:6], refs[8:], 0)
    out, out_v = refs[6:8]
    total = out_v.shape[0] - 512
    work.head(out_v)

    def load(*names):
        for copy in work.loads(names):
            copy.start()
        for copy in work.loads(names):
            copy.wait()

    @pl.when(is_feed(section))
    def _():
        load("h", "g", "first", "second", "middle")
        each(0, 2 * PAIR_TILES, lambda k: work.pair_tile(out_v, k, section < 0))
        each(0, DOWN_TILES, lambda j: work.down_tile(out_v, j))

    for kind in (WINDOW, LINEAR):

        @pl.when(section == kind)
        def _(kind=kind):
            load("some_h", "some_mixed", "some_low", "some_value", "some_g")
            if kind == WINDOW:
                each(0, 8, lambda k: work.window_tile(out_v, k))
            else:
                each(0, 2, lambda k: work.low_tile(out_v, k))
                each(0, 4, lambda k: work.value_tile(out_v, k))
            done = WINDOW_END if kind == WINDOW else LINEAR_END
            clear(out_v, done, total - done)

    store = pltpu.make_async_copy(out_v.at[pl.ds(0, total), :], out, work.in_sem.at[0])
    store.start()
    store.wait()


def products(sources, total_rows):
    return pl.pallas_call(
        products_kernel,
        out_shape=jax.ShapeDtypeStruct((total_rows, 128), BF),
        in_specs=[any_spec()] * 5 + [vmem_spec()],
        out_specs=any_spec(),
        scratch_shapes=[pltpu.VMEM((total_rows + 512, 128), BF)] + product_scratch(MICRO * LEN, 3),
        compiler_params=pltpu.CompilerParams(vmem_limit_bytes=60 * MIB),
        name="products",
    )(*sources)


PLACES = 4


def reduce_kernel(*refs):
    section = lax.axis_index("section")
    batch = lax.axis_index("batch")
    place, core = batch // 2, lax.rem(batch, 2)
    mate = place + 1 - 2 * lax.rem(place, 2)
    out, part, own, passing, total, flat, sems = refs[6:13]
    ex_send, ex_recv, send, recv, out_sem = sems
    width = own.shape[1]
    step_rows = width - HEAD_ROWS
    piece = width // CHUNKS
    feed_here = is_feed(section)
    base = jnp.where(feed_here, place // 2, 0) * (4 * step_rows)
    work = Products(refs[:6], refs[13:], base)
    barrier = pltpu.get_barrier_semaphore()

    def greet(other):
        pl.semaphore_signal(barrier, inc=1, device_id=(section, other), device_id_type=MESH)

    window_here = (section == WINDOW) & (place < 2)
    pair_here = feed_here | window_here
    linear_here = section == LINEAR
    sets = (
        (feed_here & (place < 2), ("h", "first")),
        (feed_here & (place == 2), ("middle", "g")),
        (feed_here & (place == 3), ("h", "second")),
        (window_here & (place == 0), ("all_h", "all_value")),
        (window_here & (place == 1), ("all_h", "all_low")),
        (linear_here, ("some_h", "few_low")),
    )
    for here, names in sets:

        @pl.when(here)
        def _(names=names):
            for copy in work.loads(names):
                copy.start()

    greet(2 * place + 1 - core)

    @pl.when(place > 0)
    def _():
        greet(batch - 2)

    @pl.when(place < PLACES - 1)
    def _():
        greet(batch + 2)

    @pl.when(base == 0)
    def _():
        work.head(part)

    pl.semaphore_wait(barrier, jnp.where((place > 0) & (place < PLACES - 1), 3, 2))
    for here, names in sets:

        @pl.when(here)
        def _(names=names):
            for copy in work.loads(names):
                copy.wait()

    late_sets = (
        (feed_here & (place < 2), ("second",)),
        (feed_here & (place == 2), ("h", "second")),
        (feed_here & (place == 3), ("middle", "g")),
        (window_here & (place == 0), ("all_mixed", "all_g", "all_low")),
        (window_here & (place == 1), ("all_value", "all_mixed", "all_g")),
        (linear_here, ("some_mixed", "some_value", "some_g")),
    )

    def late(act):
        for here, names in late_sets:

            @pl.when(here)
            def _(names=names):
                for copy in work.loads(names):
                    act(copy)

    late(lambda copy: copy.start())

    def rows_of(i):
        return pl.ds(pl.multiple_of(i * piece, 16), piece)

    def share(index, i):
        return pl.ds(pl.multiple_of(step_rows * index - base + i * piece, 16), piece)

    def swap(to, i):
        slot = lax.rem(to, 2)
        return pltpu.make_async_remote_copy(
            src_ref=part.at[share(2 * to + 1 - core, i), :],
            dst_ref=own.at[slot, rows_of(i), :],
            send_sem=ex_send.at[slot, i],
            recv_sem=ex_recv.at[slot, i],
            device_id=(section, 2 * place + 1 - core),
            device_id_type=MESH,
        )

    def go(source, slot, to, i, other):
        return pltpu.make_async_remote_copy(
            src_ref=source,
            dst_ref=passing.at[slot, rows_of(i), :],
            send_sem=send.at[lax.rem(to, 2), i],
            recv_sem=recv.at[slot, i],
            device_id=(section, other),
            device_id_type=MESH,
        )

    def arrived(slot, i):
        here = passing.at[slot, rows_of(i), :]
        pltpu.make_async_copy(here, here, recv.at[slot, i]).wait()

    def release(to, before, after, limits=(CHUNKS, CHUNKS)):
        def bound(row, parity):
            most = jnp.where(parity == 0, limits[0], limits[1])
            return jnp.minimum(jnp.maximum(row - parity * step_rows, 0) // piece, most)

        def add(i):
            slot = lax.rem(to, 2)
            rows = rows_of(i)
            swap(to, i).wait_recv()
            mine = part[share(2 * to + core, i), :].astype(F32)
            own[slot, rows, :] = (own[slot, rows, :].astype(F32) + mine).astype(BF)
            source = own.at[slot, rows, :]

            @pl.when(pair_here & (to == mate))
            def _():
                go(source, 0, to, i, 2 * mate + core).start()

            @pl.when(linear_here & (place == PLACES - 1))
            def _():
                go(source, slot, to, i, batch - 2).start()

            @pl.when(linear_here & (place == 0) & (to == 1))
            def _():
                go(source, 2, to, i, batch + 2).start()

        each(bound(before, 1 - core), bound(after, 1 - core), lambda i: swap(to, i).start())
        each(bound(before, core), bound(after, core), add)

    def swapped(to, limits=(CHUNKS, CHUNKS)):
        each(0, jnp.where(core == 0, limits[1], limits[0]), lambda i: swap(to, i).wait_send())

    def store(which):
        rows = out.shape[1] // 128
        early = (CHUNKS - 1) * piece - 32
        begin, size = ((0, early), (early, rows - early))[which]
        source = pl.ds(pl.multiple_of((8 + batch + begin) * 128, 128), size * 128)
        return pltpu.make_async_copy(
            flat.at[:, source], out.at[:, pl.ds(begin * 128, size * 128)], out_sem.at[which]
        )

    def emit(i):
        cols = pl.ds(pl.multiple_of(i * piece * 128, 1024), piece * 128)
        flat[0:1, cols] = total[...].reshape(1, piece * 128)

    whole = 2 * step_rows + HEAD_ROWS

    @pl.when(feed_here)
    def _():
        upper = place >= 2
        share_tiles = 2 * step_rows // PAIR_ROWS
        upper_tiles = 2 * PAIR_TILES - 2 * share_tiles

        def pair(t):
            turned = jnp.where(t < share_tiles, t + share_tiles, jnp.where(t == share_tiles, share_tiles - 1, t - share_tiles - 1))
            k = jnp.where(place == 0, turned, t)
            k = jnp.where(upper, jnp.where(t == upper_tiles, 2 * share_tiles - 1, 2 * share_tiles + t), k)
            tail_only = upper & (t == upper_tiles)

            @pl.when(jnp.logical_not(upper) & (k == PAIR_TILES))
            def _():
                late(lambda copy: copy.wait())

            work.pair_tile(part, k, tail_only)
            start = HEAD_ROWS + PAIR_ROWS * k - base
            stop = start + PAIR_ROWS
            ends_late = (place == 0) & (k == share_tiles - 1)
            to = base // (2 * step_rows)
            early = jnp.where(k == share_tiles - 2, whole, jnp.where(k < share_tiles - 2, stop, start))
            before_0 = jnp.where(tail_only, 0, jnp.where(upper & (k == 2 * share_tiles), piece, start))
            after_0 = jnp.where(tail_only, piece, jnp.where(place == 0, early, stop))
            release(to, before_0, after_0)
            before_1 = jnp.where(ends_late, 0, jnp.where((place == 0) & (k == share_tiles), piece, start - 2 * step_rows))
            after_1 = jnp.where(ends_late, piece, stop - 2 * step_rows)
            release(to + 1, before_1, after_1)

        def down(j):
            work.down_tile(part, j)
            start = DOWN_ROW + 2048 * j - base
            stop = start + 2048
            early = jnp.where(j == 1, whole, jnp.where(j < 1, stop, start))
            release(2, start, jnp.where(place == 2, early, stop))
            release(3, start - 2 * step_rows, stop - 2 * step_rows)

        def turn(t):
            @pl.when(t == 1)
            def _():
                @pl.when(place == 2)
                def _():
                    late(lambda copy: copy.wait())

                each(0, jnp.where(upper, upper_tiles + 1, 2 * share_tiles), pair)

                @pl.when(place == 3)
                def _():
                    late(lambda copy: copy.wait())

            mate_first = place == 2
            first = jnp.where(mate_first & (t == 0), 2, 0)
            last = jnp.where(mate_first & (t == 1), 2, DOWN_TILES)
            here = upper & (mate_first | (t == 1))
            each(first, jnp.where(here, last, first), down)

        each(0, 2, turn)
        swapped(mate)
        swapped(place)

    @pl.when(window_here)
    def _():
        def tile(t, carry):
            k = lax.rem(t + jnp.where(place == 0, 4, 0), 8)

            @pl.when(t == jnp.where(place == 0, 2, 4))
            def _():
                late(lambda copy: copy.wait())

            work.window_tile(part, k)
            start = HEAD_ROWS + 4096 * k
            stop = start + 4096

            @pl.when(k == 7)
            def _():
                clear(part, WINDOW_END, 4 * step_rows + HEAD_ROWS - WINDOW_END)

            stop_0 = jnp.where(place == 0, jnp.where(k < 3, stop, jnp.where(k == 3, whole, start)), stop)
            stop_1 = jnp.where(k == 7, whole, stop - 2 * step_rows)
            release(0, start, stop_0)
            release(1, start - 2 * step_rows, stop_1)
            return carry

        lax.fori_loop(0, 8, tile, 0)
        for to in range(2):
            swapped(to)

    @pl.when(linear_here)
    def _():
        filled = [max(0, min(CHUNKS, -(-(LINEAR_END - step_rows * index) // piece))) for index in range(4)]
        limits = (tuple(filled[:2]), tuple(filled[2:]))
        cover = max(step_rows * index + piece * filled[index] for index in range(4) if filled[index])
        clear(part, LINEAR_END, cover - LINEAR_END)

        def low(k):
            work.low_tile(part, k)
            start = HEAD_ROWS + 2048 * k
            release(0, start, start + 2048, limits[0])

        def value(k):
            work.value_tile(part, k)
            start = HEAD_ROWS + 4096 * (k + 1)
            stop = jnp.where(k == 3, cover, start + 4096)
            release(0, start, stop, limits[0])
            release(1, start - 2 * step_rows, stop - 2 * step_rows, limits[1])

        def pass_on(to, i):
            rows = rows_of(i)
            arrived(to, i)
            added = passing[to, rows, :].astype(F32) + own[to, rows, :].astype(F32)
            passing[to, rows, :] = added.astype(BF)
            go(passing.at[to, rows, :], to, to, i, batch - 2).start()

        ahead = jnp.where((place == 2) & (core == 0), 2, 0)

        def value_and_on(k):
            value(k)
            each(jnp.minimum(jnp.maximum(k - 1, 0), ahead), jnp.minimum(k, ahead), functools.partial(pass_on, 0))

        each(0, 2, low)
        late(lambda copy: copy.wait())
        each(0, 4, value_and_on)

        def own_count(to):
            return jnp.where(core == 0, limits[to][0], limits[to][1])

        @pl.when((place == 1) | (place == 2))
        def _():
            each(ahead, own_count(0), functools.partial(pass_on, 0))

        @pl.when(place == 2)
        def _():
            each(0, own_count(1), functools.partial(pass_on, 1))

        for to in range(2):
            swapped(to, limits[to])

        def sum_up(i):
            rows = rows_of(i)

            @pl.when((place == 0) & (i < own_count(0)))
            def _():
                arrived(0, i)
                total[...] = own[0, rows, :].astype(F32) + passing[0, rows, :].astype(F32)

            @pl.when((place == 1) & (i < own_count(1)))
            def _():
                arrived(1, i)
                arrived(2, i)
                both_ways = passing[1, rows, :].astype(F32) + passing[2, rows, :].astype(F32)
                total[...] = own[1, rows, :].astype(F32) + both_ways

            emit(i)

        here = jnp.where(place == 0, own_count(0), jnp.where(place == 1, own_count(1), 0))
        total[...] = jnp.zeros_like(total)
        each(here, CHUNKS, emit)
        each(0, here - 1, sum_up)

        @pl.when(here == CHUNKS)
        def _():
            store(0).start()

        each(jnp.maximum(here - 1, 0), here, sum_up)

        @pl.when(here < CHUNKS)
        def _():
            store(0).start()

        @pl.when((place == 1) | (place >= 2))
        def _():
            each(0, own_count(0), lambda i: go(passing.at[0, rows_of(i), :], 0, 0, i, batch - 2).wait_send())

        @pl.when((place == 0) | (place >= 2))
        def _():
            each(0, own_count(1), lambda i: go(passing.at[0, rows_of(i), :], 0, 1, i, batch - 2).wait_send())

    @pl.when((section == WINDOW) & (place >= 2))
    def _():
        total[...] = jnp.zeros_like(total)
        each(0, CHUNKS, emit)
        store(0).start()

    @pl.when(pair_here)
    def _():
        slot = lax.rem(place, 2)

        def sum_up(i):
            rows = rows_of(i)
            arrived(0, i)
            total[...] = own[slot, rows, :].astype(F32) + passing[0, rows, :].astype(F32)
            emit(i)

        each(0, CHUNKS - 1, sum_up)
        store(0).start()
        each(CHUNKS - 1, CHUNKS, sum_up)
        other = 2 * mate + core
        each(0, CHUNKS, lambda i: go(passing.at[0, rows_of(i), :], 0, mate, i, other).wait_send())

    store(1).start()
    store(0).wait()
    store(1).wait()


def reduce_products(sources, total_rows, batches):
    step_rows = (total_rows - 8) // batches - 1
    width = step_rows + HEAD_ROWS
    return pl.pallas_call(
        reduce_kernel,
        out_shape=jax.ShapeDtypeStruct((1, (step_rows + 1) * 128), F32),
        in_specs=[any_spec()] * 5 + [vmem_spec()],
        out_specs=any_spec(),
        scratch_shapes=[
            pltpu.VMEM((4 * step_rows + HEAD_ROWS + 512, 128), BF),
            pltpu.VMEM((2, width, 128), BF),
            pltpu.VMEM((3, width, 128), BF),
            pltpu.VMEM((width // CHUNKS, 128), F32),
            pltpu.VMEM((1, width * 128), F32),
            (
                pltpu.SemaphoreType.DMA((2, CHUNKS)),
                pltpu.SemaphoreType.DMA((2, CHUNKS)),
                pltpu.SemaphoreType.DMA((2, CHUNKS)),
                pltpu.SemaphoreType.DMA((3, CHUNKS)),
                pltpu.SemaphoreType.DMA((2,)),
            ),
        ]
        + product_scratch(2 * MICRO * LEN, 2),
        compiler_params=pltpu.CompilerParams(
            collective_id=1, has_side_effects=True, vmem_limit_bytes=60 * MIB
        ),
        name="reduce_products",
    )(*sources)


def shards(tokens, cotangent, params, lengths):
    batches = lax.axis_size("batch")
    paired = batches == 2 * PLACES
    acts, d_inputs, normed, middle, d_first, d_second, grads, d_gain = train(
        tokens, cotangent, params, lengths, paired
    )
    total_rows = params.shape[1] // 128 + 8
    sources = (normed, d_first, d_second, middle, grads, d_gain)
    if paired:
        mine = reduce_products(sources, total_rows, batches)
    else:
        parts = products(sources, total_rows)
        mine = lax.psum_scatter(parts[8:].reshape(-1), "batch", scatter_dimension=0, tiled=True)
        mine = mine.astype(F32)[None]
    return acts[None], d_inputs[None], mine


def solution(mesh):
    return jax.shard_map(
        shards,
        mesh=mesh,
        in_specs=(P("batch", None), P("batch", None), P("section", None), P("batch", None, None)),
        out_specs=(P("section", "batch", None), P("section", "batch", None), P("section", "batch")),
        check_vma=False,
    )
```

```python
import functools
import math

import jax
import jax.numpy as jnp
from jax import lax
from jax.experimental import pallas as pl
from jax.experimental.pallas import tpu as pltpu
from jax.sharding import PartitionSpec as P

D = 1024
FF = 2752
FP = 2816
HEADS = 16
FEAT = 16
WIN = 64
MICRO = 2
LEN = 256
EPSILON = 1e-06
SCALE = 1.0 / math.sqrt(D)
LINEAR, FEED, WINDOW, FEED2 = 0, 1, 2, 3
MIB = 2**20
MESH = pl.DeviceIdType.MESH
BF = jnp.bfloat16
F32 = jnp.float32


def any_spec():
    return pl.BlockSpec(memory_space=pl.ANY)


def vmem_spec():
    return pl.BlockSpec(memory_space=pltpu.VMEM)


def dot(left, right):
    return jnp.dot(left, right, preferred_element_type=F32)


def dot_t(left, right):
    return lax.dot_general(left, right, (((1,), (1,)), ((), ())), preferred_element_type=F32)


def dot_0(left, right):
    return lax.dot_general(left, right, (((0,), (0,)), ((), ())), preferred_element_type=F32)


def block256(index):
    return pl.ds(pl.multiple_of(index * 256, 256), 256)


def each(first, last, act):
    def step(i, carry):
        act(i)
        return carry

    lax.fori_loop(first, last, step, 0)


def is_feed(section):
    return (section == FEED) | (section == FEED2)


PAIR_STEP = 32 * FF
ROW_STEP = 64 * D
AHEAD = 12


def prepare(section, flat, wide_v, tall_v, chunk, blocks, woven, load_sem):
    def run(steps, count, first, work):
        def load(i):
            slot = lax.rem(i, AHEAD)
            return pltpu.make_async_copy(
                flat.at[:, pl.ds(pl.multiple_of(first + i * count, 1024), count)],
                chunk.at[slot, :, pl.ds(0, count)],
                load_sem.at[slot],
            )

        def start(i, carry):
            load(i).start()
            return carry

        lax.fori_loop(0, AHEAD, start, 0)

        def step(i, carry):
            load(i).wait()
            rows = count // 128
            blocks[pl.ds(0, rows), :] = chunk[lax.rem(i, AHEAD), :, pl.ds(0, count)].astype(F32).reshape(rows, 128)
            work(i)

            @pl.when(i + AHEAD < steps)
            def _():
                load(i + AHEAD).start()

            return carry

        lax.fori_loop(0, steps, step, 0)

    def rows_of(index, count):
        return pl.ds(pl.multiple_of(index * count, count), count)

    def pair_work(i):
        low_half = lax.broadcasted_iota(jnp.int32, (16, 128), 1) < 64
        rolled = pltpu.roll(blocks[pl.ds(21, 16, stride=43), :], 64, 1)
        for c in range(22):
            even = blocks[pl.ds(c, 16, stride=43), :]
            if c == 21:
                even = jnp.where(low_half, even, 0.0)
                odd = jnp.where(low_half, rolled, 0.0)
            else:
                after = pltpu.roll(blocks[pl.ds(22 + c, 16, stride=43), :], 64, 1)
                odd = jnp.where(low_half, rolled, after)
                rolled = after
            woven[c, pl.ds(0, 16, stride=2), :] = even
            woven[c, pl.ds(1, 16, stride=2), :] = odd
        rows = rows_of(lax.rem(i, 32), 32)
        for c in range(22):
            wide_v[i // 32, rows, pl.ds(128 * c, 128)] = woven[c].astype(BF)

    def row_work(target, rows, first_col):
        for c in range(8):
            target[rows, pl.ds(first_col + 128 * c, 128)] = blocks[pl.ds(c, 64, stride=8), :].astype(BF)

    def square(i, first, target, first_col):
        @pl.when((i >= first) & (i < first + 16))
        def _():
            row_work(target, rows_of(i - first, 64), first_col)

    @pl.when(is_feed(section))
    def _():
        run(64, PAIR_STEP, D, pair_work)
        run(43, ROW_STEP, D + 2 * D * FF, lambda i: row_work(tall_v, rows_of(i, 64), 0))
        tall_v[pl.ds(FF, FP - FF), :] = jnp.zeros((FP - FF, D), BF)

    @pl.when(section == WINDOW)
    def _():
        def work(i):
            square(i, 0, wide_v.at[0], 0)
            square(i, 16, wide_v.at[0], D)
            square(i, 32, wide_v.at[1], 0)
            square(i, 48, tall_v, 0)

        run(64, ROW_STEP, D, work)

    @pl.when(section == LINEAR)
    def _():
        def work(i):
            for part in range(2):

                @pl.when(i // 4 == part)
                def _(part=part):
                    rows = rows_of(i - 4 * part, 256)
                    for c in range(2):
                        cols = pl.ds(part * HEADS * FEAT + 128 * c, 128)
                        wide_v[0, rows, cols] = blocks[pl.ds(c, 256, stride=2), :].astype(BF)

            square(i, 8, wide_v.at[1], 0)
            square(i, 24, tall_v, 0)

        run(40, ROW_STEP, D, work)


ROWS = 128
CHUNKS_OF = LEN // ROWS


def lanes_of_head(kind, block, half):
    lanes = lax.broadcasted_iota(jnp.int32, (1, 128), 1)
    if kind == WINDOW:
        return lanes // 64 == half
    return lanes // FEAT == lax.rem(2 * block + half, 8)


def lanes_of_value(half):
    return lax.broadcasted_iota(jnp.int32, (1, 128), 1) // 64 == half


def only(mask, values):
    return jnp.where(mask, values, jnp.zeros_like(values))


def both(masks, values):
    return jnp.concatenate([only(masks[0], values), only(masks[1], values)], axis=0)


def merge(masks, stacked):
    return only(masks[0], stacked[:ROWS]) + only(masks[1], stacked[ROWS:])


def block_of(index, first=0):
    return pl.ds(pl.multiple_of(first + index * 128, 128), 128)


def query_index(kind, block):
    return block if kind == WINDOW else block // 4


def low_width(kind):
    return D if kind == WINDOW else HEADS * FEAT


def mask_of(kind, doc_col, doc_row, first_row):
    shape = (doc_col.shape[0], doc_row.shape[1])
    rows = lax.broadcasted_iota(jnp.int32, shape, 0) + first_row
    cols = lax.broadcasted_iota(jnp.int32, shape, 1)
    mask = (doc_col == doc_row) & (cols <= rows)
    if kind == WINDOW:
        mask = mask & (rows - cols < WIN)
    return mask.astype(F32)


def root_of(kind):
    return 1.0 / math.sqrt(D // HEADS if kind == WINDOW else FEAT)


def out_scale(kind):
    return {LINEAR: 8.0, WINDOW: 4.0, FEED: 1.0}[kind] * SCALE


def train_kernel(
    swapping,
    tokens, cotangent, flat, lengths,
    acts, d_inputs, normed, middle, d_first, d_second, grads, d_gain,
    wide_v, tall_v, gain_v, docs_v, z_v, h_v, x_v, g_v, dz_v, first_v, second_v, mid_v, dh_v, gain_sum, far_gain,
    wide_t, tall_t, inverse_v, mask_v, dy_v, dq_v, dk_v, dv_v, chunk, blocks, woven,
    load_sem, gain_sem, in_sem, act_sem, out_sem, on_send, on_recv, back_send, back_recv, far_send, far_recv,
):
    section = lax.axis_index("section")
    batch = lax.axis_index("batch")
    last = lax.axis_size("section") - 1
    batches = lax.axis_size("batch")
    steps = MICRO * CHUNKS_OF
    count = steps * ROWS
    barrier = pltpu.get_barrier_semaphore()

    far = lax.rem(batch + batches // 2, batches)
    nobody = section < 0
    lower = batch < batches // 2
    gives = is_feed(section) | ((section == WINDOW) & jnp.logical_not(lower)) if swapping else nobody
    takes = is_feed(section) | ((section == WINDOW) & lower) if swapping else nobody

    @pl.when(gives | takes)
    def _():
        pl.semaphore_signal(barrier, inc=1, device_id=(section, far), device_id_type=MESH)

    @pl.when(section > 0)
    def _():
        pl.semaphore_signal(barrier, inc=1, device_id=(section - 1, batch), device_id_type=MESH)

    @pl.when(section < last)
    def _():
        pl.semaphore_signal(barrier, inc=1, device_id=(section + 1, batch), device_id_type=MESH)

    gain_copy = pltpu.make_async_copy(flat.at[:, pl.ds(0, D)], gain_v, gain_sem)
    gain_copy.start()
    token_copy = pltpu.make_async_copy(tokens, z_v.at[pl.ds(0, count), :], in_sem.at[0])
    tangent_copy = pltpu.make_async_copy(cotangent, g_v.at[pl.ds(0, count), :], in_sem.at[1])

    @pl.when(section == 0)
    def _():
        token_copy.start()

    @pl.when(section == last)
    def _():
        tangent_copy.start()

    places = lax.broadcasted_iota(jnp.int32, (1, LEN), 1)
    for micro in range(MICRO):
        end = 0
        ids = jnp.zeros((1, LEN), F32)
        for document in range(lengths.shape[2]):
            end = end + lengths[0, micro, document]
            ids += (places >= end).astype(F32)
        docs_v[micro] = ids
    prepare(section, flat, wide_v, tall_v, chunk, blocks, woven, load_sem)
    gain_copy.wait()
    gain = 1.0 + gain_v[...].astype(F32) / 8.0
    gain_sum[...] = jnp.zeros_like(gain_sum)

    @pl.when(section == 0)
    def _():
        token_copy.wait()

    @pl.when(section == last)
    def _():
        tangent_copy.wait()

    greeted = jnp.where((section > 0) & (section < last), 2, 1)
    pl.semaphore_wait(barrier, greeted + jnp.where(gives | takes, 1, 0))

    def rows_at(step, phase=0):
        return pl.ds(pl.multiple_of(phase * count + step * ROWS, ROWS), ROWS)

    def hand_on(step):
        rows = rows_at(step)
        return pltpu.make_async_remote_copy(
            src_ref=x_v.at[rows, :],
            dst_ref=z_v.at[rows, :],
            send_sem=on_send.at[step],
            recv_sem=on_recv.at[step],
            device_id=(section + 1, batch),
            device_id_type=MESH,
        )

    def hand_back(step):
        rows = rows_at(step)
        return pltpu.make_async_remote_copy(
            src_ref=x_v.at[rows, :],
            dst_ref=g_v.at[rows, :],
            send_sem=back_send.at[step],
            recv_sem=back_recv.at[step],
            device_id=(section - 1, batch),
            device_id_type=MESH,
        )

    def far_copy(kind, step=0):
        rows, target = rows_at(step), rows_at(step, 1)
        source, target = (
            (z_v.at[rows, :], z_v.at[target, :]),
            (g_v.at[rows, :], g_v.at[target, :]),
            (gain_sum, far_gain),
            (docs_v.at[pl.ds(0, MICRO)], docs_v.at[pl.ds(MICRO, MICRO)]),
        )[kind]
        return pltpu.make_async_remote_copy(
            src_ref=source,
            dst_ref=target,
            send_sem=far_send.at[kind, step],
            recv_sem=far_recv.at[kind, step],
            device_id=(section, far),
            device_id_type=MESH,
        )

    @pl.when(gives)
    def _():
        far_copy(3).start()

    @pl.when(gives & (section == last))
    def _():
        for step in range(steps):
            far_copy(1, step).start()

    def act_out(step):
        rows = rows_at(step)
        return pltpu.make_async_copy(x_v.at[rows, :], acts.at[rows, :], act_sem.at[0, step])

    def forward_outs(phase, step):
        rows, target = rows_at(step), rows_at(step, phase)
        return [
            pltpu.make_async_copy(h_v.at[rows, :], normed.at[target, :], act_sem.at[1, step]),
            pltpu.make_async_copy(mid_v.at[rows, :], middle.at[target, :], act_sem.at[2, step]),
        ]

    def gradient_out(step):
        rows = rows_at(step)
        return pltpu.make_async_copy(dz_v.at[rows, :], d_inputs.at[rows, :], out_sem.at[0, step])

    def backward_outs(phase, step):
        rows, target = rows_at(step), rows_at(step, phase)
        return [
            pltpu.make_async_copy(g_v.at[target, :], grads.at[target, :], out_sem.at[1, step]),
            pltpu.make_async_copy(first_v.at[rows, :], d_first.at[target, :], out_sem.at[2, step]),
            pltpu.make_async_copy(second_v.at[rows, :], d_second.at[target, :], out_sem.at[3, step]),
        ]


    def forward_step(phase, step, hidden, project):
        rows, here = rows_at(step), rows_at(step, phase)
        own = phase == 0

        @pl.when(own & (section > 0))
        def _():
            hand_on(step).wait_recv()

        @pl.when(own & gives)
        def _():
            far_copy(0, step).start()

        @pl.when(jnp.logical_not(own))
        def _():
            far_copy(0, step).wait_recv()

        z = z_v[here, :].astype(F32)
        scaled = lax.rsqrt(jnp.mean(z * z, axis=1, keepdims=True) + EPSILON)
        h_v[rows, :] = (z * scaled * gain).astype(BF)
        hidden(rows)

        @pl.when(own)
        def _():
            x_v[rows, :] = (z_v[here, :].astype(F32) + project(rows)).astype(BF)

            @pl.when(section < last)
            def _():
                hand_on(step).start()

            act_out(step).start()

        for copy in forward_outs(phase, step):
            copy.start()

    def backward_step(phase, step, unhidden, back):
        rows, here = rows_at(step), rows_at(step, phase)
        own = phase == 0

        @pl.when(own & (section < last))
        def _():
            hand_back(step).wait_recv()

            @pl.when(gives)
            def _():
                far_copy(1, step).start()

        @pl.when(jnp.logical_not(own))
        def _():
            far_copy(1, step).wait_recv()

        unhidden(here, rows)

        @pl.when(own)
        def _():
            dh_v[...] = back(rows) * SCALE

            @pl.when(section < last)
            def _():
                hand_on(step).wait_send()

            act_out(step).wait()
            z = z_v[rows, :].astype(F32)
            scaled = lax.rsqrt(jnp.mean(z * z, axis=1, keepdims=True) + EPSILON)
            unit = z * scaled
            d_normed = dh_v[...]
            gain_sum[0:1, :] += jnp.sum(d_normed * unit, axis=0, keepdims=True) * 0.125
            d_unit = d_normed * gain
            d_z = scaled * (d_unit - unit * jnp.mean(d_unit * unit, axis=1, keepdims=True))
            d_z += g_v[rows, :].astype(F32)
            dz_v[rows, :] = d_z
            x_v[rows, :] = d_z.astype(BF)

            @pl.when(section > 0)
            def _():
                hand_back(step).start()

            gradient_out(step).start()

        for copy in backward_outs(phase, step):
            copy.start()

    def turn_weights(low, high):
        def wide_piece(which, t):
            wide_t[which, block256(t), :] = wide_v[which, :, block256(t)].T

        def tall_piece(t):
            tall_t[:, block256(t)] = tall_v[block256(t), :].T

        each(0, low // 256, functools.partial(wide_piece, 0))
        each(0, high // 256, functools.partial(wide_piece, 1))
        each(0, high // 256, tall_piece)

    def kept_at(kind, index):
        width = 2 * low_width(kind)
        room = (FP - width) // 256 * 4
        over = index >= room
        place = jnp.where(over, index - room, index)
        first = jnp.where(over, D, width) + place // 4 * 256
        rows = pl.ds(pl.multiple_of(first, 256), 256)
        return wide_t.at[jnp.where(over, 1, 0), rows, block256(lax.rem(place, 4))]

    def feed_hidden(rows):
        half = FP // 2

        for part in range(2):
            cols = pl.ds(part * half, half)
            gate = dot(h_v[rows, :], wide_v[0, :, cols]) * SCALE
            up = dot(h_v[rows, :], wide_v[1, :, cols]) * SCALE
            sig = 1.0 / (1.0 + jnp.exp(-gate))
            silu = gate * sig
            first_v[rows, cols] = (up * (sig + silu * (1.0 - sig))).astype(BF)
            second_v[rows, cols] = silu.astype(BF)
            mid_v[rows, cols] = (silu * up).astype(BF)

    def feed_project(rows):
        return dot(mid_v[rows, :], tall_v[...]) * SCALE

    def feed_unhidden(here, rows):
        half = FP // 2

        for part in range(2):
            cols = pl.ds(part * half, half)
            d_mid = dot(g_v[here, :], tall_t[:, cols]) * SCALE
            first_v[rows, cols] = (d_mid * first_v[rows, cols].astype(F32)).astype(BF)
            second_v[rows, cols] = (d_mid * second_v[rows, cols].astype(F32)).astype(BF)

    def feed_back(rows):
        return dot(first_v[rows, :], wide_t[0]) + dot(second_v[rows, :], wide_t[1])

    def attend_hidden(kind, phase, micro, part, rows):
        width = low_width(kind)
        span = ROWS * (part + 1)
        keys_at = pl.ds(pl.multiple_of(micro * LEN, LEN), span)
        step = micro * CHUNKS_OF + part
        first_v[rows, pl.ds(0, 2 * width)] = (dot(h_v[rows, :], wide_v[0, :, pl.ds(0, 2 * width)]) * SCALE).astype(BF)
        second_v[rows, pl.ds(0, D)] = (dot(h_v[rows, :], wide_v[1, :, pl.ds(0, D)]) * SCALE).astype(BF)
        cols = pl.ds(0, span)
        index = phase * MICRO + micro
        own_docs = jnp.broadcast_to(docs_v[index, :, pl.ds(part * ROWS, ROWS)], (8, ROWS))
        mask_v[:, cols] = mask_of(kind, own_docs.T[:, 0:1], docs_v[index, :, cols], part * ROWS)

        def block(t, carry):
            index = query_index(kind, t)
            queries = first_v[rows, block_of(index)]
            keys = first_v[keys_at, block_of(index, width)]
            values = second_v[keys_at, block_of(t)]
            heads = [lanes_of_head(kind, t, half) for half in range(2)]
            scores = (dot_t(both(heads, queries), keys) * root_of(kind)).reshape(2, ROWS, span)
            mask = mask_v[:, cols]
            if kind == WINDOW:
                kept = jnp.where((mask > 0.0)[None], scores, -1e30)
                raised = jnp.exp(kept - jnp.max(kept, axis=2, keepdims=True))
            else:
                slope = mask[None] * (1.0 + scores)
                kept_at(kind, (steps + step) * 8 + t)[:, cols] = slope.astype(BF).reshape(2 * ROWS, span)
                raised = 0.5 * (mask[None] + slope * slope)
            raised = raised.astype(BF).reshape(2 * ROWS, span)
            kept_at(kind, step * 8 + t)[:, cols] = raised
            summed = dot(raised, jnp.concatenate([values, jnp.ones((span, 128), BF)], axis=1))
            inverse = 1.0 / summed[:, 128:]
            sides = [lanes_of_value(half) for half in range(2)]
            mid_v[rows, block_of(t)] = merge(sides, summed[:, :128] * inverse).astype(BF)
            inverse_v[rows, block_of(t)] = merge(sides, inverse)
            return carry

        lax.fori_loop(0, 8, block, 0, unroll=UNROLL)

    def attend_project(kind, rows):
        return dot(mid_v[rows, pl.ds(0, D)], tall_v[pl.ds(0, D), :]) * out_scale(kind)

    def attend_unhidden(kind, micro, part, here, rows):
        width = low_width(kind)
        span = ROWS * (part + 1)
        keys_at = pl.ds(pl.multiple_of(micro * LEN, LEN), span)
        own = pl.ds(0, span)
        step = micro * CHUNKS_OF + part
        d_mixed = dot(g_v[here, :], tall_t[:, pl.ds(0, D)]) * out_scale(kind)
        dy_v[...] = (d_mixed * inverse_v[rows, :]).astype(BF)
        if part == CHUNKS_OF - 1:
            dk_v[...] = jnp.zeros_like(dk_v)
            dv_v[...] = jnp.zeros_like(dv_v)
        if kind == LINEAR:
            dq_v[...] = jnp.zeros_like(dq_v)

        def block(t, carry):
            index = query_index(kind, t)
            queries = first_v[rows, block_of(index)]
            keys = first_v[keys_at, block_of(index, width)]
            values = second_v[keys_at, block_of(t)]
            heads = [lanes_of_head(kind, t, half) for half in range(2)]
            sides = [lanes_of_value(half) for half in range(2)]
            d_mixed = both(sides, dy_v[:, block_of(t)])
            mixed = mid_v[rows, block_of(t)].astype(F32)
            shift = jnp.sum(d_mixed.astype(F32) * jnp.concatenate([mixed, mixed], axis=0), axis=1, keepdims=True)
            d_weights = dot_t(d_mixed, values) - shift
            raised = kept_at(kind, step * 8 + t)[:, own]
            slope = raised if kind == WINDOW else kept_at(kind, (steps + step) * 8 + t)[:, own]
            d_scores = (slope.astype(F32) * d_weights).astype(BF)
            dv_v[own, block_of(t)] += dot_0(raised, d_mixed)
            d_queries = merge(heads, dot(d_scores, keys)) * root_of(kind)
            dk_v[own, block_of(index)] += dot_0(d_scores, both(heads, queries)) * root_of(kind)
            if kind == WINDOW:
                dq_v[:, block_of(t)] = d_queries
            else:
                dq_v[:, block_of(index)] += d_queries
            return carry

        lax.fori_loop(0, 8, block, 0, unroll=UNROLL)
        done = pl.ds(part * ROWS, ROWS)
        first_v[rows, pl.ds(0, width)] = dq_v[:, pl.ds(0, width)].astype(BF)
        first_v[rows, pl.ds(width, width)] = dk_v[done, pl.ds(0, width)].astype(BF)
        second_v[rows, pl.ds(0, D)] = dv_v[done, :].astype(BF)

    def attend_back(kind, rows):
        width = low_width(kind)
        total = dot(first_v[rows, pl.ds(0, 2 * width)], wide_t[0, pl.ds(0, 2 * width), :])
        total += dot(second_v[rows, pl.ds(0, D)], wide_t[1, pl.ds(0, D), :])
        return total

    @pl.when(section == last)
    def _():
        turn_weights(FP, FP)

    @pl.when(section == WINDOW)
    def _():
        turn_weights(2 * D, D)

    def one_phase(phase, carry):
        own = phase == 0

        @pl.when(is_feed(section))
        def _():
            turns = jnp.where(own & (section == last), MICRO, 1)
            span = steps // turns

            def backward(step):
                micro, part = step // CHUNKS_OF, CHUNKS_OF - 1 - lax.rem(step, CHUNKS_OF)
                backward_step(phase, micro * CHUNKS_OF + part, feed_unhidden, feed_back)

            def turn(index):
                here = (index * span, index * span + span)
                each(*here, lambda step: forward_step(phase, step, feed_hidden, feed_project))

                @pl.when(own & (section < last))
                def _():
                    turn_weights(FP, FP)

                each(*here, backward)

            each(0, turns, turn)

        for kind in (WINDOW, LINEAR):

            @pl.when(section == kind)
            def _(kind=kind):
                def forward(micro, inner):
                    for part in range(CHUNKS_OF):
                        forward_step(
                            phase,
                            micro * CHUNKS_OF + part,
                            functools.partial(attend_hidden, kind, phase, micro, part),
                            functools.partial(attend_project, kind),
                        )
                    return inner

                lax.fori_loop(0, MICRO, forward, 0)

        for kind in (WINDOW, LINEAR):

            @pl.when(section == kind)
            def _(kind=kind):
                def backward(micro, inner):
                    for part in reversed(range(CHUNKS_OF)):
                        backward_step(
                            phase,
                            micro * CHUNKS_OF + part,
                            functools.partial(attend_unhidden, kind, micro, part),
                            functools.partial(attend_back, kind),
                        )
                    return inner

                if kind == LINEAR:
                    turn_weights(2 * low_width(kind), D)
                lax.fori_loop(0, MICRO, backward, 0)

        @pl.when(own & gives)
        def _():
            far_copy(2).start()

        def finish(step, inner):
            @pl.when(own)
            def _():
                @pl.when(section > 0)
                def _():
                    hand_back(step).wait_send()

                gradient_out(step).wait()

            for copy in forward_outs(phase, step) + backward_outs(phase, step):
                copy.wait()
            return inner

        lax.fori_loop(0, steps, finish, 0)

        @pl.when(own & takes)
        def _():
            far_copy(3).wait_recv()

        return carry

    lax.fori_loop(0, jnp.where(takes, 2, 1), one_phase, 0)
    d_gain[...] = gain_sum[...]

    @pl.when(takes)
    def _():
        far_copy(2).wait_recv()
        d_gain[...] += far_gain[...]

    @pl.when(gives)
    def _():
        for kind in range(2):
            for step in range(steps):
                far_copy(kind, step).wait_send()
        far_copy(2).wait_send()
        far_copy(3).wait_send()


UNROLL = 4


def train(tokens, cotangent, flat, lengths, swapping):
    count = MICRO * LEN
    steps = MICRO * CHUNKS_OF
    kept = 2 * count if swapping else count
    return pl.pallas_call(
        functools.partial(train_kernel, swapping),
        out_shape=(
            jax.ShapeDtypeStruct((count, D), BF),
            jax.ShapeDtypeStruct((count, D), F32),
            jax.ShapeDtypeStruct((kept, D), BF),
            jax.ShapeDtypeStruct((kept, FP), BF),
            jax.ShapeDtypeStruct((kept, FP), BF),
            jax.ShapeDtypeStruct((kept, FP), BF),
            jax.ShapeDtypeStruct((kept, D), BF),
            jax.ShapeDtypeStruct((8, D), F32),
        ),
        in_specs=[any_spec()] * 3 + [pl.BlockSpec(memory_space=pltpu.SMEM)],
        out_specs=(any_spec(),) * 7 + (vmem_spec(),),
        scratch_shapes=[
            pltpu.VMEM((2, D, FP), BF),
            pltpu.VMEM((FP, D), BF),
            pltpu.VMEM((1, D), BF),
            pltpu.VMEM((2 * MICRO, 1, LEN), F32),
            pltpu.VMEM((2 * count, D), BF),
            pltpu.VMEM((count, D), BF),
            pltpu.VMEM((count, D), BF),
            pltpu.VMEM((2 * count, D), BF),
            pltpu.VMEM((count, D), F32),
            pltpu.VMEM((count, FP), BF),
            pltpu.VMEM((count, FP), BF),
            pltpu.VMEM((count, FP), BF),
            pltpu.VMEM((ROWS, D), F32),
            pltpu.VMEM((8, D), F32),
            pltpu.VMEM((8, D), F32),
            pltpu.VMEM((2, FP, D), BF),
            pltpu.VMEM((D, FP), BF),
            pltpu.VMEM((count, D), F32),
            pltpu.VMEM((ROWS, LEN), F32),
            pltpu.VMEM((ROWS, D), BF),
            pltpu.VMEM((ROWS, D), F32),
            pltpu.VMEM((LEN, D), F32),
            pltpu.VMEM((LEN, D), F32),
            pltpu.VMEM((AHEAD, 1, PAIR_STEP), BF),
            pltpu.VMEM((PAIR_STEP // 128, 128), F32),
            pltpu.VMEM((22, 32, 128), F32),
            pltpu.SemaphoreType.DMA((AHEAD,)),
            pltpu.SemaphoreType.DMA,
            pltpu.SemaphoreType.DMA((2,)),
            pltpu.SemaphoreType.DMA((3, steps)),
            pltpu.SemaphoreType.DMA((4, steps)),
            pltpu.SemaphoreType.DMA((steps,)),
            pltpu.SemaphoreType.DMA((steps,)),
            pltpu.SemaphoreType.DMA((steps,)),
            pltpu.SemaphoreType.DMA((steps,)),
            pltpu.SemaphoreType.DMA((4, steps)),
            pltpu.SemaphoreType.DMA((4, steps)),
        ],
        compiler_params=pltpu.CompilerParams(
            collective_id=0, has_side_effects=True, vmem_limit_bytes=62 * MIB
        ),
        name="train",
    )(tokens, cotangent, flat, lengths)


HEAD_ROWS = 16
PAIRS = 64
PAIR_ROWS = PAIRS * 43
PAIR_TILES = D // 2 // PAIRS
CHUNKS = 11


class Products:
    def __init__(self, sources, scratch, base):
        self.normed, self.d_first, self.d_second, self.middle, self.grads, self.d_gain = sources
        self.left_v, self.d_v, self.woven, self.stage, self.in_sem = scratch
        self.base = base

    def fetch(self, source, target, index):
        return pltpu.make_async_copy(source, target, self.in_sem.at[index])

    def loads(self, names):
        count = self.left_v.shape[1]
        some = pl.ds(0, MICRO * LEN)
        every = pl.ds(0, count)
        low, both, high = pl.ds(0, D), pl.ds(0, 2 * D), pl.ds(D, D)
        table = {
            "h": (self.normed, self.left_v.at[0], 0),
            "g": (self.grads, self.left_v.at[1], 1),
            "first": (self.d_first, self.d_v.at[0], 2),
            "second": (self.d_second, self.d_v.at[1], 3),
            "middle": (self.middle, self.d_v.at[self.middle_slot()], 4),
        }
        for prefix, rows in (("all_", every), ("some_", some)):
            table[prefix + "h"] = (self.normed.at[rows, :], self.left_v.at[0, rows, :], 0)
            table[prefix + "mixed"] = (self.middle.at[rows, low], self.left_v.at[1, rows, :], 1)
            table[prefix + "low"] = (self.d_first.at[rows, both], self.d_v.at[0, rows, both], 2)
            table[prefix + "value"] = (self.d_second.at[rows, low], self.d_v.at[1, rows, low], 3)
            few = pl.ds(0, 2 * HEADS * FEAT)
            table["few_low"] = (self.d_first.at[some, few], self.d_v.at[0, some, few], 2)
            table[prefix + "g"] = (self.grads.at[rows, :], self.d_v.at[1, rows, high], 4)
        return [self.fetch(*table[name]) for name in names]

    def middle_slot(self):
        return 2 if self.d_v.shape[0] == 3 else 0

    def head(self, out):
        stage = self.stage
        stage[pl.ds(0, 8), :] = jnp.zeros((8, 128), F32)
        stage[pl.ds(8, 8), :] = self.d_gain[0:1, :].reshape(8, 128)
        out[pl.ds(0, 16), :] = stage[pl.ds(0, 16), :].astype(BF)

    def cut(self, out, first_row, rows, piece, scale):
        target_row = first_row - self.base

        def step(j, carry):
            source = pl.ds(pl.multiple_of(j * piece, 16), piece)
            target = pl.ds(pl.multiple_of(target_row + j * piece, 16), piece)
            out[target, :] = (self.stage[source, :] * scale).astype(BF)
            return carry

        lax.fori_loop(0, rows // piece, step, 0)

    def pairs(self, which, first_pair):
        count = PAIRS
        stage, woven = self.stage, self.woven
        half = FP // 2
        low_half = lax.broadcasted_iota(jnp.int32, (count, 128), 1) < 64
        left = self.left_v[0, :, pl.ds(pl.multiple_of(2 * first_pair, 128), 2 * count)]
        for part in range(2):
            piece = dot_0(left, self.d_v[which, :, pl.ds(part * half, half)])
            for c in range(11):
                woven[11 * part + c, pl.ds(0, 2 * count), :] = piece[:, 128 * c : 128 * c + 128]
        for c in range(22):
            stage[pl.ds(c, count, stride=43), :] = woven[c, pl.ds(0, count, stride=2), :]
        before = woven[21, pl.ds(0, count, stride=2), :]
        for c in range(22):
            here = pltpu.roll(woven[c, pl.ds(1, count, stride=2), :], 64, 1)
            stage[pl.ds(21 + c, count, stride=43), :] = jnp.where(low_half, before, here)
            before = here

    def pair_tile(self, out, k, tail_only):
        self.pairs(k // PAIR_TILES, lax.rem(k, PAIR_TILES) * PAIRS)

        @pl.when(jnp.logical_not(tail_only))
        def _():
            self.cut(out, HEAD_ROWS + k * PAIR_ROWS, PAIR_ROWS, 688, SCALE)

        @pl.when(tail_only)
        def _():
            target = pl.ds(pl.multiple_of((k + 1) * PAIR_ROWS - self.base, 16), 16)
            out[target, :] = (self.stage[pl.ds(PAIR_ROWS - 16, 16), :] * SCALE).astype(BF)

    def tall(self, out, left, right, stride, rows, first_row, scale, piece):
        product = dot_0(left, right)
        for c in range(stride):
            self.stage[pl.ds(c, rows, stride=stride), :] = product[:, 128 * c : 128 * c + 128]
        self.cut(out, first_row, rows * stride, piece, scale)

    def down_tile(self, out, j):
        left = self.d_v[self.middle_slot(), :, pl.ds(pl.multiple_of(256 * j, 256), 256)]
        self.tall(out, left, self.left_v[1], 8, 256, DOWN_ROW + 2048 * j, SCALE, 512)

    def window_tile(self, out, k):
        which = k // 4
        left = self.left_v[which // 3, :, block256(lax.rem(k, 4))]
        right = self.d_v[which // 2, :, pl.ds(pl.multiple_of(lax.rem(which, 2) * D, D), D)]
        scale = jnp.where(which < 3, SCALE, out_scale(WINDOW))
        self.tall(out, left, right, 8, 256, HEAD_ROWS + 2048 * k, scale, 512)

    def low_tile(self, out, k):
        some = pl.ds(0, MICRO * LEN)
        width = HEADS * FEAT
        right = self.d_v[0, some, pl.ds(pl.multiple_of(k * width, width), width)]
        self.tall(out, self.left_v[0, some, :], right, 2, D, HEAD_ROWS + k * 2048, SCALE, 512)

    def value_tile(self, out, k):
        some = pl.ds(0, MICRO * LEN)
        left = self.left_v[k // 2, some, pl.ds(pl.multiple_of(lax.rem(k, 2) * 512, 512), 512)]
        right = self.d_v[1, some, pl.ds(pl.multiple_of(k // 2 * D, D), D)]
        scale = jnp.where(k < 2, SCALE, out_scale(LINEAR))
        self.tall(out, left, right, 8, 512, HEAD_ROWS + 4096 * (k + 1), scale, 512)


DOWN_ROW = HEAD_ROWS + 2 * PAIR_TILES * PAIR_ROWS
DOWN_TILES = FP // 256
WINDOW_END = HEAD_ROWS + 4 * 8192
LINEAR_END = HEAD_ROWS + 20480


def product_scratch(count, slots):
    return [
        pltpu.VMEM((2, count, D), BF),
        pltpu.VMEM((slots, count, FP), BF),
        pltpu.VMEM((22, 2 * PAIRS, 128), F32),
        pltpu.VMEM((4096, 128), F32),
        pltpu.SemaphoreType.DMA((5,)),
    ]


def clear(out, first_row, rows):
    def step(i, carry):
        out[pl.ds(pl.multiple_of(first_row + i * 128, 16), 128), :] = jnp.zeros((128, 128), BF)
        return carry

    lax.fori_loop(0, rows // 128, step, 0)
    if rows % 128:
        out[pl.ds(first_row + rows // 128 * 128, rows % 128), :] = jnp.zeros((rows % 128, 128), BF)


def products_kernel(*refs):
    section = lax.axis_index("section")
    work = Products(refs[:6], refs[8:], 0)
    out, out_v = refs[6:8]
    total = out_v.shape[0] - 512
    work.head(out_v)

    def load(*names):
        for copy in work.loads(names):
            copy.start()
        for copy in work.loads(names):
            copy.wait()

    @pl.when(is_feed(section))
    def _():
        load("h", "g", "first", "second", "middle")
        each(0, 2 * PAIR_TILES, lambda k: work.pair_tile(out_v, k, section < 0))
        each(0, DOWN_TILES, lambda j: work.down_tile(out_v, j))

    for kind in (WINDOW, LINEAR):

        @pl.when(section == kind)
        def _(kind=kind):
            load("some_h", "some_mixed", "some_low", "some_value", "some_g")
            if kind == WINDOW:
                each(0, 16, lambda k: work.window_tile(out_v, k))
            else:
                each(0, 2, lambda k: work.low_tile(out_v, k))
                each(0, 4, lambda k: work.value_tile(out_v, k))
            done = WINDOW_END if kind == WINDOW else LINEAR_END
            clear(out_v, done, total - done)

    store = pltpu.make_async_copy(out_v.at[pl.ds(0, total), :], out, work.in_sem.at[0])
    store.start()
    store.wait()


def products(sources, total_rows):
    return pl.pallas_call(
        products_kernel,
        out_shape=jax.ShapeDtypeStruct((total_rows, 128), BF),
        in_specs=[any_spec()] * 5 + [vmem_spec()],
        out_specs=any_spec(),
        scratch_shapes=[pltpu.VMEM((total_rows + 512, 128), BF)] + product_scratch(MICRO * LEN, 3),
        compiler_params=pltpu.CompilerParams(vmem_limit_bytes=60 * MIB),
        name="products",
    )(*sources)


PLACES = 4


def reduce_kernel(*refs):
    section = lax.axis_index("section")
    batch = lax.axis_index("batch")
    place, core = batch // 2, lax.rem(batch, 2)
    mate = place + 1 - 2 * lax.rem(place, 2)
    out, part, own, passing, total, flat, sems = refs[6:13]
    ex_send, ex_recv, send, recv, out_sem = sems
    width = own.shape[1]
    step_rows = width - HEAD_ROWS
    piece = width // CHUNKS
    feed_here = is_feed(section)
    base = jnp.where(feed_here, place // 2, 0) * (4 * step_rows)
    work = Products(refs[:6], refs[13:], base)
    barrier = pltpu.get_barrier_semaphore()

    def greet(other):
        pl.semaphore_signal(barrier, inc=1, device_id=(section, other), device_id_type=MESH)

    window_here = (section == WINDOW) & (place < 2)
    pair_here = feed_here | window_here
    linear_here = section == LINEAR
    sets = (
        (feed_here & (place < 2), ("h", "first")),
        (feed_here & (place == 2), ("middle", "g")),
        (feed_here & (place == 3), ("h", "second")),
        (window_here & (place == 0), ("all_h", "all_value")),
        (window_here & (place == 1), ("all_h", "all_low")),
        (linear_here, ("some_h", "few_low")),
    )
    for here, names in sets:

        @pl.when(here)
        def _(names=names):
            for copy in work.loads(names):
                copy.start()

    greet(2 * place + 1 - core)

    @pl.when(place > 0)
    def _():
        greet(batch - 2)

    @pl.when(place < PLACES - 1)
    def _():
        greet(batch + 2)

    @pl.when(base == 0)
    def _():
        work.head(part)

    pl.semaphore_wait(barrier, jnp.where((place > 0) & (place < PLACES - 1), 3, 2))
    for here, names in sets:

        @pl.when(here)
        def _(names=names):
            for copy in work.loads(names):
                copy.wait()

    late_sets = (
        (feed_here & (place < 2), ("second",)),
        (feed_here & (place == 2), ("h", "second")),
        (feed_here & (place == 3), ("middle", "g")),
        (window_here & (place == 0), ("all_mixed", "all_g", "all_low")),
        (window_here & (place == 1), ("all_value", "all_mixed", "all_g")),
        (linear_here, ("some_mixed", "some_value", "some_g")),
    )

    def late(act):
        for here, names in late_sets:

            @pl.when(here)
            def _(names=names):
                for copy in work.loads(names):
                    act(copy)

    late(lambda copy: copy.start())

    def rows_of(i):
        return pl.ds(pl.multiple_of(i * piece, 16), piece)

    def share(index, i):
        return pl.ds(pl.multiple_of(step_rows * index - base + i * piece, 16), piece)

    def swap(to, i):
        slot = lax.rem(to, 2)
        return pltpu.make_async_remote_copy(
            src_ref=part.at[share(2 * to + 1 - core, i), :],
            dst_ref=own.at[slot, rows_of(i), :],
            send_sem=ex_send.at[slot, i],
            recv_sem=ex_recv.at[slot, i],
            device_id=(section, 2 * place + 1 - core),
            device_id_type=MESH,
        )

    def go(source, slot, to, i, other):
        return pltpu.make_async_remote_copy(
            src_ref=source,
            dst_ref=passing.at[slot, rows_of(i), :],
            send_sem=send.at[lax.rem(to, 2), i],
            recv_sem=recv.at[slot, i],
            device_id=(section, other),
            device_id_type=MESH,
        )

    def arrived(slot, i):
        here = passing.at[slot, rows_of(i), :]
        pltpu.make_async_copy(here, here, recv.at[slot, i]).wait()

    def release(to, before, after, limits=(CHUNKS, CHUNKS)):
        def bound(row, parity):
            most = jnp.where(parity == 0, limits[0], limits[1])
            return jnp.minimum(jnp.maximum(row - parity * step_rows, 0) // piece, most)

        def add(i):
            slot = lax.rem(to, 2)
            rows = rows_of(i)
            swap(to, i).wait_recv()
            mine = part[share(2 * to + core, i), :].astype(F32)
            own[slot, rows, :] = (own[slot, rows, :].astype(F32) + mine).astype(BF)
            source = own.at[slot, rows, :]

            @pl.when(pair_here & (to == mate))
            def _():
                go(source, 0, to, i, 2 * mate + core).start()

            @pl.when(linear_here & (place == PLACES - 1))
            def _():
                go(source, slot, to, i, batch - 2).start()

            @pl.when(linear_here & (place == 0) & (to == 1))
            def _():
                go(source, 2, to, i, batch + 2).start()

        each(bound(before, 1 - core), bound(after, 1 - core), lambda i: swap(to, i).start())
        each(bound(before, core), bound(after, core), add)

    def swapped(to, limits=(CHUNKS, CHUNKS)):
        each(0, jnp.where(core == 0, limits[1], limits[0]), lambda i: swap(to, i).wait_send())

    def store(which):
        rows = out.shape[1] // 128
        early = (CHUNKS - 1) * piece - 32
        begin, size = ((0, early), (early, rows - early))[which]
        source = pl.ds(pl.multiple_of((8 + batch + begin) * 128, 128), size * 128)
        return pltpu.make_async_copy(
            flat.at[:, source], out.at[:, pl.ds(begin * 128, size * 128)], out_sem.at[which]
        )

    def emit(i):
        cols = pl.ds(pl.multiple_of(i * piece * 128, 1024), piece * 128)
        flat[0:1, cols] = total[...].reshape(1, piece * 128)

    whole = 2 * step_rows + HEAD_ROWS

    @pl.when(feed_here)
    def _():
        upper = place >= 2
        share_tiles = 2 * step_rows // PAIR_ROWS
        upper_tiles = 2 * PAIR_TILES - 2 * share_tiles

        def pair(t):
            turned = jnp.where(t < share_tiles, t + share_tiles, jnp.where(t == share_tiles, share_tiles - 1, t - share_tiles - 1))
            k = jnp.where(place == 0, turned, t)
            k = jnp.where(upper, jnp.where(t == upper_tiles, 2 * share_tiles - 1, 2 * share_tiles + t), k)
            tail_only = upper & (t == upper_tiles)

            @pl.when(jnp.logical_not(upper) & (k == PAIR_TILES))
            def _():
                late(lambda copy: copy.wait())

            work.pair_tile(part, k, tail_only)
            start = HEAD_ROWS + PAIR_ROWS * k - base
            stop = start + PAIR_ROWS
            ends_late = (place == 0) & (k == share_tiles - 1)
            to = base // (2 * step_rows)
            early = jnp.where(k == share_tiles - 2, whole, jnp.where(k < share_tiles - 2, stop, start))
            before_0 = jnp.where(tail_only, 0, jnp.where(upper & (k == 2 * share_tiles), piece, start))
            after_0 = jnp.where(tail_only, piece, jnp.where(place == 0, early, stop))
            release(to, before_0, after_0)
            before_1 = jnp.where(ends_late, 0, jnp.where((place == 0) & (k == share_tiles), piece, start - 2 * step_rows))
            after_1 = jnp.where(ends_late, piece, stop - 2 * step_rows)
            release(to + 1, before_1, after_1)

        def down(j):
            work.down_tile(part, j)
            start = DOWN_ROW + 2048 * j - base
            stop = start + 2048
            early = jnp.where(j == 1, whole, jnp.where(j < 1, stop, start))
            release(2, start, jnp.where(place == 2, early, stop))
            release(3, start - 2 * step_rows, stop - 2 * step_rows)

        def turn(t):
            @pl.when(t == 1)
            def _():
                @pl.when(place == 2)
                def _():
                    late(lambda copy: copy.wait())

                each(0, jnp.where(upper, upper_tiles + 1, 2 * share_tiles), pair)

                @pl.when(place == 3)
                def _():
                    late(lambda copy: copy.wait())

            mate_first = place == 2
            first = jnp.where(mate_first & (t == 0), 2, 0)
            last = jnp.where(mate_first & (t == 1), 2, DOWN_TILES)
            here = upper & (mate_first | (t == 1))
            each(first, jnp.where(here, last, first), down)

        each(0, 2, turn)
        swapped(mate)
        swapped(place)

    @pl.when(window_here)
    def _():
        def tile(t, carry):
            k = lax.rem(t + jnp.where(place == 0, 8, 0), 16)

            @pl.when(t == jnp.where(place == 0, 4, 8))
            def _():
                late(lambda copy: copy.wait())

            work.window_tile(part, k)
            start = HEAD_ROWS + 2048 * k
            stop = start + 2048

            @pl.when(k == 15)
            def _():
                clear(part, WINDOW_END, 4 * step_rows + HEAD_ROWS - WINDOW_END)

            stop_0 = jnp.where(place == 0, jnp.where(k < 7, stop, jnp.where(k == 7, whole, start)), stop)
            stop_1 = jnp.where(k == 15, whole, stop - 2 * step_rows)
            release(0, start, stop_0)
            release(1, start - 2 * step_rows, stop_1)
            return carry

        lax.fori_loop(0, 16, tile, 0)
        for to in range(2):
            swapped(to)

    @pl.when(linear_here)
    def _():
        filled = [max(0, min(CHUNKS, -(-(LINEAR_END - step_rows * index) // piece))) for index in range(4)]
        limits = (tuple(filled[:2]), tuple(filled[2:]))
        cover = max(step_rows * index + piece * filled[index] for index in range(4) if filled[index])
        clear(part, LINEAR_END, cover - LINEAR_END)

        def low(k):
            work.low_tile(part, k)
            start = HEAD_ROWS + 2048 * k
            release(0, start, start + 2048, limits[0])

        def value(k):
            work.value_tile(part, k)
            start = HEAD_ROWS + 4096 * (k + 1)
            stop = jnp.where(k == 3, cover, start + 4096)
            release(0, start, stop, limits[0])
            release(1, start - 2 * step_rows, stop - 2 * step_rows, limits[1])

        def pass_on(to, i):
            rows = rows_of(i)
            arrived(to, i)
            added = passing[to, rows, :].astype(F32) + own[to, rows, :].astype(F32)
            passing[to, rows, :] = added.astype(BF)
            go(passing.at[to, rows, :], to, to, i, batch - 2).start()

        ahead = jnp.where((place == 2) & (core == 0), 2, 0)

        def value_and_on(k):
            value(k)
            each(jnp.minimum(jnp.maximum(k - 1, 0), ahead), jnp.minimum(k, ahead), functools.partial(pass_on, 0))

        each(0, 2, low)
        late(lambda copy: copy.wait())
        each(0, 4, value_and_on)

        def own_count(to):
            return jnp.where(core == 0, limits[to][0], limits[to][1])

        @pl.when((place == 1) | (place == 2))
        def _():
            each(ahead, own_count(0), functools.partial(pass_on, 0))

        @pl.when(place == 2)
        def _():
            each(0, own_count(1), functools.partial(pass_on, 1))

        for to in range(2):
            swapped(to, limits[to])

        def sum_up(i):
            rows = rows_of(i)

            @pl.when((place == 0) & (i < own_count(0)))
            def _():
                arrived(0, i)
                total[...] = own[0, rows, :].astype(F32) + passing[0, rows, :].astype(F32)

            @pl.when((place == 1) & (i < own_count(1)))
            def _():
                arrived(1, i)
                arrived(2, i)
                both_ways = passing[1, rows, :].astype(F32) + passing[2, rows, :].astype(F32)
                total[...] = own[1, rows, :].astype(F32) + both_ways

            emit(i)

        here = jnp.where(place == 0, own_count(0), jnp.where(place == 1, own_count(1), 0))
        total[...] = jnp.zeros_like(total)
        each(here, CHUNKS, emit)
        each(0, here - 1, sum_up)

        @pl.when(here == CHUNKS)
        def _():
            store(0).start()

        each(jnp.maximum(here - 1, 0), here, sum_up)

        @pl.when(here < CHUNKS)
        def _():
            store(0).start()

        @pl.when((place == 1) | (place >= 2))
        def _():
            each(0, own_count(0), lambda i: go(passing.at[0, rows_of(i), :], 0, 0, i, batch - 2).wait_send())

        @pl.when((place == 0) | (place >= 2))
        def _():
            each(0, own_count(1), lambda i: go(passing.at[0, rows_of(i), :], 0, 1, i, batch - 2).wait_send())

    @pl.when((section == WINDOW) & (place >= 2))
    def _():
        total[...] = jnp.zeros_like(total)
        each(0, CHUNKS, emit)
        store(0).start()

    @pl.when(pair_here)
    def _():
        slot = lax.rem(place, 2)

        def sum_up(i):
            rows = rows_of(i)
            arrived(0, i)
            total[...] = own[slot, rows, :].astype(F32) + passing[0, rows, :].astype(F32)
            emit(i)

        each(0, CHUNKS - 1, sum_up)
        store(0).start()
        each(CHUNKS - 1, CHUNKS, sum_up)
        other = 2 * mate + core
        each(0, CHUNKS, lambda i: go(passing.at[0, rows_of(i), :], 0, mate, i, other).wait_send())

    store(1).start()
    store(0).wait()
    store(1).wait()


def reduce_products(sources, total_rows, batches):
    step_rows = (total_rows - 8) // batches - 1
    width = step_rows + HEAD_ROWS
    return pl.pallas_call(
        reduce_kernel,
        out_shape=jax.ShapeDtypeStruct((1, (step_rows + 1) * 128), F32),
        in_specs=[any_spec()] * 5 + [vmem_spec()],
        out_specs=any_spec(),
        scratch_shapes=[
            pltpu.VMEM((4 * step_rows + HEAD_ROWS + 512, 128), BF),
            pltpu.VMEM((2, width, 128), BF),
            pltpu.VMEM((3, width, 128), BF),
            pltpu.VMEM((width // CHUNKS, 128), F32),
            pltpu.VMEM((1, width * 128), F32),
            (
                pltpu.SemaphoreType.DMA((2, CHUNKS)),
                pltpu.SemaphoreType.DMA((2, CHUNKS)),
                pltpu.SemaphoreType.DMA((2, CHUNKS)),
                pltpu.SemaphoreType.DMA((3, CHUNKS)),
                pltpu.SemaphoreType.DMA((2,)),
            ),
        ]
        + product_scratch(2 * MICRO * LEN, 2),
        compiler_params=pltpu.CompilerParams(
            collective_id=1, has_side_effects=True, vmem_limit_bytes=60 * MIB
        ),
        name="reduce_products",
    )(*sources)


def shards(tokens, cotangent, params, lengths):
    batches = lax.axis_size("batch")
    paired = batches == 2 * PLACES
    acts, d_inputs, normed, middle, d_first, d_second, grads, d_gain = train(
        tokens, cotangent, params, lengths, paired
    )
    total_rows = params.shape[1] // 128 + 8
    sources = (normed, d_first, d_second, middle, grads, d_gain)
    if paired:
        mine = reduce_products(sources, total_rows, batches)
    else:
        parts = products(sources, total_rows)
        mine = lax.psum_scatter(parts[8:].reshape(-1), "batch", scatter_dimension=0, tiled=True)
        mine = mine.astype(F32)[None]
    return acts[None], d_inputs[None], mine


def solution(mesh):
    return jax.shard_map(
        shards,
        mesh=mesh,
        in_specs=(P("batch", None), P("batch", None), P("section", None), P("batch", None, None)),
        out_specs=(P("section", "batch", None), P("section", "batch", None), P("section", "batch")),
        check_vma=False,
    )
```

```python
import functools
import math

import jax
import jax.numpy as jnp
from jax import lax
from jax.experimental import pallas as pl
from jax.experimental.pallas import tpu as pltpu
from jax.sharding import PartitionSpec as P

D = 1024
FF = 2752
FP = 2816
HEADS = 16
FEAT = 16
WIN = 64
MICRO = 2
LEN = 256
EPSILON = 1e-06
SCALE = 1.0 / math.sqrt(D)
LINEAR, FEED, WINDOW, FEED2 = 0, 1, 2, 3
MIB = 2**20
MESH = pl.DeviceIdType.MESH
BF = jnp.bfloat16
F32 = jnp.float32


def any_spec():
    return pl.BlockSpec(memory_space=pl.ANY)


def vmem_spec():
    return pl.BlockSpec(memory_space=pltpu.VMEM)


def dot(left, right):
    return jnp.dot(left, right, preferred_element_type=F32)


def dot_t(left, right):
    return lax.dot_general(left, right, (((1,), (1,)), ((), ())), preferred_element_type=F32)


def dot_0(left, right):
    return lax.dot_general(left, right, (((0,), (0,)), ((), ())), preferred_element_type=F32)


def block256(index):
    return pl.ds(pl.multiple_of(index * 256, 256), 256)


def each(first, last, act):
    def step(i, carry):
        act(i)
        return carry

    lax.fori_loop(first, last, step, 0)


def is_feed(section):
    return (section == FEED) | (section == FEED2)


PAIR_STEP = 32 * FF
ROW_STEP = 64 * D
AHEAD = 12


def prepare(section, flat, wide_v, tall_v, chunk, blocks, woven, load_sem):
    def run(steps, count, first, work):
        def load(i):
            slot = lax.rem(i, AHEAD)
            return pltpu.make_async_copy(
                flat.at[:, pl.ds(pl.multiple_of(first + i * count, 1024), count)],
                chunk.at[slot, :, pl.ds(0, count)],
                load_sem.at[slot],
            )

        def start(i, carry):
            load(i).start()
            return carry

        lax.fori_loop(0, AHEAD, start, 0)

        def step(i, carry):
            load(i).wait()
            rows = count // 128
            blocks[pl.ds(0, rows), :] = chunk[lax.rem(i, AHEAD), :, pl.ds(0, count)].astype(F32).reshape(rows, 128)
            work(i)

            @pl.when(i + AHEAD < steps)
            def _():
                load(i + AHEAD).start()

            return carry

        lax.fori_loop(0, steps, step, 0)

    def rows_of(index, count):
        return pl.ds(pl.multiple_of(index * count, count), count)

    def pair_work(i):
        low_half = lax.broadcasted_iota(jnp.int32, (16, 128), 1) < 64
        rolled = pltpu.roll(blocks[pl.ds(21, 16, stride=43), :], 64, 1)
        for c in range(22):
            even = blocks[pl.ds(c, 16, stride=43), :]
            if c == 21:
                even = jnp.where(low_half, even, 0.0)
                odd = jnp.where(low_half, rolled, 0.0)
            else:
                after = pltpu.roll(blocks[pl.ds(22 + c, 16, stride=43), :], 64, 1)
                odd = jnp.where(low_half, rolled, after)
                rolled = after
            woven[c, pl.ds(0, 16, stride=2), :] = even
            woven[c, pl.ds(1, 16, stride=2), :] = odd
        rows = rows_of(lax.rem(i, 32), 32)
        for c in range(22):
            wide_v[i // 32, rows, pl.ds(128 * c, 128)] = woven[c].astype(BF)

    def row_work(target, rows, first_col):
        for c in range(8):
            target[rows, pl.ds(first_col + 128 * c, 128)] = blocks[pl.ds(c, 64, stride=8), :].astype(BF)

    def square(i, first, target, first_col):
        @pl.when((i >= first) & (i < first + 16))
        def _():
            row_work(target, rows_of(i - first, 64), first_col)

    @pl.when(is_feed(section))
    def _():
        run(64, PAIR_STEP, D, pair_work)
        run(43, ROW_STEP, D + 2 * D * FF, lambda i: row_work(tall_v, rows_of(i, 64), 0))
        tall_v[pl.ds(FF, FP - FF), :] = jnp.zeros((FP - FF, D), BF)

    @pl.when(section == WINDOW)
    def _():
        def work(i):
            square(i, 0, wide_v.at[0], 0)
            square(i, 16, wide_v.at[0], D)
            square(i, 32, wide_v.at[1], 0)
            square(i, 48, tall_v, 0)

        run(64, ROW_STEP, D, work)

    @pl.when(section == LINEAR)
    def _():
        def work(i):
            for part in range(2):

                @pl.when(i // 4 == part)
                def _(part=part):
                    rows = rows_of(i - 4 * part, 256)
                    for c in range(2):
                        cols = pl.ds(part * HEADS * FEAT + 128 * c, 128)
                        wide_v[0, rows, cols] = blocks[pl.ds(c, 256, stride=2), :].astype(BF)

            square(i, 8, wide_v.at[1], 0)
            square(i, 24, tall_v, 0)

        run(40, ROW_STEP, D, work)


ROWS = 128
CHUNKS_OF = LEN // ROWS
HANDS = 2


def lanes_of_head(kind, block, half):
    lanes = lax.broadcasted_iota(jnp.int32, (1, 128), 1)
    if kind == WINDOW:
        return lanes // 64 == half
    return lanes // FEAT == lax.rem(2 * block + half, 8)


def lanes_of_value(half):
    return lax.broadcasted_iota(jnp.int32, (1, 128), 1) // 64 == half


def only(mask, values):
    return jnp.where(mask, values, jnp.zeros_like(values))


def both(masks, values):
    return jnp.concatenate([only(masks[0], values), only(masks[1], values)], axis=0)


def merge(masks, stacked):
    return only(masks[0], stacked[:ROWS]) + only(masks[1], stacked[ROWS:])


def block_of(index, first=0):
    return pl.ds(pl.multiple_of(first + index * 128, 128), 128)


def query_index(kind, block):
    return block if kind == WINDOW else block // 4


def low_width(kind):
    return D if kind == WINDOW else HEADS * FEAT


def mask_of(kind, doc_col, doc_row, first_row):
    shape = (doc_col.shape[0], doc_row.shape[1])
    rows = lax.broadcasted_iota(jnp.int32, shape, 0) + first_row
    cols = lax.broadcasted_iota(jnp.int32, shape, 1)
    mask = (doc_col == doc_row) & (cols <= rows)
    if kind == WINDOW:
        mask = mask & (rows - cols < WIN)
    return mask.astype(F32)


def root_of(kind):
    return 1.0 / math.sqrt(D // HEADS if kind == WINDOW else FEAT)


def out_scale(kind):
    return {LINEAR: 8.0, WINDOW: 4.0, FEED: 1.0}[kind] * SCALE


def train_kernel(
    swapping,
    tokens, cotangent, flat, lengths,
    acts, d_inputs, normed, middle, d_first, d_second, grads, d_gain,
    wide_v, tall_v, gain_v, docs_v, z_v, h_v, x_v, g_v, dz_v, first_v, second_v, mid_v, dh_v, gain_sum, far_gain,
    wide_t, tall_t, inverse_v, mask_v, dy_v, dq_v, dk_v, dv_v, chunk, blocks, woven,
    load_sem, gain_sem, in_sem, act_sem, out_sem, on_send, on_recv, back_send, back_recv, far_send, far_recv,
):
    section = lax.axis_index("section")
    batch = lax.axis_index("batch")
    last = lax.axis_size("section") - 1
    batches = lax.axis_size("batch")
    steps = MICRO * CHUNKS_OF
    count = steps * ROWS
    barrier = pltpu.get_barrier_semaphore()

    far = lax.rem(batch + batches // 2, batches)
    nobody = section < 0
    lower = batch < batches // 2
    gives = is_feed(section) | ((section == WINDOW) & jnp.logical_not(lower)) if swapping else nobody
    takes = is_feed(section) | ((section == WINDOW) & lower) if swapping else nobody

    @pl.when(gives | takes)
    def _():
        pl.semaphore_signal(barrier, inc=1, device_id=(section, far), device_id_type=MESH)

    @pl.when(section > 0)
    def _():
        pl.semaphore_signal(barrier, inc=1, device_id=(section - 1, batch), device_id_type=MESH)

    @pl.when(section < last)
    def _():
        pl.semaphore_signal(barrier, inc=1, device_id=(section + 1, batch), device_id_type=MESH)

    gain_copy = pltpu.make_async_copy(flat.at[:, pl.ds(0, D)], gain_v, gain_sem)
    gain_copy.start()
    token_copy = pltpu.make_async_copy(tokens, z_v.at[pl.ds(0, count), :], in_sem.at[0])
    tangent_copy = pltpu.make_async_copy(cotangent, g_v.at[pl.ds(0, count), :], in_sem.at[1])

    @pl.when(section == 0)
    def _():
        token_copy.start()

    @pl.when(section == last)
    def _():
        tangent_copy.start()

    places = lax.broadcasted_iota(jnp.int32, (1, LEN), 1)
    for micro in range(MICRO):
        end = 0
        ids = jnp.zeros((1, LEN), F32)
        for document in range(lengths.shape[2]):
            end = end + lengths[0, micro, document]
            ids += (places >= end).astype(F32)
        docs_v[micro] = ids
    prepare(section, flat, wide_v, tall_v, chunk, blocks, woven, load_sem)
    gain_copy.wait()
    gain = 1.0 + gain_v[...].astype(F32) / 8.0
    gain_sum[...] = jnp.zeros_like(gain_sum)

    @pl.when(section == 0)
    def _():
        token_copy.wait()

    @pl.when(section == last)
    def _():
        tangent_copy.wait()

    greeted = jnp.where((section > 0) & (section < last), 2, 1)
    pl.semaphore_wait(barrier, greeted + jnp.where(gives | takes, 1, 0))

    def rows_at(step, phase=0):
        return pl.ds(pl.multiple_of(phase * count + step * ROWS, ROWS), ROWS)

    def piece_at(step, piece, phase=0):
        size = ROWS // HANDS
        return pl.ds(pl.multiple_of(phase * count + step * ROWS + piece * size, size), size)

    def hand_on(step, piece):
        rows = piece_at(step, piece)
        return pltpu.make_async_remote_copy(
            src_ref=x_v.at[rows, :],
            dst_ref=z_v.at[rows, :],
            send_sem=on_send.at[step, piece],
            recv_sem=on_recv.at[step, piece],
            device_id=(section + 1, batch),
            device_id_type=MESH,
        )

    def hand_back(step, piece):
        rows = piece_at(step, piece)
        return pltpu.make_async_remote_copy(
            src_ref=x_v.at[rows, :],
            dst_ref=g_v.at[rows, :],
            send_sem=back_send.at[step, piece],
            recv_sem=back_recv.at[step, piece],
            device_id=(section - 1, batch),
            device_id_type=MESH,
        )

    def far_copy(kind, step=0, piece=0):
        rows, target = piece_at(step, piece), piece_at(step, piece, 1)
        source, target = (
            (z_v.at[rows, :], z_v.at[target, :]),
            (g_v.at[rows, :], g_v.at[target, :]),
            (gain_sum, far_gain),
            (docs_v.at[pl.ds(0, MICRO)], docs_v.at[pl.ds(MICRO, MICRO)]),
        )[kind]
        return pltpu.make_async_remote_copy(
            src_ref=source,
            dst_ref=target,
            send_sem=far_send.at[kind, step, piece],
            recv_sem=far_recv.at[kind, step, piece],
            device_id=(section, far),
            device_id_type=MESH,
        )

    @pl.when(gives)
    def _():
        far_copy(3).start()

    @pl.when(gives & (section == last))
    def _():
        for step in range(steps):
            for piece in range(HANDS):
                far_copy(1, step, piece).start()

    def act_out(step):
        rows = rows_at(step)
        return pltpu.make_async_copy(x_v.at[rows, :], acts.at[rows, :], act_sem.at[0, step])

    def forward_outs(phase, step):
        rows, target = rows_at(step), rows_at(step, phase)
        return [
            pltpu.make_async_copy(h_v.at[rows, :], normed.at[target, :], act_sem.at[1, step]),
            pltpu.make_async_copy(mid_v.at[rows, :], middle.at[target, :], act_sem.at[2, step]),
        ]

    def gradient_out(step):
        rows = rows_at(step)
        return pltpu.make_async_copy(dz_v.at[rows, :], d_inputs.at[rows, :], out_sem.at[0, step])

    def backward_outs(phase, step):
        rows, target = rows_at(step), rows_at(step, phase)
        return [
            pltpu.make_async_copy(g_v.at[target, :], grads.at[target, :], out_sem.at[1, step]),
            pltpu.make_async_copy(first_v.at[rows, :], d_first.at[target, :], out_sem.at[2, step]),
            pltpu.make_async_copy(second_v.at[rows, :], d_second.at[target, :], out_sem.at[3, step]),
        ]


    def forward_step(phase, step, hidden, project):
        rows, here = rows_at(step), rows_at(step, phase)
        own = phase == 0

        for piece in range(HANDS):

            @pl.when(own & (section > 0))
            def _(piece=piece):
                hand_on(step, piece).wait_recv()

            @pl.when(own & gives)
            def _(piece=piece):
                far_copy(0, step, piece).start()

            @pl.when(jnp.logical_not(own))
            def _(piece=piece):
                far_copy(0, step, piece).wait_recv()

        z = z_v[here, :].astype(F32)
        scaled = lax.rsqrt(jnp.mean(z * z, axis=1, keepdims=True) + EPSILON)
        h_v[rows, :] = (z * scaled * gain).astype(BF)
        hidden(rows)

        @pl.when(own)
        def _():
            x_v[rows, :] = (z_v[here, :].astype(F32) + project(rows)).astype(BF)

            @pl.when(section < last)
            def _():
                for piece in range(HANDS):
                    hand_on(step, piece).start()

            act_out(step).start()

        for copy in forward_outs(phase, step):
            copy.start()

    def backward_step(phase, step, unhidden, back):
        rows, here = rows_at(step), rows_at(step, phase)
        own = phase == 0

        for piece in range(HANDS):

            @pl.when(own & (section < last))
            def _(piece=piece):
                hand_back(step, piece).wait_recv()

                @pl.when(gives)
                def _():
                    far_copy(1, step, piece).start()

            @pl.when(jnp.logical_not(own))
            def _(piece=piece):
                far_copy(1, step, piece).wait_recv()

        unhidden(here, rows)

        @pl.when(own)
        def _():
            dh_v[...] = back(rows) * SCALE

            @pl.when(section < last)
            def _():
                for piece in range(HANDS):
                    hand_on(step, piece).wait_send()

            act_out(step).wait()
            z = z_v[rows, :].astype(F32)
            scaled = lax.rsqrt(jnp.mean(z * z, axis=1, keepdims=True) + EPSILON)
            unit = z * scaled
            d_normed = dh_v[...]
            gain_sum[0:1, :] += jnp.sum(d_normed * unit, axis=0, keepdims=True) * 0.125
            d_unit = d_normed * gain
            d_z = scaled * (d_unit - unit * jnp.mean(d_unit * unit, axis=1, keepdims=True))
            d_z += g_v[rows, :].astype(F32)
            dz_v[rows, :] = d_z
            x_v[rows, :] = d_z.astype(BF)

            @pl.when(section > 0)
            def _():
                for piece in range(HANDS):
                    hand_back(step, piece).start()

            gradient_out(step).start()

        for copy in backward_outs(phase, step):
            copy.start()

    def turn_weights(low, high):
        def wide_piece(which, t):
            wide_t[which, block256(t), :] = wide_v[which, :, block256(t)].T

        def tall_piece(t):
            tall_t[:, block256(t)] = tall_v[block256(t), :].T

        each(0, low // 256, functools.partial(wide_piece, 0))
        each(0, high // 256, functools.partial(wide_piece, 1))
        each(0, high // 256, tall_piece)

    def kept_at(kind, index):
        width = 2 * low_width(kind)
        room = (FP - width) // 256 * 4
        over = index >= room
        place = jnp.where(over, index - room, index)
        first = jnp.where(over, D, width) + place // 4 * 256
        rows = pl.ds(pl.multiple_of(first, 256), 256)
        return wide_t.at[jnp.where(over, 1, 0), rows, block256(lax.rem(place, 4))]

    def feed_hidden(rows):
        half = FP // 2

        for part in range(2):
            cols = pl.ds(part * half, half)
            gate = dot(h_v[rows, :], wide_v[0, :, cols]) * SCALE
            up = dot(h_v[rows, :], wide_v[1, :, cols]) * SCALE
            sig = 1.0 / (1.0 + jnp.exp(-gate))
            silu = gate * sig
            first_v[rows, cols] = (up * (sig + silu * (1.0 - sig))).astype(BF)
            second_v[rows, cols] = silu.astype(BF)
            mid_v[rows, cols] = (silu * up).astype(BF)

    def feed_project(rows):
        return dot(mid_v[rows, :], tall_v[...]) * SCALE

    def feed_unhidden(here, rows):
        half = FP // 2

        for part in range(2):
            cols = pl.ds(part * half, half)
            d_mid = dot(g_v[here, :], tall_t[:, cols]) * SCALE
            first_v[rows, cols] = (d_mid * first_v[rows, cols].astype(F32)).astype(BF)
            second_v[rows, cols] = (d_mid * second_v[rows, cols].astype(F32)).astype(BF)

    def feed_back(rows):
        return dot(first_v[rows, :], wide_t[0]) + dot(second_v[rows, :], wide_t[1])

    def attend_hidden(kind, phase, micro, part, rows):
        width = low_width(kind)
        span = ROWS * (part + 1)
        keys_at = pl.ds(pl.multiple_of(micro * LEN, LEN), span)
        step = micro * CHUNKS_OF + part
        first_v[rows, pl.ds(0, 2 * width)] = (dot(h_v[rows, :], wide_v[0, :, pl.ds(0, 2 * width)]) * SCALE).astype(BF)
        second_v[rows, pl.ds(0, D)] = (dot(h_v[rows, :], wide_v[1, :, pl.ds(0, D)]) * SCALE).astype(BF)
        cols = pl.ds(0, span)
        index = phase * MICRO + micro
        own_docs = jnp.broadcast_to(docs_v[index, :, pl.ds(part * ROWS, ROWS)], (8, ROWS))
        mask_v[:, cols] = mask_of(kind, own_docs.T[:, 0:1], docs_v[index, :, cols], part * ROWS)

        def block(t, carry):
            index = query_index(kind, t)
            queries = first_v[rows, block_of(index)]
            keys = first_v[keys_at, block_of(index, width)]
            values = second_v[keys_at, block_of(t)]
            heads = [lanes_of_head(kind, t, half) for half in range(2)]
            scores = (dot_t(both(heads, queries), keys) * root_of(kind)).reshape(2, ROWS, span)
            mask = mask_v[:, cols]
            if kind == WINDOW:
                kept = jnp.where((mask > 0.0)[None], scores, -1e30)
                raised = jnp.exp(kept - jnp.max(kept, axis=2, keepdims=True))
            else:
                slope = mask[None] * (1.0 + scores)
                kept_at(kind, (steps + step) * 8 + t)[:, cols] = slope.astype(BF).reshape(2 * ROWS, span)
                raised = 0.5 * (mask[None] + slope * slope)
            raised = raised.astype(BF).reshape(2 * ROWS, span)
            kept_at(kind, step * 8 + t)[:, cols] = raised
            summed = dot(raised, jnp.concatenate([values, jnp.ones((span, 128), BF)], axis=1))
            inverse = 1.0 / summed[:, 128:]
            sides = [lanes_of_value(half) for half in range(2)]
            mid_v[rows, block_of(t)] = merge(sides, summed[:, :128] * inverse).astype(BF)
            inverse_v[rows, block_of(t)] = merge(sides, inverse)
            return carry

        lax.fori_loop(0, 8, block, 0, unroll=UNROLL)

    def attend_project(kind, rows):
        return dot(mid_v[rows, pl.ds(0, D)], tall_v[pl.ds(0, D), :]) * out_scale(kind)

    def attend_unhidden(kind, micro, part, here, rows):
        width = low_width(kind)
        span = ROWS * (part + 1)
        keys_at = pl.ds(pl.multiple_of(micro * LEN, LEN), span)
        own = pl.ds(0, span)
        step = micro * CHUNKS_OF + part
        d_mixed = dot(g_v[here, :], tall_t[:, pl.ds(0, D)]) * out_scale(kind)
        dy_v[...] = (d_mixed * inverse_v[rows, :]).astype(BF)
        if part == CHUNKS_OF - 1:
            dk_v[...] = jnp.zeros_like(dk_v)
            dv_v[...] = jnp.zeros_like(dv_v)
        if kind == LINEAR:
            dq_v[...] = jnp.zeros_like(dq_v)

        def block(t, carry):
            index = query_index(kind, t)
            queries = first_v[rows, block_of(index)]
            keys = first_v[keys_at, block_of(index, width)]
            values = second_v[keys_at, block_of(t)]
            heads = [lanes_of_head(kind, t, half) for half in range(2)]
            sides = [lanes_of_value(half) for half in range(2)]
            d_mixed = both(sides, dy_v[:, block_of(t)])
            mixed = mid_v[rows, block_of(t)].astype(F32)
            shift = jnp.sum(d_mixed.astype(F32) * jnp.concatenate([mixed, mixed], axis=0), axis=1, keepdims=True)
            d_weights = dot_t(d_mixed, values) - shift
            raised = kept_at(kind, step * 8 + t)[:, own]
            slope = raised if kind == WINDOW else kept_at(kind, (steps + step) * 8 + t)[:, own]
            d_scores = (slope.astype(F32) * d_weights).astype(BF)
            dv_v[own, block_of(t)] += dot_0(raised, d_mixed)
            d_queries = merge(heads, dot(d_scores, keys)) * root_of(kind)
            dk_v[own, block_of(index)] += dot_0(d_scores, both(heads, queries)) * root_of(kind)
            if kind == WINDOW:
                dq_v[:, block_of(t)] = d_queries
            else:
                dq_v[:, block_of(index)] += d_queries
            return carry

        lax.fori_loop(0, 8, block, 0, unroll=UNROLL)
        done = pl.ds(part * ROWS, ROWS)
        first_v[rows, pl.ds(0, width)] = dq_v[:, pl.ds(0, width)].astype(BF)
        first_v[rows, pl.ds(width, width)] = dk_v[done, pl.ds(0, width)].astype(BF)
        second_v[rows, pl.ds(0, D)] = dv_v[done, :].astype(BF)

    def attend_back(kind, rows):
        width = low_width(kind)
        total = dot(first_v[rows, pl.ds(0, 2 * width)], wide_t[0, pl.ds(0, 2 * width), :])
        total += dot(second_v[rows, pl.ds(0, D)], wide_t[1, pl.ds(0, D), :])
        return total

    @pl.when(section == last)
    def _():
        turn_weights(FP, FP)

    @pl.when(section == WINDOW)
    def _():
        turn_weights(2 * D, D)

    def one_phase(phase, carry):
        own = phase == 0

        @pl.when(is_feed(section))
        def _():
            turns = jnp.where(own & (section == last), MICRO, 1)
            span = steps // turns

            def backward(step):
                micro, part = step // CHUNKS_OF, CHUNKS_OF - 1 - lax.rem(step, CHUNKS_OF)
                backward_step(phase, micro * CHUNKS_OF + part, feed_unhidden, feed_back)

            def turn(index):
                here = (index * span, index * span + span)
                each(*here, lambda step: forward_step(phase, step, feed_hidden, feed_project))

                @pl.when(own & (section < last))
                def _():
                    turn_weights(FP, FP)

                each(*here, backward)

            each(0, turns, turn)

        for kind in (WINDOW, LINEAR):

            @pl.when(section == kind)
            def _(kind=kind):
                def forward(micro, inner):
                    for part in range(CHUNKS_OF):
                        forward_step(
                            phase,
                            micro * CHUNKS_OF + part,
                            functools.partial(attend_hidden, kind, phase, micro, part),
                            functools.partial(attend_project, kind),
                        )
                    return inner

                lax.fori_loop(0, MICRO, forward, 0)

        for kind in (WINDOW, LINEAR):

            @pl.when(section == kind)
            def _(kind=kind):
                def backward(micro, inner):
                    for part in reversed(range(CHUNKS_OF)):
                        backward_step(
                            phase,
                            micro * CHUNKS_OF + part,
                            functools.partial(attend_unhidden, kind, micro, part),
                            functools.partial(attend_back, kind),
                        )
                    return inner

                if kind == LINEAR:
                    turn_weights(2 * low_width(kind), D)
                lax.fori_loop(0, MICRO, backward, 0)

        @pl.when(own & gives)
        def _():
            far_copy(2).start()

        def finish(step, inner):
            @pl.when(own)
            def _():
                @pl.when(section > 0)
                def _():
                    for piece in range(HANDS):
                        hand_back(step, piece).wait_send()

                gradient_out(step).wait()

            for copy in forward_outs(phase, step) + backward_outs(phase, step):
                copy.wait()
            return inner

        lax.fori_loop(0, steps, finish, 0)

        @pl.when(own & takes)
        def _():
            far_copy(3).wait_recv()

        return carry

    lax.fori_loop(0, jnp.where(takes, 2, 1), one_phase, 0)
    d_gain[...] = gain_sum[...]

    @pl.when(takes)
    def _():
        far_copy(2).wait_recv()
        d_gain[...] += far_gain[...]

    @pl.when(gives)
    def _():
        for kind in range(2):
            for step in range(steps):
                for piece in range(HANDS):
                    far_copy(kind, step, piece).wait_send()
        far_copy(2).wait_send()
        far_copy(3).wait_send()


UNROLL = 4


def train(tokens, cotangent, flat, lengths, swapping):
    count = MICRO * LEN
    steps = MICRO * CHUNKS_OF
    kept = 2 * count if swapping else count
    return pl.pallas_call(
        functools.partial(train_kernel, swapping),
        out_shape=(
            jax.ShapeDtypeStruct((count, D), BF),
            jax.ShapeDtypeStruct((count, D), F32),
            jax.ShapeDtypeStruct((kept, D), BF),
            jax.ShapeDtypeStruct((kept, FP), BF),
            jax.ShapeDtypeStruct((kept, FP), BF),
            jax.ShapeDtypeStruct((kept, FP), BF),
            jax.ShapeDtypeStruct((kept, D), BF),
            jax.ShapeDtypeStruct((8, D), F32),
        ),
        in_specs=[any_spec()] * 3 + [pl.BlockSpec(memory_space=pltpu.SMEM)],
        out_specs=(any_spec(),) * 7 + (vmem_spec(),),
        scratch_shapes=[
            pltpu.VMEM((2, D, FP), BF),
            pltpu.VMEM((FP, D), BF),
            pltpu.VMEM((1, D), BF),
            pltpu.VMEM((2 * MICRO, 1, LEN), F32),
            pltpu.VMEM((2 * count, D), BF),
            pltpu.VMEM((count, D), BF),
            pltpu.VMEM((count, D), BF),
            pltpu.VMEM((2 * count, D), BF),
            pltpu.VMEM((count, D), F32),
            pltpu.VMEM((count, FP), BF),
            pltpu.VMEM((count, FP), BF),
            pltpu.VMEM((count, FP), BF),
            pltpu.VMEM((ROWS, D), F32),
            pltpu.VMEM((8, D), F32),
            pltpu.VMEM((8, D), F32),
            pltpu.VMEM((2, FP, D), BF),
            pltpu.VMEM((D, FP), BF),
            pltpu.VMEM((count, D), F32),
            pltpu.VMEM((ROWS, LEN), F32),
            pltpu.VMEM((ROWS, D), BF),
            pltpu.VMEM((ROWS, D), F32),
            pltpu.VMEM((LEN, D), F32),
            pltpu.VMEM((LEN, D), F32),
            pltpu.VMEM((AHEAD, 1, PAIR_STEP), BF),
            pltpu.VMEM((PAIR_STEP // 128, 128), F32),
            pltpu.VMEM((22, 32, 128), F32),
            pltpu.SemaphoreType.DMA((AHEAD,)),
            pltpu.SemaphoreType.DMA,
            pltpu.SemaphoreType.DMA((2,)),
            pltpu.SemaphoreType.DMA((3, steps)),
            pltpu.SemaphoreType.DMA((4, steps)),
            pltpu.SemaphoreType.DMA((steps, HANDS)),
            pltpu.SemaphoreType.DMA((steps, HANDS)),
            pltpu.SemaphoreType.DMA((steps, HANDS)),
            pltpu.SemaphoreType.DMA((steps, HANDS)),
            pltpu.SemaphoreType.DMA((4, steps, HANDS)),
            pltpu.SemaphoreType.DMA((4, steps, HANDS)),
        ],
        compiler_params=pltpu.CompilerParams(
            collective_id=0, has_side_effects=True, vmem_limit_bytes=62 * MIB
        ),
        name="train",
    )(tokens, cotangent, flat, lengths)


HEAD_ROWS = 16
PAIRS = 64
PAIR_ROWS = PAIRS * 43
PAIR_TILES = D // 2 // PAIRS
CHUNKS = 11


class Products:
    def __init__(self, sources, scratch, base):
        self.normed, self.d_first, self.d_second, self.middle, self.grads, self.d_gain = sources
        self.left_v, self.d_v, self.woven, self.stage, self.in_sem = scratch
        self.base = base

    def fetch(self, source, target, index):
        return pltpu.make_async_copy(source, target, self.in_sem.at[index])

    def loads(self, names):
        count = self.left_v.shape[1]
        some = pl.ds(0, MICRO * LEN)
        every = pl.ds(0, count)
        low, both, high = pl.ds(0, D), pl.ds(0, 2 * D), pl.ds(D, D)
        table = {
            "h": (self.normed, self.left_v.at[0], 0),
            "g": (self.grads, self.left_v.at[1], 1),
            "first": (self.d_first, self.d_v.at[0], 2),
            "second": (self.d_second, self.d_v.at[1], 3),
            "middle": (self.middle, self.d_v.at[self.middle_slot()], 4),
        }
        for prefix, rows in (("all_", every), ("some_", some)):
            table[prefix + "h"] = (self.normed.at[rows, :], self.left_v.at[0, rows, :], 0)
            table[prefix + "mixed"] = (self.middle.at[rows, low], self.left_v.at[1, rows, :], 1)
            table[prefix + "low"] = (self.d_first.at[rows, both], self.d_v.at[0, rows, both], 2)
            table[prefix + "value"] = (self.d_second.at[rows, low], self.d_v.at[1, rows, low], 3)
            few = pl.ds(0, 2 * HEADS * FEAT)
            table["few_low"] = (self.d_first.at[some, few], self.d_v.at[0, some, few], 2)
            table[prefix + "g"] = (self.grads.at[rows, :], self.d_v.at[1, rows, high], 4)
        return [self.fetch(*table[name]) for name in names]

    def middle_slot(self):
        return 2 if self.d_v.shape[0] == 3 else 0

    def head(self, out):
        stage = self.stage
        stage[pl.ds(0, 8), :] = jnp.zeros((8, 128), F32)
        stage[pl.ds(8, 8), :] = self.d_gain[0:1, :].reshape(8, 128)
        out[pl.ds(0, 16), :] = stage[pl.ds(0, 16), :].astype(BF)

    def cut(self, out, first_row, rows, piece, scale):
        target_row = first_row - self.base

        def step(j, carry):
            source = pl.ds(pl.multiple_of(j * piece, 16), piece)
            target = pl.ds(pl.multiple_of(target_row + j * piece, 16), piece)
            out[target, :] = (self.stage[source, :] * scale).astype(BF)
            return carry

        lax.fori_loop(0, rows // piece, step, 0)

    def pairs(self, which, first_pair):
        count = PAIRS
        stage, woven = self.stage, self.woven
        half = FP // 2
        low_half = lax.broadcasted_iota(jnp.int32, (count, 128), 1) < 64
        left = self.left_v[0, :, pl.ds(pl.multiple_of(2 * first_pair, 128), 2 * count)]
        for part in range(2):
            piece = dot_0(left, self.d_v[which, :, pl.ds(part * half, half)])
            for c in range(11):
                woven[11 * part + c, pl.ds(0, 2 * count), :] = piece[:, 128 * c : 128 * c + 128]
        for c in range(22):
            stage[pl.ds(c, count, stride=43), :] = woven[c, pl.ds(0, count, stride=2), :]
        before = woven[21, pl.ds(0, count, stride=2), :]
        for c in range(22):
            here = pltpu.roll(woven[c, pl.ds(1, count, stride=2), :], 64, 1)
            stage[pl.ds(21 + c, count, stride=43), :] = jnp.where(low_half, before, here)
            before = here

    def pair_tile(self, out, k, tail_only):
        self.pairs(k // PAIR_TILES, lax.rem(k, PAIR_TILES) * PAIRS)

        @pl.when(jnp.logical_not(tail_only))
        def _():
            self.cut(out, HEAD_ROWS + k * PAIR_ROWS, PAIR_ROWS, 688, SCALE)

        @pl.when(tail_only)
        def _():
            target = pl.ds(pl.multiple_of((k + 1) * PAIR_ROWS - self.base, 16), 16)
            out[target, :] = (self.stage[pl.ds(PAIR_ROWS - 16, 16), :] * SCALE).astype(BF)

    def tall(self, out, left, right, stride, rows, first_row, scale, piece):
        product = dot_0(left, right)
        for c in range(stride):
            self.stage[pl.ds(c, rows, stride=stride), :] = product[:, 128 * c : 128 * c + 128]
        self.cut(out, first_row, rows * stride, piece, scale)

    def down_tile(self, out, j):
        left = self.d_v[self.middle_slot(), :, pl.ds(pl.multiple_of(256 * j, 256), 256)]
        self.tall(out, left, self.left_v[1], 8, 256, DOWN_ROW + 2048 * j, SCALE, 512)

    def window_tile(self, out, k):
        which = k // 4
        left = self.left_v[which // 3, :, block256(lax.rem(k, 4))]
        right = self.d_v[which // 2, :, pl.ds(pl.multiple_of(lax.rem(which, 2) * D, D), D)]
        scale = jnp.where(which < 3, SCALE, out_scale(WINDOW))
        self.tall(out, left, right, 8, 256, HEAD_ROWS + 2048 * k, scale, 512)

    def low_tile(self, out, k):
        some = pl.ds(0, MICRO * LEN)
        width = HEADS * FEAT
        right = self.d_v[0, some, pl.ds(pl.multiple_of(k * width, width), width)]
        self.tall(out, self.left_v[0, some, :], right, 2, D, HEAD_ROWS + k * 2048, SCALE, 512)

    def value_tile(self, out, k):
        some = pl.ds(0, MICRO * LEN)
        left = self.left_v[k // 2, some, pl.ds(pl.multiple_of(lax.rem(k, 2) * 512, 512), 512)]
        right = self.d_v[1, some, pl.ds(pl.multiple_of(k // 2 * D, D), D)]
        scale = jnp.where(k < 2, SCALE, out_scale(LINEAR))
        self.tall(out, left, right, 8, 512, HEAD_ROWS + 4096 * (k + 1), scale, 512)


DOWN_ROW = HEAD_ROWS + 2 * PAIR_TILES * PAIR_ROWS
DOWN_TILES = FP // 256
WINDOW_END = HEAD_ROWS + 4 * 8192
LINEAR_END = HEAD_ROWS + 20480


def product_scratch(count, slots):
    return [
        pltpu.VMEM((2, count, D), BF),
        pltpu.VMEM((slots, count, FP), BF),
        pltpu.VMEM((22, 2 * PAIRS, 128), F32),
        pltpu.VMEM((4096, 128), F32),
        pltpu.SemaphoreType.DMA((5,)),
    ]


def clear(out, first_row, rows):
    def step(i, carry):
        out[pl.ds(pl.multiple_of(first_row + i * 128, 16), 128), :] = jnp.zeros((128, 128), BF)
        return carry

    lax.fori_loop(0, rows // 128, step, 0)
    if rows % 128:
        out[pl.ds(first_row + rows // 128 * 128, rows % 128), :] = jnp.zeros((rows % 128, 128), BF)


def products_kernel(*refs):
    section = lax.axis_index("section")
    work = Products(refs[:6], refs[8:], 0)
    out, out_v = refs[6:8]
    total = out_v.shape[0] - 512
    work.head(out_v)

    def load(*names):
        for copy in work.loads(names):
            copy.start()
        for copy in work.loads(names):
            copy.wait()

    @pl.when(is_feed(section))
    def _():
        load("h", "g", "first", "second", "middle")
        each(0, 2 * PAIR_TILES, lambda k: work.pair_tile(out_v, k, section < 0))
        each(0, DOWN_TILES, lambda j: work.down_tile(out_v, j))

    for kind in (WINDOW, LINEAR):

        @pl.when(section == kind)
        def _(kind=kind):
            load("some_h", "some_mixed", "some_low", "some_value", "some_g")
            if kind == WINDOW:
                each(0, 16, lambda k: work.window_tile(out_v, k))
            else:
                each(0, 2, lambda k: work.low_tile(out_v, k))
                each(0, 4, lambda k: work.value_tile(out_v, k))
            done = WINDOW_END if kind == WINDOW else LINEAR_END
            clear(out_v, done, total - done)

    store = pltpu.make_async_copy(out_v.at[pl.ds(0, total), :], out, work.in_sem.at[0])
    store.start()
    store.wait()


def products(sources, total_rows):
    return pl.pallas_call(
        products_kernel,
        out_shape=jax.ShapeDtypeStruct((total_rows, 128), BF),
        in_specs=[any_spec()] * 5 + [vmem_spec()],
        out_specs=any_spec(),
        scratch_shapes=[pltpu.VMEM((total_rows + 512, 128), BF)] + product_scratch(MICRO * LEN, 3),
        compiler_params=pltpu.CompilerParams(vmem_limit_bytes=60 * MIB),
        name="products",
    )(*sources)


PLACES = 4


def reduce_kernel(*refs):
    section = lax.axis_index("section")
    batch = lax.axis_index("batch")
    place, core = batch // 2, lax.rem(batch, 2)
    mate = place + 1 - 2 * lax.rem(place, 2)
    out, part, own, passing, total, flat, sems = refs[6:13]
    ex_send, ex_recv, send, recv, out_sem = sems
    width = own.shape[1]
    step_rows = width - HEAD_ROWS
    piece = width // CHUNKS
    feed_here = is_feed(section)
    base = jnp.where(feed_here, place // 2, 0) * (4 * step_rows)
    work = Products(refs[:6], refs[13:], base)
    barrier = pltpu.get_barrier_semaphore()

    def greet(other):
        pl.semaphore_signal(barrier, inc=1, device_id=(section, other), device_id_type=MESH)

    window_here = (section == WINDOW) & (place < 2)
    pair_here = feed_here | window_here
    linear_here = section == LINEAR
    sets = (
        (feed_here & (place < 2), ("h", "first")),
        (feed_here & (place == 2), ("middle", "g")),
        (feed_here & (place == 3), ("h", "second")),
        (window_here & (place == 0), ("all_h", "all_value")),
        (window_here & (place == 1), ("all_h", "all_low")),
        (linear_here, ("some_h", "few_low")),
    )
    for here, names in sets:

        @pl.when(here)
        def _(names=names):
            for copy in work.loads(names):
                copy.start()

    greet(2 * place + 1 - core)

    @pl.when(place > 0)
    def _():
        greet(batch - 2)

    @pl.when(place < PLACES - 1)
    def _():
        greet(batch + 2)

    @pl.when(base == 0)
    def _():
        work.head(part)

    pl.semaphore_wait(barrier, jnp.where((place > 0) & (place < PLACES - 1), 3, 2))
    for here, names in sets:

        @pl.when(here)
        def _(names=names):
            for copy in work.loads(names):
                copy.wait()

    late_sets = (
        (feed_here & (place < 2), ("second",)),
        (feed_here & (place == 2), ("h", "second")),
        (feed_here & (place == 3), ("middle", "g")),
        (window_here & (place == 0), ("all_mixed", "all_g", "all_low")),
        (window_here & (place == 1), ("all_value", "all_mixed", "all_g")),
        (linear_here, ("some_mixed", "some_value", "some_g")),
    )

    def late(act):
        for here, names in late_sets:

            @pl.when(here)
            def _(names=names):
                for copy in work.loads(names):
                    act(copy)

    late(lambda copy: copy.start())

    def rows_of(i):
        return pl.ds(pl.multiple_of(i * piece, 16), piece)

    def share(index, i):
        return pl.ds(pl.multiple_of(step_rows * index - base + i * piece, 16), piece)

    def swap(to, i):
        slot = lax.rem(to, 2)
        return pltpu.make_async_remote_copy(
            src_ref=part.at[share(2 * to + 1 - core, i), :],
            dst_ref=own.at[slot, rows_of(i), :],
            send_sem=ex_send.at[slot, i],
            recv_sem=ex_recv.at[slot, i],
            device_id=(section, 2 * place + 1 - core),
            device_id_type=MESH,
        )

    def go(source, slot, to, i, other):
        return pltpu.make_async_remote_copy(
            src_ref=source,
            dst_ref=passing.at[slot, rows_of(i), :],
            send_sem=send.at[lax.rem(to, 2), i],
            recv_sem=recv.at[slot, i],
            device_id=(section, other),
            device_id_type=MESH,
        )

    def arrived(slot, i):
        here = passing.at[slot, rows_of(i), :]
        pltpu.make_async_copy(here, here, recv.at[slot, i]).wait()

    def release(to, before, after, limits=(CHUNKS, CHUNKS)):
        def bound(row, parity):
            most = jnp.where(parity == 0, limits[0], limits[1])
            return jnp.minimum(jnp.maximum(row - parity * step_rows, 0) // piece, most)

        def add(i):
            slot = lax.rem(to, 2)
            rows = rows_of(i)
            swap(to, i).wait_recv()
            mine = part[share(2 * to + core, i), :].astype(F32)
            own[slot, rows, :] = (own[slot, rows, :].astype(F32) + mine).astype(BF)
            source = own.at[slot, rows, :]

            @pl.when(pair_here & (to == mate))
            def _():
                go(source, 0, to, i, 2 * mate + core).start()

            @pl.when(linear_here & (place == PLACES - 1))
            def _():
                go(source, slot, to, i, batch - 2).start()

            @pl.when(linear_here & (place == 0) & (to == 1))
            def _():
                go(source, 2, to, i, batch + 2).start()

        each(bound(before, 1 - core), bound(after, 1 - core), lambda i: swap(to, i).start())
        each(bound(before, core), bound(after, core), add)

    def swapped(to, limits=(CHUNKS, CHUNKS)):
        each(0, jnp.where(core == 0, limits[1], limits[0]), lambda i: swap(to, i).wait_send())

    def store(which):
        rows = out.shape[1] // 128
        early = (CHUNKS - 1) * piece - 32
        begin, size = ((0, early), (early, rows - early))[which]
        source = pl.ds(pl.multiple_of((8 + batch + begin) * 128, 128), size * 128)
        return pltpu.make_async_copy(
            flat.at[:, source], out.at[:, pl.ds(begin * 128, size * 128)], out_sem.at[which]
        )

    def emit(i):
        cols = pl.ds(pl.multiple_of(i * piece * 128, 1024), piece * 128)
        flat[0:1, cols] = total[...].reshape(1, piece * 128)

    whole = 2 * step_rows + HEAD_ROWS

    @pl.when(feed_here)
    def _():
        upper = place >= 2
        share_tiles = 2 * step_rows // PAIR_ROWS
        upper_tiles = 2 * PAIR_TILES - 2 * share_tiles

        def pair(t):
            turned = jnp.where(t < share_tiles, t + share_tiles, jnp.where(t == share_tiles, share_tiles - 1, t - share_tiles - 1))
            k = jnp.where(place == 0, turned, t)
            k = jnp.where(upper, jnp.where(t == upper_tiles, 2 * share_tiles - 1, 2 * share_tiles + t), k)
            tail_only = upper & (t == upper_tiles)

            @pl.when(jnp.logical_not(upper) & (k == PAIR_TILES))
            def _():
                late(lambda copy: copy.wait())

            work.pair_tile(part, k, tail_only)
            start = HEAD_ROWS + PAIR_ROWS * k - base
            stop = start + PAIR_ROWS
            ends_late = (place == 0) & (k == share_tiles - 1)
            to = base // (2 * step_rows)
            early = jnp.where(k == share_tiles - 2, whole, jnp.where(k < share_tiles - 2, stop, start))
            before_0 = jnp.where(tail_only, 0, jnp.where(upper & (k == 2 * share_tiles), piece, start))
            after_0 = jnp.where(tail_only, piece, jnp.where(place == 0, early, stop))
            release(to, before_0, after_0)
            before_1 = jnp.where(ends_late, 0, jnp.where((place == 0) & (k == share_tiles), piece, start - 2 * step_rows))
            after_1 = jnp.where(ends_late, piece, stop - 2 * step_rows)
            release(to + 1, before_1, after_1)

        def down(j):
            work.down_tile(part, j)
            start = DOWN_ROW + 2048 * j - base
            stop = start + 2048
            early = jnp.where(j == 1, whole, jnp.where(j < 1, stop, start))
            release(2, start, jnp.where(place == 2, early, stop))
            release(3, start - 2 * step_rows, stop - 2 * step_rows)

        def turn(t):
            @pl.when(t == 1)
            def _():
                @pl.when(place == 2)
                def _():
                    late(lambda copy: copy.wait())

                each(0, jnp.where(upper, upper_tiles + 1, 2 * share_tiles), pair)

                @pl.when(place == 3)
                def _():
                    late(lambda copy: copy.wait())

            mate_first = place == 2
            first = jnp.where(mate_first & (t == 0), 2, 0)
            last = jnp.where(mate_first & (t == 1), 2, DOWN_TILES)
            here = upper & (mate_first | (t == 1))
            each(first, jnp.where(here, last, first), down)

        each(0, 2, turn)
        swapped(mate)
        swapped(place)

    @pl.when(window_here)
    def _():
        def tile(t, carry):
            k = lax.rem(t + jnp.where(place == 0, 8, 0), 16)

            @pl.when(t == jnp.where(place == 0, 4, 8))
            def _():
                late(lambda copy: copy.wait())

            work.window_tile(part, k)
            start = HEAD_ROWS + 2048 * k
            stop = start + 2048

            @pl.when(k == 15)
            def _():
                clear(part, WINDOW_END, 4 * step_rows + HEAD_ROWS - WINDOW_END)

            stop_0 = jnp.where(place == 0, jnp.where(k < 7, stop, jnp.where(k == 7, whole, start)), stop)
            stop_1 = jnp.where(k == 15, whole, stop - 2 * step_rows)
            release(0, start, stop_0)
            release(1, start - 2 * step_rows, stop_1)
            return carry

        lax.fori_loop(0, 16, tile, 0)
        for to in range(2):
            swapped(to)

    @pl.when(linear_here)
    def _():
        filled = [max(0, min(CHUNKS, -(-(LINEAR_END - step_rows * index) // piece))) for index in range(4)]
        limits = (tuple(filled[:2]), tuple(filled[2:]))
        cover = max(step_rows * index + piece * filled[index] for index in range(4) if filled[index])
        clear(part, LINEAR_END, cover - LINEAR_END)

        def low(k):
            work.low_tile(part, k)
            start = HEAD_ROWS + 2048 * k
            release(0, start, start + 2048, limits[0])

        def value(k):
            work.value_tile(part, k)
            start = HEAD_ROWS + 4096 * (k + 1)
            stop = jnp.where(k == 3, cover, start + 4096)
            release(0, start, stop, limits[0])
            release(1, start - 2 * step_rows, stop - 2 * step_rows, limits[1])

        def pass_on(to, i):
            rows = rows_of(i)
            arrived(to, i)
            added = passing[to, rows, :].astype(F32) + own[to, rows, :].astype(F32)
            passing[to, rows, :] = added.astype(BF)
            go(passing.at[to, rows, :], to, to, i, batch - 2).start()

        ahead = jnp.where((place == 2) & (core == 0), 2, 0)

        def value_and_on(k):
            value(k)
            each(jnp.minimum(jnp.maximum(k - 1, 0), ahead), jnp.minimum(k, ahead), functools.partial(pass_on, 0))

        each(0, 2, low)
        late(lambda copy: copy.wait())
        each(0, 4, value_and_on)

        def own_count(to):
            return jnp.where(core == 0, limits[to][0], limits[to][1])

        @pl.when((place == 1) | (place == 2))
        def _():
            each(ahead, own_count(0), functools.partial(pass_on, 0))

        @pl.when(place == 2)
        def _():
            each(0, own_count(1), functools.partial(pass_on, 1))

        for to in range(2):
            swapped(to, limits[to])

        def sum_up(i):
            rows = rows_of(i)

            @pl.when((place == 0) & (i < own_count(0)))
            def _():
                arrived(0, i)
                total[...] = own[0, rows, :].astype(F32) + passing[0, rows, :].astype(F32)

            @pl.when((place == 1) & (i < own_count(1)))
            def _():
                arrived(1, i)
                arrived(2, i)
                both_ways = passing[1, rows, :].astype(F32) + passing[2, rows, :].astype(F32)
                total[...] = own[1, rows, :].astype(F32) + both_ways

            emit(i)

        here = jnp.where(place == 0, own_count(0), jnp.where(place == 1, own_count(1), 0))
        total[...] = jnp.zeros_like(total)
        each(here, CHUNKS, emit)
        each(0, here - 1, sum_up)

        @pl.when(here == CHUNKS)
        def _():
            store(0).start()

        each(jnp.maximum(here - 1, 0), here, sum_up)

        @pl.when(here < CHUNKS)
        def _():
            store(0).start()

        @pl.when((place == 1) | (place >= 2))
        def _():
            each(0, own_count(0), lambda i: go(passing.at[0, rows_of(i), :], 0, 0, i, batch - 2).wait_send())

        @pl.when((place == 0) | (place >= 2))
        def _():
            each(0, own_count(1), lambda i: go(passing.at[0, rows_of(i), :], 0, 1, i, batch - 2).wait_send())

    @pl.when((section == WINDOW) & (place >= 2))
    def _():
        total[...] = jnp.zeros_like(total)
        each(0, CHUNKS, emit)
        store(0).start()

    @pl.when(pair_here)
    def _():
        slot = lax.rem(place, 2)

        def sum_up(i):
            rows = rows_of(i)
            arrived(0, i)
            total[...] = own[slot, rows, :].astype(F32) + passing[0, rows, :].astype(F32)
            emit(i)

        each(0, CHUNKS - 1, sum_up)
        store(0).start()
        each(CHUNKS - 1, CHUNKS, sum_up)
        other = 2 * mate + core
        each(0, CHUNKS, lambda i: go(passing.at[0, rows_of(i), :], 0, mate, i, other).wait_send())

    store(1).start()
    store(0).wait()
    store(1).wait()


def reduce_products(sources, total_rows, batches):
    step_rows = (total_rows - 8) // batches - 1
    width = step_rows + HEAD_ROWS
    return pl.pallas_call(
        reduce_kernel,
        out_shape=jax.ShapeDtypeStruct((1, (step_rows + 1) * 128), F32),
        in_specs=[any_spec()] * 5 + [vmem_spec()],
        out_specs=any_spec(),
        scratch_shapes=[
            pltpu.VMEM((4 * step_rows + HEAD_ROWS + 512, 128), BF),
            pltpu.VMEM((2, width, 128), BF),
            pltpu.VMEM((3, width, 128), BF),
            pltpu.VMEM((width // CHUNKS, 128), F32),
            pltpu.VMEM((1, width * 128), F32),
            (
                pltpu.SemaphoreType.DMA((2, CHUNKS)),
                pltpu.SemaphoreType.DMA((2, CHUNKS)),
                pltpu.SemaphoreType.DMA((2, CHUNKS)),
                pltpu.SemaphoreType.DMA((3, CHUNKS)),
                pltpu.SemaphoreType.DMA((2,)),
            ),
        ]
        + product_scratch(2 * MICRO * LEN, 2),
        compiler_params=pltpu.CompilerParams(
            collective_id=1, has_side_effects=True, vmem_limit_bytes=60 * MIB
        ),
        name="reduce_products",
    )(*sources)


def shards(tokens, cotangent, params, lengths):
    batches = lax.axis_size("batch")
    paired = batches == 2 * PLACES
    acts, d_inputs, normed, middle, d_first, d_second, grads, d_gain = train(
        tokens, cotangent, params, lengths, paired
    )
    total_rows = params.shape[1] // 128 + 8
    sources = (normed, d_first, d_second, middle, grads, d_gain)
    if paired:
        mine = reduce_products(sources, total_rows, batches)
    else:
        parts = products(sources, total_rows)
        mine = lax.psum_scatter(parts[8:].reshape(-1), "batch", scatter_dimension=0, tiled=True)
        mine = mine.astype(F32)[None]
    return acts[None], d_inputs[None], mine


def solution(mesh):
    return jax.shard_map(
        shards,
        mesh=mesh,
        in_specs=(P("batch", None), P("batch", None), P("section", None), P("batch", None, None)),
        out_specs=(P("section", "batch", None), P("section", "batch", None), P("section", "batch")),
        check_vma=False,
    )
```

```python
import functools
import math

import jax
import jax.numpy as jnp
from jax import lax
from jax.experimental import pallas as pl
from jax.experimental.pallas import tpu as pltpu
from jax.sharding import PartitionSpec as P

D = 1024
FF = 2752
FP = 2816
HEADS = 16
FEAT = 16
WIN = 64
MICRO = 2
LEN = 256
EPSILON = 1e-06
SCALE = 1.0 / math.sqrt(D)
LINEAR, FEED, WINDOW, FEED2 = 0, 1, 2, 3
MIB = 2**20
MESH = pl.DeviceIdType.MESH
BF = jnp.bfloat16
F32 = jnp.float32


def any_spec():
    return pl.BlockSpec(memory_space=pl.ANY)


def vmem_spec():
    return pl.BlockSpec(memory_space=pltpu.VMEM)


def dot(left, right):
    return jnp.dot(left, right, preferred_element_type=F32)


def dot_t(left, right):
    return lax.dot_general(left, right, (((1,), (1,)), ((), ())), preferred_element_type=F32)


def dot_0(left, right):
    return lax.dot_general(left, right, (((0,), (0,)), ((), ())), preferred_element_type=F32)


def block256(index):
    return pl.ds(pl.multiple_of(index * 256, 256), 256)


def each(first, last, act):
    def step(i, carry):
        act(i)
        return carry

    lax.fori_loop(first, last, step, 0)


def is_feed(section):
    return (section == FEED) | (section == FEED2)


PAIR_STEP = 32 * FF
ROW_STEP = 64 * D
AHEAD = 12


def prepare(section, flat, wide_v, tall_v, chunk, blocks, woven, load_sem):
    def run(steps, count, first, work):
        def load(i):
            slot = lax.rem(i, AHEAD)
            return pltpu.make_async_copy(
                flat.at[:, pl.ds(pl.multiple_of(first + i * count, 1024), count)],
                chunk.at[slot, :, pl.ds(0, count)],
                load_sem.at[slot],
            )

        def start(i, carry):
            load(i).start()
            return carry

        lax.fori_loop(0, AHEAD, start, 0)

        def step(i, carry):
            load(i).wait()
            rows = count // 128
            blocks[pl.ds(0, rows), :] = chunk[lax.rem(i, AHEAD), :, pl.ds(0, count)].astype(F32).reshape(rows, 128)
            work(i)

            @pl.when(i + AHEAD < steps)
            def _():
                load(i + AHEAD).start()

            return carry

        lax.fori_loop(0, steps, step, 0)

    def rows_of(index, count):
        return pl.ds(pl.multiple_of(index * count, count), count)

    def pair_work(i):
        low_half = lax.broadcasted_iota(jnp.int32, (16, 128), 1) < 64
        rolled = pltpu.roll(blocks[pl.ds(21, 16, stride=43), :], 64, 1)
        for c in range(22):
            even = blocks[pl.ds(c, 16, stride=43), :]
            if c == 21:
                even = jnp.where(low_half, even, 0.0)
                odd = jnp.where(low_half, rolled, 0.0)
            else:
                after = pltpu.roll(blocks[pl.ds(22 + c, 16, stride=43), :], 64, 1)
                odd = jnp.where(low_half, rolled, after)
                rolled = after
            woven[c, pl.ds(0, 16, stride=2), :] = even
            woven[c, pl.ds(1, 16, stride=2), :] = odd
        rows = rows_of(lax.rem(i, 32), 32)
        for c in range(22):
            wide_v[i // 32, rows, pl.ds(128 * c, 128)] = woven[c].astype(BF)

    def row_work(target, rows, first_col):
        for c in range(8):
            target[rows, pl.ds(first_col + 128 * c, 128)] = blocks[pl.ds(c, 64, stride=8), :].astype(BF)

    def square(i, first, target, first_col):
        @pl.when((i >= first) & (i < first + 16))
        def _():
            row_work(target, rows_of(i - first, 64), first_col)

    @pl.when(is_feed(section))
    def _():
        run(64, PAIR_STEP, D, pair_work)
        run(43, ROW_STEP, D + 2 * D * FF, lambda i: row_work(tall_v, rows_of(i, 64), 0))
        tall_v[pl.ds(FF, FP - FF), :] = jnp.zeros((FP - FF, D), BF)

    @pl.when(section == WINDOW)
    def _():
        def work(i):
            square(i, 0, wide_v.at[0], 0)
            square(i, 16, wide_v.at[0], D)
            square(i, 32, wide_v.at[1], 0)
            square(i, 48, tall_v, 0)

        run(64, ROW_STEP, D, work)

    @pl.when(section == LINEAR)
    def _():
        def work(i):
            for part in range(2):

                @pl.when(i // 4 == part)
                def _(part=part):
                    rows = rows_of(i - 4 * part, 256)
                    for c in range(2):
                        cols = pl.ds(part * HEADS * FEAT + 128 * c, 128)
                        wide_v[0, rows, cols] = blocks[pl.ds(c, 256, stride=2), :].astype(BF)

            square(i, 8, wide_v.at[1], 0)
            square(i, 24, tall_v, 0)

        run(40, ROW_STEP, D, work)


ROWS = 128
CHUNKS_OF = LEN // ROWS
HANDS = 2


def lanes_of_head(kind, block, half):
    lanes = lax.broadcasted_iota(jnp.int32, (1, 128), 1)
    if kind == WINDOW:
        return lanes // 64 == half
    return lanes // FEAT == lax.rem(2 * block + half, 8)


def lanes_of_value(half):
    return lax.broadcasted_iota(jnp.int32, (1, 128), 1) // 64 == half


def only(mask, values):
    return jnp.where(mask, values, jnp.zeros_like(values))


def both(masks, values):
    return jnp.concatenate([only(masks[0], values), only(masks[1], values)], axis=0)


def merge(masks, stacked):
    return only(masks[0], stacked[:ROWS]) + only(masks[1], stacked[ROWS:])


def block_of(index, first=0):
    return pl.ds(pl.multiple_of(first + index * 128, 128), 128)


def query_index(kind, block):
    return block if kind == WINDOW else block // 4


def low_width(kind):
    return D if kind == WINDOW else HEADS * FEAT


def mask_of(kind, doc_col, doc_row, first_row):
    shape = (doc_col.shape[0], doc_row.shape[1])
    rows = lax.broadcasted_iota(jnp.int32, shape, 0) + first_row
    cols = lax.broadcasted_iota(jnp.int32, shape, 1)
    mask = (doc_col == doc_row) & (cols <= rows)
    if kind == WINDOW:
        mask = mask & (rows - cols < WIN)
    return mask.astype(F32)


def root_of(kind):
    return 1.0 / math.sqrt(D // HEADS if kind == WINDOW else FEAT)


def out_scale(kind):
    return {LINEAR: 8.0, WINDOW: 4.0, FEED: 1.0}[kind] * SCALE


def train_kernel(
    swapping,
    tokens, cotangent, flat, lengths,
    acts, d_inputs, normed, middle, d_first, d_second, grads, d_gain,
    wide_v, tall_v, gain_v, docs_v, z_v, h_v, x_v, g_v, dz_v, first_v, second_v, mid_v, dh_v, gain_sum, far_gain,
    wide_t, tall_t, inverse_v, mask_v, dy_v, dq_v, dk_v, dv_v, chunk, blocks, woven,
    load_sem, gain_sem, in_sem, act_sem, out_sem, on_send, on_recv, back_send, back_recv, far_send, far_recv,
):
    section = lax.axis_index("section")
    batch = lax.axis_index("batch")
    last = lax.axis_size("section") - 1
    batches = lax.axis_size("batch")
    steps = MICRO * CHUNKS_OF
    count = steps * ROWS
    barrier = pltpu.get_barrier_semaphore()

    far = lax.rem(batch + batches // 2, batches)
    nobody = section < 0
    lower = batch < batches // 2
    gives = is_feed(section) | ((section == WINDOW) & jnp.logical_not(lower)) if swapping else nobody
    takes = is_feed(section) | ((section == WINDOW) & lower) if swapping else nobody

    @pl.when(gives | takes)
    def _():
        pl.semaphore_signal(barrier, inc=1, device_id=(section, far), device_id_type=MESH)

    @pl.when(section > 0)
    def _():
        pl.semaphore_signal(barrier, inc=1, device_id=(section - 1, batch), device_id_type=MESH)

    @pl.when(section < last)
    def _():
        pl.semaphore_signal(barrier, inc=1, device_id=(section + 1, batch), device_id_type=MESH)

    gain_copy = pltpu.make_async_copy(flat.at[:, pl.ds(0, D)], gain_v, gain_sem)
    gain_copy.start()
    token_copy = pltpu.make_async_copy(tokens, z_v.at[pl.ds(0, count), :], in_sem.at[0])
    tangent_copy = pltpu.make_async_copy(cotangent, g_v.at[pl.ds(0, count), :], in_sem.at[1])

    @pl.when(section == 0)
    def _():
        token_copy.start()

    @pl.when(section == last)
    def _():
        tangent_copy.start()

    places = lax.broadcasted_iota(jnp.int32, (1, LEN), 1)
    for micro in range(MICRO):
        end = 0
        ids = jnp.zeros((1, LEN), F32)
        for document in range(lengths.shape[2]):
            end = end + lengths[0, micro, document]
            ids += (places >= end).astype(F32)
        docs_v[micro] = ids
    prepare(section, flat, wide_v, tall_v, chunk, blocks, woven, load_sem)
    gain_copy.wait()
    gain = 1.0 + gain_v[...].astype(F32) / 8.0
    gain_sum[...] = jnp.zeros_like(gain_sum)

    @pl.when(section == 0)
    def _():
        token_copy.wait()

    @pl.when(section == last)
    def _():
        tangent_copy.wait()

    greeted = jnp.where((section > 0) & (section < last), 2, 1)
    pl.semaphore_wait(barrier, greeted + jnp.where(gives | takes, 1, 0))

    def rows_at(step, phase=0):
        return pl.ds(pl.multiple_of(phase * count + step * ROWS, ROWS), ROWS)

    def piece_at(step, piece, phase=0):
        size = ROWS // HANDS
        return pl.ds(pl.multiple_of(phase * count + step * ROWS + piece * size, size), size)

    def hand_on(step, piece):
        rows = piece_at(step, piece)
        return pltpu.make_async_remote_copy(
            src_ref=x_v.at[rows, :],
            dst_ref=z_v.at[rows, :],
            send_sem=on_send.at[step, piece],
            recv_sem=on_recv.at[step, piece],
            device_id=(section + 1, batch),
            device_id_type=MESH,
        )

    def hand_back(step, piece):
        rows = piece_at(step, piece)
        return pltpu.make_async_remote_copy(
            src_ref=x_v.at[rows, :],
            dst_ref=g_v.at[rows, :],
            send_sem=back_send.at[step, piece],
            recv_sem=back_recv.at[step, piece],
            device_id=(section - 1, batch),
            device_id_type=MESH,
        )

    def far_copy(kind, step=0, piece=0):
        rows, target = piece_at(step, piece), piece_at(step, piece, 1)
        source, target = (
            (z_v.at[rows, :], z_v.at[target, :]),
            (g_v.at[rows, :], g_v.at[target, :]),
            (gain_sum, far_gain),
            (docs_v.at[pl.ds(0, MICRO)], docs_v.at[pl.ds(MICRO, MICRO)]),
        )[kind]
        return pltpu.make_async_remote_copy(
            src_ref=source,
            dst_ref=target,
            send_sem=far_send.at[kind, step, piece],
            recv_sem=far_recv.at[kind, step, piece],
            device_id=(section, far),
            device_id_type=MESH,
        )

    @pl.when(gives)
    def _():
        far_copy(3).start()

    @pl.when(gives & (section == last))
    def _():
        for step in range(steps):
            for piece in range(HANDS):
                far_copy(1, step, piece).start()

    def act_out(step):
        rows = rows_at(step)
        return pltpu.make_async_copy(x_v.at[rows, :], acts.at[rows, :], act_sem.at[0, step])

    def forward_outs(phase, step):
        rows, target = rows_at(step), rows_at(step, phase)
        return [
            pltpu.make_async_copy(h_v.at[rows, :], normed.at[target, :], act_sem.at[1, step]),
            pltpu.make_async_copy(mid_v.at[rows, :], middle.at[target, :], act_sem.at[2, step]),
        ]

    def gradient_out(step):
        rows = rows_at(step)
        return pltpu.make_async_copy(dz_v.at[rows, :], d_inputs.at[rows, :], out_sem.at[0, step])

    def backward_outs(phase, step):
        rows, target = rows_at(step), rows_at(step, phase)
        return [
            pltpu.make_async_copy(g_v.at[target, :], grads.at[target, :], out_sem.at[1, step]),
            pltpu.make_async_copy(first_v.at[rows, :], d_first.at[target, :], out_sem.at[2, step]),
            pltpu.make_async_copy(second_v.at[rows, :], d_second.at[target, :], out_sem.at[3, step]),
        ]


    def forward_step(phase, step, hidden, project):
        rows, here = rows_at(step), rows_at(step, phase)
        own = phase == 0

        for piece in range(HANDS):

            @pl.when(own & (section > 0))
            def _(piece=piece):
                hand_on(step, piece).wait_recv()

            @pl.when(own & gives)
            def _(piece=piece):
                far_copy(0, step, piece).start()

            @pl.when(jnp.logical_not(own))
            def _(piece=piece):
                far_copy(0, step, piece).wait_recv()

        z = z_v[here, :].astype(F32)
        scaled = lax.rsqrt(jnp.mean(z * z, axis=1, keepdims=True) + EPSILON)
        h_v[rows, :] = (z * scaled * gain).astype(BF)
        hidden(rows)

        @pl.when(own)
        def _():
            x_v[rows, :] = (z_v[here, :].astype(F32) + project(rows)).astype(BF)

            @pl.when(section < last)
            def _():
                for piece in range(HANDS):
                    hand_on(step, piece).start()

            act_out(step).start()

        for copy in forward_outs(phase, step):
            copy.start()

    def backward_step(phase, step, unhidden, back):
        rows, here = rows_at(step), rows_at(step, phase)
        own = phase == 0

        for piece in range(HANDS):

            @pl.when(own & (section < last))
            def _(piece=piece):
                hand_back(step, piece).wait_recv()

                @pl.when(gives)
                def _():
                    far_copy(1, step, piece).start()

            @pl.when(jnp.logical_not(own))
            def _(piece=piece):
                far_copy(1, step, piece).wait_recv()

        unhidden(here, rows)

        @pl.when(own)
        def _():
            dh_v[...] = back(rows) * SCALE

            @pl.when(section < last)
            def _():
                for piece in range(HANDS):
                    hand_on(step, piece).wait_send()

            act_out(step).wait()
            z = z_v[rows, :].astype(F32)
            scaled = lax.rsqrt(jnp.mean(z * z, axis=1, keepdims=True) + EPSILON)
            unit = z * scaled
            d_normed = dh_v[...]
            gain_sum[0:1, :] += jnp.sum(d_normed * unit, axis=0, keepdims=True) * 0.125
            d_unit = d_normed * gain
            d_z = scaled * (d_unit - unit * jnp.mean(d_unit * unit, axis=1, keepdims=True))
            d_z += g_v[rows, :].astype(F32)
            dz_v[rows, :] = d_z
            x_v[rows, :] = d_z.astype(BF)

            @pl.when(section > 0)
            def _():
                for piece in range(HANDS):
                    hand_back(step, piece).start()

            gradient_out(step).start()

        for copy in backward_outs(phase, step):
            copy.start()

    def turn_weights(low, high):
        def wide_piece(which, t):
            wide_t[which, block256(t), :] = wide_v[which, :, block256(t)].T

        def tall_piece(t):
            tall_t[:, block256(t)] = tall_v[block256(t), :].T

        each(0, low // 256, functools.partial(wide_piece, 0))
        each(0, high // 256, functools.partial(wide_piece, 1))
        each(0, high // 256, tall_piece)

    def kept_at(kind, index):
        width = 2 * low_width(kind)
        room = (FP - width) // 256 * 4
        over = index >= room
        place = jnp.where(over, index - room, index)
        first = jnp.where(over, D, width) + place // 4 * 256
        rows = pl.ds(pl.multiple_of(first, 256), 256)
        return wide_t.at[jnp.where(over, 1, 0), rows, block256(lax.rem(place, 4))]

    def feed_hidden(rows):
        half = FP // 2

        for part in range(2):
            cols = pl.ds(part * half, half)
            gate = dot(h_v[rows, :], wide_v[0, :, cols]) * SCALE
            up = dot(h_v[rows, :], wide_v[1, :, cols]) * SCALE
            sig = 1.0 / (1.0 + jnp.exp(-gate))
            silu = gate * sig
            first_v[rows, cols] = (up * (sig + silu * (1.0 - sig))).astype(BF)
            second_v[rows, cols] = silu.astype(BF)
            mid_v[rows, cols] = (silu * up).astype(BF)

    def feed_project(rows):
        return dot(mid_v[rows, :], tall_v[...]) * SCALE

    def feed_unhidden(here, rows):
        half = FP // 2

        for part in range(2):
            cols = pl.ds(part * half, half)
            d_mid = dot(g_v[here, :], tall_t[:, cols]) * SCALE
            first_v[rows, cols] = (d_mid * first_v[rows, cols].astype(F32)).astype(BF)
            second_v[rows, cols] = (d_mid * second_v[rows, cols].astype(F32)).astype(BF)

    def feed_back(rows):
        return dot(first_v[rows, :], wide_t[0]) + dot(second_v[rows, :], wide_t[1])

    def attend_hidden(kind, phase, micro, part, rows):
        width = low_width(kind)
        span = ROWS * (part + 1)
        keys_at = pl.ds(pl.multiple_of(micro * LEN, LEN), span)
        step = micro * CHUNKS_OF + part
        first_v[rows, pl.ds(0, 2 * width)] = (dot(h_v[rows, :], wide_v[0, :, pl.ds(0, 2 * width)]) * SCALE).astype(BF)
        second_v[rows, pl.ds(0, D)] = (dot(h_v[rows, :], wide_v[1, :, pl.ds(0, D)]) * SCALE).astype(BF)
        cols = pl.ds(0, span)
        index = phase * MICRO + micro
        own_docs = jnp.broadcast_to(docs_v[index, :, pl.ds(part * ROWS, ROWS)], (8, ROWS))
        mask_v[:, cols] = mask_of(kind, own_docs.T[:, 0:1], docs_v[index, :, cols], part * ROWS)

        def block(t, carry):
            index = query_index(kind, t)
            queries = first_v[rows, block_of(index)]
            keys = first_v[keys_at, block_of(index, width)]
            values = second_v[keys_at, block_of(t)]
            heads = [lanes_of_head(kind, t, half) for half in range(2)]
            scores = (dot_t(both(heads, queries), keys) * root_of(kind)).reshape(2, ROWS, span)
            mask = mask_v[:, cols]
            if kind == WINDOW:
                kept = jnp.where((mask > 0.0)[None], scores, -1e30)
                raised = jnp.exp(kept - jnp.max(kept, axis=2, keepdims=True))
            else:
                slope = mask[None] * (1.0 + scores)
                kept_at(kind, (steps + step) * 8 + t)[:, cols] = slope.astype(BF).reshape(2 * ROWS, span)
                raised = 0.5 * (mask[None] + slope * slope)
            raised = raised.astype(BF).reshape(2 * ROWS, span)
            kept_at(kind, step * 8 + t)[:, cols] = raised
            summed = dot(raised, jnp.concatenate([values, jnp.ones((span, 128), BF)], axis=1))
            inverse = 1.0 / summed[:, 128:]
            sides = [lanes_of_value(half) for half in range(2)]
            mid_v[rows, block_of(t)] = merge(sides, summed[:, :128] * inverse).astype(BF)
            inverse_v[rows, block_of(t)] = merge(sides, inverse)
            return carry

        lax.fori_loop(0, 8, block, 0, unroll=UNROLL)

    def attend_project(kind, rows):
        return dot(mid_v[rows, pl.ds(0, D)], tall_v[pl.ds(0, D), :]) * out_scale(kind)

    def attend_unhidden(kind, micro, part, here, rows):
        width = low_width(kind)
        span = ROWS * (part + 1)
        keys_at = pl.ds(pl.multiple_of(micro * LEN, LEN), span)
        own = pl.ds(0, span)
        step = micro * CHUNKS_OF + part
        d_mixed = dot(g_v[here, :], tall_t[:, pl.ds(0, D)]) * out_scale(kind)
        dy_v[...] = (d_mixed * inverse_v[rows, :]).astype(BF)
        if part == CHUNKS_OF - 1:
            dk_v[...] = jnp.zeros_like(dk_v)
            dv_v[...] = jnp.zeros_like(dv_v)
        if kind == LINEAR:
            dq_v[...] = jnp.zeros_like(dq_v)

        def block(t, carry):
            index = query_index(kind, t)
            queries = first_v[rows, block_of(index)]
            keys = first_v[keys_at, block_of(index, width)]
            values = second_v[keys_at, block_of(t)]
            heads = [lanes_of_head(kind, t, half) for half in range(2)]
            sides = [lanes_of_value(half) for half in range(2)]
            d_mixed = both(sides, dy_v[:, block_of(t)])
            mixed = mid_v[rows, block_of(t)].astype(F32)
            shift = jnp.sum(d_mixed.astype(F32) * jnp.concatenate([mixed, mixed], axis=0), axis=1, keepdims=True)
            d_weights = dot_t(d_mixed, values) - shift
            raised = kept_at(kind, step * 8 + t)[:, own]
            slope = raised if kind == WINDOW else kept_at(kind, (steps + step) * 8 + t)[:, own]
            d_scores = (slope.astype(F32) * d_weights).astype(BF)
            dv_v[own, block_of(t)] += dot_0(raised, d_mixed)
            d_queries = merge(heads, dot(d_scores, keys)) * root_of(kind)
            dk_v[own, block_of(index)] += dot_0(d_scores, both(heads, queries)) * root_of(kind)
            if kind == WINDOW:
                dq_v[:, block_of(t)] = d_queries
            else:
                dq_v[:, block_of(index)] += d_queries
            return carry

        lax.fori_loop(0, 8, block, 0, unroll=UNROLL)
        done = pl.ds(part * ROWS, ROWS)
        first_v[rows, pl.ds(0, width)] = dq_v[:, pl.ds(0, width)].astype(BF)
        first_v[rows, pl.ds(width, width)] = dk_v[done, pl.ds(0, width)].astype(BF)
        second_v[rows, pl.ds(0, D)] = dv_v[done, :].astype(BF)

    def attend_back(kind, rows):
        width = low_width(kind)
        total = dot(first_v[rows, pl.ds(0, 2 * width)], wide_t[0, pl.ds(0, 2 * width), :])
        total += dot(second_v[rows, pl.ds(0, D)], wide_t[1, pl.ds(0, D), :])
        return total

    @pl.when(section == last)
    def _():
        turn_weights(FP, FP)

    @pl.when(section == WINDOW)
    def _():
        turn_weights(2 * D, D)

    def one_phase(phase, carry):
        own = phase == 0

        @pl.when(is_feed(section))
        def _():
            turns = jnp.where(own & (section == last), MICRO, 1)
            span = steps // turns

            def backward(step):
                micro, part = step // CHUNKS_OF, CHUNKS_OF - 1 - lax.rem(step, CHUNKS_OF)
                backward_step(phase, micro * CHUNKS_OF + part, feed_unhidden, feed_back)

            def turn(index):
                here = (index * span, index * span + span)
                each(*here, lambda step: forward_step(phase, step, feed_hidden, feed_project))

                @pl.when(own & (section < last))
                def _():
                    turn_weights(FP, FP)

                each(*here, backward)

            each(0, turns, turn)

        for kind in (WINDOW, LINEAR):

            @pl.when(section == kind)
            def _(kind=kind):
                def forward(micro, inner):
                    for part in range(CHUNKS_OF):
                        forward_step(
                            phase,
                            micro * CHUNKS_OF + part,
                            functools.partial(attend_hidden, kind, phase, micro, part),
                            functools.partial(attend_project, kind),
                        )
                    return inner

                lax.fori_loop(0, MICRO, forward, 0)

        for kind in (WINDOW, LINEAR):

            @pl.when(section == kind)
            def _(kind=kind):
                def backward(micro, inner):
                    for part in reversed(range(CHUNKS_OF)):
                        backward_step(
                            phase,
                            micro * CHUNKS_OF + part,
                            functools.partial(attend_unhidden, kind, micro, part),
                            functools.partial(attend_back, kind),
                        )
                    return inner

                if kind == LINEAR:
                    turn_weights(2 * low_width(kind), D)
                lax.fori_loop(0, MICRO, backward, 0)

        @pl.when(own & gives)
        def _():
            far_copy(2).start()

        def finish(step, inner):
            @pl.when(own)
            def _():
                @pl.when(section > 0)
                def _():
                    for piece in range(HANDS):
                        hand_back(step, piece).wait_send()

                gradient_out(step).wait()

            for copy in forward_outs(phase, step) + backward_outs(phase, step):
                copy.wait()
            return inner

        lax.fori_loop(0, steps, finish, 0)

        @pl.when(own & takes)
        def _():
            far_copy(3).wait_recv()

        return carry

    lax.fori_loop(0, jnp.where(takes, 2, 1), one_phase, 0)
    d_gain[...] = gain_sum[...]

    @pl.when(takes)
    def _():
        far_copy(2).wait_recv()
        d_gain[...] += far_gain[...]

    @pl.when(gives)
    def _():
        for kind in range(2):
            for step in range(steps):
                for piece in range(HANDS):
                    far_copy(kind, step, piece).wait_send()
        far_copy(2).wait_send()
        far_copy(3).wait_send()


UNROLL = 4


def train(tokens, cotangent, flat, lengths, swapping):
    count = MICRO * LEN
    steps = MICRO * CHUNKS_OF
    kept = 2 * count if swapping else count
    return pl.pallas_call(
        functools.partial(train_kernel, swapping),
        out_shape=(
            jax.ShapeDtypeStruct((count, D), BF),
            jax.ShapeDtypeStruct((count, D), F32),
            jax.ShapeDtypeStruct((kept, D), BF),
            jax.ShapeDtypeStruct((kept, FP), BF),
            jax.ShapeDtypeStruct((kept, FP), BF),
            jax.ShapeDtypeStruct((kept, FP), BF),
            jax.ShapeDtypeStruct((kept, D), BF),
            jax.ShapeDtypeStruct((8, D), F32),
        ),
        in_specs=[any_spec()] * 3 + [pl.BlockSpec(memory_space=pltpu.SMEM)],
        out_specs=(any_spec(),) * 7 + (vmem_spec(),),
        scratch_shapes=[
            pltpu.VMEM((2, D, FP), BF),
            pltpu.VMEM((FP, D), BF),
            pltpu.VMEM((1, D), BF),
            pltpu.VMEM((2 * MICRO, 1, LEN), F32),
            pltpu.VMEM((2 * count, D), BF),
            pltpu.VMEM((count, D), BF),
            pltpu.VMEM((count, D), BF),
            pltpu.VMEM((2 * count, D), BF),
            pltpu.VMEM((count, D), F32),
            pltpu.VMEM((count, FP), BF),
            pltpu.VMEM((count, FP), BF),
            pltpu.VMEM((count, FP), BF),
            pltpu.VMEM((ROWS, D), F32),
            pltpu.VMEM((8, D), F32),
            pltpu.VMEM((8, D), F32),
            pltpu.VMEM((2, FP, D), BF),
            pltpu.VMEM((D, FP), BF),
            pltpu.VMEM((count, D), F32),
            pltpu.VMEM((ROWS, LEN), F32),
            pltpu.VMEM((ROWS, D), BF),
            pltpu.VMEM((ROWS, D), F32),
            pltpu.VMEM((LEN, D), F32),
            pltpu.VMEM((LEN, D), F32),
            pltpu.VMEM((AHEAD, 1, PAIR_STEP), BF),
            pltpu.VMEM((PAIR_STEP // 128, 128), F32),
            pltpu.VMEM((22, 32, 128), F32),
            pltpu.SemaphoreType.DMA((AHEAD,)),
            pltpu.SemaphoreType.DMA,
            pltpu.SemaphoreType.DMA((2,)),
            pltpu.SemaphoreType.DMA((3, steps)),
            pltpu.SemaphoreType.DMA((4, steps)),
            pltpu.SemaphoreType.DMA((steps, HANDS)),
            pltpu.SemaphoreType.DMA((steps, HANDS)),
            pltpu.SemaphoreType.DMA((steps, HANDS)),
            pltpu.SemaphoreType.DMA((steps, HANDS)),
            pltpu.SemaphoreType.DMA((4, steps, HANDS)),
            pltpu.SemaphoreType.DMA((4, steps, HANDS)),
        ],
        compiler_params=pltpu.CompilerParams(
            collective_id=0, has_side_effects=True, vmem_limit_bytes=62 * MIB
        ),
        name="train",
    )(tokens, cotangent, flat, lengths)


HEAD_ROWS = 16
PAIRS = 64
PAIR_ROWS = PAIRS * 43
PAIR_TILES = D // 2 // PAIRS
CHUNKS = 11


class Products:
    def __init__(self, sources, scratch, base):
        self.normed, self.d_first, self.d_second, self.middle, self.grads, self.d_gain = sources
        self.left_v, self.d_v, self.woven, self.stage, self.in_sem = scratch
        self.base = base

    def fetch(self, source, target, index):
        return pltpu.make_async_copy(source, target, self.in_sem.at[index])

    def loads(self, names):
        count = self.left_v.shape[1]
        some = pl.ds(0, MICRO * LEN)
        every = pl.ds(0, count)
        low, both, high = pl.ds(0, D), pl.ds(0, 2 * D), pl.ds(D, D)
        table = {
            "h": (self.normed, self.left_v.at[0], 0),
            "g": (self.grads, self.left_v.at[1], 1),
            "first": (self.d_first, self.d_v.at[0], 2),
            "second": (self.d_second, self.d_v.at[1], 3),
            "middle": (self.middle, self.d_v.at[self.middle_slot()], 4),
        }
        for prefix, rows in (("all_", every), ("some_", some)):
            table[prefix + "h"] = (self.normed.at[rows, :], self.left_v.at[0, rows, :], 0)
            table[prefix + "mixed"] = (self.middle.at[rows, low], self.left_v.at[1, rows, :], 1)
            table[prefix + "low"] = (self.d_first.at[rows, both], self.d_v.at[0, rows, both], 2)
            table[prefix + "value"] = (self.d_second.at[rows, low], self.d_v.at[1, rows, low], 3)
            few = pl.ds(0, 2 * HEADS * FEAT)
            table["few_low"] = (self.d_first.at[some, few], self.d_v.at[0, some, few], 2)
            table[prefix + "g"] = (self.grads.at[rows, :], self.d_v.at[1, rows, high], 4)
        return [self.fetch(*table[name]) for name in names]

    def middle_slot(self):
        return 2 if self.d_v.shape[0] == 3 else 0

    def head(self, out):
        stage = self.stage
        stage[pl.ds(0, 8), :] = jnp.zeros((8, 128), F32)
        stage[pl.ds(8, 8), :] = self.d_gain[0:1, :].reshape(8, 128)
        out[pl.ds(0, 16), :] = stage[pl.ds(0, 16), :].astype(BF)

    def cut(self, out, first_row, rows, piece, scale):
        target_row = first_row - self.base

        def step(j, carry):
            source = pl.ds(pl.multiple_of(j * piece, 16), piece)
            target = pl.ds(pl.multiple_of(target_row + j * piece, 16), piece)
            out[target, :] = (self.stage[source, :] * scale).astype(BF)
            return carry

        lax.fori_loop(0, rows // piece, step, 0)

    def pairs(self, which, first_pair):
        count = PAIRS
        stage, woven = self.stage, self.woven
        half = FP // 2
        low_half = lax.broadcasted_iota(jnp.int32, (count, 128), 1) < 64
        left = self.left_v[0, :, pl.ds(pl.multiple_of(2 * first_pair, 128), 2 * count)]
        for part in range(2):
            piece = dot_0(left, self.d_v[which, :, pl.ds(part * half, half)])
            for c in range(11):
                woven[11 * part + c, pl.ds(0, 2 * count), :] = piece[:, 128 * c : 128 * c + 128]
        for c in range(22):
            stage[pl.ds(c, count, stride=43), :] = woven[c, pl.ds(0, count, stride=2), :]
        before = woven[21, pl.ds(0, count, stride=2), :]
        for c in range(22):
            here = pltpu.roll(woven[c, pl.ds(1, count, stride=2), :], 64, 1)
            stage[pl.ds(21 + c, count, stride=43), :] = jnp.where(low_half, before, here)
            before = here

    def pair_tile(self, out, k, tail_only):
        self.pairs(k // PAIR_TILES, lax.rem(k, PAIR_TILES) * PAIRS)

        @pl.when(jnp.logical_not(tail_only))
        def _():
            self.cut(out, HEAD_ROWS + k * PAIR_ROWS, PAIR_ROWS, 688, SCALE)

        @pl.when(tail_only)
        def _():
            target = pl.ds(pl.multiple_of((k + 1) * PAIR_ROWS - self.base, 16), 16)
            out[target, :] = (self.stage[pl.ds(PAIR_ROWS - 16, 16), :] * SCALE).astype(BF)

    def tall(self, out, left, right, stride, rows, first_row, scale, piece):
        product = dot_0(left, right)
        for c in range(stride):
            self.stage[pl.ds(c, rows, stride=stride), :] = product[:, 128 * c : 128 * c + 128]
        self.cut(out, first_row, rows * stride, piece, scale)

    def down_tile(self, out, j):
        left = self.d_v[self.middle_slot(), :, pl.ds(pl.multiple_of(256 * j, 256), 256)]
        self.tall(out, left, self.left_v[1], 8, 256, DOWN_ROW + 2048 * j, SCALE, 512)

    def window_tile(self, out, k):
        which = k // 4
        left = self.left_v[which // 3, :, block256(lax.rem(k, 4))]
        right = self.d_v[which // 2, :, pl.ds(pl.multiple_of(lax.rem(which, 2) * D, D), D)]
        scale = jnp.where(which < 3, SCALE, out_scale(WINDOW))
        self.tall(out, left, right, 8, 256, HEAD_ROWS + 2048 * k, scale, 512)

    def low_tile(self, out, k):
        some = pl.ds(0, MICRO * LEN)
        width = HEADS * FEAT
        right = self.d_v[0, some, pl.ds(pl.multiple_of(k * width, width), width)]
        self.tall(out, self.left_v[0, some, :], right, 2, D, HEAD_ROWS + k * 2048, SCALE, 512)

    def value_tile(self, out, k):
        some = pl.ds(0, MICRO * LEN)
        left = self.left_v[k // 4, some, block256(lax.rem(k, 4))]
        right = self.d_v[1, some, pl.ds(pl.multiple_of(k // 4 * D, D), D)]
        scale = jnp.where(k < 4, SCALE, out_scale(LINEAR))
        self.tall(out, left, right, 8, 256, HEAD_ROWS + 2048 * (k + 2), scale, 512)


DOWN_ROW = HEAD_ROWS + 2 * PAIR_TILES * PAIR_ROWS
DOWN_TILES = FP // 256
WINDOW_END = HEAD_ROWS + 4 * 8192
LINEAR_END = HEAD_ROWS + 20480


def product_scratch(count, slots):
    return [
        pltpu.VMEM((2, count, D), BF),
        pltpu.VMEM((slots, count, FP), BF),
        pltpu.VMEM((22, 2 * PAIRS, 128), F32),
        pltpu.VMEM((4096, 128), F32),
        pltpu.SemaphoreType.DMA((5,)),
    ]


def clear(out, first_row, rows):
    def step(i, carry):
        out[pl.ds(pl.multiple_of(first_row + i * 128, 16), 128), :] = jnp.zeros((128, 128), BF)
        return carry

    lax.fori_loop(0, rows // 128, step, 0)
    if rows % 128:
        out[pl.ds(first_row + rows // 128 * 128, rows % 128), :] = jnp.zeros((rows % 128, 128), BF)


def products_kernel(*refs):
    section = lax.axis_index("section")
    work = Products(refs[:6], refs[8:], 0)
    out, out_v = refs[6:8]
    total = out_v.shape[0] - 512
    work.head(out_v)

    def load(*names):
        for copy in work.loads(names):
            copy.start()
        for copy in work.loads(names):
            copy.wait()

    @pl.when(is_feed(section))
    def _():
        load("h", "g", "first", "second", "middle")
        each(0, 2 * PAIR_TILES, lambda k: work.pair_tile(out_v, k, section < 0))
        each(0, DOWN_TILES, lambda j: work.down_tile(out_v, j))

    for kind in (WINDOW, LINEAR):

        @pl.when(section == kind)
        def _(kind=kind):
            load("some_h", "some_mixed", "some_low", "some_value", "some_g")
            if kind == WINDOW:
                each(0, 16, lambda k: work.window_tile(out_v, k))
            else:
                each(0, 2, lambda k: work.low_tile(out_v, k))
                each(0, 8, lambda k: work.value_tile(out_v, k))
            done = WINDOW_END if kind == WINDOW else LINEAR_END
            clear(out_v, done, total - done)

    store = pltpu.make_async_copy(out_v.at[pl.ds(0, total), :], out, work.in_sem.at[0])
    store.start()
    store.wait()


def products(sources, total_rows):
    return pl.pallas_call(
        products_kernel,
        out_shape=jax.ShapeDtypeStruct((total_rows, 128), BF),
        in_specs=[any_spec()] * 5 + [vmem_spec()],
        out_specs=any_spec(),
        scratch_shapes=[pltpu.VMEM((total_rows + 512, 128), BF)] + product_scratch(MICRO * LEN, 3),
        compiler_params=pltpu.CompilerParams(vmem_limit_bytes=60 * MIB),
        name="products",
    )(*sources)


PLACES = 4


def reduce_kernel(*refs):
    section = lax.axis_index("section")
    batch = lax.axis_index("batch")
    place, core = batch // 2, lax.rem(batch, 2)
    mate = place + 1 - 2 * lax.rem(place, 2)
    out, part, own, passing, total, flat, sems = refs[6:13]
    ex_send, ex_recv, send, recv, out_sem = sems
    width = own.shape[1]
    step_rows = width - HEAD_ROWS
    piece = width // CHUNKS
    feed_here = is_feed(section)
    base = jnp.where(feed_here, place // 2, 0) * (4 * step_rows)
    work = Products(refs[:6], refs[13:], base)
    barrier = pltpu.get_barrier_semaphore()

    def greet(other):
        pl.semaphore_signal(barrier, inc=1, device_id=(section, other), device_id_type=MESH)

    window_here = (section == WINDOW) & (place < 2)
    pair_here = feed_here | window_here
    linear_here = section == LINEAR
    sets = (
        (feed_here & (place < 2), ("h", "first")),
        (feed_here & (place == 2), ("middle", "g")),
        (feed_here & (place == 3), ("h", "second")),
        (window_here & (place == 0), ("all_h", "all_value")),
        (window_here & (place == 1), ("all_h", "all_low")),
        (linear_here, ("some_h", "few_low")),
    )
    for here, names in sets:

        @pl.when(here)
        def _(names=names):
            for copy in work.loads(names):
                copy.start()

    greet(2 * place + 1 - core)

    @pl.when(place > 0)
    def _():
        greet(batch - 2)

    @pl.when(place < PLACES - 1)
    def _():
        greet(batch + 2)

    @pl.when(base == 0)
    def _():
        work.head(part)

    pl.semaphore_wait(barrier, jnp.where((place > 0) & (place < PLACES - 1), 3, 2))
    for here, names in sets:

        @pl.when(here)
        def _(names=names):
            for copy in work.loads(names):
                copy.wait()

    late_sets = (
        (feed_here & (place < 2), ("second",)),
        (feed_here & (place == 2), ("h", "second")),
        (feed_here & (place == 3), ("middle", "g")),
        (window_here & (place == 0), ("all_mixed", "all_g", "all_low")),
        (window_here & (place == 1), ("all_value", "all_mixed", "all_g")),
        (linear_here, ("some_mixed", "some_value", "some_g")),
    )

    def late(act):
        for here, names in late_sets:

            @pl.when(here)
            def _(names=names):
                for copy in work.loads(names):
                    act(copy)

    late(lambda copy: copy.start())

    def rows_of(i):
        return pl.ds(pl.multiple_of(i * piece, 16), piece)

    def share(index, i):
        return pl.ds(pl.multiple_of(step_rows * index - base + i * piece, 16), piece)

    def swap(to, i):
        slot = lax.rem(to, 2)
        return pltpu.make_async_remote_copy(
            src_ref=part.at[share(2 * to + 1 - core, i), :],
            dst_ref=own.at[slot, rows_of(i), :],
            send_sem=ex_send.at[slot, i],
            recv_sem=ex_recv.at[slot, i],
            device_id=(section, 2 * place + 1 - core),
            device_id_type=MESH,
        )

    def go(source, slot, to, i, other):
        return pltpu.make_async_remote_copy(
            src_ref=source,
            dst_ref=passing.at[slot, rows_of(i), :],
            send_sem=send.at[lax.rem(to, 2), i],
            recv_sem=recv.at[slot, i],
            device_id=(section, other),
            device_id_type=MESH,
        )

    def arrived(slot, i):
        here = passing.at[slot, rows_of(i), :]
        pltpu.make_async_copy(here, here, recv.at[slot, i]).wait()

    def release(to, before, after, limits=(CHUNKS, CHUNKS)):
        def bound(row, parity):
            most = jnp.where(parity == 0, limits[0], limits[1])
            return jnp.minimum(jnp.maximum(row - parity * step_rows, 0) // piece, most)

        def add(i):
            slot = lax.rem(to, 2)
            rows = rows_of(i)
            swap(to, i).wait_recv()
            mine = part[share(2 * to + core, i), :].astype(F32)
            own[slot, rows, :] = (own[slot, rows, :].astype(F32) + mine).astype(BF)
            source = own.at[slot, rows, :]

            @pl.when(pair_here & (to == mate))
            def _():
                go(source, 0, to, i, 2 * mate + core).start()

            @pl.when(linear_here & (place == PLACES - 1))
            def _():
                go(source, slot, to, i, batch - 2).start()

            @pl.when(linear_here & (place == 0) & (to == 1))
            def _():
                go(source, 2, to, i, batch + 2).start()

        each(bound(before, 1 - core), bound(after, 1 - core), lambda i: swap(to, i).start())
        each(bound(before, core), bound(after, core), add)

    def swapped(to, limits=(CHUNKS, CHUNKS)):
        each(0, jnp.where(core == 0, limits[1], limits[0]), lambda i: swap(to, i).wait_send())

    def store(which):
        rows = out.shape[1] // 128
        early = (CHUNKS - 1) * piece - 32
        begin, size = ((0, early), (early, rows - early))[which]
        source = pl.ds(pl.multiple_of((8 + batch + begin) * 128, 128), size * 128)
        return pltpu.make_async_copy(
            flat.at[:, source], out.at[:, pl.ds(begin * 128, size * 128)], out_sem.at[which]
        )

    def emit(i):
        cols = pl.ds(pl.multiple_of(i * piece * 128, 1024), piece * 128)
        flat[0:1, cols] = total[...].reshape(1, piece * 128)

    whole = 2 * step_rows + HEAD_ROWS

    @pl.when(feed_here)
    def _():
        upper = place >= 2
        share_tiles = 2 * step_rows // PAIR_ROWS
        upper_tiles = 2 * PAIR_TILES - 2 * share_tiles

        def pair(t):
            turned = jnp.where(t < share_tiles, t + share_tiles, jnp.where(t == share_tiles, share_tiles - 1, t - share_tiles - 1))
            k = jnp.where(place == 0, turned, t)
            k = jnp.where(upper, jnp.where(t == upper_tiles, 2 * share_tiles - 1, 2 * share_tiles + t), k)
            tail_only = upper & (t == upper_tiles)

            @pl.when(jnp.logical_not(upper) & (k == PAIR_TILES))
            def _():
                late(lambda copy: copy.wait())

            work.pair_tile(part, k, tail_only)
            start = HEAD_ROWS + PAIR_ROWS * k - base
            stop = start + PAIR_ROWS
            ends_late = (place == 0) & (k == share_tiles - 1)
            to = base // (2 * step_rows)
            early = jnp.where(k == share_tiles - 2, whole, jnp.where(k < share_tiles - 2, stop, start))
            before_0 = jnp.where(tail_only, 0, jnp.where(upper & (k == 2 * share_tiles), piece, start))
            after_0 = jnp.where(tail_only, piece, jnp.where(place == 0, early, stop))
            release(to, before_0, after_0)
            before_1 = jnp.where(ends_late, 0, jnp.where((place == 0) & (k == share_tiles), piece, start - 2 * step_rows))
            after_1 = jnp.where(ends_late, piece, stop - 2 * step_rows)
            release(to + 1, before_1, after_1)

        def down(j):
            work.down_tile(part, j)
            start = DOWN_ROW + 2048 * j - base
            stop = start + 2048
            early = jnp.where(j == 1, whole, jnp.where(j < 1, stop, start))
            release(2, start, jnp.where(place == 2, early, stop))
            release(3, start - 2 * step_rows, stop - 2 * step_rows)

        def turn(t):
            @pl.when(t == 1)
            def _():
                @pl.when(place == 2)
                def _():
                    late(lambda copy: copy.wait())

                each(0, jnp.where(upper, upper_tiles + 1, 2 * share_tiles), pair)

                @pl.when(place == 3)
                def _():
                    late(lambda copy: copy.wait())

            mate_first = place == 2
            first = jnp.where(mate_first & (t == 0), 2, 0)
            last = jnp.where(mate_first & (t == 1), 2, DOWN_TILES)
            here = upper & (mate_first | (t == 1))
            each(first, jnp.where(here, last, first), down)

        each(0, 2, turn)
        swapped(mate)
        swapped(place)

    @pl.when(window_here)
    def _():
        def tile(t, carry):
            k = lax.rem(t + jnp.where(place == 0, 8, 0), 16)

            @pl.when(t == jnp.where(place == 0, 4, 8))
            def _():
                late(lambda copy: copy.wait())

            work.window_tile(part, k)
            start = HEAD_ROWS + 2048 * k
            stop = start + 2048

            @pl.when(k == 15)
            def _():
                clear(part, WINDOW_END, 4 * step_rows + HEAD_ROWS - WINDOW_END)

            stop_0 = jnp.where(place == 0, jnp.where(k < 7, stop, jnp.where(k == 7, whole, start)), stop)
            stop_1 = jnp.where(k == 15, whole, stop - 2 * step_rows)
            release(0, start, stop_0)
            release(1, start - 2 * step_rows, stop_1)
            return carry

        lax.fori_loop(0, 16, tile, 0)
        for to in range(2):
            swapped(to)

    @pl.when(linear_here)
    def _():
        filled = [max(0, min(CHUNKS, -(-(LINEAR_END - step_rows * index) // piece))) for index in range(4)]
        limits = (tuple(filled[:2]), tuple(filled[2:]))
        cover = max(step_rows * index + piece * filled[index] for index in range(4) if filled[index])
        clear(part, LINEAR_END, cover - LINEAR_END)

        def low(k):
            work.low_tile(part, k)
            start = HEAD_ROWS + 2048 * k
            release(0, start, start + 2048, limits[0])

        def value(k):
            work.value_tile(part, k)
            start = HEAD_ROWS + 2048 * (k + 2)
            stop = jnp.where(k == 7, cover, start + 2048)
            release(0, start, stop, limits[0])
            release(1, start - 2 * step_rows, stop - 2 * step_rows, limits[1])

        def pass_on(to, i):
            rows = rows_of(i)
            arrived(to, i)
            added = passing[to, rows, :].astype(F32) + own[to, rows, :].astype(F32)
            passing[to, rows, :] = added.astype(BF)
            go(passing.at[to, rows, :], to, to, i, batch - 2).start()

        ahead = jnp.where((place == 2) & (core == 0), 2, 0)

        def value_and_on(k):
            value(k)
            done, next_done = jnp.maximum(k - 2, 0) // 2, jnp.maximum(k - 1, 0) // 2
            each(jnp.minimum(done, ahead), jnp.minimum(next_done, ahead), functools.partial(pass_on, 0))

        each(0, 2, low)
        late(lambda copy: copy.wait())
        each(0, 8, value_and_on)

        def own_count(to):
            return jnp.where(core == 0, limits[to][0], limits[to][1])

        @pl.when((place == 1) | (place == 2))
        def _():
            each(ahead, own_count(0), functools.partial(pass_on, 0))

        @pl.when(place == 2)
        def _():
            each(0, own_count(1), functools.partial(pass_on, 1))

        for to in range(2):
            swapped(to, limits[to])

        def sum_up(i):
            rows = rows_of(i)

            @pl.when((place == 0) & (i < own_count(0)))
            def _():
                arrived(0, i)
                total[...] = own[0, rows, :].astype(F32) + passing[0, rows, :].astype(F32)

            @pl.when((place == 1) & (i < own_count(1)))
            def _():
                arrived(1, i)
                arrived(2, i)
                both_ways = passing[1, rows, :].astype(F32) + passing[2, rows, :].astype(F32)
                total[...] = own[1, rows, :].astype(F32) + both_ways

            emit(i)

        here = jnp.where(place == 0, own_count(0), jnp.where(place == 1, own_count(1), 0))
        total[...] = jnp.zeros_like(total)
        each(here, CHUNKS, emit)
        each(0, here - 1, sum_up)

        @pl.when(here == CHUNKS)
        def _():
            store(0).start()

        each(jnp.maximum(here - 1, 0), here, sum_up)

        @pl.when(here < CHUNKS)
        def _():
            store(0).start()

        @pl.when((place == 1) | (place >= 2))
        def _():
            each(0, own_count(0), lambda i: go(passing.at[0, rows_of(i), :], 0, 0, i, batch - 2).wait_send())

        @pl.when((place == 0) | (place >= 2))
        def _():
            each(0, own_count(1), lambda i: go(passing.at[0, rows_of(i), :], 0, 1, i, batch - 2).wait_send())

    @pl.when((section == WINDOW) & (place >= 2))
    def _():
        total[...] = jnp.zeros_like(total)
        each(0, CHUNKS, emit)
        store(0).start()

    @pl.when(pair_here)
    def _():
        slot = lax.rem(place, 2)

        def sum_up(i):
            rows = rows_of(i)
            arrived(0, i)
            total[...] = own[slot, rows, :].astype(F32) + passing[0, rows, :].astype(F32)
            emit(i)

        each(0, CHUNKS - 1, sum_up)
        store(0).start()
        each(CHUNKS - 1, CHUNKS, sum_up)
        other = 2 * mate + core
        each(0, CHUNKS, lambda i: go(passing.at[0, rows_of(i), :], 0, mate, i, other).wait_send())

    store(1).start()
    store(0).wait()
    store(1).wait()


def reduce_products(sources, total_rows, batches):
    step_rows = (total_rows - 8) // batches - 1
    width = step_rows + HEAD_ROWS
    return pl.pallas_call(
        reduce_kernel,
        out_shape=jax.ShapeDtypeStruct((1, (step_rows + 1) * 128), F32),
        in_specs=[any_spec()] * 5 + [vmem_spec()],
        out_specs=any_spec(),
        scratch_shapes=[
            pltpu.VMEM((4 * step_rows + HEAD_ROWS + 512, 128), BF),
            pltpu.VMEM((2, width, 128), BF),
            pltpu.VMEM((3, width, 128), BF),
            pltpu.VMEM((width // CHUNKS, 128), F32),
            pltpu.VMEM((1, width * 128), F32),
            (
                pltpu.SemaphoreType.DMA((2, CHUNKS)),
                pltpu.SemaphoreType.DMA((2, CHUNKS)),
                pltpu.SemaphoreType.DMA((2, CHUNKS)),
                pltpu.SemaphoreType.DMA((3, CHUNKS)),
                pltpu.SemaphoreType.DMA((2,)),
            ),
        ]
        + product_scratch(2 * MICRO * LEN, 2),
        compiler_params=pltpu.CompilerParams(
            collective_id=1, has_side_effects=True, vmem_limit_bytes=60 * MIB
        ),
        name="reduce_products",
    )(*sources)


def shards(tokens, cotangent, params, lengths):
    batches = lax.axis_size("batch")
    paired = batches == 2 * PLACES
    acts, d_inputs, normed, middle, d_first, d_second, grads, d_gain = train(
        tokens, cotangent, params, lengths, paired
    )
    total_rows = params.shape[1] // 128 + 8
    sources = (normed, d_first, d_second, middle, grads, d_gain)
    if paired:
        mine = reduce_products(sources, total_rows, batches)
    else:
        parts = products(sources, total_rows)
        mine = lax.psum_scatter(parts[8:].reshape(-1), "batch", scatter_dimension=0, tiled=True)
        mine = mine.astype(F32)[None]
    return acts[None], d_inputs[None], mine


def solution(mesh):
    return jax.shard_map(
        shards,
        mesh=mesh,
        in_specs=(P("batch", None), P("batch", None), P("section", None), P("batch", None, None)),
        out_specs=(P("section", "batch", None), P("section", "batch", None), P("section", "batch")),
        check_vma=False,
    )
```
